32 devices in a mesh: gx: 2 (over y), gy: 4 (over z), gz: 4 (over x, core).
Axes of the slice: x: 2, y: 2, z: 4, core: 2. Of those that a mesh axis runs over, the one named last changes fastest.
Arguments:
- checkpoint_store: bfloat16 [32, 9, 1, 32, 256], P('gz', None, None, 'gy', 'gx'), may hold values from -6 to 6
- holder_peer: int32 [2, 4, 4, 8], P('gx', 'gy'), may hold values from 0 to 3, as said below
- holder_slot: int32 [2, 4, 4, 8], P('gx', 'gy'), may hold values from 0 to 7, as said below
- adjoint_state: float32 [9, 32, 32, 256], P(None, 'gz', 'gy', 'gx'), may hold values from -6 to 6
- lame_lambda: float32 [32, 32, 256], P('gz', 'gy', 'gx'), may hold values from 0.1 to 0.3
- lame_mu: float32 [32, 32, 256], P('gz', 'gy', 'gx'), may hold values from 0.05 to 0.15
- buoyancy: float32 [32, 32, 256], P('gz', 'gy', 'gx'), may hold values from 0.25 to 0.5
- source_cell: int32 [4, 4, 2, 4], P('gz', 'gy', 'gx'), may hold values from 0 to 8191
- wavelet: float32 [64], replicated, may hold values from -6 to 6
- receiver_cell: int32 [4, 4, 2, 64], P('gz', 'gy', 'gx'), may hold values from 0 to 8191
- traces: float32 [4, 4, 2, 64, 64], P('gz', 'gy', 'gx'), may hold values from -6 to 6
- plan: int32 [2], replicated, may hold values from 0 to 63
Outputs:
- adjoint_final: float32 [9, 32, 32, 256], P(None, 'gz', 'gy', 'gx')
- image_lambda: float32 [32, 32, 256], P('gz', 'gy', 'gx')
- image_mu: float32 [32, 32, 256], P('gz', 'gy', 'gx')
The draws below stay inside these ranges and needn't reach their ends.
Inputs may be any that keep to these rules, and one draw needn't show every extreme that they name: `holder_peer`: within each group of bricks sharing x and y bricks, every holder's 8 slots hold exactly one piece each; for every brick one holder supplies exactly 5 of its pieces and each other holder exactly one. `holder_slot`: slots of one holder are distinct over the pieces it holds.
All inputs are finite; a program needn't handle non-finite values.
Results may differ from the reference program's by a relative error of at most 0.0003.
Values may be sent and summed in bfloat16 or wider, within the bound.
No kernel may reach another device: no remote copies, remote signals or barrier semaphores. Data moves between devices by JAX's collectives and lax.ppermute only.
A program may use at most 128 MiB of HBM per device.

```python
import jax
import jax.numpy as jnp

CX = 128
CY = 8
CZ = 8
PIECES = 8
STEPS = 2
NT = 64
SRC_DEV = 4
REC_DEV = 64
LAYERS = 1
CAP = 5
SLOTS = 32
NX = 256
NY = 32
NZ = 32
N_GX = 2
N_GY = 4
N_GZ = 4


def holder_tables(key):
    base_key = jax.random.fold_in(key, 11)
    key_rotation, key_ordering, key_slotting = jax.random.split(base_key, 3)
    groups = N_GX * N_GY
    rotation = jax.random.randint(key_rotation, (groups, 1, 1), 0, N_GZ)
    requester = jnp.arange(N_GZ, dtype=jnp.int32)[None, :, None]
    piece_index = jnp.arange(PIECES, dtype=jnp.int32)[None, None, :]
    favoured = (requester + rotation) % N_GZ
    others = (requester + rotation + 1 + piece_index - CAP) % N_GZ
    listed = jnp.where(piece_index < CAP, favoured, others)
    listed = jnp.broadcast_to(listed, (groups, N_GZ, PIECES))
    scores = jax.random.randint(key_ordering, (groups, N_GZ, PIECES), 0, 65536) * PIECES + piece_index
    ordering = jnp.argsort(scores, axis=-1)
    peers = jnp.take_along_axis(listed, ordering, axis=-1)
    item_count = N_GZ * PIECES
    flat_peers = peers.reshape(groups, item_count)
    slot_scores = jax.random.randint(key_slotting, (groups, item_count), 0, 65536) * item_count + jnp.arange(item_count, dtype=jnp.int32)[None, :]
    same_holder = flat_peers[:, :, None] == flat_peers[:, None, :]
    earlier = slot_scores[:, None, :] < slot_scores[:, :, None]
    slots = jnp.sum((same_holder & earlier).astype(jnp.int32), axis=2)
    return (peers.reshape(N_GX, N_GY, N_GZ, PIECES).astype(jnp.int32), slots.reshape(N_GX, N_GY, N_GZ, PIECES).astype(jnp.int32))


def draw_holder_peer(key, part):
    return holder_tables(key)[0]


def draw_holder_slot(key, part):
    return holder_tables(key)[1]


def place_ends(result, rng, least, high):
    shape = result.shape
    place = [jax.random.randint(jax.random.fold_in(rng, axis), (), 0, shape[axis]) for axis in range(len(shape))]
    result = result.at[tuple(place)].set(least)
    longest = shape.index(max(shape))
    place[longest] = (place[longest] + 1) % shape[longest]
    return result.at[tuple(place)].set(high)


def block_scale(own_key, shape, cuts, least, high):
    loudness, own = 1.0, jax.random.fold_in(own_key, 6)
    for dim, blocks in cuts:
        steps = jnp.exp(jax.random.uniform(jax.random.fold_in(own, dim), (blocks,), jnp.float32, least / len(cuts), high / len(cuts)))
        loudness = loudness * jnp.repeat(steps, shape[dim] // blocks).reshape([-1 if axis == dim else 1 for axis in range(len(shape))])
    return loudness


def bell_draw(rng, dims, width, most, cuts=(), held_as=jnp.bfloat16):
    factor_of = block_scale(rng, dims, cuts, -0.22, 0.18) if cuts else 1.0
    values = jax.random.normal(rng, dims, jnp.float32) * width * factor_of
    return jnp.minimum(jnp.maximum(values, -most), most).astype(held_as)


def setup_inputs(seed: int = 0) -> dict:
    key_of = jax.random.split(jax.random.key(seed), 13)
    checkpoint_store = bell_draw(key_of[0], (SLOTS, 9, LAYERS, NY, NX), 1.0, 6.0, ((0, 4), (3, 4), (4, 2)))
    holder_peer = draw_holder_peer(jax.random.fold_in(key_of[12], 71), 0)
    holder_slot = draw_holder_slot(jax.random.fold_in(key_of[12], 71), 0)
    adjoint_state = bell_draw(key_of[3], (9, NZ, NY, NX), 1.0, 6.0, ((1, 4), (2, 4), (3, 2)), jnp.float32)
    lame_lambda = jnp.clip(0.1 + 0.20000001043081284 * jax.random.uniform(key_of[4], (NZ, NY, NX), jnp.float32) ** block_scale(key_of[4], (NZ, NY, NX), ((0, 4), (1, 4), (2, 2)), -0.2, 0.2), 0.1, 0.3)
    lame_mu = jnp.clip(0.05 + 0.10000001 * jax.random.uniform(key_of[5], (NZ, NY, NX), jnp.float32) ** block_scale(key_of[5], (NZ, NY, NX), ((0, 4), (1, 4), (2, 2)), -0.2, 0.2), 0.05, 0.15)
    buoyancy = jnp.clip(0.25 + 0.25 * jax.random.uniform(key_of[6], (NZ, NY, NX), jnp.float32) ** block_scale(key_of[6], (NZ, NY, NX), ((0, 4), (1, 4), (2, 2)), -0.2, 0.2), 0.25, 0.5)
    source_cell = place_ends(jax.random.randint(key_of[7], (N_GZ, N_GY, N_GX, SRC_DEV), 0, CZ * CY * CX), jax.random.fold_in(key_of[7], 1), 0, (CZ * CY * CX) - 1).astype(jnp.int32)
    wavelet = bell_draw(key_of[8], (NT,), 1.0, 6.0, (), jnp.float32)
    receiver_cell = place_ends(jax.random.randint(key_of[9], (N_GZ, N_GY, N_GX, REC_DEV), 0, CZ * CY * CX), jax.random.fold_in(key_of[9], 1), 0, (CZ * CY * CX) - 1).astype(jnp.int32)
    traces = bell_draw(key_of[10], (N_GZ, N_GY, N_GX, NT, REC_DEV), 1.0, 6.0, ((0, 4), (1, 4), (2, 2)), jnp.float32)
    plan = jax.random.randint(key_of[11], (STEPS,), 0, NT).astype(jnp.int32)
    return dict(checkpoint_store=checkpoint_store, holder_peer=holder_peer, holder_slot=holder_slot, adjoint_state=adjoint_state, lame_lambda=lame_lambda, lame_mu=lame_mu, buoyancy=buoyancy, source_cell=source_cell, wavelet=wavelet, receiver_cell=receiver_cell, traces=traces, plan=plan)


along_z = 0
along_y = 1
along_x = 2


def shifted(padded, which_axis, offset):
    extents = padded.shape[-3:]
    starts = [1, 1, 1]
    starts[which_axis] = 1 + offset
    return padded[..., starts[0]:starts[0] + extents[0] - 2, starts[1]:starts[1] + extents[1] - 2, starts[2]:starts[2] + extents[2] - 2]


def ahead(padded, which_axis):
    return shifted(padded, which_axis, 1) - shifted(padded, which_axis, 0)


def behind(padded, which_axis):
    return shifted(padded, which_axis, 0) - shifted(padded, which_axis, -1)


def velocity_rates(stress_pad, buoyancy):
    rate_x = buoyancy * (ahead(stress_pad[0], along_x) + behind(stress_pad[3], along_y) + behind(stress_pad[4], along_z))
    rate_y = buoyancy * (behind(stress_pad[3], along_x) + ahead(stress_pad[1], along_y) + behind(stress_pad[5], along_z))
    rate_z = buoyancy * (behind(stress_pad[4], along_x) + behind(stress_pad[5], along_y) + ahead(stress_pad[2], along_z))
    return jnp.stack([rate_x, rate_y, rate_z])


def stress_rates(velocity_pad, lame_lambda, lame_mu):
    strain_xx = behind(velocity_pad[0], along_x)
    strain_yy = behind(velocity_pad[1], along_y)
    strain_zz = behind(velocity_pad[2], along_z)
    dilation = strain_xx + strain_yy + strain_zz
    rate_xx = lame_lambda * dilation + 2.0 * lame_mu * strain_xx
    rate_yy = lame_lambda * dilation + 2.0 * lame_mu * strain_yy
    rate_zz = lame_lambda * dilation + 2.0 * lame_mu * strain_zz
    rate_xy = lame_mu * (ahead(velocity_pad[0], along_y) + ahead(velocity_pad[1], along_x))
    rate_xz = lame_mu * (ahead(velocity_pad[0], along_z) + ahead(velocity_pad[2], along_x))
    rate_yz = lame_mu * (ahead(velocity_pad[1], along_z) + ahead(velocity_pad[2], along_y))
    return jnp.stack([rate_xx, rate_yy, rate_zz, rate_xy, rate_xz, rate_yz])


def imaging_terms(forward_stress, adjoint_stress):
    pressure_fwd = forward_stress[0] + forward_stress[1] + forward_stress[2]
    pressure_adj = adjoint_stress[0] + adjoint_stress[1] + adjoint_stress[2]
    term_lambda = pressure_fwd * pressure_adj
    term_mu = (forward_stress[0] * adjoint_stress[0] + forward_stress[1] * adjoint_stress[1]
               + forward_stress[2] * adjoint_stress[2]
               + 2.0 * (forward_stress[3] * adjoint_stress[3] + forward_stress[4] * adjoint_stress[4]
                        + forward_stress[5] * adjoint_stress[5]))
    return term_lambda, term_mu


def pad_whole(stack):
    return jnp.pad(stack, ((0, 0), (1, 1), (1, 1), (1, 1)))


def global_cells(cells):
    brick_z = jnp.arange(N_GZ, dtype=jnp.int32)[:, None, None, None]
    brick_y = jnp.arange(N_GY, dtype=jnp.int32)[None, :, None, None]
    brick_x = jnp.arange(N_GX, dtype=jnp.int32)[None, None, :, None]
    plane = CY * CX
    z_index = brick_z * CZ + cells // plane
    y_index = brick_y * CY + (cells // CX) % CY
    x_index = brick_x * CX + cells % CX
    return z_index.reshape(-1), y_index.reshape(-1), x_index.reshape(-1)


def inject(stress, cell_lists, values):
    z_index, y_index, x_index = cell_lists
    normal = stress[:3].at[:, z_index, y_index, x_index].add(values)
    return jnp.concatenate([normal, stress[3:]], axis=0)


def reference(checkpoint_store, holder_peer, holder_slot, adjoint_state, lame_lambda, lame_mu, buoyancy,
              source_cell, wavelet, receiver_cell, traces, plan):
    store_view = checkpoint_store.reshape(N_GZ * PIECES, 9, LAYERS, N_GY, CY, N_GX, CX)
    rows = jnp.transpose(holder_peer * PIECES + holder_slot, (2, 3, 1, 0)).astype(jnp.int32)
    brick_y = jnp.arange(N_GY, dtype=jnp.int32)[None, None, :, None]
    brick_x = jnp.arange(N_GX, dtype=jnp.int32)[None, None, None, :]
    picked = store_view[rows, :, :, brick_y, :, brick_x, :]
    state = jnp.transpose(picked, (4, 0, 1, 5, 2, 6, 3, 7)).reshape(9, NZ, NY, NX).astype(jnp.float32)
    source_lists = global_cells(source_cell)
    receiver_lists = global_cells(receiver_cell)
    snapshots = [state[3:]]
    for step_now in range(STEPS):
        velocity = state[:3] + velocity_rates(pad_whole(state[3:]), buoyancy)
        stress = state[3:] + stress_rates(pad_whole(velocity), lame_lambda, lame_mu)
        stress = inject(stress, source_lists, wavelet[plan[step_now]])
        state = jnp.concatenate([velocity, stress], axis=0)
        snapshots.append(stress)
    adjoint = adjoint_state
    image_lambda = jnp.zeros((NZ, NY, NX), jnp.float32)
    image_mu = jnp.zeros((NZ, NY, NX), jnp.float32)
    for step_now in reversed(range(STEPS)):
        samples = traces[:, :, :, plan[step_now], :].reshape(-1)
        stress = inject(adjoint[3:], receiver_lists, samples)
        term_lambda, term_mu = imaging_terms(snapshots[step_now + 1], stress)
        image_lambda = image_lambda + term_lambda
        image_mu = image_mu + term_mu
        stress = stress - stress_rates(pad_whole(adjoint[:3]), lame_lambda, lame_mu)
        velocity = adjoint[:3] - velocity_rates(pad_whole(stress), buoyancy)
        adjoint = jnp.concatenate([velocity, stress], axis=0)
    return adjoint, image_lambda, image_mu
```

```python
import functools

import jax
import jax.numpy as jnp
from jax import lax
from jax.experimental import pallas as pl
from jax.experimental.pallas import tpu as pltpu
from jax.sharding import PartitionSpec as P

VX, VY, VZ, SXX, SYY, SZZ, SXY, SXZ, SYZ = range(9)
FWD, ADJ, BUOY, LAM, MU, INJ, SRC = 0, 9, 18, 19, 20, 21, 22
FIELDS = 23
HALO = 2

ADJ_Y = {VX: (2, 2), VY: (2, 2), VZ: (2, 2), SXX: (1, 1), SYY: (1, 2), SZZ: (1, 1), SXY: (2, 1), SXZ: (1, 1), SYZ: (2, 1)}
ADJ_Z = {VX: (2, 2), VY: (2, 2), VZ: (2, 2), SXX: (1, 1), SYY: (1, 1), SZZ: (1, 2), SXY: (1, 1), SXZ: (2, 1), SYZ: (2, 1)}
FWD_Y = {VX: (1, 2), VY: (2, 1), VZ: (1, 2), SXX: (1, 2), SYY: (2, 2), SZZ: (1, 2), SXY: (2, 2), SXZ: (1, 2), SYZ: (2, 2)}
OTHER = {BUOY: (2, 2), LAM: (1, 2), MU: (2, 2), INJ: (0, 1), SRC: (1, 1)}

F32_Y = {**{ADJ + f: c for f, c in ADJ_Y.items()}, **OTHER}
F32_Z = {**{ADJ + f: c for f, c in ADJ_Z.items()}, **OTHER}

VMEM_LIMIT = 48 * 1024 * 1024


def params():
    return pltpu.CompilerParams(vmem_limit_bytes=VMEM_LIMIT)


def vmem():
    return pl.BlockSpec(memory_space=pltpu.VMEM)


def smem():
    return pl.BlockSpec(memory_space=pltpu.SMEM)


def lo_cells(table, count):
    return [(f, count - d, -d) for f in sorted(table) for d in range(table[f][0], 0, -1)]


def hi_cells(table, count):
    return [(f, d, count + d) for f in sorted(table) for d in range(table[f][1])]


def split(value):
    high = value.astype(jnp.bfloat16)
    low = (value - high.astype(jnp.float32)).astype(jnp.bfloat16)
    return high, low


def joined(high, low):
    return high.astype(jnp.float32) + low.astype(jnp.float32)


def start_kernel(cz, store, adjoint, lam, mu, buoy, source, wavelet, receiver, traces, plan, out, inj):
    rows, lanes = cz * adjoint.shape[2], adjoint.shape[3]
    cells = receiver[...]
    count = cells.shape[1]
    row_hot = (lax.broadcasted_iota(jnp.int32, (rows, count), 0) == cells // lanes).astype(jnp.float32)
    lane_hit = lax.broadcasted_iota(jnp.int32, (lanes, count), 0) == cells % lanes
    for index, step in ((0, 1), (1, 0)):
        sample = traces[pl.ds(plan[step], 1), :]
        field = lax.dot_general(
            row_hot,
            jnp.where(lane_hit, sample, 0.0),
            (((1,), (1,)), ((), ())),
            precision=lax.Precision.HIGHEST,
            preferred_element_type=jnp.float32,
        )
        inj[index] = field.reshape(inj.shape[1:])
    flat = lax.broadcasted_iota(jnp.int32, (rows, lanes), 0) * lanes + lax.broadcasted_iota(jnp.int32, (rows, lanes), 1)
    for step in range(2):
        value = wavelet[plan[step]]
        field = jnp.zeros((rows, lanes), jnp.float32)
        for j in range(source.shape[3]):
            field = field + jnp.where(flat == source[0, 0, 0, j], value, 0.0)
        inj[2 + step] = field.reshape(inj.shape[1:])

    def own(field, layer):
        if field == BUOY:
            return buoy[layer]
        if field == LAM:
            return lam[layer]
        if field == MU:
            return mu[layer]
        if field == INJ:
            return inj[1, layer]
        if field == SRC:
            return inj[2, layer]
        value = adjoint[field - ADJ, layer]
        if SXX <= field - ADJ <= SZZ:
            value = value + inj[0, layer]
        return value

    slots, nine = store.shape[0], store.shape[1]
    for s in range(slots):
        for f in range(nine):
            out[s * nine + f] = store[s, f, 0]
    base = slots * nine
    faces = lo_cells(F32_Z, cz) + hi_cells(F32_Z, cz)
    for i, (field, layer, _) in enumerate(faces):
        high, low = split(own(field, layer))
        out[base + i] = high
        out[base + len(faces) + i] = low


def column_kernel(cz, gathered, peer, slot, place, adjoint, lam, mu, buoy, inj, main, strip, send):
    lanes = main.shape[3]
    layers = cz + 2 * HALO
    pieces = slot.shape[1]
    me, count = place[2], place[3]
    below, above = jnp.maximum(me - 1, 0), jnp.minimum(me + 1, count - 1)
    has_below = (me > 0).astype(jnp.float32)
    has_above = (me < count - 1).astype(jnp.float32)
    base = pieces * 9

    for z in range(layers):
        if z < HALO:
            brick, piece, keep = below, cz - HALO + z, has_below
        elif z < HALO + cz:
            brick, piece, keep = me, z - HALO, None
        else:
            brick, piece, keep = above, z - HALO - cz, has_above
        holder = peer[brick, piece]
        row = slot[brick, piece] * 9
        for f in range(9):
            value = gathered[holder, row + f].astype(jnp.float32)
            main[FWD + f, z] = value if keep is None else value * keep
    own = {BUOY: buoy, LAM: lam, MU: mu, INJ: inj.at[1], SRC: inj.at[2]}
    for z in range(cz):
        for f in range(9):
            value = adjoint[f, z]
            if SXX <= f <= SZZ:
                value = value + inj[0, z]
            main[ADJ + f, HALO + z] = value
        for f, ref in own.items():
            main[f, HALO + z] = ref[z]
    lo, hi = lo_cells(F32_Z, cz), hi_cells(F32_Z, cz)
    total = len(lo) + len(hi)
    zero = jnp.zeros(main.shape[2:], jnp.float32)
    have = {}
    for i, (field, _, index) in enumerate(lo + hi):
        have[field, HALO + index] = i
    for f in range(ADJ, FIELDS):
        for z in (0, 1, layers - 2, layers - 1):
            if (f, z) in have:
                i = have[f, z]
                source, keep = (below, has_below) if z < HALO else (above, has_above)
                main[f, z] = joined(gathered[source, base + i], gathered[source, base + total + i]) * keep
            else:
                main[f, z] = zero

    lane = lax.broadcasted_iota(jnp.int32, main.shape[2:], 1)
    position = lane % 8
    group = lane // 8
    for f in range(FIELDS):
        tile = zero
        for z in range(layers):
            value = main[f, z]
            tail = pltpu.roll(value, (8 * z + 2) % lanes, 1)
            head = pltpu.roll(value, (8 * z + 6) % lanes, 1)
            here = group == z
            tile = jnp.where(here & (position < 2), tail, jnp.where(here & (position >= 6), head, tile))
        strip[f] = tile
        high, low = split(tile)
        send[f] = high
        if f >= ADJ:
            send[FIELDS + f - ADJ] = low


def rows_kernel(cz, cy, main, strip, from_left, from_right, place, strips, up, down, packed):
    lanes = main.shape[3]
    layers = cz + 2 * HALO
    has_left = (place[0] > 0).astype(jnp.float32)
    has_right = (place[0] < place[1] - 1).astype(jnp.float32)
    lane = lax.broadcasted_iota(jnp.int32, main.shape[2:], 1)
    position = lane % 8
    for f in range(FIELDS):
        left, right = from_left[f].astype(jnp.float32), from_right[f].astype(jnp.float32)
        if f >= ADJ:
            left = left + from_left[FIELDS + f - ADJ].astype(jnp.float32)
            right = right + from_right[FIELDS + f - ADJ].astype(jnp.float32)
        left = pltpu.roll(left * has_left, 4, 1)
        right = pltpu.roll(right * has_right, lanes - 4, 1)
        tile = jnp.where((position == 4) | (position == 5), left, strip[f])
        tile = jnp.where((position == 2) | (position == 3), right, tile)
        strips[f] = tile
    for out, cells in ((up, lo_cells), (down, hi_cells)):
        tiles = 0
        for table, narrow in ((FWD_Y, True), (F32_Y, False)):
            rows = [(f, z, y) for f, y, _ in cells(table, cy) for z in range(layers + 1)]
            for r, (f, z, y) in enumerate(rows):
                value = strips[f, y : y + 1, :] if z == layers else main[f, z, y : y + 1, :]
                packed[r // 8, r % 8 : r % 8 + 1, :] = value
            used = -(-len(rows) // 8)
            for t in range(used):
                high, low = split(packed[t])
                out[tiles + t] = high
                if not narrow:
                    out[tiles + used + t] = low
            tiles += used if narrow else 2 * used


def row_tiles(cells, cz, cy):
    layers = cz + 2 * HALO
    narrow = -(-len(cells(FWD_Y, cy)) * (layers + 1) // 8)
    wide = -(-len(cells(F32_Y, cy)) * (layers + 1) // 8)
    return narrow + 2 * wide


def window_kernel(cz, cy, main, strips, from_lower, from_upper, inj, final, image_lam, image_mu, ring, packed, keep):
    lanes = main.shape[3]
    layers = cz + 2 * HALO
    ring_rows = ring.shape[2]
    for f in range(FIELDS):
        for z in range(layers + 1):
            ring[f, z, 0:cy, :] = strips[f] if z == layers else main[f, z]
            ring[f, z, cy:ring_rows, :] = jnp.zeros((ring_rows - cy, lanes), jnp.float32)
    for source, cells in ((from_lower, lo_cells), (from_upper, hi_cells)):
        tiles = 0
        for table, narrow in ((FWD_Y, True), (F32_Y, False)):
            rows = [(f, z, y % ring_rows) for f, _, y in cells(table, cy) for z in range(layers + 1)]
            used = -(-len(rows) // 8)
            for t in range(used):
                value = source[tiles + t].astype(jnp.float32)
                if not narrow:
                    value = value + source[tiles + used + t].astype(jnp.float32)
                packed[t] = value
            for r, (f, z, y) in enumerate(rows):
                ring[f, z, y : y + 1, :] = packed[r // 8, r % 8 : r % 8 + 1, :]
            tiles += used if narrow else 2 * used

    lane = lax.broadcasted_iota(jnp.int32, (ring_rows, lanes), 1)
    first_lane, last_lane = lane == 0, lane == lanes - 1
    edge = layers

    def at(f, z):
        return ring[f, z]

    def x_next(f, z):
        value = at(f, z)
        if z == edge:
            return pltpu.roll(value, lanes - 1, 1)
        beyond = pltpu.roll(at(f, edge), (lanes - 1 - (8 * z + 2)) % lanes, 1)
        return jnp.where(last_lane, beyond, pltpu.roll(value, lanes - 1, 1))

    def x_prev(f, z):
        value = at(f, z)
        if z == edge:
            return pltpu.roll(value, 1, 1)
        beyond = pltpu.roll(at(f, edge), (lanes - (8 * z + 5)) % lanes, 1)
        return jnp.where(first_lane, beyond, pltpu.roll(value, 1, 1))

    def y_next(f, z):
        return pltpu.roll(at(f, z), ring_rows - 1, 0)

    def y_prev(f, z):
        return pltpu.roll(at(f, z), 1, 0)

    def z_next(f, z):
        return pltpu.roll(at(f, edge), lanes - 8, 1) if z == edge else at(f, z + 1)

    def z_prev(f, z):
        return pltpu.roll(at(f, edge), 8, 1) if z == edge else at(f, z - 1)

    def velocity_rates(base, z, want):
        buoy = at(BUOY, z)
        sxx, syy, szz = (functools.partial(at, base + f) for f in (SXX, SYY, SZZ))
        sxy, sxz, syz = (functools.partial(at, base + f) for f in (SXY, SXZ, SYZ))
        out = {}
        if VX in want:
            out[VX] = buoy * (
                (x_next(base + SXX, z) - sxx(z)) + (sxy(z) - y_prev(base + SXY, z)) + (sxz(z) - z_prev(base + SXZ, z))
            )
        if VY in want:
            out[VY] = buoy * (
                (sxy(z) - x_prev(base + SXY, z)) + (y_next(base + SYY, z) - syy(z)) + (syz(z) - z_prev(base + SYZ, z))
            )
        if VZ in want:
            out[VZ] = buoy * (
                (sxz(z) - x_prev(base + SXZ, z)) + (syz(z) - y_prev(base + SYZ, z)) + (z_next(base + SZZ, z) - szz(z))
            )
        return out

    def stress_rates(base, z, want):
        lam, mu = at(LAM, z), at(MU, z)
        vx, vy, vz = at(base + VX, z), at(base + VY, z), at(base + VZ, z)
        out = {}
        if SXX in want:
            exx = vx - x_prev(base + VX, z)
            eyy = vy - y_prev(base + VY, z)
            ezz = vz - z_prev(base + VZ, z)
            common = lam * (exx + eyy + ezz)
            twice = 2.0 * mu
            out[SXX] = common + twice * exx
            out[SYY] = common + twice * eyy
            out[SZZ] = common + twice * ezz
        if SXY in want:
            out[SXY] = mu * ((y_next(base + VX, z) - vx) + (x_next(base + VY, z) - vy))
        if SXZ in want:
            out[SXZ] = mu * ((z_next(base + VX, z) - vx) + (x_next(base + VZ, z) - vz))
            out[SYZ] = mu * ((z_next(base + VY, z) - vy) + (y_next(base + VZ, z) - vz))
        return out

    def spread(ranges):
        for z in list(range(layers)) + [edge]:
            want = {f for f, (a, b) in ranges.items() if z == edge or a <= z < b}
            if want:
                yield z, want

    def velocity_step(base, sign, ranges):
        for z, want in spread(ranges):
            for f, rate in velocity_rates(base, z, want).items():
                ring[base + f, z] = at(base + f, z) + rate if sign > 0 else at(base + f, z) - rate

    def stress_step(base, sign, ranges, before=None, after=None):
        for z, want in spread(ranges):
            for f, rate in stress_rates(base, z, want).items():
                value, normal = at(base + f, z), f in (SXX, SYY, SZZ)
                if before is not None and normal:
                    value = value + at(before, z)
                value = value + rate if sign > 0 else value - rate
                if after is not None and normal:
                    value = value + at(after, z)
                ring[base + f, z] = value

    def terms(f, a):
        term_lam = (f[0] + f[1] + f[2]) * (a[0] + a[1] + a[2])
        term_mu = f[0] * a[0] + f[1] * a[1] + f[2] * a[2] + 2.0 * (f[3] * a[3] + f[4] * a[4] + f[5] * a[5])
        return term_lam, term_mu

    inner = (HALO, HALO + cz)
    n = layers
    stress_step(ADJ, -1, {SXX: (1, n), SXY: (0, n), SXZ: (0, n - 1)})
    velocity_step(FWD, 1, {VX: (1, n), VY: (1, n), VZ: (0, n - 1)})
    stress_step(FWD, 1, {SXX: (1, n - 1), SXY: (1, n - 1), SXZ: (1, n - 1)}, after=SRC)
    for z in range(*inner):
        f = [ring[FWD + s, z, 0:cy, :] for s in range(SXX, SYZ + 1)]
        a = [ring[ADJ + s, z, 0:cy, :] for s in range(SXX, SYZ + 1)]
        a = [value + ring[INJ, z, 0:cy, :] for value in a[:3]] + a[3:]
        keep[0, z - HALO], keep[1, z - HALO] = terms(f, a)
    velocity_step(FWD, 1, {VX: (2, n - 1), VY: (2, n - 1), VZ: (1, n - 2)})
    everything = set(range(SXX, SYZ + 1))
    for z in range(*inner):
        rates = stress_rates(FWD, z, everything)
        f = []
        for s in range(SXX, SYZ + 1):
            value = (at(FWD + s, z) + rates[s])[0:cy, :]
            f.append(value + inj[3, z - HALO] if s <= SZZ else value)
        a = [main[ADJ + s, z] for s in range(SXX, SYZ + 1)]
        term_lam, term_mu = terms(f, a)
        image_lam[z - HALO] = term_lam + keep[0, z - HALO]
        image_mu[z - HALO] = term_mu + keep[1, z - HALO]
    velocity_step(ADJ, -1, {VX: (1, n - 1), VY: (1, n - 1), VZ: (1, n - 1)})
    stress_step(ADJ, -1, {SXX: (2, n - 1), SXY: (1, n - 1), SXZ: (1, n - 2)}, before=INJ)
    for z in range(*inner):
        rates = velocity_rates(ADJ, z, {VX, VY, VZ})
        for f in (VX, VY, VZ):
            final[f, z - HALO] = (at(ADJ + f, z) - rates[f])[0:cy, :]
        for s in range(SXX, SYZ + 1):
            final[s, z - HALO] = ring[ADJ + s, z, 0:cy, :]


def exchange(value, axis):
    count = lax.axis_size(axis)
    if count == 2:
        other = lax.ppermute(value, axis, [(0, 1), (1, 0)])
        return other, other
    return (
        lax.ppermute(value, axis, [(i, i + 1) for i in range(count - 1)]),
        lax.ppermute(value, axis, [(i + 1, i) for i in range(count - 1)]),
    )


def on_device(
    checkpoint_store,
    holder_peer,
    holder_slot,
    adjoint_state,
    lame_lambda,
    lame_mu,
    buoyancy,
    source_cell,
    wavelet,
    receiver_cell,
    traces,
    plan,
):
    cz, cy, cx = lame_mu.shape
    layers = cz + 2 * HALO
    bf16, f32 = jnp.bfloat16, jnp.float32
    slots = checkpoint_store.shape[0]
    faces = len(lo_cells(F32_Z, cz)) + len(hi_cells(F32_Z, cz))
    place = jnp.stack([
        lax.axis_index("gx"), jnp.int32(lax.axis_size("gx")), lax.axis_index("gz"), jnp.int32(lax.axis_size("gz")),
    ]).astype(jnp.int32)

    outgoing, inj = pl.pallas_call(
        functools.partial(start_kernel, cz),
        out_shape=(
            jax.ShapeDtypeStruct((slots * 9 + 2 * faces, cy, cx), bf16),
            jax.ShapeDtypeStruct((4, cz, cy, cx), f32),
        ),
        in_specs=[vmem()] * 5 + [smem(), smem(), vmem(), vmem(), smem()],
        out_specs=(vmem(), vmem()),
        compiler_params=params(),
    )(
        checkpoint_store,
        adjoint_state,
        lame_lambda,
        lame_mu,
        buoyancy,
        source_cell,
        wavelet,
        receiver_cell.reshape(1, -1),
        traces.reshape(traces.shape[-2:]),
        plan,
    )
    gathered = lax.all_gather(outgoing, "gz", axis=0)

    main, strip, send = pl.pallas_call(
        functools.partial(column_kernel, cz),
        out_shape=(
            jax.ShapeDtypeStruct((FIELDS, layers, cy, cx), f32),
            jax.ShapeDtypeStruct((FIELDS, cy, cx), f32),
            jax.ShapeDtypeStruct((2 * FIELDS - ADJ, cy, cx), bf16),
        ),
        in_specs=[vmem(), smem(), smem(), smem()] + [vmem()] * 5,
        out_specs=(vmem(), vmem(), vmem()),
        compiler_params=params(),
    )(gathered, holder_peer[0, 0], holder_slot[0, 0], place, adjoint_state, lame_lambda, lame_mu, buoyancy, inj)
    from_left, from_right = exchange(send, "gx")

    most = max(-(-len(cells(table, cy)) * (layers + 1) // 8) for cells in (lo_cells, hi_cells) for table in (FWD_Y, F32_Y))
    strips, up, down = pl.pallas_call(
        functools.partial(rows_kernel, cz, cy),
        out_shape=(
            jax.ShapeDtypeStruct((FIELDS, cy, cx), f32),
            jax.ShapeDtypeStruct((row_tiles(lo_cells, cz, cy), cy, cx), bf16),
            jax.ShapeDtypeStruct((row_tiles(hi_cells, cz, cy), cy, cx), bf16),
        ),
        in_specs=[vmem()] * 4 + [smem()],
        out_specs=(vmem(), vmem(), vmem()),
        scratch_shapes=[pltpu.VMEM((most, 8, cx), f32)],
        compiler_params=params(),
    )(main, strip, from_left, from_right, place)
    count = lax.axis_size("gy")
    from_lower = lax.ppermute(up, "gy", [(i, i + 1) for i in range(count - 1)])
    from_upper = lax.ppermute(down, "gy", [(i + 1, i) for i in range(count - 1)])

    return pl.pallas_call(
        functools.partial(window_kernel, cz, cy),
        out_shape=(
            jax.ShapeDtypeStruct((9, cz, cy, cx), f32),
            jax.ShapeDtypeStruct((cz, cy, cx), f32),
            jax.ShapeDtypeStruct((cz, cy, cx), f32),
        ),
        in_specs=[vmem()] * 5,
        out_specs=(vmem(), vmem(), vmem()),
        scratch_shapes=[
            pltpu.VMEM((FIELDS, layers + 1, 2 * cy, cx), f32),
            pltpu.VMEM((most, 8, cx), f32),
            pltpu.VMEM((2, cz, cy, cx), f32),
        ],
        compiler_params=params(),
    )(main, strips, from_lower, from_upper, inj)


def solution(mesh):
    return jax.shard_map(
        on_device,
        mesh=mesh,
        in_specs=(
            P("gz", None, None, "gy", "gx"),
            P("gx", "gy", None, None),
            P("gx", "gy", None, None),
            P(None, "gz", "gy", "gx"),
            P("gz", "gy", "gx"),
            P("gz", "gy", "gx"),
            P("gz", "gy", "gx"),
            P("gz", "gy", "gx", None),
            P(),
            P("gz", "gy", "gx", None),
            P("gz", "gy", "gx", None, None),
            P(),
        ),
        out_specs=(P(None, "gz", "gy", "gx"), P("gz", "gy", "gx"), P("gz", "gy", "gx")),
        check_vma=False,
    )
```

```python
import functools

import jax
import jax.numpy as jnp
from jax import lax
from jax.experimental import pallas as pl
from jax.experimental.pallas import tpu as pltpu
from jax.sharding import PartitionSpec as P

VX, VY, VZ, SXX, SYY, SZZ, SXY, SXZ, SYZ = range(9)
FWD, ADJ, BUOY, LAM, MU, INJ, SRC = 0, 9, 18, 19, 20, 21, 22
FIELDS = 23
HALO = 2

ADJ_Z = {VX: (2, 2), VY: (2, 2), VZ: (2, 2), SXX: (1, 1), SYY: (1, 1), SZZ: (1, 2), SXY: (1, 1), SXZ: (2, 1), SYZ: (2, 1)}
OTHER_Z = {BUOY: (2, 2), LAM: (1, 2), MU: (2, 2), INJ: (0, 1), SRC: (1, 1)}
F32_Z = {**{ADJ + f: c for f, c in ADJ_Z.items()}, **OTHER_Z}

Y_ROWS = {
    FWD + VX: (None, (2, -1, 1), (1, -1, 1), (2, -2, 0)),
    FWD + VY: ((2, -2, 0), (1, -1, 1), (2, -1, 1), None),
    FWD + VZ: (None, (1, -2, 1), (1, -1, 1), (2, -2, 0)),
    FWD + SXX: (None, (2, -1, 1), (1, -1, 1), (2, -2, 1)),
    FWD + SYY: ((2, -2, 0), (1, -1, 1), (1, 0, 1), (2, -1, 1)),
    FWD + SZZ: (None, (1, -1, 1), (1, 0, 1), (2, -1, 0)),
    FWD + SXY: ((2, -1, 1), (1, 0, 1), (1, -1, 1), (2, -2, 0)),
    FWD + SXZ: (None, (1, -1, 1), (0, -1, 1), (1, -2, 1)),
    FWD + SYZ: ((1, -2, 1), (0, -1, 1), (1, -1, 1), (2, -2, 0)),
    ADJ + VX: ((2, -2, 0), (1, -1, 1), (1, -1, 1), (2, -2, 1)),
    ADJ + VY: ((2, -1, 1), (1, 0, 1), (1, -1, 1), (2, -2, 0)),
    ADJ + VZ: ((2, -2, 0), (1, -1, 1), (0, -1, 1), (1, -2, 0)),
    ADJ + SXX: (None, (2, -2, 1), (2, -2, 1), None),
    ADJ + SYY: (None, (2, -1, 1), (1, -1, 1), (2, -2, 0)),
    ADJ + SZZ: (None, (2, -1, 0), (1, -1, 0), None),
    ADJ + SXY: ((2, -2, 0), (1, -1, 1), (2, -2, 1), None),
    ADJ + SXZ: (None, (1, -2, 1), (1, -2, 1), None),
    ADJ + SYZ: ((2, -2, 0), (1, -1, 1), (1, -2, 0), None),
    BUOY: ((2, -2, 0), (1, -1, 1), (1, -1, 1), (2, -2, 0)),
    LAM: (None, (2, -1, 1), (1, -1, 1), (2, -2, 0)),
    MU: ((2, -2, 0), (1, -1, 1), (1, -1, 1), (2, -2, 0)),
    INJ: (None, None, (2, -2, 0), None),
    SRC: (None, (2, -2, 0), (2, -1, 1), None),
}

VMEM_LIMIT = 48 * 1024 * 1024


def vmem():
    return pl.BlockSpec(memory_space=pltpu.VMEM)


def hbm():
    return pl.BlockSpec(memory_space=pl.ANY)


def faces(cz, up):
    near, far = [], []
    for f in sorted(F32_Z):
        before, after = F32_Z[f]
        depth = before if up else after
        for d in range(depth):
            layer = cz - 1 - d if up else d
            (far if d else near).append((f, layer, HALO - 1 - d if up else HALO + cz + d))
    return near, far


def face_counts(cz):
    sides = [faces(cz, up) for up in (True, False)]
    return max(len(s[0]) for s in sides), max(len(s[1]) for s in sides)


def y_rows(cz, cy, up):
    layers = cz + 2 * HALO
    narrow, wide = [], []
    for f in sorted(Y_ROWS):
        for offset in (-1, -2) if up else (0, 1):
            spec = Y_ROWS[f][offset + HALO]
            if spec is None:
                continue
            source = cy + offset if up else offset
            target = 2 * cy + offset if up else cy + offset
            listed = list(range(spec[0], layers + spec[1])) + [layers] * spec[2]
            near = offset in (-1, 0)
            (wide if f >= ADJ and near else narrow).extend((f, z, source, target) for z in listed)
    return narrow, wide


def row_counts(cz, cy):
    sides = [y_rows(cz, cy, up) for up in (True, False)]
    return tuple(max(-(-len(s[i]) // 8) for s in sides) for i in (0, 1))


def split(value):
    high = value.astype(jnp.bfloat16)
    low = (value - high.astype(jnp.float32)).astype(jnp.bfloat16)
    return high, low


def joined(high, low):
    return high.astype(jnp.float32) + low.astype(jnp.float32)


def even_mask(axis, shape):
    return jnp.full(shape, lax.rem(lax.axis_index(axis), 2), jnp.int32) == 0


def copies(sems, *pairs):
    out = [pltpu.make_async_copy(source, target, sems.at[i]) for i, (source, target) in enumerate(pairs)]
    for copy in out:
        copy.start()
    return out


def start_kernel(
    cz, store, adjoint, lam, mu, buoy, source, wavelet, receiver, traces, plan,
    near_out, far_out, own, cells, samples, spots, wave, steps, sems,
):
    cy, lanes = own.shape[2], own.shape[3]
    rows = cz * cy
    tiles = store.shape[0]
    small = copies(sems, (plan, steps), (wavelet, wave), (source, spots), (receiver, cells), (traces, samples))
    large = copies(
        sems.at[pl.ds(len(small), 5)],
        (adjoint, own.at[pl.ds(0, 9)]),
        (buoy, own.at[BUOY - ADJ]),
        (lam, own.at[LAM - ADJ]),
        (mu, own.at[MU - ADJ]),
        (store, near_out.at[pl.ds(0, tiles)]),
    )
    for copy in small:
        copy.wait()
    listed = cells[...]
    count = listed.shape[1]
    row_hot = (lax.broadcasted_iota(jnp.int32, (rows, count), 0) == listed // lanes).astype(jnp.float32)
    lane_hit = lax.broadcasted_iota(jnp.int32, (lanes, count), 0) == listed % lanes
    injected = []
    for step in (1, 0):
        sample = samples[pl.ds(steps[step], 1), :]
        field = lax.dot_general(
            row_hot,
            jnp.where(lane_hit, sample, 0.0),
            (((1,), (1,)), ((), ())),
            precision=lax.Precision.HIGHEST,
            preferred_element_type=jnp.float32,
        )
        injected.append(field.reshape(cz, cy, lanes))
    own[INJ - ADJ] = injected[1]
    flat = lax.broadcasted_iota(jnp.int32, (rows, lanes), 0) * lanes + lax.broadcasted_iota(jnp.int32, (rows, lanes), 1)
    for step in range(2):
        value = wave[steps[step]]
        field = jnp.zeros((rows, lanes), jnp.float32)
        for j in range(source.shape[1]):
            field = field + jnp.where(flat == spots[0, j], value, 0.0)
        own[SRC - ADJ + step] = field.reshape(cz, cy, lanes)
    for copy in large:
        copy.wait()
    for f in (SXX, SYY, SZZ):
        own[f] = own[f] + injected[0]

    even = even_mask("gz", (cy, lanes))
    near, far = face_counts(cz)
    up, down = faces(cz, True), faces(cz, False)
    zero = jnp.zeros((cy, lanes), jnp.float32)

    def tile(side, i):
        return own[side[i][0] - ADJ, side[i][1]] if i < len(side) else zero

    for i in range(near):
        above, below = tile(up[0], i), tile(down[0], i)
        for out, base, value in (
            (near_out, tiles, jnp.where(even, above, below)),
            (far_out, 0, jnp.where(even, below, above)),
        ):
            out[base + i], out[base + near + i] = split(value)
    for i in range(far):
        above, below = tile(up[1], i), tile(down[1], i)
        near_out[tiles + 2 * near + i] = jnp.where(even, above, below).astype(jnp.bfloat16)
        far_out[2 * near + i] = jnp.where(even, below, above).astype(jnp.bfloat16)


def column_kernel(
    cz, store, core, chip, both, far, peer, slot, own, main, strip, send_a, send_b, stores, peers, slots, sems
):
    cy, lanes = main.shape[2], main.shape[3]
    layers = cz + 2 * HALO
    tiles = store.shape[0]
    me = lax.axis_index("gz")
    count = lax.axis_size("gz")
    moves = copies(
        sems,
        (peer, peers),
        (slot, slots),
        (store, stores.at[me]),
        (core.at[pl.ds(0, tiles)], stores.at[me ^ 1]),
        (chip, stores.at[me ^ 2]),
        (both, stores.at[me ^ 3]),
    )
    for z in range(cz):
        for f in range(ADJ, FIELDS):
            main[f, HALO + z] = own[f - ADJ, z]
    near, _ = face_counts(cz)
    even = even_mask("gz", (cy, lanes))
    zero = jnp.zeros((cy, lanes), jnp.float32)
    filled = set()
    for up in (True, False):
        for depth, listed in enumerate(faces(cz, up)):
            for i, (f, _, z) in enumerate(listed):
                values = []
                for ref, base in ((core, tiles), (far, 0)):
                    if depth == 0:
                        values.append(joined(ref[base + i], ref[base + near + i]))
                    else:
                        values.append(ref[base + 2 * near + i].astype(jnp.float32))
                main[f, z] = jnp.where(even, values[1], values[0]) if up else jnp.where(even, values[0], values[1])
                filled.add((f, z))
    for f in range(ADJ, FIELDS):
        for z in (0, 1, layers - 2, layers - 1):
            if (f, z) not in filled:
                main[f, z] = zero

    lane = lax.broadcasted_iota(jnp.int32, (cy, lanes), 1)
    position = lane % 8
    group = lane // 8

    def make_strip(f):
        tile = zero
        for z in range(layers):
            value = main[f, z]
            tail = pltpu.roll(value, (8 * z + 2) % lanes, 1)
            head = pltpu.roll(value, (8 * z + 6) % lanes, 1)
            here = group == z
            tile = jnp.where(here & (position < 2), tail, jnp.where(here & (position >= 6), head, tile))
        strip[f] = tile

    for f in range(ADJ, FIELDS):
        make_strip(f)
    for move in moves:
        move.wait()
    below, above = jnp.maximum(me - 1, 0), jnp.minimum(me + 1, count - 1)
    has_below = (me > 0).astype(jnp.float32)
    has_above = (me < count - 1).astype(jnp.float32)
    for z in range(layers):
        if z < HALO:
            brick, piece, keep = below, cz - HALO + z, has_below
        elif z < HALO + cz:
            brick, piece, keep = me, z - HALO, None
        else:
            brick, piece, keep = above, z - HALO - cz, has_above
        holder = peers[brick, piece]
        row = slots[brick, piece] * 9
        for f in range(9):
            value = stores[holder, row + f].astype(jnp.float32)
            main[FWD + f, z] = value if keep is None else value * keep
    for f in range(9):
        make_strip(f)
    even_x = even_mask("gx", (cy, lanes))
    for out, tail_from_even in ((send_a, True), (send_b, False)):
        if out is None:
            continue
        place = 0
        for fields, narrow in ((range(ADJ), True), (range(ADJ, FIELDS), False)):
            quads = [fields[i : i + 4] for i in range(0, len(fields), 4)]
            for i, quad in enumerate(quads):
                tile = zero
                for g, f in enumerate(quad):
                    tail, head = strip[f], pltpu.roll(strip[f], lanes - 6, 1)
                    value = jnp.where(even_x, tail, head) if tail_from_even else jnp.where(even_x, head, tail)
                    value = value if g == 0 else pltpu.roll(value, 2 * g, 1)
                    tile = jnp.where(position // 2 == g, value, tile)
                high, low = split(tile)
                out[place + i] = high
                if not narrow:
                    out[place + len(quads) + i] = low
            place += len(quads) if narrow else 2 * len(quads)


def x_tiles():
    return -(-ADJ // 4) + 2 * -(-(FIELDS - ADJ) // 4)


def rows_kernel(cz, main, strip, from_a, from_b, strips, send_a, send_b, packed):
    cy, lanes = main.shape[2], main.shape[3]
    layers = cz + 2 * HALO
    lane = lax.broadcasted_iota(jnp.int32, (cy, lanes), 1)
    position = lane % 8
    even_x = even_mask("gx", (cy, lanes))
    zero = jnp.zeros((cy, lanes), jnp.float32)
    place = 0
    for fields, narrow in ((range(ADJ), True), (range(ADJ, FIELDS), False)):
        quads = [fields[i : i + 4] for i in range(0, len(fields), 4)]
        for i, quad in enumerate(quads):
            got = []
            for ref in (from_a, from_b):
                if ref is None:
                    got.append(zero)
                elif narrow:
                    got.append(ref[place + i].astype(jnp.float32))
                else:
                    got.append(joined(ref[place + i], ref[place + len(quads) + i]))
            right, left = jnp.where(even_x, got[0], got[1]), jnp.where(even_x, got[1], got[0])
            for g, f in enumerate(quad):
                tile = jnp.where(position // 2 == 1, pltpu.roll(right, (2 - 2 * g) % lanes, 1), strip[f])
                strips[f] = jnp.where(position // 2 == 2, pltpu.roll(left, (4 - 2 * g) % lanes, 1), tile)
        place += len(quads) if narrow else 2 * len(quads)
    narrow, wide = row_counts(cz, cy)
    for side, up in enumerate((True, False)):
        for base, listed in zip((0, narrow), y_rows(cz, cy, up)):
            for r, (f, z, y, _) in enumerate(listed):
                value = strips[f, y : y + 1, :] if z == layers else main[f, z, y : y + 1, :]
                packed[side, base + r // 8, r % 8 : r % 8 + 1, :] = value
    even_y = even_mask("gy", (cy, lanes))
    for t in range(narrow + wide):
        up, down = packed[0, t], packed[1, t]
        for out, value in ((send_a, jnp.where(even_y, up, down)), (send_b, jnp.where(even_y, down, up))):
            if out is None:
                continue
            if t < narrow:
                out[t] = value.astype(jnp.bfloat16)
            else:
                out[t], out[wide + t] = split(value)


def window_kernel(cz, main, strips, from_a, from_b, own, final, image_lam, image_mu, ring, packed, keep):
    cy, lanes = main.shape[2], main.shape[3]
    layers = cz + 2 * HALO
    ring_rows = ring.shape[2]
    even_y = even_mask("gy", (cy, lanes))
    zero = jnp.zeros((cy, lanes), jnp.float32)
    for f in range(FIELDS):
        for z in range(layers + 1):
            ring[f, z, 0:cy, :] = strips[f] if z == layers else main[f, z]
            ring[f, z, cy:ring_rows, :] = jnp.zeros((ring_rows - cy, lanes), jnp.float32)
    narrow, wide = row_counts(cz, cy)
    for t in range(narrow + wide):
        got = []
        for ref in (from_a, from_b):
            if ref is None:
                got.append(zero)
            elif t < narrow:
                got.append(ref[t].astype(jnp.float32))
            else:
                got.append(joined(ref[t], ref[wide + t]))
        packed[0, t] = jnp.where(even_y, got[1], got[0])
        packed[1, t] = jnp.where(even_y, got[0], got[1])
    for side, up in enumerate((True, False)):
        for base, listed in zip((0, narrow), y_rows(cz, cy, up)):
            for r, (f, z, _, y) in enumerate(listed):
                ring[f, z, y : y + 1, :] = packed[side, base + r // 8, r % 8 : r % 8 + 1, :]

    lane = lax.broadcasted_iota(jnp.int32, (ring_rows, lanes), 1)
    first_lane, last_lane = lane == 0, lane == lanes - 1
    edge = layers

    def at(f, z):
        return ring[f, z]

    def x_next(f, z):
        value = at(f, z)
        if z == edge:
            return pltpu.roll(value, lanes - 1, 1)
        beyond = pltpu.roll(at(f, edge), (lanes - 1 - (8 * z + 2)) % lanes, 1)
        return jnp.where(last_lane, beyond, pltpu.roll(value, lanes - 1, 1))

    def x_prev(f, z):
        value = at(f, z)
        if z == edge:
            return pltpu.roll(value, 1, 1)
        beyond = pltpu.roll(at(f, edge), (lanes - (8 * z + 5)) % lanes, 1)
        return jnp.where(first_lane, beyond, pltpu.roll(value, 1, 1))

    def y_next(f, z):
        return pltpu.roll(at(f, z), ring_rows - 1, 0)

    def y_prev(f, z):
        return pltpu.roll(at(f, z), 1, 0)

    def z_next(f, z):
        return pltpu.roll(at(f, edge), lanes - 8, 1) if z == edge else at(f, z + 1)

    def z_prev(f, z):
        return pltpu.roll(at(f, edge), 8, 1) if z == edge else at(f, z - 1)

    def velocity_rates(base, z, want):
        buoy = at(BUOY, z)
        sxx, syy, szz = (functools.partial(at, base + f) for f in (SXX, SYY, SZZ))
        sxy, sxz, syz = (functools.partial(at, base + f) for f in (SXY, SXZ, SYZ))
        out = {}
        if VX in want:
            out[VX] = buoy * (
                (x_next(base + SXX, z) - sxx(z)) + (sxy(z) - y_prev(base + SXY, z)) + (sxz(z) - z_prev(base + SXZ, z))
            )
        if VY in want:
            out[VY] = buoy * (
                (sxy(z) - x_prev(base + SXY, z)) + (y_next(base + SYY, z) - syy(z)) + (syz(z) - z_prev(base + SYZ, z))
            )
        if VZ in want:
            out[VZ] = buoy * (
                (sxz(z) - x_prev(base + SXZ, z)) + (syz(z) - y_prev(base + SYZ, z)) + (z_next(base + SZZ, z) - szz(z))
            )
        return out

    def stress_rates(base, z, want):
        lam, mu = at(LAM, z), at(MU, z)
        vx, vy, vz = at(base + VX, z), at(base + VY, z), at(base + VZ, z)
        out = {}
        if SXX in want:
            exx = vx - x_prev(base + VX, z)
            eyy = vy - y_prev(base + VY, z)
            ezz = vz - z_prev(base + VZ, z)
            common = lam * (exx + eyy + ezz)
            twice = 2.0 * mu
            out[SXX] = common + twice * exx
            out[SYY] = common + twice * eyy
            out[SZZ] = common + twice * ezz
        if SXY in want:
            out[SXY] = mu * ((y_next(base + VX, z) - vx) + (x_next(base + VY, z) - vy))
        if SXZ in want:
            out[SXZ] = mu * ((z_next(base + VX, z) - vx) + (x_next(base + VZ, z) - vz))
            out[SYZ] = mu * ((z_next(base + VY, z) - vy) + (y_next(base + VZ, z) - vz))
        return out

    def spread(ranges):
        for z in list(range(layers)) + [edge]:
            want = {f for f, (a, b) in ranges.items() if z == edge or a <= z < b}
            if want:
                yield z, want

    def velocity_step(base, sign, ranges):
        for z, want in spread(ranges):
            for f, rate in velocity_rates(base, z, want).items():
                ring[base + f, z] = at(base + f, z) + rate if sign > 0 else at(base + f, z) - rate

    def stress_step(base, sign, ranges, before=None, after=None):
        for z, want in spread(ranges):
            for f, rate in stress_rates(base, z, want).items():
                value, normal = at(base + f, z), f in (SXX, SYY, SZZ)
                if before is not None and normal:
                    value = value + at(before, z)
                value = value + rate if sign > 0 else value - rate
                if after is not None and normal:
                    value = value + at(after, z)
                ring[base + f, z] = value

    def terms(f, a):
        term_lam = (f[0] + f[1] + f[2]) * (a[0] + a[1] + a[2])
        term_mu = f[0] * a[0] + f[1] * a[1] + f[2] * a[2] + 2.0 * (f[3] * a[3] + f[4] * a[4] + f[5] * a[5])
        return term_lam, term_mu

    inner = (HALO, HALO + cz)
    n = layers
    stress_step(ADJ, -1, {SXX: (1, n), SXY: (0, n), SXZ: (0, n - 1)})
    velocity_step(FWD, 1, {VX: (1, n), VY: (1, n), VZ: (0, n - 1)})
    stress_step(FWD, 1, {SXX: (1, n - 1), SXY: (1, n - 1), SXZ: (1, n - 1)}, after=SRC)
    for z in range(*inner):
        f = [ring[FWD + s, z, 0:cy, :] for s in range(SXX, SYZ + 1)]
        a = [ring[ADJ + s, z, 0:cy, :] for s in range(SXX, SYZ + 1)]
        a = [value + ring[INJ, z, 0:cy, :] for value in a[:3]] + a[3:]
        keep[0, z - HALO], keep[1, z - HALO] = terms(f, a)
    velocity_step(FWD, 1, {VX: (2, n - 1), VY: (2, n - 1), VZ: (1, n - 2)})
    everything = set(range(SXX, SYZ + 1))
    for z in range(*inner):
        rates = stress_rates(FWD, z, everything)
        f = []
        for s in range(SXX, SYZ + 1):
            value = (at(FWD + s, z) + rates[s])[0:cy, :]
            f.append(value + own[SRC - ADJ + 1, z - HALO] if s <= SZZ else value)
        a = [own[s, z - HALO] for s in range(SXX, SYZ + 1)]
        term_lam, term_mu = terms(f, a)
        image_lam[z - HALO] = term_lam + keep[0, z - HALO]
        image_mu[z - HALO] = term_mu + keep[1, z - HALO]
    velocity_step(ADJ, -1, {VX: (1, n - 1), VY: (1, n - 1), VZ: (1, n - 1)})
    stress_step(ADJ, -1, {SXX: (2, n - 1), SXY: (1, n - 1), SXZ: (1, n - 2)}, before=INJ)
    for z in range(*inner):
        rates = velocity_rates(ADJ, z, {VX, VY, VZ})
        for f in (VX, VY, VZ):
            final[f, z - HALO] = (at(ADJ + f, z) - rates[f])[0:cy, :]
        for s in range(SXX, SYZ + 1):
            final[s, z - HALO] = ring[ADJ + s, z, 0:cy, :]


def swap_pairs(count, first):
    return [(i + d, i + 1 - d) for i in range(first, count - 1, 2) for d in (0, 1)]


def swapped(value_a, value_b, axis):
    count = lax.axis_size(axis)
    got_a = lax.ppermute(value_a, axis, swap_pairs(count, 0))
    return got_a, None if value_b is None else lax.ppermute(value_b, axis, swap_pairs(count, 1))


def stay(value, spec):
    return pltpu.with_memory_space_constraint(value, pltpu.HBM) if spec.memory_space == pl.ANY else value


def kernel_call(body, args, in_specs, out_shape, scratch_shapes=()):
    here = [a is not None for a in args]
    there = [o is not None for o in out_shape]

    def run(*refs):
        refs = iter(refs)
        full = [next(refs) if h else None for h in here + there]
        body(*full, *refs)

    out = iter(
        pl.pallas_call(
            run,
            out_shape=tuple(o for o in out_shape if o is not None),
            in_specs=[s for s, h in zip(in_specs, here) if h],
            out_specs=tuple(vmem() for h in there if h),
            scratch_shapes=list(scratch_shapes),
            compiler_params=pltpu.CompilerParams(vmem_limit_bytes=VMEM_LIMIT),
        )(*[stay(a, s) for a, s in zip(args, in_specs) if a is not None])
    )
    return tuple(next(out) if h else None for h in there)


def on_device(
    checkpoint_store,
    holder_peer,
    holder_slot,
    adjoint_state,
    lame_lambda,
    lame_mu,
    buoyancy,
    source_cell,
    wavelet,
    receiver_cell,
    traces,
    plan,
):
    cz, cy, cx = lame_mu.shape
    layers = cz + 2 * HALO
    bf16, f32 = jnp.bfloat16, jnp.float32
    store = checkpoint_store.reshape(-1, cy, cx)
    tiles = store.shape[0]
    peer, slot = holder_peer[0, 0], holder_slot[0, 0]
    source, receiver = source_cell.reshape(1, -1), receiver_cell.reshape(1, -1)
    traces = traces.reshape(traces.shape[-2:])
    holders = lax.axis_size("gz")
    assert holders == 4
    near, far = face_counts(cz)
    face = 2 * near + far

    def shape(*dims, dtype=f32):
        return jax.ShapeDtypeStruct(dims, dtype)

    chip = lax.ppermute(store, "gz", [(i, i ^ 2) for i in range(holders)])
    to_core, to_far, own = kernel_call(
        functools.partial(start_kernel, cz),
        (store, adjoint_state, lame_lambda, lame_mu, buoyancy, source, wavelet, receiver, traces, plan),
        [hbm()] * 10,
        (shape(tiles + face, cy, cx, dtype=bf16), shape(face, cy, cx, dtype=bf16), shape(15, cz, cy, cx)),
        [
            pltpu.VMEM(receiver.shape, jnp.int32),
            pltpu.VMEM(traces.shape, f32),
            pltpu.SMEM(source.shape, jnp.int32),
            pltpu.SMEM(wavelet.shape, f32),
            pltpu.SMEM(plan.shape, jnp.int32),
            pltpu.SemaphoreType.DMA((10,)),
        ],
    )
    core, far_face = swapped(to_core, to_far, "gz")
    both = lax.ppermute(chip, "gz", [(i, i ^ 1) for i in range(holders)])

    wide_x, wide_y = lax.axis_size("gx") > 2, lax.axis_size("gy") > 2
    x_send = shape(x_tiles(), cy, cx, dtype=bf16)
    main, strip, x_a, x_b = kernel_call(
        functools.partial(column_kernel, cz),
        (store, core, chip, both, far_face, peer, slot, own),
        [hbm()] + [vmem()] * 4 + [hbm()] * 2 + [vmem()],
        (shape(FIELDS, layers, cy, cx), shape(FIELDS, cy, cx), x_send, x_send if wide_x else None),
        [
            pltpu.VMEM((holders, tiles, cy, cx), bf16),
            pltpu.SMEM(peer.shape, jnp.int32),
            pltpu.SMEM(slot.shape, jnp.int32),
            pltpu.SemaphoreType.DMA((6,)),
        ],
    )
    from_a, from_b = swapped(x_a, x_b, "gx")

    narrow, wide = row_counts(cz, cy)
    y_send = shape(narrow + 2 * wide, cy, cx, dtype=bf16)
    strips, y_a, y_b = kernel_call(
        functools.partial(rows_kernel, cz),
        (main, strip, from_a, from_b),
        [vmem()] * 4,
        (shape(FIELDS, cy, cx), y_send, y_send if wide_y else None),
        [pltpu.VMEM((2, narrow + wide, 8, cx), f32)],
    )
    from_a, from_b = swapped(y_a, y_b, "gy")

    return kernel_call(
        functools.partial(window_kernel, cz),
        (main, strips, from_a, from_b, own),
        [vmem()] * 5,
        (shape(9, cz, cy, cx), shape(cz, cy, cx), shape(cz, cy, cx)),
        [
            pltpu.VMEM((FIELDS, layers + 1, 2 * cy, cx), f32),
            pltpu.VMEM((2, narrow + wide, 8, cx), f32),
            pltpu.VMEM((2, cz, cy, cx), f32),
        ],
    )


def solution(mesh):
    return jax.shard_map(
        on_device,
        mesh=mesh,
        in_specs=(
            P("gz", None, None, "gy", "gx"),
            P("gx", "gy", None, None),
            P("gx", "gy", None, None),
            P(None, "gz", "gy", "gx"),
            P("gz", "gy", "gx"),
            P("gz", "gy", "gx"),
            P("gz", "gy", "gx"),
            P("gz", "gy", "gx", None),
            P(),
            P("gz", "gy", "gx", None),
            P("gz", "gy", "gx", None, None),
            P(),
        ),
        out_specs=(P(None, "gz", "gy", "gx"), P("gz", "gy", "gx"), P("gz", "gy", "gx")),
        check_vma=False,
    )
```

```python
import functools

import jax
import jax.numpy as jnp
from jax import lax
from jax.experimental import pallas as pl
from jax.experimental.pallas import tpu as pltpu
from jax.sharding import PartitionSpec as P

VX, VY, VZ, SXX, SYY, SZZ, SXY, SXZ, SYZ = range(9)
FWD, ADJ, BUOY, LAM, MU, INJ, SRC = 0, 9, 18, 19, 20, 21, 22
FIELDS = 23
HALO = 2

ADJ_Z = {VX: (2, 2), VY: (2, 2), VZ: (2, 2), SXX: (1, 1), SYY: (1, 1), SZZ: (1, 2), SXY: (1, 1), SXZ: (2, 1), SYZ: (2, 1)}
OTHER_Z = {BUOY: (2, 2), LAM: (1, 2), MU: (2, 2), INJ: (0, 1), SRC: (1, 1)}
F32_Z = {**{ADJ + f: c for f, c in ADJ_Z.items()}, **OTHER_Z}

Y_ROWS = {
    FWD + VX: (None, (2, -1, 1), (1, -1, 1), (2, -2, 0)),
    FWD + VY: ((2, -2, 0), (1, -1, 1), (2, -1, 1), None),
    FWD + VZ: (None, (1, -2, 1), (1, -1, 1), (2, -2, 0)),
    FWD + SXX: (None, (2, -1, 1), (1, -1, 1), (2, -2, 1)),
    FWD + SYY: ((2, -2, 0), (1, -1, 1), (1, 0, 1), (2, -1, 1)),
    FWD + SZZ: (None, (1, -1, 1), (1, 0, 1), (2, -1, 0)),
    FWD + SXY: ((2, -1, 1), (1, 0, 1), (1, -1, 1), (2, -2, 0)),
    FWD + SXZ: (None, (1, -1, 1), (0, -1, 1), (1, -2, 1)),
    FWD + SYZ: ((1, -2, 1), (0, -1, 1), (1, -1, 1), (2, -2, 0)),
    ADJ + VX: ((2, -2, 0), (1, -1, 1), (1, -1, 1), (2, -2, 1)),
    ADJ + VY: ((2, -1, 1), (1, 0, 1), (1, -1, 1), (2, -2, 0)),
    ADJ + VZ: ((2, -2, 0), (1, -1, 1), (0, -1, 1), (1, -2, 0)),
    ADJ + SXX: (None, (2, -2, 1), (2, -2, 1), None),
    ADJ + SYY: (None, (2, -1, 1), (1, -1, 1), (2, -2, 0)),
    ADJ + SZZ: (None, (2, -1, 0), (1, -1, 0), None),
    ADJ + SXY: ((2, -2, 0), (1, -1, 1), (2, -2, 1), None),
    ADJ + SXZ: (None, (1, -2, 1), (1, -2, 1), None),
    ADJ + SYZ: ((2, -2, 0), (1, -1, 1), (1, -2, 0), None),
    BUOY: ((2, -2, 0), (1, -1, 1), (1, -1, 1), (2, -2, 0)),
    LAM: (None, (2, -1, 1), (1, -1, 1), (2, -2, 0)),
    MU: ((2, -2, 0), (1, -1, 1), (1, -1, 1), (2, -2, 0)),
    INJ: (None, None, (2, -2, 0), None),
    SRC: (None, (2, -2, 0), (2, -1, 1), None),
}

VMEM_LIMIT = 48 * 1024 * 1024


def vmem():
    return pl.BlockSpec(memory_space=pltpu.VMEM)


def hbm():
    return pl.BlockSpec(memory_space=pl.ANY)


def faces(cz, up):
    near, far = [], []
    for f in sorted(F32_Z):
        before, after = F32_Z[f]
        depth = before if up else after
        for d in range(depth):
            layer = cz - 1 - d if up else d
            (far if d else near).append((f, layer, HALO - 1 - d if up else HALO + cz + d))
    return near, far


def face_counts(cz):
    sides = [faces(cz, up) for up in (True, False)]
    return max(len(s[0]) for s in sides), max(len(s[1]) for s in sides)


def y_rows(cz, cy, up):
    layers = cz + 2 * HALO
    narrow, wide = [], []
    for f in sorted(Y_ROWS):
        for offset in (-1, -2) if up else (0, 1):
            spec = Y_ROWS[f][offset + HALO]
            if spec is None:
                continue
            source = cy + offset if up else offset
            target = 2 * cy + offset if up else cy + offset
            listed = list(range(spec[0], layers + spec[1])) + [layers] * spec[2]
            near = offset in (-1, 0)
            (wide if f >= ADJ and near else narrow).extend((f, z, source, target) for z in listed)
    return narrow, wide


def row_counts(cz, cy):
    sides = [y_rows(cz, cy, up) for up in (True, False)]
    return tuple(max(-(-len(s[i]) // 8) for s in sides) for i in (0, 1))


def split(value):
    high = value.astype(jnp.bfloat16)
    low = (value - high.astype(jnp.float32)).astype(jnp.bfloat16)
    return high, low


def joined(high, low):
    return high.astype(jnp.float32) + low.astype(jnp.float32)


def even_mask(axes, shape):
    total = sum(lax.axis_index(a) for a in ((axes,) if isinstance(axes, str) else axes))
    return jnp.full(shape, lax.rem(total, 2), jnp.int32) == 0


def copies(sems, *pairs):
    out = [pltpu.make_async_copy(source, target, sems.at[i]) for i, (source, target) in enumerate(pairs)]
    for copy in out:
        copy.start()
    return out


def pack_rows(cz, cy, row_of, packed, send_a, send_b):
    narrow, wide = row_counts(cz, cy)
    for side, up in enumerate((True, False)):
        for base, listed in zip((0, narrow), y_rows(cz, cy, up)):
            for r, (f, z, y, _) in enumerate(listed):
                packed[side, base + r // 8, r % 8 : r % 8 + 1, :] = row_of(f, z, y)
    even = even_mask(("gy", "gz"), packed.shape[2:])
    for t in range(narrow + wide):
        up, down = packed[0, t], packed[1, t]
        for out, value in ((send_a, jnp.where(even, up, down)), (send_b, jnp.where(even, down, up))):
            if out is None:
                continue
            if t < narrow:
                out[t] = value.astype(jnp.bfloat16)
            else:
                out[t], out[wide + t] = split(value)


def unpack_rows(cz, cy, from_a, from_b, packed, put_row):
    narrow, wide = row_counts(cz, cy)
    even = even_mask(("gy", "gz"), packed.shape[2:])
    for t in range(narrow + wide):
        got = []
        for ref in (from_a, from_b):
            if ref is None:
                got.append(jnp.zeros(packed.shape[2:], jnp.float32))
            elif t < narrow:
                got.append(ref[t].astype(jnp.float32))
            else:
                got.append(joined(ref[t], ref[wide + t]))
        packed[0, t] = jnp.where(even, got[1], got[0])
        packed[1, t] = jnp.where(even, got[0], got[1])
    for side, up in enumerate((True, False)):
        for base, listed in zip((0, narrow), y_rows(cz, cy, up)):
            for r, (f, z, _, y) in enumerate(listed):
                put_row(f, z, y, packed[side, base + r // 8, r % 8 : r % 8 + 1, :])


def start_kernel(
    cz, adjoint, lam, mu, buoy, source, wavelet, receiver, traces, plan,
    out, own, cells, samples, spots, wave, steps, sems,
):
    cy, lanes = own.shape[2], own.shape[3]
    rows = cz * cy
    small = copies(sems, (plan, steps), (wavelet, wave), (source, spots), (receiver, cells), (traces, samples))
    large = copies(
        sems.at[pl.ds(len(small), 4)],
        (adjoint, own.at[pl.ds(0, 9)]),
        (buoy, own.at[BUOY - ADJ]),
        (lam, own.at[LAM - ADJ]),
        (mu, own.at[MU - ADJ]),
    )
    for copy in small:
        copy.wait()
    listed = cells[...]
    count = listed.shape[1]
    row_hot = (lax.broadcasted_iota(jnp.int32, (rows, count), 0) == listed // lanes).astype(jnp.float32)
    lane_hit = lax.broadcasted_iota(jnp.int32, (lanes, count), 0) == listed % lanes
    injected = []
    for step in (1, 0):
        sample = samples[pl.ds(steps[step], 1), :]
        field = lax.dot_general(
            row_hot,
            jnp.where(lane_hit, sample, 0.0),
            (((1,), (1,)), ((), ())),
            precision=lax.Precision.HIGHEST,
            preferred_element_type=jnp.float32,
        )
        injected.append(field.reshape(cz, cy, lanes))
    own[INJ - ADJ] = injected[1]
    flat = lax.broadcasted_iota(jnp.int32, (rows, lanes), 0) * lanes + lax.broadcasted_iota(jnp.int32, (rows, lanes), 1)
    for step in range(2):
        value = wave[steps[step]]
        field = jnp.zeros((rows, lanes), jnp.float32)
        for j in range(source.shape[1]):
            field = field + jnp.where(flat == spots[0, j], value, 0.0)
        own[SRC - ADJ + step] = field.reshape(cz, cy, lanes)
    for copy in large:
        copy.wait()
    for f in (SXX, SYY, SZZ):
        own[f] = own[f] + injected[0]

    even = even_mask("gz", (cy, lanes))
    near, far = face_counts(cz)
    up, down = faces(cz, True), faces(cz, False)
    zero = jnp.zeros((cy, lanes), jnp.float32)

    def tile(side, i):
        return own[side[i][0] - ADJ, side[i][1]] if i < len(side) else zero

    face = 2 * near + far
    for i in range(near):
        above, below = tile(up[0], i), tile(down[0], i)
        for base, value in ((0, jnp.where(even, above, below)), (face, jnp.where(even, below, above))):
            out[base + i], out[base + near + i] = split(value)
    for i in range(far):
        above, below = tile(up[1], i), tile(down[1], i)
        out[2 * near + i] = jnp.where(even, above, below).astype(jnp.bfloat16)
        out[face + 2 * near + i] = jnp.where(even, below, above).astype(jnp.bfloat16)


def strip_of(main, layers):
    cy, lanes = main(0).shape
    lane = lax.broadcasted_iota(jnp.int32, (cy, lanes), 1)
    position = lane % 8
    group = lane // 8
    tile = jnp.zeros((cy, lanes), jnp.float32)
    for z in range(layers):
        tail = pltpu.roll(main(z), (8 * z + 2) % lanes, 1)
        head = pltpu.roll(main(z), (8 * z + 6) % lanes, 1)
        here = group == z
        tile = jnp.where(here & (position < 2), tail, jnp.where(here & (position >= 6), head, tile))
    return tile


def halo_kernel(cz, core, far, own, ring):
    cy, lanes = own.shape[2], own.shape[3]
    layers = cz + 2 * HALO
    ring_rows = ring.shape[2]
    near, _ = face_counts(cz)
    even = even_mask("gz", (cy, lanes))
    zero = jnp.zeros((cy, lanes), jnp.float32)
    for f in range(ring.shape[0]):
        for z in range(cz):
            ring[f, HALO + z, 0:cy, :] = own[f, z]
    filled = set()
    for up in (True, False):
        for depth, listed in enumerate(faces(cz, up)):
            for i, (f, _, z) in enumerate(listed):
                values = []
                for ref in (core, far):
                    if depth == 0:
                        values.append(joined(ref[i], ref[near + i]))
                    else:
                        values.append(ref[2 * near + i].astype(jnp.float32))
                value = jnp.where(even, values[1], values[0]) if up else jnp.where(even, values[0], values[1])
                ring[f - ADJ, z, 0:cy, :] = value
                filled.add((f - ADJ, z))
    for f in range(ring.shape[0]):
        for z in (0, 1, layers - 2, layers - 1):
            if (f, z) not in filled:
                ring[f, z, 0:cy, :] = zero
        ring[f, layers, 0:cy, :] = strip_of(lambda z: ring[f, z, 0:cy, :], layers)
        for z in range(layers + 1):
            ring[f, z, cy:ring_rows, :] = jnp.zeros((ring_rows - cy, lanes), jnp.float32)


def column_kernel(
    cz, store, core, chip, both, peer, slot, ring_w, ring, send_a, send_b, stores, peers, slots, sems
):
    cy, lanes = core.shape[1], core.shape[2]
    layers = cz + 2 * HALO
    ring_rows = ring.shape[2]
    tiles = store.shape[0]
    me = lax.axis_index("gz")
    count = lax.axis_size("gz")
    moves = copies(
        sems,
        (peer, peers),
        (slot, slots),
        (store, stores.at[me]),
        (core, stores.at[me ^ 1]),
        (chip, stores.at[me ^ 2]),
        (both, stores.at[me ^ 3]),
    )
    zero = jnp.zeros((cy, lanes), jnp.float32)
    for f in range(9):
        for z in range(layers + 1):
            ring[f, z, cy:ring_rows, :] = jnp.zeros((ring_rows - cy, lanes), jnp.float32)
    for move in moves:
        move.wait()
    below, above = jnp.maximum(me - 1, 0), jnp.minimum(me + 1, count - 1)
    has_below = (me > 0).astype(jnp.float32)
    has_above = (me < count - 1).astype(jnp.float32)
    for z in range(layers):
        if z < HALO:
            brick, piece, keep = below, cz - HALO + z, has_below
        elif z < HALO + cz:
            brick, piece, keep = me, z - HALO, None
        else:
            brick, piece, keep = above, z - HALO - cz, has_above
        holder = peers[brick, piece]
        row = slots[brick, piece] * 9
        for f in range(9):
            value = stores[holder, row + f].astype(jnp.float32)
            ring[f, z, 0:cy, :] = value if keep is None else value * keep
    for f in range(9):
        ring[f, layers, 0:cy, :] = strip_of(lambda z: ring[f, z, 0:cy, :], layers)
    strip = [ring[f, layers, 0:cy, :] for f in range(9)]
    strip += [ring_w[f, layers, 0:cy, :] for f in range(ring_w.shape[0])]
    position = lax.broadcasted_iota(jnp.int32, (cy, lanes), 1) % 8
    even_x = even_mask("gx", (cy, lanes))
    for out, tail_from_even in ((send_a, True), (send_b, False)):
        if out is None:
            continue
        place = 0
        for fields, narrow in ((range(ADJ), True), (range(ADJ, FIELDS), False)):
            quads = [fields[i : i + 4] for i in range(0, len(fields), 4)]
            for i, quad in enumerate(quads):
                tile = zero
                for g, f in enumerate(quad):
                    tail, head = strip[f], pltpu.roll(strip[f], lanes - 6, 1)
                    value = jnp.where(even_x, tail, head) if tail_from_even else jnp.where(even_x, head, tail)
                    value = value if g == 0 else pltpu.roll(value, 2 * g, 1)
                    tile = jnp.where(position // 2 == g, value, tile)
                high, low = split(tile)
                out[place + i] = high
                if not narrow:
                    out[place + len(quads) + i] = low
            place += len(quads) if narrow else 2 * len(quads)


def x_tiles():
    return -(-ADJ // 4) + 2 * -(-(FIELDS - ADJ) // 4)


def rows_kernel(cz, ring_f, ring_w, from_a, from_b, strips, send_a, send_b, packed):
    cy, lanes = strips.shape[1], strips.shape[2]
    layers = cz + 2 * HALO
    strip = [ring_f[f, layers, 0:cy, :] for f in range(9)]
    strip += [ring_w[f, layers, 0:cy, :] for f in range(ring_w.shape[0])]
    position = lax.broadcasted_iota(jnp.int32, (cy, lanes), 1) % 8
    even_x = even_mask("gx", (cy, lanes))
    zero = jnp.zeros((cy, lanes), jnp.float32)
    place = 0
    for fields, narrow in ((range(ADJ), True), (range(ADJ, FIELDS), False)):
        quads = [fields[i : i + 4] for i in range(0, len(fields), 4)]
        for i, quad in enumerate(quads):
            got = []
            for ref in (from_a, from_b):
                if ref is None:
                    got.append(zero)
                elif narrow:
                    got.append(ref[place + i].astype(jnp.float32))
                else:
                    got.append(joined(ref[place + i], ref[place + len(quads) + i]))
            right, left = jnp.where(even_x, got[0], got[1]), jnp.where(even_x, got[1], got[0])
            for g, f in enumerate(quad):
                tile = jnp.where(position // 2 == 1, pltpu.roll(right, (2 - 2 * g) % lanes, 1), strip[f])
                strips[f] = jnp.where(position // 2 == 2, pltpu.roll(left, (4 - 2 * g) % lanes, 1), tile)
        place += len(quads) if narrow else 2 * len(quads)

    def row_of(f, z, y):
        if z == layers:
            return strips[f, y : y + 1, :]
        return ring_f[f, z, y : y + 1, :] if f < ADJ else ring_w[f - ADJ, z, y : y + 1, :]

    pack_rows(cz, cy, row_of, packed, send_a, send_b)


class Ring:
    def __init__(self, ring_f, ring_w):
        self.parts = ring_f, ring_w

    def __getitem__(self, key):
        f = key[0]
        return self.parts[0][key] if f < ADJ else self.parts[1][(f - ADJ, *key[1:])]

    def __setitem__(self, key, value):
        f = key[0]
        if f < ADJ:
            self.parts[0][key] = value
        else:
            self.parts[1][(f - ADJ, *key[1:])] = value


def window_kernel(
    cz, ring_f_in, ring_w_in, strips, from_a, from_b, own, final, image_lam, image_mu, ring_f, ring_w, packed, keep
):
    cy, lanes = own.shape[2], own.shape[3]
    layers = cz + 2 * HALO
    ring_rows = ring_f.shape[2]
    ring = Ring(ring_f, ring_w)
    for f in range(FIELDS):
        ring[f, layers, 0:cy, :] = strips[f]

    def put_row(f, z, y, value):
        ring[f, z, y : y + 1, :] = value

    unpack_rows(cz, cy, from_a, from_b, packed, put_row)

    lane = lax.broadcasted_iota(jnp.int32, (ring_rows, lanes), 1)
    first_lane, last_lane = lane == 0, lane == lanes - 1
    edge = layers

    def at(f, z):
        return ring[f, z]

    def x_next(f, z):
        value = at(f, z)
        if z == edge:
            return pltpu.roll(value, lanes - 1, 1)
        beyond = pltpu.roll(at(f, edge), (lanes - 1 - (8 * z + 2)) % lanes, 1)
        return jnp.where(last_lane, beyond, pltpu.roll(value, lanes - 1, 1))

    def x_prev(f, z):
        value = at(f, z)
        if z == edge:
            return pltpu.roll(value, 1, 1)
        beyond = pltpu.roll(at(f, edge), (lanes - (8 * z + 5)) % lanes, 1)
        return jnp.where(first_lane, beyond, pltpu.roll(value, 1, 1))

    def y_next(f, z):
        return pltpu.roll(at(f, z), ring_rows - 1, 0)

    def y_prev(f, z):
        return pltpu.roll(at(f, z), 1, 0)

    def z_next(f, z):
        return pltpu.roll(at(f, edge), lanes - 8, 1) if z == edge else at(f, z + 1)

    def z_prev(f, z):
        return pltpu.roll(at(f, edge), 8, 1) if z == edge else at(f, z - 1)

    def velocity_rates(base, z, want):
        buoy = at(BUOY, z)
        sxx, syy, szz = (functools.partial(at, base + f) for f in (SXX, SYY, SZZ))
        sxy, sxz, syz = (functools.partial(at, base + f) for f in (SXY, SXZ, SYZ))
        out = {}
        if VX in want:
            out[VX] = buoy * (
                (x_next(base + SXX, z) - sxx(z)) + (sxy(z) - y_prev(base + SXY, z)) + (sxz(z) - z_prev(base + SXZ, z))
            )
        if VY in want:
            out[VY] = buoy * (
                (sxy(z) - x_prev(base + SXY, z)) + (y_next(base + SYY, z) - syy(z)) + (syz(z) - z_prev(base + SYZ, z))
            )
        if VZ in want:
            out[VZ] = buoy * (
                (sxz(z) - x_prev(base + SXZ, z)) + (syz(z) - y_prev(base + SYZ, z)) + (z_next(base + SZZ, z) - szz(z))
            )
        return out

    def stress_rates(base, z, want):
        lam, mu = at(LAM, z), at(MU, z)
        vx, vy, vz = at(base + VX, z), at(base + VY, z), at(base + VZ, z)
        out = {}
        if SXX in want:
            exx = vx - x_prev(base + VX, z)
            eyy = vy - y_prev(base + VY, z)
            ezz = vz - z_prev(base + VZ, z)
            common = lam * (exx + eyy + ezz)
            twice = 2.0 * mu
            out[SXX] = common + twice * exx
            out[SYY] = common + twice * eyy
            out[SZZ] = common + twice * ezz
        if SXY in want:
            out[SXY] = mu * ((y_next(base + VX, z) - vx) + (x_next(base + VY, z) - vy))
        if SXZ in want:
            out[SXZ] = mu * ((z_next(base + VX, z) - vx) + (x_next(base + VZ, z) - vz))
            out[SYZ] = mu * ((z_next(base + VY, z) - vy) + (y_next(base + VZ, z) - vz))
        return out

    def spread(ranges):
        for z in list(range(layers)) + [edge]:
            want = {f for f, (a, b) in ranges.items() if z == edge or a <= z < b}
            if want:
                yield z, want

    def velocity_step(base, sign, ranges):
        for z, want in spread(ranges):
            for f, rate in velocity_rates(base, z, want).items():
                ring[base + f, z] = at(base + f, z) + rate if sign > 0 else at(base + f, z) - rate

    def stress_step(base, sign, ranges, before=None, after=None):
        for z, want in spread(ranges):
            for f, rate in stress_rates(base, z, want).items():
                value, normal = at(base + f, z), f in (SXX, SYY, SZZ)
                if before is not None and normal:
                    value = value + at(before, z)
                value = value + rate if sign > 0 else value - rate
                if after is not None and normal:
                    value = value + at(after, z)
                ring[base + f, z] = value

    def terms(f, a):
        term_lam = (f[0] + f[1] + f[2]) * (a[0] + a[1] + a[2])
        term_mu = f[0] * a[0] + f[1] * a[1] + f[2] * a[2] + 2.0 * (f[3] * a[3] + f[4] * a[4] + f[5] * a[5])
        return term_lam, term_mu

    inner = (HALO, HALO + cz)
    n = layers
    stress_step(ADJ, -1, {SXX: (1, n), SXY: (0, n), SXZ: (0, n - 1)})
    velocity_step(FWD, 1, {VX: (1, n), VY: (1, n), VZ: (0, n - 1)})
    stress_step(FWD, 1, {SXX: (1, n - 1), SXY: (1, n - 1), SXZ: (1, n - 1)}, after=SRC)
    for z in range(*inner):
        f = [ring[FWD + s, z, 0:cy, :] for s in range(SXX, SYZ + 1)]
        a = [ring[ADJ + s, z, 0:cy, :] for s in range(SXX, SYZ + 1)]
        a = [value + ring[INJ, z, 0:cy, :] for value in a[:3]] + a[3:]
        keep[0, z - HALO], keep[1, z - HALO] = terms(f, a)
    velocity_step(FWD, 1, {VX: (2, n - 1), VY: (2, n - 1), VZ: (1, n - 2)})
    everything = set(range(SXX, SYZ + 1))
    for z in range(*inner):
        rates = stress_rates(FWD, z, everything)
        f = []
        for s in range(SXX, SYZ + 1):
            value = (at(FWD + s, z) + rates[s])[0:cy, :]
            f.append(value + own[SRC - ADJ + 1, z - HALO] if s <= SZZ else value)
        a = [own[s, z - HALO] for s in range(SXX, SYZ + 1)]
        term_lam, term_mu = terms(f, a)
        image_lam[z - HALO] = term_lam + keep[0, z - HALO]
        image_mu[z - HALO] = term_mu + keep[1, z - HALO]
    velocity_step(ADJ, -1, {VX: (1, n - 1), VY: (1, n - 1), VZ: (1, n - 1)})
    stress_step(ADJ, -1, {SXX: (2, n - 1), SXY: (1, n - 1), SXZ: (1, n - 2)}, before=INJ)
    for z in range(*inner):
        rates = velocity_rates(ADJ, z, {VX, VY, VZ})
        for f in (VX, VY, VZ):
            final[f, z - HALO] = (at(ADJ + f, z) - rates[f])[0:cy, :]
        for s in range(SXX, SYZ + 1):
            final[s, z - HALO] = ring[ADJ + s, z, 0:cy, :]


def swap_pairs(count, first):
    return [(i + d, i + 1 - d) for i in range(first, count - 1, 2) for d in (0, 1)]


def swapped(value_a, value_b, axis):
    count = lax.axis_size(axis)
    got_a = lax.ppermute(value_a, axis, swap_pairs(count, 0))
    return got_a, None if value_b is None else lax.ppermute(value_b, axis, swap_pairs(count, 1))


def stay(value, spec):
    return pltpu.with_memory_space_constraint(value, pltpu.HBM) if spec.memory_space == pl.ANY else value


def kernel_call(body, args, in_specs, out_shape, scratch_shapes=(), aliases=None):
    here = [a is not None for a in args]
    there = [o is not None for o in out_shape]

    def run(*refs):
        refs = iter(refs)
        full = [next(refs) if h else None for h in here + there]
        body(*full, *refs)

    out = iter(
        pl.pallas_call(
            run,
            out_shape=tuple(o for o in out_shape if o is not None),
            in_specs=[s for s, h in zip(in_specs, here) if h],
            out_specs=tuple(vmem() for h in there if h),
            scratch_shapes=list(scratch_shapes),
            input_output_aliases=aliases or {},
            compiler_params=pltpu.CompilerParams(vmem_limit_bytes=VMEM_LIMIT),
        )(*[stay(a, s) for a, s in zip(args, in_specs) if a is not None])
    )
    return tuple(next(out) if h else None for h in there)


def on_device(
    checkpoint_store,
    holder_peer,
    holder_slot,
    adjoint_state,
    lame_lambda,
    lame_mu,
    buoyancy,
    source_cell,
    wavelet,
    receiver_cell,
    traces,
    plan,
):
    cz, cy, cx = lame_mu.shape
    layers = cz + 2 * HALO
    bf16, f32 = jnp.bfloat16, jnp.float32
    store = checkpoint_store.reshape(-1, cy, cx)
    tiles = store.shape[0]
    peer, slot = holder_peer[0, 0], holder_slot[0, 0]
    source, receiver = source_cell.reshape(1, -1), receiver_cell.reshape(1, -1)
    traces = traces.reshape(traces.shape[-2:])
    holders = lax.axis_size("gz")
    assert holders == 4
    near, far = face_counts(cz)
    face = 2 * near + far

    def shape(*dims, dtype=f32):
        return jax.ShapeDtypeStruct(dims, dtype)

    wide_x = lax.axis_size("gx") > 2
    chip = lax.ppermute(store, "gz", [(i, i ^ 2) for i in range(holders)])
    core = lax.ppermute(store, "gz", [(i, i ^ 1) for i in range(holders)])
    to_core, own = kernel_call(
        functools.partial(start_kernel, cz),
        (adjoint_state, lame_lambda, lame_mu, buoyancy, source, wavelet, receiver, traces, plan),
        [hbm()] * 9,
        (shape(2 * face, cy, cx, dtype=bf16), shape(15, cz, cy, cx)),
        [
            pltpu.VMEM(receiver.shape, jnp.int32),
            pltpu.VMEM(traces.shape, f32),
            pltpu.SMEM(source.shape, jnp.int32),
            pltpu.SMEM(wavelet.shape, f32),
            pltpu.SMEM(plan.shape, jnp.int32),
            pltpu.SemaphoreType.DMA((9,)),
        ],
    )
    core_faces = lax.ppermute(to_core, "gz", [(i, i ^ 1) for i in range(holders)])
    far_face = lax.ppermute(core_faces[face:], "gz", [(0, 2), (3, 1)])
    both = lax.ppermute(chip, "gz", [(i, i ^ 1) for i in range(holders)])

    (ring_w,) = kernel_call(
        functools.partial(halo_kernel, cz),
        (core_faces, far_face, own),
        [vmem()] * 3,
        (shape(FIELDS - ADJ, layers + 1, 2 * cy, cx),),
    )
    x_send = shape(x_tiles(), cy, cx, dtype=bf16)
    ring_f, x_a, x_b = kernel_call(
        functools.partial(column_kernel, cz),
        (store, core, chip, both, peer, slot, ring_w),
        [hbm()] + [vmem()] * 3 + [hbm()] * 2 + [vmem()],
        (shape(ADJ, layers + 1, 2 * cy, cx), x_send, x_send if wide_x else None),
        [
            pltpu.VMEM((holders, tiles, cy, cx), bf16),
            pltpu.SMEM(peer.shape, jnp.int32),
            pltpu.SMEM(slot.shape, jnp.int32),
            pltpu.SemaphoreType.DMA((6,)),
        ],
    )
    from_a, from_b = swapped(x_a, x_b, "gx")

    narrow, wide = row_counts(cz, cy)
    y_send = shape(narrow + 2 * wide, cy, cx, dtype=bf16)
    strips, y_a, y_b = kernel_call(
        functools.partial(rows_kernel, cz),
        (ring_f, ring_w, from_a, from_b),
        [vmem()] * 4,
        (shape(FIELDS, cy, cx), y_send, y_send),
        [pltpu.VMEM((2, narrow + wide, 8, cx), f32)],
    )
    gy = lax.axis_size("gy")
    turns = [
        [
            (i * holders + c, j * holders + c)
            for c in range(holders)
            for i, j in swap_pairs(gy, (c + turn) % 2)
        ]
        for turn in (0, 1)
    ]
    from_a = lax.ppermute(y_a, ("gy", "gz"), turns[0])
    from_b = lax.ppermute(y_b, ("gy", "gz"), turns[1])

    result = kernel_call(
        functools.partial(window_kernel, cz),
        (ring_f, ring_w, strips, from_a, from_b, own),
        [vmem()] * 6,
        (
            shape(9, cz, cy, cx),
            shape(cz, cy, cx),
            shape(cz, cy, cx),
            shape(*ring_f.shape),
            shape(*ring_w.shape),
        ),
        [
            pltpu.VMEM((2, narrow + wide, 8, cx), f32),
            pltpu.VMEM((2, cz, cy, cx), f32),
        ],
        {0: 3, 1: 4},
    )
    return result[:3]


def solution(mesh):
    return jax.shard_map(
        on_device,
        mesh=mesh,
        in_specs=(
            P("gz", None, None, "gy", "gx"),
            P("gx", "gy", None, None),
            P("gx", "gy", None, None),
            P(None, "gz", "gy", "gx"),
            P("gz", "gy", "gx"),
            P("gz", "gy", "gx"),
            P("gz", "gy", "gx"),
            P("gz", "gy", "gx", None),
            P(),
            P("gz", "gy", "gx", None),
            P("gz", "gy", "gx", None, None),
            P(),
        ),
        out_specs=(P(None, "gz", "gy", "gx"), P("gz", "gy", "gx"), P("gz", "gy", "gx")),
        check_vma=False,
    )
```

```python
import functools

import jax
import jax.numpy as jnp
from jax import lax
from jax.experimental import pallas as pl
from jax.experimental.pallas import tpu as pltpu
from jax.sharding import PartitionSpec as P

VX, VY, VZ, SXX, SYY, SZZ, SXY, SXZ, SYZ = range(9)
FWD, ADJ, BUOY, LAM, MU, INJ, SRC = 0, 9, 18, 19, 20, 21, 22
FIELDS = 23
HALO = 2

ADJ_Z = {VX: (2, 2), VY: (2, 2), VZ: (2, 2), SXX: (1, 1), SYY: (1, 1), SZZ: (1, 2), SXY: (1, 1), SXZ: (2, 1), SYZ: (2, 1)}
OTHER_Z = {BUOY: (2, 2), LAM: (1, 2), MU: (2, 2), INJ: (0, 1), SRC: (1, 1)}
F32_Z = {**{ADJ + f: c for f, c in ADJ_Z.items()}, **OTHER_Z}

Y_ROWS = {
    FWD + VX: (None, (2, -1, 1), (1, -1, 1), (2, -2, 0)),
    FWD + VY: ((2, -2, 0), (1, -1, 1), (2, -1, 1), None),
    FWD + VZ: (None, (1, -2, 1), (1, -1, 1), (2, -2, 0)),
    FWD + SXX: (None, (2, -1, 1), (1, -1, 1), (2, -2, 1)),
    FWD + SYY: ((2, -2, 0), (1, -1, 1), (1, 0, 1), (2, -1, 1)),
    FWD + SZZ: (None, (1, -1, 1), (1, 0, 1), (2, -1, 0)),
    FWD + SXY: ((2, -1, 1), (1, 0, 1), (1, -1, 1), (2, -2, 0)),
    FWD + SXZ: (None, (1, -1, 1), (0, -1, 1), (1, -2, 1)),
    FWD + SYZ: ((1, -2, 1), (0, -1, 1), (1, -1, 1), (2, -2, 0)),
    ADJ + VX: ((2, -2, 0), (1, -1, 1), (1, -1, 1), (2, -2, 1)),
    ADJ + VY: ((2, -1, 1), (1, 0, 1), (1, -1, 1), (2, -2, 0)),
    ADJ + VZ: ((2, -2, 0), (1, -1, 1), (0, -1, 1), (1, -2, 0)),
    ADJ + SXX: (None, (2, -2, 1), (2, -2, 1), None),
    ADJ + SYY: (None, (2, -1, 1), (1, -1, 1), (2, -2, 0)),
    ADJ + SZZ: (None, (2, -1, 0), (1, -1, 0), None),
    ADJ + SXY: ((2, -2, 0), (1, -1, 1), (2, -2, 1), None),
    ADJ + SXZ: (None, (1, -2, 1), (1, -2, 1), None),
    ADJ + SYZ: ((2, -2, 0), (1, -1, 1), (1, -2, 0), None),
    BUOY: ((2, -2, 0), (1, -1, 1), (1, -1, 1), (2, -2, 0)),
    LAM: (None, (2, -1, 1), (1, -1, 1), (2, -2, 0)),
    MU: ((2, -2, 0), (1, -1, 1), (1, -1, 1), (2, -2, 0)),
    INJ: (None, None, (2, -2, 0), None),
    SRC: (None, (2, -2, 0), (2, -1, 1), None),
}

VMEM_LIMIT = 48 * 1024 * 1024


def vmem():
    return pl.BlockSpec(memory_space=pltpu.VMEM)


def hbm():
    return pl.BlockSpec(memory_space=pl.ANY)


def faces(cz, up):
    near, far = [], []
    for f in sorted(F32_Z):
        before, after = F32_Z[f]
        depth = before if up else after
        for d in range(depth):
            layer = cz - 1 - d if up else d
            (far if d else near).append((f, layer, HALO - 1 - d if up else HALO + cz + d))
    return near, far


def face_counts(cz):
    sides = [faces(cz, up) for up in (True, False)]
    return max(len(s[0]) for s in sides), max(len(s[1]) for s in sides)


def y_rows(cz, cy, up):
    layers = cz + 2 * HALO
    narrow, wide = [], []
    for f in sorted(Y_ROWS):
        for offset in (-1, -2) if up else (0, 1):
            spec = Y_ROWS[f][offset + HALO]
            if spec is None:
                continue
            source = cy + offset if up else offset
            target = 2 * cy + offset if up else cy + offset
            listed = list(range(spec[0], layers + spec[1])) + [layers] * spec[2]
            near = offset in (-1, 0)
            (wide if f >= ADJ and near else narrow).extend((f, z, source, target) for z in listed)
    return narrow, wide


def row_counts(cz, cy):
    sides = [y_rows(cz, cy, up) for up in (True, False)]
    return tuple(max(-(-len(s[i]) // 8) for s in sides) for i in (0, 1))


def split(value):
    high = value.astype(jnp.bfloat16)
    low = (value - high.astype(jnp.float32)).astype(jnp.bfloat16)
    return high, low


def joined(high, low):
    return high.astype(jnp.float32) + low.astype(jnp.float32)


def even_mask(axes, shape):
    total = sum(lax.axis_index(a) for a in ((axes,) if isinstance(axes, str) else axes))
    return jnp.full(shape, lax.rem(total, 2), jnp.int32) == 0


def has_neighbours(axis):
    index = lax.axis_index(axis)
    return (index > 0).astype(jnp.float32), (index < lax.axis_size(axis) - 1).astype(jnp.float32)


def copies(sems, *pairs):
    out = [pltpu.make_async_copy(source, target, sems.at[i]) for i, (source, target) in enumerate(pairs)]
    for copy in out:
        copy.start()
    return out


def pack_rows(cz, cy, row_of, packed, send_a, send_b):
    narrow, wide = row_counts(cz, cy)
    for side, up in enumerate((True, False)):
        for base, listed in zip((0, narrow), y_rows(cz, cy, up)):
            for r, (f, z, y, _) in enumerate(listed):
                packed[side, base + r // 8, r % 8 : r % 8 + 1, :] = row_of(f, z, y)
    even = even_mask(("gy", "gz"), packed.shape[2:])
    for t in range(narrow + wide):
        up, down = packed[0, t], packed[1, t]
        for out, value in ((send_a, jnp.where(even, up, down)), (send_b, jnp.where(even, down, up))):
            if out is None:
                continue
            if t < narrow:
                out[t] = value.astype(jnp.bfloat16)
            else:
                out[t], out[wide + t] = split(value)


def unpack_rows(cz, cy, from_a, from_b, packed, put_row):
    narrow, wide = row_counts(cz, cy)
    has_lower, has_upper = has_neighbours("gy")
    even = even_mask(("gy", "gz"), packed.shape[2:])
    for t in range(narrow + wide):
        got = []
        for ref in (from_a, from_b):
            if ref is None:
                got.append(jnp.zeros(packed.shape[2:], jnp.float32))
            elif t < narrow:
                got.append(ref[t].astype(jnp.float32))
            else:
                got.append(joined(ref[t], ref[wide + t]))
        packed[0, t] = jnp.where(even, got[1], got[0]) * has_lower
        packed[1, t] = jnp.where(even, got[0], got[1]) * has_upper
    for side, up in enumerate((True, False)):
        for base, listed in zip((0, narrow), y_rows(cz, cy, up)):
            for r, (f, z, _, y) in enumerate(listed):
                put_row(f, z, y, packed[side, base + r // 8, r % 8 : r % 8 + 1, :])


def start_kernel(
    cz, store, adjoint, lam, mu, buoy, source, wavelet, receiver, traces, plan,
    near_out, far_out, own, cells, samples, spots, wave, steps, sems,
):
    cy, lanes = own.shape[2], own.shape[3]
    rows = cz * cy
    tiles = store.shape[0]
    small = copies(sems, (plan, steps), (wavelet, wave), (source, spots), (receiver, cells), (traces, samples))
    large = copies(
        sems.at[pl.ds(len(small), 5)],
        (adjoint, own.at[pl.ds(0, 9)]),
        (buoy, own.at[BUOY - ADJ]),
        (lam, own.at[LAM - ADJ]),
        (mu, own.at[MU - ADJ]),
        (store, near_out.at[pl.ds(0, tiles)]),
    )
    for copy in small:
        copy.wait()
    listed = cells[...]
    count = listed.shape[1]
    row_hot = (lax.broadcasted_iota(jnp.int32, (rows, count), 0) == listed // lanes).astype(jnp.float32)
    lane_hit = lax.broadcasted_iota(jnp.int32, (lanes, count), 0) == listed % lanes
    injected = []
    for step in (1, 0):
        sample = samples[pl.ds(steps[step], 1), :]
        field = lax.dot_general(
            row_hot,
            jnp.where(lane_hit, sample, 0.0),
            (((1,), (1,)), ((), ())),
            precision=lax.Precision.HIGHEST,
            preferred_element_type=jnp.float32,
        )
        injected.append(field.reshape(cz, cy, lanes))
    own[INJ - ADJ] = injected[1]
    flat = lax.broadcasted_iota(jnp.int32, (rows, lanes), 0) * lanes + lax.broadcasted_iota(jnp.int32, (rows, lanes), 1)
    for step in range(2):
        value = wave[steps[step]]
        field = jnp.zeros((rows, lanes), jnp.float32)
        for j in range(source.shape[1]):
            field = field + jnp.where(flat == spots[0, j], value, 0.0)
        own[SRC - ADJ + step] = field.reshape(cz, cy, lanes)
    for copy in large:
        copy.wait()
    for f in (SXX, SYY, SZZ):
        own[f] = own[f] + injected[0]

    even = even_mask("gz", (cy, lanes))
    near, far = face_counts(cz)
    up, down = faces(cz, True), faces(cz, False)
    zero = jnp.zeros((cy, lanes), jnp.float32)

    def tile(side, i):
        return own[side[i][0] - ADJ, side[i][1]] if i < len(side) else zero

    for i in range(near):
        above, below = tile(up[0], i), tile(down[0], i)
        for out, base, value in (
            (near_out, tiles, jnp.where(even, above, below)),
            (far_out, 0, jnp.where(even, below, above)),
        ):
            out[base + i], out[base + near + i] = split(value)
    for i in range(far):
        above, below = tile(up[1], i), tile(down[1], i)
        near_out[tiles + 2 * near + i] = jnp.where(even, above, below).astype(jnp.bfloat16)
        far_out[2 * near + i] = jnp.where(even, below, above).astype(jnp.bfloat16)
    for i in range(2 * near + far, far_out.shape[0]):
        far_out[i] = zero.astype(jnp.bfloat16)


def strip_of(main, layers):
    cy, lanes = main(0).shape
    lane = lax.broadcasted_iota(jnp.int32, (cy, lanes), 1)
    position = lane % 8
    group = lane // 8
    tile = jnp.zeros((cy, lanes), jnp.float32)
    for z in range(layers):
        tail = pltpu.roll(main(z), (8 * z + 2) % lanes, 1)
        head = pltpu.roll(main(z), (8 * z + 6) % lanes, 1)
        here = group == z
        tile = jnp.where(here & (position < 2), tail, jnp.where(here & (position >= 6), head, tile))
    return tile


def halo_kernel(cz, tiles, core, far, own, ring):
    cy, lanes = own.shape[2], own.shape[3]
    layers = cz + 2 * HALO
    ring_rows = ring.shape[2]
    near, _ = face_counts(cz)
    even = even_mask("gz", (cy, lanes))
    has_below, has_above = has_neighbours("gz")
    zero = jnp.zeros((cy, lanes), jnp.float32)
    for f in range(ring.shape[0]):
        for z in range(cz):
            ring[f, HALO + z, 0:cy, :] = own[f, z]
    filled = set()
    for up in (True, False):
        for depth, listed in enumerate(faces(cz, up)):
            for i, (f, _, z) in enumerate(listed):
                values = []
                for ref, base in ((core, tiles), (far, 0)):
                    if depth == 0:
                        values.append(joined(ref[base + i], ref[base + near + i]))
                    else:
                        values.append(ref[base + 2 * near + i].astype(jnp.float32))
                value = jnp.where(even, values[1], values[0]) if up else jnp.where(even, values[0], values[1])
                ring[f - ADJ, z, 0:cy, :] = value * (has_below if up else has_above)
                filled.add((f - ADJ, z))
    for f in range(ring.shape[0]):
        for z in (0, 1, layers - 2, layers - 1):
            if (f, z) not in filled:
                ring[f, z, 0:cy, :] = zero
        ring[f, layers, 0:cy, :] = strip_of(lambda z: ring[f, z, 0:cy, :], layers)
        for z in range(layers + 1):
            ring[f, z, cy:ring_rows, :] = jnp.zeros((ring_rows - cy, lanes), jnp.float32)


def column_kernel(
    cz, store, core, chip, both, peer, slot, ring_w, ring, send_a, send_b, stores, peers, slots, sems
):
    cy, lanes = core.shape[1], core.shape[2]
    layers = cz + 2 * HALO
    ring_rows = ring.shape[2]
    tiles = store.shape[0]
    me = lax.axis_index("gz")
    count = lax.axis_size("gz")
    moves = copies(
        sems,
        (peer, peers),
        (slot, slots),
        (store, stores.at[me]),
        (core.at[pl.ds(0, tiles)], stores.at[me ^ 1]),
        (chip, stores.at[me ^ 2]),
        (both, stores.at[me ^ 3]),
    )
    zero = jnp.zeros((cy, lanes), jnp.float32)
    for f in range(9):
        for z in range(layers + 1):
            ring[f, z, cy:ring_rows, :] = jnp.zeros((ring_rows - cy, lanes), jnp.float32)
    for move in moves:
        move.wait()
    below, above = jnp.maximum(me - 1, 0), jnp.minimum(me + 1, count - 1)
    has_below, has_above = has_neighbours("gz")
    for z in range(layers):
        if z < HALO:
            brick, piece, keep = below, cz - HALO + z, has_below
        elif z < HALO + cz:
            brick, piece, keep = me, z - HALO, None
        else:
            brick, piece, keep = above, z - HALO - cz, has_above
        holder = peers[brick, piece]
        row = slots[brick, piece] * 9
        for f in range(9):
            value = stores[holder, row + f].astype(jnp.float32)
            ring[f, z, 0:cy, :] = value if keep is None else value * keep
    for f in range(9):
        ring[f, layers, 0:cy, :] = strip_of(lambda z: ring[f, z, 0:cy, :], layers)
    strip = [ring[f, layers, 0:cy, :] for f in range(9)]
    strip += [ring_w[f, layers, 0:cy, :] for f in range(ring_w.shape[0])]
    position = lax.broadcasted_iota(jnp.int32, (cy, lanes), 1) % 8
    even_x = even_mask("gx", (cy, lanes))
    for out, tail_from_even in ((send_a, True), (send_b, False)):
        if out is None:
            continue
        place = 0
        for fields, narrow in ((range(ADJ), True), (range(ADJ, FIELDS), False)):
            quads = [fields[i : i + 4] for i in range(0, len(fields), 4)]
            for i, quad in enumerate(quads):
                tile = zero
                for g, f in enumerate(quad):
                    tail, head = strip[f], pltpu.roll(strip[f], lanes - 6, 1)
                    value = jnp.where(even_x, tail, head) if tail_from_even else jnp.where(even_x, head, tail)
                    value = value if g == 0 else pltpu.roll(value, 2 * g, 1)
                    tile = jnp.where(position // 2 == g, value, tile)
                high, low = split(tile)
                out[place + i] = high
                if not narrow:
                    out[place + len(quads) + i] = low
            place += len(quads) if narrow else 2 * len(quads)


def x_tiles():
    return -(-ADJ // 4) + 2 * -(-(FIELDS - ADJ) // 4)


def rows_kernel(cz, ring_f, ring_w, from_a, from_b, strips, send_a, send_b, packed):
    cy, lanes = strips.shape[1], strips.shape[2]
    layers = cz + 2 * HALO
    strip = [ring_f[f, layers, 0:cy, :] for f in range(9)]
    strip += [ring_w[f, layers, 0:cy, :] for f in range(ring_w.shape[0])]
    position = lax.broadcasted_iota(jnp.int32, (cy, lanes), 1) % 8
    even_x = even_mask("gx", (cy, lanes))
    has_left, has_right = has_neighbours("gx")
    zero = jnp.zeros((cy, lanes), jnp.float32)
    place = 0
    for fields, narrow in ((range(ADJ), True), (range(ADJ, FIELDS), False)):
        quads = [fields[i : i + 4] for i in range(0, len(fields), 4)]
        for i, quad in enumerate(quads):
            got = []
            for ref in (from_a, from_b):
                if ref is None:
                    got.append(zero)
                elif narrow:
                    got.append(ref[place + i].astype(jnp.float32))
                else:
                    got.append(joined(ref[place + i], ref[place + len(quads) + i]))
            right = jnp.where(even_x, got[0], got[1]) * has_right
            left = jnp.where(even_x, got[1], got[0]) * has_left
            for g, f in enumerate(quad):
                tile = jnp.where(position // 2 == 1, pltpu.roll(right, (2 - 2 * g) % lanes, 1), strip[f])
                strips[f] = jnp.where(position // 2 == 2, pltpu.roll(left, (4 - 2 * g) % lanes, 1), tile)
        place += len(quads) if narrow else 2 * len(quads)

    def row_of(f, z, y):
        if z == layers:
            return strips[f, y : y + 1, :]
        return ring_f[f, z, y : y + 1, :] if f < ADJ else ring_w[f - ADJ, z, y : y + 1, :]

    pack_rows(cz, cy, row_of, packed, send_a, send_b)


class Ring:
    def __init__(self, ring_f, ring_w):
        self.parts = ring_f, ring_w

    def __getitem__(self, key):
        f = key[0]
        return self.parts[0][key] if f < ADJ else self.parts[1][(f - ADJ, *key[1:])]

    def __setitem__(self, key, value):
        f = key[0]
        if f < ADJ:
            self.parts[0][key] = value
        else:
            self.parts[1][(f - ADJ, *key[1:])] = value


def window_kernel(
    cz, ring_f_in, ring_w_in, strips, from_a, from_b, own, final, image_lam, image_mu, ring_f, ring_w, packed, keep
):
    cy, lanes = own.shape[2], own.shape[3]
    layers = cz + 2 * HALO
    ring_rows = ring_f.shape[2]
    ring = Ring(ring_f, ring_w)
    for f in range(FIELDS):
        ring[f, layers, 0:cy, :] = strips[f]

    def put_row(f, z, y, value):
        ring[f, z, y : y + 1, :] = value

    unpack_rows(cz, cy, from_a, from_b, packed, put_row)

    lane = lax.broadcasted_iota(jnp.int32, (ring_rows, lanes), 1)
    first_lane, last_lane = lane == 0, lane == lanes - 1
    edge = layers

    def at(f, z):
        return ring[f, z]

    def x_next(f, z):
        value = at(f, z)
        if z == edge:
            return pltpu.roll(value, lanes - 1, 1)
        beyond = pltpu.roll(at(f, edge), (lanes - 1 - (8 * z + 2)) % lanes, 1)
        return jnp.where(last_lane, beyond, pltpu.roll(value, lanes - 1, 1))

    def x_prev(f, z):
        value = at(f, z)
        if z == edge:
            return pltpu.roll(value, 1, 1)
        beyond = pltpu.roll(at(f, edge), (lanes - (8 * z + 5)) % lanes, 1)
        return jnp.where(first_lane, beyond, pltpu.roll(value, 1, 1))

    def y_next(f, z):
        return pltpu.roll(at(f, z), ring_rows - 1, 0)

    def y_prev(f, z):
        return pltpu.roll(at(f, z), 1, 0)

    def z_next(f, z):
        return pltpu.roll(at(f, edge), lanes - 8, 1) if z == edge else at(f, z + 1)

    def z_prev(f, z):
        return pltpu.roll(at(f, edge), 8, 1) if z == edge else at(f, z - 1)

    def velocity_rates(base, z, want):
        buoy = at(BUOY, z)
        sxx, syy, szz = (functools.partial(at, base + f) for f in (SXX, SYY, SZZ))
        sxy, sxz, syz = (functools.partial(at, base + f) for f in (SXY, SXZ, SYZ))
        out = {}
        if VX in want:
            out[VX] = buoy * (
                (x_next(base + SXX, z) - sxx(z)) + (sxy(z) - y_prev(base + SXY, z)) + (sxz(z) - z_prev(base + SXZ, z))
            )
        if VY in want:
            out[VY] = buoy * (
                (sxy(z) - x_prev(base + SXY, z)) + (y_next(base + SYY, z) - syy(z)) + (syz(z) - z_prev(base + SYZ, z))
            )
        if VZ in want:
            out[VZ] = buoy * (
                (sxz(z) - x_prev(base + SXZ, z)) + (syz(z) - y_prev(base + SYZ, z)) + (z_next(base + SZZ, z) - szz(z))
            )
        return out

    def stress_rates(base, z, want):
        lam, mu = at(LAM, z), at(MU, z)
        vx, vy, vz = at(base + VX, z), at(base + VY, z), at(base + VZ, z)
        out = {}
        if SXX in want:
            exx = vx - x_prev(base + VX, z)
            eyy = vy - y_prev(base + VY, z)
            ezz = vz - z_prev(base + VZ, z)
            common = lam * (exx + eyy + ezz)
            twice = 2.0 * mu
            out[SXX] = common + twice * exx
            out[SYY] = common + twice * eyy
            out[SZZ] = common + twice * ezz
        if SXY in want:
            out[SXY] = mu * ((y_next(base + VX, z) - vx) + (x_next(base + VY, z) - vy))
        if SXZ in want:
            out[SXZ] = mu * ((z_next(base + VX, z) - vx) + (x_next(base + VZ, z) - vz))
            out[SYZ] = mu * ((z_next(base + VY, z) - vy) + (y_next(base + VZ, z) - vz))
        return out

    def spread(ranges):
        for z in list(range(layers)) + [edge]:
            want = {f for f, (a, b) in ranges.items() if z == edge or a <= z < b}
            if want:
                yield z, want

    def velocity_step(base, sign, ranges):
        for z, want in spread(ranges):
            for f, rate in velocity_rates(base, z, want).items():
                ring[base + f, z] = at(base + f, z) + rate if sign > 0 else at(base + f, z) - rate

    def stress_step(base, sign, ranges, before=None, after=None):
        for z, want in spread(ranges):
            for f, rate in stress_rates(base, z, want).items():
                value, normal = at(base + f, z), f in (SXX, SYY, SZZ)
                if before is not None and normal:
                    value = value + at(before, z)
                value = value + rate if sign > 0 else value - rate
                if after is not None and normal:
                    value = value + at(after, z)
                ring[base + f, z] = value

    def terms(f, a):
        term_lam = (f[0] + f[1] + f[2]) * (a[0] + a[1] + a[2])
        term_mu = f[0] * a[0] + f[1] * a[1] + f[2] * a[2] + 2.0 * (f[3] * a[3] + f[4] * a[4] + f[5] * a[5])
        return term_lam, term_mu

    inner = (HALO, HALO + cz)
    n = layers
    stress_step(ADJ, -1, {SXX: (1, n), SXY: (0, n), SXZ: (0, n - 1)})
    velocity_step(FWD, 1, {VX: (1, n), VY: (1, n), VZ: (0, n - 1)})
    stress_step(FWD, 1, {SXX: (1, n - 1), SXY: (1, n - 1), SXZ: (1, n - 1)}, after=SRC)
    for z in range(*inner):
        f = [ring[FWD + s, z, 0:cy, :] for s in range(SXX, SYZ + 1)]
        a = [ring[ADJ + s, z, 0:cy, :] for s in range(SXX, SYZ + 1)]
        a = [value + ring[INJ, z, 0:cy, :] for value in a[:3]] + a[3:]
        keep[0, z - HALO], keep[1, z - HALO] = terms(f, a)
    velocity_step(FWD, 1, {VX: (2, n - 1), VY: (2, n - 1), VZ: (1, n - 2)})
    everything = set(range(SXX, SYZ + 1))
    for z in range(*inner):
        rates = stress_rates(FWD, z, everything)
        f = []
        for s in range(SXX, SYZ + 1):
            value = (at(FWD + s, z) + rates[s])[0:cy, :]
            f.append(value + own[SRC - ADJ + 1, z - HALO] if s <= SZZ else value)
        a = [own[s, z - HALO] for s in range(SXX, SYZ + 1)]
        term_lam, term_mu = terms(f, a)
        image_lam[z - HALO] = term_lam + keep[0, z - HALO]
        image_mu[z - HALO] = term_mu + keep[1, z - HALO]
    velocity_step(ADJ, -1, {VX: (1, n - 1), VY: (1, n - 1), VZ: (1, n - 1)})
    stress_step(ADJ, -1, {SXX: (2, n - 1), SXY: (1, n - 1), SXZ: (1, n - 2)}, before=INJ)
    for z in range(*inner):
        rates = velocity_rates(ADJ, z, {VX, VY, VZ})
        for f in (VX, VY, VZ):
            final[f, z - HALO] = (at(ADJ + f, z) - rates[f])[0:cy, :]
        for s in range(SXX, SYZ + 1):
            final[s, z - HALO] = ring[ADJ + s, z, 0:cy, :]


def swap_pairs(count, first):
    pairs = [(i + d, i + 1 - d) for i in range(first, count - 1, 2) for d in (0, 1)]
    return pairs + [(i, i) for i in range(count) if i not in dict(pairs)]


def swapped(value_a, value_b, axis):
    count = lax.axis_size(axis)
    got_a = lax.ppermute(value_a, axis, swap_pairs(count, 0))
    return got_a, None if value_b is None else lax.ppermute(value_b, axis, swap_pairs(count, 1))


def stay(value, spec):
    return pltpu.with_memory_space_constraint(value, pltpu.HBM) if spec.memory_space == pl.ANY else value


def kernel_call(body, args, in_specs, out_shape, scratch_shapes=(), aliases=None):
    here = [a is not None for a in args]
    there = [o is not None for o in out_shape]

    def run(*refs):
        refs = iter(refs)
        full = [next(refs) if h else None for h in here + there]
        body(*full, *refs)

    out = iter(
        pl.pallas_call(
            run,
            out_shape=tuple(o for o in out_shape if o is not None),
            in_specs=[s for s, h in zip(in_specs, here) if h],
            out_specs=tuple(vmem() for h in there if h),
            scratch_shapes=list(scratch_shapes),
            input_output_aliases=aliases or {},
            compiler_params=pltpu.CompilerParams(vmem_limit_bytes=VMEM_LIMIT),
        )(*[stay(a, s) for a, s in zip(args, in_specs) if a is not None])
    )
    return tuple(next(out) if h else None for h in there)


def on_device(
    checkpoint_store,
    holder_peer,
    holder_slot,
    adjoint_state,
    lame_lambda,
    lame_mu,
    buoyancy,
    source_cell,
    wavelet,
    receiver_cell,
    traces,
    plan,
):
    cz, cy, cx = lame_mu.shape
    layers = cz + 2 * HALO
    bf16, f32 = jnp.bfloat16, jnp.float32
    store = checkpoint_store.reshape(-1, cy, cx)
    tiles = store.shape[0]
    peer, slot = holder_peer[0, 0], holder_slot[0, 0]
    source, receiver = source_cell.reshape(1, -1), receiver_cell.reshape(1, -1)
    traces = traces.reshape(traces.shape[-2:])
    holders = lax.axis_size("gz")
    assert holders == 4
    near, far = face_counts(cz)
    face = 2 * near + far

    def shape(*dims, dtype=f32):
        return jax.ShapeDtypeStruct(dims, dtype)

    wide_x = lax.axis_size("gx") > 2
    chip = lax.ppermute(store, "gz", [(i, i ^ 2) for i in range(holders)])
    to_core, to_far, own = kernel_call(
        functools.partial(start_kernel, cz),
        (store, adjoint_state, lame_lambda, lame_mu, buoyancy, source, wavelet, receiver, traces, plan),
        [hbm()] * 10,
        (shape(tiles + face, cy, cx, dtype=bf16), shape(tiles + 4, cy, cx, dtype=bf16), shape(15, cz, cy, cx)),
        [
            pltpu.VMEM(receiver.shape, jnp.int32),
            pltpu.VMEM(traces.shape, f32),
            pltpu.SMEM(source.shape, jnp.int32),
            pltpu.SMEM(wavelet.shape, f32),
            pltpu.SMEM(plan.shape, jnp.int32),
            pltpu.SemaphoreType.DMA((10,)),
        ],
    )
    core = lax.ppermute(to_core, "gz", [(i, i ^ 1) for i in range(holders)])
    far_face = lax.ppermute(to_far, "gz", swap_pairs(holders, 1))
    both = lax.ppermute(chip, "gz", [(i, i ^ 1) for i in range(holders)])

    (ring_w,) = kernel_call(
        functools.partial(halo_kernel, cz, tiles),
        (core, far_face, own),
        [vmem()] * 3,
        (shape(FIELDS - ADJ, layers + 1, 2 * cy, cx),),
    )
    x_send = shape(x_tiles(), cy, cx, dtype=bf16)
    ring_f, x_a, x_b = kernel_call(
        functools.partial(column_kernel, cz),
        (store, core, chip, both, peer, slot, ring_w),
        [hbm()] + [vmem()] * 3 + [hbm()] * 2 + [vmem()],
        (shape(ADJ, layers + 1, 2 * cy, cx), x_send, x_send if wide_x else None),
        [
            pltpu.VMEM((holders, tiles, cy, cx), bf16),
            pltpu.SMEM(peer.shape, jnp.int32),
            pltpu.SMEM(slot.shape, jnp.int32),
            pltpu.SemaphoreType.DMA((6,)),
        ],
    )
    from_a, from_b = swapped(x_a, x_b, "gx")

    narrow, wide = row_counts(cz, cy)
    y_send = shape(narrow + 2 * wide, cy, cx, dtype=bf16)
    strips, y_a, y_b = kernel_call(
        functools.partial(rows_kernel, cz),
        (ring_f, ring_w, from_a, from_b),
        [vmem()] * 4,
        (shape(FIELDS, cy, cx), y_send, y_send),
        [pltpu.VMEM((2, narrow + wide, 8, cx), f32)],
    )
    gy = lax.axis_size("gy")
    turns = [
        [
            (i * holders + c, j * holders + c)
            for c in range(holders)
            for i, j in swap_pairs(gy, (c + turn) % 2)
        ]
        for turn in (0, 1)
    ]
    from_a = lax.ppermute(y_a, ("gy", "gz"), turns[0])
    from_b = lax.ppermute(y_b, ("gy", "gz"), turns[1])

    result = kernel_call(
        functools.partial(window_kernel, cz),
        (ring_f, ring_w, strips, from_a, from_b, own),
        [vmem()] * 6,
        (
            shape(9, cz, cy, cx),
            shape(cz, cy, cx),
            shape(cz, cy, cx),
            shape(*ring_f.shape),
            shape(*ring_w.shape),
        ),
        [
            pltpu.VMEM((2, narrow + wide, 8, cx), f32),
            pltpu.VMEM((2, cz, cy, cx), f32),
        ],
        {0: 3, 1: 4},
    )
    return result[:3]


def solution(mesh):
    return jax.shard_map(
        on_device,
        mesh=mesh,
        in_specs=(
            P("gz", None, None, "gy", "gx"),
            P("gx", "gy", None, None),
            P("gx", "gy", None, None),
            P(None, "gz", "gy", "gx"),
            P("gz", "gy", "gx"),
            P("gz", "gy", "gx"),
            P("gz", "gy", "gx"),
            P("gz", "gy", "gx", None),
            P(),
            P("gz", "gy", "gx", None),
            P("gz", "gy", "gx", None, None),
            P(),
        ),
        out_specs=(P(None, "gz", "gy", "gx"), P("gz", "gy", "gx"), P("gz", "gy", "gx")),
        check_vma=False,
    )
```

```python
import functools

import jax
import jax.numpy as jnp
from jax import lax
from jax.experimental import pallas as pl
from jax.experimental.pallas import tpu as pltpu
from jax.sharding import PartitionSpec as P

VX, VY, VZ, SXX, SYY, SZZ, SXY, SXZ, SYZ = range(9)
FWD, ADJ, BUOY, LAM, MU, INJ, SRC = 0, 9, 18, 19, 20, 21, 22
FIELDS = 23
HALO = 2

ADJ_Z = {VX: (2, 2), VY: (2, 2), VZ: (2, 2), SXX: (1, 1), SYY: (1, 1), SZZ: (1, 2), SXY: (1, 1), SXZ: (2, 1), SYZ: (2, 1)}
OTHER_Z = {BUOY: (2, 2), LAM: (1, 2), MU: (2, 2), INJ: (0, 1), SRC: (1, 1)}
F32_Z = {**{ADJ + f: c for f, c in ADJ_Z.items()}, **OTHER_Z}

Y_ROWS = {
    FWD + VX: (None, (2, -1, 1), (1, -1, 1), (2, -2, 0)),
    FWD + VY: ((2, -2, 0), (1, -1, 1), (2, -1, 1), None),
    FWD + VZ: (None, (1, -2, 1), (1, -1, 1), (2, -2, 0)),
    FWD + SXX: (None, (2, -1, 1), (1, -1, 1), (2, -2, 1)),
    FWD + SYY: ((2, -2, 0), (1, -1, 1), (1, 0, 1), (2, -1, 1)),
    FWD + SZZ: (None, (1, -1, 1), (1, 0, 1), (2, -1, 0)),
    FWD + SXY: ((2, -1, 1), (1, 0, 1), (1, -1, 1), (2, -2, 0)),
    FWD + SXZ: (None, (1, -1, 1), (0, -1, 1), (1, -2, 1)),
    FWD + SYZ: ((1, -2, 1), (0, -1, 1), (1, -1, 1), (2, -2, 0)),
    ADJ + VX: ((2, -2, 0), (1, -1, 1), (1, -1, 1), (2, -2, 1)),
    ADJ + VY: ((2, -1, 1), (1, 0, 1), (1, -1, 1), (2, -2, 0)),
    ADJ + VZ: ((2, -2, 0), (1, -1, 1), (0, -1, 1), (1, -2, 0)),
    ADJ + SXX: (None, (2, -2, 1), (2, -2, 1), None),
    ADJ + SYY: (None, (2, -1, 1), (1, -1, 1), (2, -2, 0)),
    ADJ + SZZ: (None, (2, -1, 0), (1, -1, 0), None),
    ADJ + SXY: ((2, -2, 0), (1, -1, 1), (2, -2, 1), None),
    ADJ + SXZ: (None, (1, -2, 1), (1, -2, 1), None),
    ADJ + SYZ: ((2, -2, 0), (1, -1, 1), (1, -2, 0), None),
    BUOY: ((2, -2, 0), (1, -1, 1), (1, -1, 1), (2, -2, 0)),
    LAM: (None, (2, -1, 1), (1, -1, 1), (2, -2, 0)),
    MU: ((2, -2, 0), (1, -1, 1), (1, -1, 1), (2, -2, 0)),
    INJ: (None, None, (2, -2, 0), None),
    SRC: (None, (2, -2, 0), (2, -1, 1), None),
}

VMEM_LIMIT = 48 * 1024 * 1024


def vmem():
    return pl.BlockSpec(memory_space=pltpu.VMEM)


def hbm():
    return pl.BlockSpec(memory_space=pl.ANY)


def faces(cz, up):
    near, far = [], []
    for f in sorted(F32_Z):
        before, after = F32_Z[f]
        depth = before if up else after
        for d in range(depth):
            layer = cz - 1 - d if up else d
            (far if d else near).append((f, layer, HALO - 1 - d if up else HALO + cz + d))
    return near, far


def face_counts(cz):
    sides = [faces(cz, up) for up in (True, False)]
    return max(len(s[0]) for s in sides), max(len(s[1]) for s in sides)


def y_rows(cz, cy, up):
    layers = cz + 2 * HALO
    narrow, wide = [], []
    for f in sorted(Y_ROWS):
        for offset in (-1, -2) if up else (0, 1):
            spec = Y_ROWS[f][offset + HALO]
            if spec is None:
                continue
            source = cy + offset if up else offset
            target = 2 * cy + offset if up else cy + offset
            listed = list(range(spec[0], layers + spec[1])) + [layers] * spec[2]
            near = offset in (-1, 0)
            (wide if f >= ADJ and near else narrow).extend((f, z, source, target) for z in listed)
    return narrow, wide


def row_counts(cz, cy):
    sides = [y_rows(cz, cy, up) for up in (True, False)]
    return tuple(max(-(-len(s[i]) // 8) for s in sides) for i in (0, 1))


def split(value):
    high = value.astype(jnp.bfloat16)
    low = (value - high.astype(jnp.float32)).astype(jnp.bfloat16)
    return high, low


def joined(high, low):
    return high.astype(jnp.float32) + low.astype(jnp.float32)


def even_mask(axes, shape):
    total = sum(lax.axis_index(a) for a in ((axes,) if isinstance(axes, str) else axes))
    return jnp.full(shape, lax.rem(total, 2), jnp.int32) == 0


def has_neighbours(axis):
    index = lax.axis_index(axis)
    return (index > 0).astype(jnp.float32), (index < lax.axis_size(axis) - 1).astype(jnp.float32)


def copies(sems, *pairs):
    out = [pltpu.make_async_copy(source, target, sems.at[i]) for i, (source, target) in enumerate(pairs)]
    for copy in out:
        copy.start()
    return out


def pack_rows(cz, cy, row_of, packed, send_a, send_b):
    narrow, wide = row_counts(cz, cy)
    for side, up in enumerate((True, False)):
        for base, listed in zip((0, narrow), y_rows(cz, cy, up)):
            for r, (f, z, y, _) in enumerate(listed):
                packed[side, base + r // 8, r % 8 : r % 8 + 1, :] = row_of(f, z, y)
    even = even_mask(("gy", "gz"), packed.shape[2:])
    for t in range(narrow + wide):
        up, down = packed[0, t], packed[1, t]
        for out, value in ((send_a, jnp.where(even, up, down)), (send_b, jnp.where(even, down, up))):
            if out is None:
                continue
            if t < narrow:
                out[t] = value.astype(jnp.bfloat16)
            else:
                out[t], out[wide + t] = split(value)


def unpack_rows(cz, cy, from_a, from_b, packed, put_row):
    narrow, wide = row_counts(cz, cy)
    has_lower, has_upper = has_neighbours("gy")
    even = even_mask(("gy", "gz"), packed.shape[2:])
    for t in range(narrow + wide):
        got = []
        for ref in (from_a, from_b):
            if ref is None:
                got.append(jnp.zeros(packed.shape[2:], jnp.float32))
            elif t < narrow:
                got.append(ref[t].astype(jnp.float32))
            else:
                got.append(joined(ref[t], ref[wide + t]))
        packed[0, t] = jnp.where(even, got[1], got[0]) * has_lower
        packed[1, t] = jnp.where(even, got[0], got[1]) * has_upper
    for side, up in enumerate((True, False)):
        for base, listed in zip((0, narrow), y_rows(cz, cy, up)):
            for r, (f, z, _, y) in enumerate(listed):
                put_row(f, z, y, packed[side, base + r // 8, r % 8 : r % 8 + 1, :])


def start_kernel(
    cz, store, adjoint, lam, mu, buoy, source, wavelet, receiver, traces, plan,
    near_out, far_out, own, cells, samples, spots, wave, steps, sems,
):
    cy, lanes = own.shape[2], own.shape[3]
    rows = cz * cy
    tiles = store.shape[0]
    small = copies(sems, (plan, steps), (wavelet, wave), (source, spots), (receiver, cells), (traces, samples))
    large = copies(
        sems.at[pl.ds(len(small), 5)],
        (adjoint, own.at[pl.ds(0, 9)]),
        (buoy, own.at[BUOY - ADJ]),
        (lam, own.at[LAM - ADJ]),
        (mu, own.at[MU - ADJ]),
        (store, near_out.at[pl.ds(0, tiles)]),
    )
    for copy in small:
        copy.wait()
    listed = cells[...]
    count = listed.shape[1]
    row_hot = (lax.broadcasted_iota(jnp.int32, (rows, count), 0) == listed // lanes).astype(jnp.float32)
    lane_hit = lax.broadcasted_iota(jnp.int32, (lanes, count), 0) == listed % lanes
    injected = []
    for step in (1, 0):
        sample = samples[pl.ds(steps[step], 1), :]
        field = lax.dot_general(
            row_hot,
            jnp.where(lane_hit, sample, 0.0),
            (((1,), (1,)), ((), ())),
            precision=lax.Precision.HIGHEST,
            preferred_element_type=jnp.float32,
        )
        injected.append(field.reshape(cz, cy, lanes))
    own[INJ - ADJ] = injected[1]
    flat = lax.broadcasted_iota(jnp.int32, (rows, lanes), 0) * lanes + lax.broadcasted_iota(jnp.int32, (rows, lanes), 1)
    for step in range(2):
        value = wave[steps[step]]
        field = jnp.zeros((rows, lanes), jnp.float32)
        for j in range(source.shape[1]):
            field = field + jnp.where(flat == spots[0, j], value, 0.0)
        own[SRC - ADJ + step] = field.reshape(cz, cy, lanes)
    for copy in large:
        copy.wait()
    for f in (SXX, SYY, SZZ):
        own[f] = own[f] + injected[0]

    even = even_mask("gz", (cy, lanes))
    near, far = face_counts(cz)
    up, down = faces(cz, True), faces(cz, False)
    zero = jnp.zeros((cy, lanes), jnp.float32)

    def tile(side, i):
        return own[side[i][0] - ADJ, side[i][1]] if i < len(side) else zero

    for i in range(near):
        above, below = tile(up[0], i), tile(down[0], i)
        for out, base, value in (
            (near_out, tiles, jnp.where(even, above, below)),
            (far_out, 0, jnp.where(even, below, above)),
        ):
            out[base + i], out[base + near + i] = split(value)
    for i in range(far):
        above, below = tile(up[1], i), tile(down[1], i)
        near_out[tiles + 2 * near + i] = jnp.where(even, above, below).astype(jnp.bfloat16)
        far_out[2 * near + i] = jnp.where(even, below, above).astype(jnp.bfloat16)
    for i in range(2 * near + far, far_out.shape[0]):
        far_out[i] = zero.astype(jnp.bfloat16)


def strip_of(main, layers):
    cy, lanes = main(0).shape
    lane = lax.broadcasted_iota(jnp.int32, (cy, lanes), 1)
    position = lane % 8
    group = lane // 8
    tile = jnp.zeros((cy, lanes), jnp.float32)
    for z in range(layers):
        tail = pltpu.roll(main(z), (8 * z + 2) % lanes, 1)
        head = pltpu.roll(main(z), (8 * z + 6) % lanes, 1)
        here = group == z
        tile = jnp.where(here & (position < 2), tail, jnp.where(here & (position >= 6), head, tile))
    return tile


def halo_kernel(cz, tiles, core, far, own, ring):
    cy, lanes = own.shape[2], own.shape[3]
    layers = cz + 2 * HALO
    ring_rows = ring.shape[2]
    near, _ = face_counts(cz)
    even = even_mask("gz", (cy, lanes))
    has_below, has_above = has_neighbours("gz")
    zero = jnp.zeros((cy, lanes), jnp.float32)
    for f in range(ring.shape[0]):
        for z in range(cz):
            ring[f, HALO + z, 0:cy, :] = own[f, z]
    filled = set()
    for up in (True, False):
        for depth, listed in enumerate(faces(cz, up)):
            for i, (f, _, z) in enumerate(listed):
                values = []
                for ref, base in ((core, tiles), (far, 0)):
                    if depth == 0:
                        values.append(joined(ref[base + i], ref[base + near + i]))
                    else:
                        values.append(ref[base + 2 * near + i].astype(jnp.float32))
                value = jnp.where(even, values[1], values[0]) if up else jnp.where(even, values[0], values[1])
                ring[f - ADJ, z, 0:cy, :] = value * (has_below if up else has_above)
                filled.add((f - ADJ, z))
    for f in range(ring.shape[0]):
        for z in (0, 1, layers - 2, layers - 1):
            if (f, z) not in filled:
                ring[f, z, 0:cy, :] = zero
        ring[f, layers, 0:cy, :] = strip_of(lambda z: ring[f, z, 0:cy, :], layers)
        for z in range(layers + 1):
            ring[f, z, cy:ring_rows, :] = jnp.zeros((ring_rows - cy, lanes), jnp.float32)


def column_kernel(
    cz, store, core, chip, both_a, both_b, peer, slot, ring_w, ring, send_a, send_b, stores, peers, slots, sems
):
    cy, lanes = core.shape[1], core.shape[2]
    layers = cz + 2 * HALO
    ring_rows = ring.shape[2]
    tiles = store.shape[0]
    me = lax.axis_index("gz")
    count = lax.axis_size("gz")
    moves = copies(
        sems,
        (peer, peers),
        (slot, slots),
        (store, stores.at[me]),
        (core.at[pl.ds(0, tiles)], stores.at[me ^ 1]),
        (chip, stores.at[me ^ 2]),
        (both_a, stores.at[me ^ 3, pl.ds(0, both_a.shape[0])]),
        (both_b, stores.at[me ^ 3, pl.ds(both_a.shape[0], both_b.shape[0])]),
    )
    zero = jnp.zeros((cy, lanes), jnp.float32)
    for f in range(9):
        for z in range(layers + 1):
            ring[f, z, cy:ring_rows, :] = jnp.zeros((ring_rows - cy, lanes), jnp.float32)
    for move in moves:
        move.wait()
    below, above = jnp.maximum(me - 1, 0), jnp.minimum(me + 1, count - 1)
    has_below, has_above = has_neighbours("gz")
    for z in range(layers):
        if z < HALO:
            brick, piece, keep = below, cz - HALO + z, has_below
        elif z < HALO + cz:
            brick, piece, keep = me, z - HALO, None
        else:
            brick, piece, keep = above, z - HALO - cz, has_above
        holder = peers[brick, piece]
        row = slots[brick, piece] * 9
        for f in range(9):
            value = stores[holder, row + f].astype(jnp.float32)
            ring[f, z, 0:cy, :] = value if keep is None else value * keep
    for f in range(9):
        ring[f, layers, 0:cy, :] = strip_of(lambda z: ring[f, z, 0:cy, :], layers)
    strip = [ring[f, layers, 0:cy, :] for f in range(9)]
    strip += [ring_w[f, layers, 0:cy, :] for f in range(ring_w.shape[0])]
    position = lax.broadcasted_iota(jnp.int32, (cy, lanes), 1) % 8
    even_x = even_mask("gx", (cy, lanes))
    for out, tail_from_even in ((send_a, True), (send_b, False)):
        if out is None:
            continue
        place = 0
        for fields, narrow in ((range(ADJ), True), (range(ADJ, FIELDS), False)):
            quads = [fields[i : i + 4] for i in range(0, len(fields), 4)]
            for i, quad in enumerate(quads):
                tile = zero
                for g, f in enumerate(quad):
                    tail, head = strip[f], pltpu.roll(strip[f], lanes - 6, 1)
                    value = jnp.where(even_x, tail, head) if tail_from_even else jnp.where(even_x, head, tail)
                    value = value if g == 0 else pltpu.roll(value, 2 * g, 1)
                    tile = jnp.where(position // 2 == g, value, tile)
                high, low = split(tile)
                out[place + i] = high
                if not narrow:
                    out[place + len(quads) + i] = low
            place += len(quads) if narrow else 2 * len(quads)


def x_tiles():
    return -(-ADJ // 4) + 2 * -(-(FIELDS - ADJ) // 4)


def rows_kernel(cz, ring_f, ring_w, from_a, from_b, strips, send_a, send_b, packed):
    cy, lanes = strips.shape[1], strips.shape[2]
    layers = cz + 2 * HALO
    strip = [ring_f[f, layers, 0:cy, :] for f in range(9)]
    strip += [ring_w[f, layers, 0:cy, :] for f in range(ring_w.shape[0])]
    position = lax.broadcasted_iota(jnp.int32, (cy, lanes), 1) % 8
    even_x = even_mask("gx", (cy, lanes))
    has_left, has_right = has_neighbours("gx")
    zero = jnp.zeros((cy, lanes), jnp.float32)
    place = 0
    for fields, narrow in ((range(ADJ), True), (range(ADJ, FIELDS), False)):
        quads = [fields[i : i + 4] for i in range(0, len(fields), 4)]
        for i, quad in enumerate(quads):
            got = []
            for ref in (from_a, from_b):
                if ref is None:
                    got.append(zero)
                elif narrow:
                    got.append(ref[place + i].astype(jnp.float32))
                else:
                    got.append(joined(ref[place + i], ref[place + len(quads) + i]))
            right = jnp.where(even_x, got[0], got[1]) * has_right
            left = jnp.where(even_x, got[1], got[0]) * has_left
            for g, f in enumerate(quad):
                tile = jnp.where(position // 2 == 1, pltpu.roll(right, (2 - 2 * g) % lanes, 1), strip[f])
                strips[f] = jnp.where(position // 2 == 2, pltpu.roll(left, (4 - 2 * g) % lanes, 1), tile)
        place += len(quads) if narrow else 2 * len(quads)

    def row_of(f, z, y):
        if z == layers:
            return strips[f, y : y + 1, :]
        return ring_f[f, z, y : y + 1, :] if f < ADJ else ring_w[f - ADJ, z, y : y + 1, :]

    pack_rows(cz, cy, row_of, packed, send_a, send_b)


class Ring:
    def __init__(self, ring_f, ring_w):
        self.parts = ring_f, ring_w

    def __getitem__(self, key):
        f = key[0]
        return self.parts[0][key] if f < ADJ else self.parts[1][(f - ADJ, *key[1:])]

    def __setitem__(self, key, value):
        f = key[0]
        if f < ADJ:
            self.parts[0][key] = value
        else:
            self.parts[1][(f - ADJ, *key[1:])] = value


def window_kernel(
    cz, ring_f_in, ring_w_in, strips, from_a, from_b, own, final, image_lam, image_mu, ring_f, ring_w, packed, keep
):
    cy, lanes = own.shape[2], own.shape[3]
    layers = cz + 2 * HALO
    ring_rows = ring_f.shape[2]
    ring = Ring(ring_f, ring_w)
    for f in range(FIELDS):
        ring[f, layers, 0:cy, :] = strips[f]

    def put_row(f, z, y, value):
        ring[f, z, y : y + 1, :] = value

    unpack_rows(cz, cy, from_a, from_b, packed, put_row)

    lane = lax.broadcasted_iota(jnp.int32, (ring_rows, lanes), 1)
    first_lane, last_lane = lane == 0, lane == lanes - 1
    edge = layers

    def at(f, z):
        return ring[f, z]

    def x_next(f, z):
        value = at(f, z)
        if z == edge:
            return pltpu.roll(value, lanes - 1, 1)
        beyond = pltpu.roll(at(f, edge), (lanes - 1 - (8 * z + 2)) % lanes, 1)
        return jnp.where(last_lane, beyond, pltpu.roll(value, lanes - 1, 1))

    def x_prev(f, z):
        value = at(f, z)
        if z == edge:
            return pltpu.roll(value, 1, 1)
        beyond = pltpu.roll(at(f, edge), (lanes - (8 * z + 5)) % lanes, 1)
        return jnp.where(first_lane, beyond, pltpu.roll(value, 1, 1))

    def y_next(f, z):
        return pltpu.roll(at(f, z), ring_rows - 1, 0)

    def y_prev(f, z):
        return pltpu.roll(at(f, z), 1, 0)

    def z_next(f, z):
        return pltpu.roll(at(f, edge), lanes - 8, 1) if z == edge else at(f, z + 1)

    def z_prev(f, z):
        return pltpu.roll(at(f, edge), 8, 1) if z == edge else at(f, z - 1)

    def velocity_rates(base, z, want):
        buoy = at(BUOY, z)
        sxx, syy, szz = (functools.partial(at, base + f) for f in (SXX, SYY, SZZ))
        sxy, sxz, syz = (functools.partial(at, base + f) for f in (SXY, SXZ, SYZ))
        out = {}
        if VX in want:
            out[VX] = buoy * (
                (x_next(base + SXX, z) - sxx(z)) + (sxy(z) - y_prev(base + SXY, z)) + (sxz(z) - z_prev(base + SXZ, z))
            )
        if VY in want:
            out[VY] = buoy * (
                (sxy(z) - x_prev(base + SXY, z)) + (y_next(base + SYY, z) - syy(z)) + (syz(z) - z_prev(base + SYZ, z))
            )
        if VZ in want:
            out[VZ] = buoy * (
                (sxz(z) - x_prev(base + SXZ, z)) + (syz(z) - y_prev(base + SYZ, z)) + (z_next(base + SZZ, z) - szz(z))
            )
        return out

    def stress_rates(base, z, want):
        lam, mu = at(LAM, z), at(MU, z)
        vx, vy, vz = at(base + VX, z), at(base + VY, z), at(base + VZ, z)
        out = {}
        if SXX in want:
            exx = vx - x_prev(base + VX, z)
            eyy = vy - y_prev(base + VY, z)
            ezz = vz - z_prev(base + VZ, z)
            common = lam * (exx + eyy + ezz)
            twice = 2.0 * mu
            out[SXX] = common + twice * exx
            out[SYY] = common + twice * eyy
            out[SZZ] = common + twice * ezz
        if SXY in want:
            out[SXY] = mu * ((y_next(base + VX, z) - vx) + (x_next(base + VY, z) - vy))
        if SXZ in want:
            out[SXZ] = mu * ((z_next(base + VX, z) - vx) + (x_next(base + VZ, z) - vz))
            out[SYZ] = mu * ((z_next(base + VY, z) - vy) + (y_next(base + VZ, z) - vz))
        return out

    def spread(ranges):
        for z in list(range(layers)) + [edge]:
            want = {f for f, (a, b) in ranges.items() if z == edge or a <= z < b}
            if want:
                yield z, want

    def velocity_step(base, sign, ranges):
        for z, want in spread(ranges):
            for f, rate in velocity_rates(base, z, want).items():
                ring[base + f, z] = at(base + f, z) + rate if sign > 0 else at(base + f, z) - rate

    def stress_step(base, sign, ranges, before=None, after=None):
        for z, want in spread(ranges):
            for f, rate in stress_rates(base, z, want).items():
                value, normal = at(base + f, z), f in (SXX, SYY, SZZ)
                if before is not None and normal:
                    value = value + at(before, z)
                value = value + rate if sign > 0 else value - rate
                if after is not None and normal:
                    value = value + at(after, z)
                ring[base + f, z] = value

    def terms(f, a):
        term_lam = (f[0] + f[1] + f[2]) * (a[0] + a[1] + a[2])
        term_mu = f[0] * a[0] + f[1] * a[1] + f[2] * a[2] + 2.0 * (f[3] * a[3] + f[4] * a[4] + f[5] * a[5])
        return term_lam, term_mu

    inner = (HALO, HALO + cz)
    n = layers
    stress_step(ADJ, -1, {SXX: (1, n), SXY: (0, n), SXZ: (0, n - 1)})
    velocity_step(FWD, 1, {VX: (1, n), VY: (1, n), VZ: (0, n - 1)})
    stress_step(FWD, 1, {SXX: (1, n - 1), SXY: (1, n - 1), SXZ: (1, n - 1)}, after=SRC)
    for z in range(*inner):
        f = [ring[FWD + s, z, 0:cy, :] for s in range(SXX, SYZ + 1)]
        a = [ring[ADJ + s, z, 0:cy, :] for s in range(SXX, SYZ + 1)]
        a = [value + ring[INJ, z, 0:cy, :] for value in a[:3]] + a[3:]
        keep[0, z - HALO], keep[1, z - HALO] = terms(f, a)
    velocity_step(FWD, 1, {VX: (2, n - 1), VY: (2, n - 1), VZ: (1, n - 2)})
    everything = set(range(SXX, SYZ + 1))
    for z in range(*inner):
        rates = stress_rates(FWD, z, everything)
        f = []
        for s in range(SXX, SYZ + 1):
            value = (at(FWD + s, z) + rates[s])[0:cy, :]
            f.append(value + own[SRC - ADJ + 1, z - HALO] if s <= SZZ else value)
        a = [own[s, z - HALO] for s in range(SXX, SYZ + 1)]
        term_lam, term_mu = terms(f, a)
        image_lam[z - HALO] = term_lam + keep[0, z - HALO]
        image_mu[z - HALO] = term_mu + keep[1, z - HALO]
    velocity_step(ADJ, -1, {VX: (1, n - 1), VY: (1, n - 1), VZ: (1, n - 1)})
    stress_step(ADJ, -1, {SXX: (2, n - 1), SXY: (1, n - 1), SXZ: (1, n - 2)}, before=INJ)
    for z in range(*inner):
        rates = velocity_rates(ADJ, z, {VX, VY, VZ})
        for f in (VX, VY, VZ):
            final[f, z - HALO] = (at(ADJ + f, z) - rates[f])[0:cy, :]
        for s in range(SXX, SYZ + 1):
            final[s, z - HALO] = ring[ADJ + s, z, 0:cy, :]


def swap_pairs(count, first):
    pairs = [(i + d, i + 1 - d) for i in range(first, count - 1, 2) for d in (0, 1)]
    return pairs + [(i, i) for i in range(count) if i not in dict(pairs)]


def swapped(value_a, value_b, axis):
    count = lax.axis_size(axis)
    got_a = lax.ppermute(value_a, axis, swap_pairs(count, 0))
    return got_a, None if value_b is None else lax.ppermute(value_b, axis, swap_pairs(count, 1))


def stay(value, spec):
    return pltpu.with_memory_space_constraint(value, pltpu.HBM) if spec.memory_space == pl.ANY else value


def kernel_call(body, args, in_specs, out_shape, scratch_shapes=(), aliases=None):
    here = [a is not None for a in args]
    there = [o is not None for o in out_shape]

    def run(*refs):
        refs = iter(refs)
        full = [next(refs) if h else None for h in here + there]
        body(*full, *refs)

    out = iter(
        pl.pallas_call(
            run,
            out_shape=tuple(o for o in out_shape if o is not None),
            in_specs=[s for s, h in zip(in_specs, here) if h],
            out_specs=tuple(vmem() for h in there if h),
            scratch_shapes=list(scratch_shapes),
            input_output_aliases=aliases or {},
            compiler_params=pltpu.CompilerParams(vmem_limit_bytes=VMEM_LIMIT),
        )(*[stay(a, s) for a, s in zip(args, in_specs) if a is not None])
    )
    return tuple(next(out) if h else None for h in there)


def on_device(
    checkpoint_store,
    holder_peer,
    holder_slot,
    adjoint_state,
    lame_lambda,
    lame_mu,
    buoyancy,
    source_cell,
    wavelet,
    receiver_cell,
    traces,
    plan,
):
    cz, cy, cx = lame_mu.shape
    layers = cz + 2 * HALO
    bf16, f32 = jnp.bfloat16, jnp.float32
    store = checkpoint_store.reshape(-1, cy, cx)
    tiles = store.shape[0]
    peer, slot = holder_peer[0, 0], holder_slot[0, 0]
    source, receiver = source_cell.reshape(1, -1), receiver_cell.reshape(1, -1)
    traces = traces.reshape(traces.shape[-2:])
    holders = lax.axis_size("gz")
    assert holders == 4
    near, far = face_counts(cz)
    face = 2 * near + far
    half = tiles // 2

    def shape(*dims, dtype=f32):
        return jax.ShapeDtypeStruct(dims, dtype)

    wide_x = lax.axis_size("gx") > 2
    chip = lax.ppermute(store, "gz", [(i, i ^ 2) for i in range(holders)])
    to_core, to_far, own = kernel_call(
        functools.partial(start_kernel, cz),
        (store, adjoint_state, lame_lambda, lame_mu, buoyancy, source, wavelet, receiver, traces, plan),
        [hbm()] * 10,
        (shape(tiles + face, cy, cx, dtype=bf16), shape(max(face, half) + 4, cy, cx, dtype=bf16), shape(15, cz, cy, cx)),
        [
            pltpu.VMEM(receiver.shape, jnp.int32),
            pltpu.VMEM(traces.shape, f32),
            pltpu.SMEM(source.shape, jnp.int32),
            pltpu.SMEM(wavelet.shape, f32),
            pltpu.SMEM(plan.shape, jnp.int32),
            pltpu.SemaphoreType.DMA((10,)),
        ],
    )
    core = lax.ppermute(to_core, "gz", [(i, i ^ 1) for i in range(holders)])
    far_face = lax.ppermute(to_far, "gz", [(i, i ^ 3) for i in range(holders)])
    both = [lax.ppermute(part, "gz", [(i, i ^ 1) for i in range(holders)]) for part in (chip[:half], chip[half:])]

    (ring_w,) = kernel_call(
        functools.partial(halo_kernel, cz, tiles),
        (core, far_face, own),
        [vmem()] * 3,
        (shape(FIELDS - ADJ, layers + 1, 2 * cy, cx),),
    )
    x_send = shape(x_tiles(), cy, cx, dtype=bf16)
    ring_f, x_a, x_b = kernel_call(
        functools.partial(column_kernel, cz),
        (store, core, chip, *both, peer, slot, ring_w),
        [hbm()] + [vmem()] * 4 + [hbm()] * 2 + [vmem()],
        (shape(ADJ, layers + 1, 2 * cy, cx), x_send, x_send if wide_x else None),
        [
            pltpu.VMEM((holders, tiles, cy, cx), bf16),
            pltpu.SMEM(peer.shape, jnp.int32),
            pltpu.SMEM(slot.shape, jnp.int32),
            pltpu.SemaphoreType.DMA((7,)),
        ],
    )
    from_a, from_b = swapped(x_a, x_b, "gx")

    narrow, wide = row_counts(cz, cy)
    y_send = shape(narrow + 2 * wide, cy, cx, dtype=bf16)
    strips, y_a, y_b = kernel_call(
        functools.partial(rows_kernel, cz),
        (ring_f, ring_w, from_a, from_b),
        [vmem()] * 4,
        (shape(FIELDS, cy, cx), y_send, y_send),
        [pltpu.VMEM((2, narrow + wide, 8, cx), f32)],
    )
    gy = lax.axis_size("gy")
    turns = [[], []]
    for turn, pairs in enumerate(turns):
        for c in range(holders):
            first = (c + turn) % 2
            change = dict(swap_pairs(gy, first))
            pairs.extend((i * holders + c, (i * holders + (c ^ 2)) if j == i else (j * holders + c)) for i, j in change.items())
    from_a = lax.ppermute(y_a, ("gy", "gz"), turns[0])
    from_b = lax.ppermute(y_b, ("gy", "gz"), turns[1])

    result = kernel_call(
        functools.partial(window_kernel, cz),
        (ring_f, ring_w, strips, from_a, from_b, own),
        [vmem()] * 6,
        (
            shape(9, cz, cy, cx),
            shape(cz, cy, cx),
            shape(cz, cy, cx),
            shape(*ring_f.shape),
            shape(*ring_w.shape),
        ),
        [
            pltpu.VMEM((2, narrow + wide, 8, cx), f32),
            pltpu.VMEM((2, cz, cy, cx), f32),
        ],
        {0: 3, 1: 4},
    )
    return result[:3]


def solution(mesh):
    return jax.shard_map(
        on_device,
        mesh=mesh,
        in_specs=(
            P("gz", None, None, "gy", "gx"),
            P("gx", "gy", None, None),
            P("gx", "gy", None, None),
            P(None, "gz", "gy", "gx"),
            P("gz", "gy", "gx"),
            P("gz", "gy", "gx"),
            P("gz", "gy", "gx"),
            P("gz", "gy", "gx", None),
            P(),
            P("gz", "gy", "gx", None),
            P("gz", "gy", "gx", None, None),
            P(),
        ),
        out_specs=(P(None, "gz", "gy", "gx"), P("gz", "gy", "gx"), P("gz", "gy", "gx")),
        check_vma=False,
    )
```

```python
import functools

import jax
import jax.numpy as jnp
from jax import lax
from jax.experimental import pallas as pl
from jax.experimental.pallas import tpu as pltpu
from jax.sharding import PartitionSpec as P

VX, VY, VZ, SXX, SYY, SZZ, SXY, SXZ, SYZ = range(9)
FWD, ADJ, BUOY, LAM, MU, INJ, SRC = 0, 9, 18, 19, 20, 21, 22
FIELDS = 23
HALO = 2

ADJ_Z = {VX: (2, 2), VY: (2, 2), VZ: (2, 2), SXX: (1, 1), SYY: (1, 1), SZZ: (1, 2), SXY: (1, 1), SXZ: (2, 1), SYZ: (2, 1)}
OTHER_Z = {BUOY: (2, 2), LAM: (1, 2), MU: (2, 2), INJ: (0, 1), SRC: (1, 1)}
F32_Z = {**{ADJ + f: c for f, c in ADJ_Z.items()}, **OTHER_Z}

Y_ROWS = {
    FWD + VX: (None, (2, -1, 1), (1, -1, 1), (2, -2, 0)),
    FWD + VY: ((2, -2, 0), (1, -1, 1), (2, -1, 1), None),
    FWD + VZ: (None, (1, -2, 1), (1, -1, 1), (2, -2, 0)),
    FWD + SXX: (None, (2, -1, 1), (1, -1, 1), (2, -2, 1)),
    FWD + SYY: ((2, -2, 0), (1, -1, 1), (1, 0, 1), (2, -1, 1)),
    FWD + SZZ: (None, (1, -1, 1), (1, 0, 1), (2, -1, 0)),
    FWD + SXY: ((2, -1, 1), (1, 0, 1), (1, -1, 1), (2, -2, 0)),
    FWD + SXZ: (None, (1, -1, 1), (0, -1, 1), (1, -2, 1)),
    FWD + SYZ: ((1, -2, 1), (0, -1, 1), (1, -1, 1), (2, -2, 0)),
    ADJ + VX: ((2, -2, 0), (1, -1, 1), (1, -1, 1), (2, -2, 1)),
    ADJ + VY: ((2, -1, 1), (1, 0, 1), (1, -1, 1), (2, -2, 0)),
    ADJ + VZ: ((2, -2, 0), (1, -1, 1), (0, -1, 1), (1, -2, 0)),
    ADJ + SXX: (None, (2, -2, 1), (2, -2, 1), None),
    ADJ + SYY: (None, (2, -1, 1), (1, -1, 1), (2, -2, 0)),
    ADJ + SZZ: (None, (2, -1, 0), (1, -1, 0), None),
    ADJ + SXY: ((2, -2, 0), (1, -1, 1), (2, -2, 1), None),
    ADJ + SXZ: (None, (1, -2, 1), (1, -2, 1), None),
    ADJ + SYZ: ((2, -2, 0), (1, -1, 1), (1, -2, 0), None),
    BUOY: ((2, -2, 0), (1, -1, 1), (1, -1, 1), (2, -2, 0)),
    LAM: (None, (2, -1, 1), (1, -1, 1), (2, -2, 0)),
    MU: ((2, -2, 0), (1, -1, 1), (1, -1, 1), (2, -2, 0)),
    INJ: (None, None, (2, -2, 0), None),
    SRC: (None, (2, -2, 0), (2, -1, 1), None),
}

EXACT_ROWS = {-1: (ADJ + VY, ADJ + SXY, ADJ + SYZ, BUOY, SRC), 0: (ADJ + SYY, LAM, INJ, SRC)}

PAD = 1
VMEM_LIMIT = 48 * 1024 * 1024


def vmem():
    return pl.BlockSpec(memory_space=pltpu.VMEM)


def hbm():
    return pl.BlockSpec(memory_space=pl.ANY)


def faces(cz, up):
    near, far = [], []
    for f in sorted(F32_Z):
        before, after = F32_Z[f]
        depth = before if up else after
        for d in range(depth):
            layer = cz - 1 - d if up else d
            (far if d else near).append((f, layer, HALO - 1 - d if up else HALO + cz + d))
    return near, far


def face_counts(cz):
    sides = [faces(cz, up) for up in (True, False)]
    return max(len(s[0]) for s in sides), max(len(s[1]) for s in sides)


def y_rows(cz, cy, up):
    layers = cz + 2 * HALO
    narrow, wide = [], []
    for f in sorted(Y_ROWS):
        for offset in (-1, -2) if up else (0, 1):
            spec = Y_ROWS[f][offset + HALO]
            if spec is None:
                continue
            source = cy + offset if up else offset
            target = 2 * cy + offset if up else cy + offset
            listed = list(range(spec[0], layers + spec[1])) + [layers] * spec[2]
            exact = f in EXACT_ROWS.get(offset, ())
            (wide if exact else narrow).extend((f, z, source, target) for z in listed)
    return narrow, wide


def row_counts(cz, cy, up):
    return tuple(-(-len(rows) // 8) for rows in y_rows(cz, cy, up))


def row_tiles(cz, cy):
    return max(narrow + 2 * wide for narrow, wide in (row_counts(cz, cy, up) for up in (True, False)))


def split(value):
    high = value.astype(jnp.bfloat16)
    low = (value - high.astype(jnp.float32)).astype(jnp.bfloat16)
    return high, low


def joined(high, low):
    return high.astype(jnp.float32) + low.astype(jnp.float32)


def even_mask(axes, shape):
    total = sum(lax.axis_index(a) for a in ((axes,) if isinstance(axes, str) else axes))
    return jnp.full(shape, lax.rem(total, 2), jnp.int32) == 0


def has_neighbours(axis):
    index = lax.axis_index(axis)
    return (index > 0).astype(jnp.float32), (index < lax.axis_size(axis) - 1).astype(jnp.float32)


def copies(sems, *pairs):
    out = [pltpu.make_async_copy(source, target, sems.at[i]) for i, (source, target) in enumerate(pairs)]
    for copy in out:
        copy.start()
    return out


def pack_rows(cz, cy, row_of, packed, send_a, send_b):
    coded = []
    for side, up in enumerate((True, False)):
        narrow, wide = row_counts(cz, cy, up)
        for base, listed in zip((0, narrow), y_rows(cz, cy, up)):
            for r, (f, z, y, _) in enumerate(listed):
                packed[side, base + r // 8, r % 8 : r % 8 + 1, :] = row_of(f, z, y)
        rest = [split(packed[side, narrow + t])[1].astype(jnp.float32) for t in range(wide)]
        coded.append([packed[side, t] for t in range(narrow + wide)] + rest)
    even = even_mask(("gy", "gz"), packed.shape[2:])
    for t in range(send_a.shape[0]):
        up, down = (tiles[min(t, len(tiles) - 1)] for tiles in coded)
        send_a[t] = jnp.where(even, up, down).astype(jnp.bfloat16)
        send_b[t] = jnp.where(even, down, up).astype(jnp.bfloat16)


def unpack_rows(cz, cy, from_a, from_b, packed, put_row):
    has_lower, has_upper = has_neighbours("gy")
    even = even_mask(("gy", "gz"), packed.shape[2:])
    for side, (up, keep) in enumerate(((True, has_lower), (False, has_upper))):
        narrow, wide = row_counts(cz, cy, up)

        def got(t):
            a, b = from_a[t].astype(jnp.float32), from_b[t].astype(jnp.float32)
            return (jnp.where(even, b, a) if up else jnp.where(even, a, b)) * keep

        for t in range(narrow + wide):
            packed[side, t] = got(t) if t < narrow else got(t) + got(wide + t)
        for base, listed in zip((0, narrow), y_rows(cz, cy, up)):
            for r, (f, z, _, y) in enumerate(listed):
                put_row(f, z, y, packed[side, base + r // 8, r % 8 : r % 8 + 1, :])


def start_kernel(
    cz, store, adjoint, lam, mu, buoy, source, wavelet, receiver, traces, plan,
    near_out, far_out, own, cells, samples, spots, wave, steps, sems,
):
    cy, lanes = own.shape[2], own.shape[3]
    rows = cz * cy
    tiles = store.shape[0]
    small = copies(sems, (plan, steps), (wavelet, wave), (source, spots), (receiver, cells), (traces, samples))
    large = copies(
        sems.at[pl.ds(len(small), 5)],
        (adjoint, own.at[pl.ds(0, 9)]),
        (buoy, own.at[BUOY - ADJ]),
        (lam, own.at[LAM - ADJ]),
        (mu, own.at[MU - ADJ]),
        (store, near_out.at[pl.ds(0, tiles)]),
    )
    for copy in small:
        copy.wait()
    listed = cells[...]
    count = listed.shape[1]
    row_hot = (lax.broadcasted_iota(jnp.int32, (rows, count), 0) == listed // lanes).astype(jnp.float32)
    lane_hit = lax.broadcasted_iota(jnp.int32, (lanes, count), 0) == listed % lanes
    injected = []
    for step in (1, 0):
        sample = samples[pl.ds(steps[step], 1), :]
        field = lax.dot_general(
            row_hot,
            jnp.where(lane_hit, sample, 0.0),
            (((1,), (1,)), ((), ())),
            precision=lax.Precision.HIGHEST,
            preferred_element_type=jnp.float32,
        )
        injected.append(field.reshape(cz, cy, lanes))
    own[INJ - ADJ] = injected[1]
    flat = lax.broadcasted_iota(jnp.int32, (rows, lanes), 0) * lanes + lax.broadcasted_iota(jnp.int32, (rows, lanes), 1)
    for step in range(2):
        value = wave[steps[step]]
        field = jnp.zeros((rows, lanes), jnp.float32)
        for j in range(source.shape[1]):
            field = field + jnp.where(flat == spots[0, j], value, 0.0)
        own[SRC - ADJ + step] = field.reshape(cz, cy, lanes)
    for copy in large:
        copy.wait()
    for f in (SXX, SYY, SZZ):
        own[f] = own[f] + injected[0]

    even = even_mask("gz", (cy, lanes))
    near, far = face_counts(cz)
    up, down = faces(cz, True), faces(cz, False)
    zero = jnp.zeros((cy, lanes), jnp.float32)

    def tile(side, i):
        return own[side[i][0] - ADJ, side[i][1]] if i < len(side) else zero

    for i in range(near):
        above, below = tile(up[0], i), tile(down[0], i)
        for out, base, value in (
            (near_out, tiles, jnp.where(even, above, below)),
            (far_out, 0, jnp.where(even, below, above)),
        ):
            out[base + i], out[base + near + i] = split(value)
    for i in range(far):
        above, below = tile(up[1], i), tile(down[1], i)
        near_out[tiles + 2 * near + i] = jnp.where(even, above, below).astype(jnp.bfloat16)
        far_out[2 * near + i] = jnp.where(even, below, above).astype(jnp.bfloat16)
    for i in range(2 * near + far, far_out.shape[0]):
        far_out[i] = zero.astype(jnp.bfloat16)


def strip_of(main, layers):
    cy, lanes = main(0).shape
    lane = lax.broadcasted_iota(jnp.int32, (cy, lanes), 1)
    position = lane % 8
    group = lane // 8
    tile = jnp.zeros((cy, lanes), jnp.float32)
    for z in range(layers):
        tail = pltpu.roll(main(z), (8 * z + 2) % lanes, 1)
        head = pltpu.roll(main(z), (8 * z + 6) % lanes, 1)
        here = group == z
        tile = jnp.where(here & (position < 2), tail, jnp.where(here & (position >= 6), head, tile))
    return tile


def column_kernel(
    cz, store, core, chip, both_a, both_b, far, peer, slot, own,
    ring_f, ring, send_a, send_b, stores, peers, slots, sems,
):
    cy, lanes = own.shape[2], own.shape[3]
    layers = cz + 2 * HALO
    ring_rows = ring.shape[2]
    tiles = store.shape[0]
    me = lax.axis_index("gz")
    count = lax.axis_size("gz")
    moves = copies(
        sems,
        (peer, peers),
        (slot, slots),
        (store, stores.at[me]),
        (core.at[pl.ds(0, tiles)], stores.at[me ^ 1]),
        (chip, stores.at[me ^ 2]),
        (both_a, stores.at[me ^ 3, pl.ds(0, both_a.shape[0])]),
        (both_b, stores.at[me ^ 3, pl.ds(both_a.shape[0], both_b.shape[0])]),
    )
    near, _ = face_counts(cz)
    even = even_mask("gz", (cy, lanes))
    has_below, has_above = has_neighbours("gz")
    zero = jnp.zeros((cy, lanes), jnp.float32)
    for f in range(ring.shape[0]):
        for z in range(cz):
            ring[f, HALO + z, 0:cy, :] = own[f, z]
    filled = set()
    for up in (True, False):
        for depth, listed in enumerate(faces(cz, up)):
            for i, (f, _, z) in enumerate(listed):
                values = []
                for ref, base in ((core, tiles), (far, 0)):
                    if depth == 0:
                        values.append(joined(ref[base + i], ref[base + near + i]))
                    else:
                        values.append(ref[base + 2 * near + i].astype(jnp.float32))
                value = jnp.where(even, values[1], values[0]) if up else jnp.where(even, values[0], values[1])
                ring[f - ADJ, z, 0:cy, :] = value * (has_below if up else has_above)
                filled.add((f - ADJ, z))
    for f in range(ring.shape[0]):
        for z in (0, 1, layers - 2, layers - 1):
            if (f, z) not in filled:
                ring[f, z, 0:cy, :] = zero
        ring[f, layers, 0:cy, :] = strip_of(lambda z: ring[f, z, 0:cy, :], layers)
        for z in range(layers + 1):
            ring[f, z, cy:ring_rows, :] = jnp.zeros((ring_rows - cy, lanes), jnp.float32)
    for f in range(ring_f.shape[0]):
        for z in range(layers + 1):
            ring_f[f, z, cy:ring_rows, :] = jnp.zeros((ring_rows - cy, lanes), jnp.float32)
    strip = [ring[f, layers, 0:cy, :] for f in range(ring.shape[0])]
    for move in moves:
        move.wait()
    below, above = jnp.maximum(me - 1, 0), jnp.minimum(me + 1, count - 1)
    for z in range(layers):
        if z < HALO:
            brick, piece, keep = below, cz - HALO + z, has_below
        elif z < HALO + cz:
            brick, piece, keep = me, z - HALO, None
        else:
            brick, piece, keep = above, z - HALO - cz, has_above
        holder = peers[brick, piece]
        row = slots[brick, piece] * 9
        for f in range(9):
            value = stores[holder, row + f].astype(jnp.float32)
            ring_f[f, z, 0:cy, :] = value if keep is None else value * keep
    for f in range(9):
        ring_f[f, layers, 0:cy, :] = strip_of(lambda z: ring_f[f, z, 0:cy, :], layers)
    strip = [ring_f[f, layers, 0:cy, :] for f in range(9)] + strip
    position = lax.broadcasted_iota(jnp.int32, (cy, lanes), 1) % 8
    even_x = even_mask("gx", (cy, lanes))
    for out, tail_from_even in ((send_a, True), (send_b, False)):
        if out is None:
            continue
        place = 0
        for fields, narrow in ((range(ADJ), True), (range(ADJ, FIELDS), False)):
            quads = [fields[i : i + 4] for i in range(0, len(fields), 4)]
            for i, quad in enumerate(quads):
                tile = zero
                for g, f in enumerate(quad):
                    tail, head = strip[f], pltpu.roll(strip[f], lanes - 6, 1)
                    value = jnp.where(even_x, tail, head) if tail_from_even else jnp.where(even_x, head, tail)
                    value = value if g == 0 else pltpu.roll(value, 2 * g, 1)
                    tile = jnp.where(position // 2 == g, value, tile)
                high, low = split(tile)
                out[place + i] = high
                if not narrow:
                    out[place + len(quads) + i] = low
            place += len(quads) if narrow else 2 * len(quads)


def x_tiles():
    return -(-ADJ // 4) + 2 * -(-(FIELDS - ADJ) // 4)


def rows_kernel(cz, ring_f, ring_w, from_a, from_b, strips, send_a, send_b, packed):
    cy, lanes = strips.shape[1], strips.shape[2]
    layers = cz + 2 * HALO
    strip = [ring_f[f, layers, 0:cy, :] for f in range(9)]
    strip += [ring_w[f, layers, 0:cy, :] for f in range(ring_w.shape[0])]
    position = lax.broadcasted_iota(jnp.int32, (cy, lanes), 1) % 8
    even_x = even_mask("gx", (cy, lanes))
    has_left, has_right = has_neighbours("gx")
    zero = jnp.zeros((cy, lanes), jnp.float32)
    place = 0
    for fields, narrow in ((range(ADJ), True), (range(ADJ, FIELDS), False)):
        quads = [fields[i : i + 4] for i in range(0, len(fields), 4)]
        for i, quad in enumerate(quads):
            got = []
            for ref in (from_a, from_b):
                if ref is None:
                    got.append(zero)
                elif narrow:
                    got.append(ref[place + i].astype(jnp.float32))
                else:
                    got.append(joined(ref[place + i], ref[place + len(quads) + i]))
            right = jnp.where(even_x, got[0], got[1]) * has_right
            left = jnp.where(even_x, got[1], got[0]) * has_left
            for g, f in enumerate(quad):
                tile = jnp.where(position // 2 == 1, pltpu.roll(right, (2 - 2 * g) % lanes, 1), strip[f])
                strips[f] = jnp.where(position // 2 == 2, pltpu.roll(left, (4 - 2 * g) % lanes, 1), tile)
        place += len(quads) if narrow else 2 * len(quads)

    def row_of(f, z, y):
        if z == layers:
            return strips[f, y : y + 1, :]
        return ring_f[f, z, y : y + 1, :] if f < ADJ else ring_w[f - ADJ, z, y : y + 1, :]

    pack_rows(cz, cy, row_of, packed, send_a, send_b)


class Ring:
    def __init__(self, ring_f, ring_w):
        self.parts = ring_f, ring_w

    def __getitem__(self, key):
        f = key[0]
        return self.parts[0][key] if f < ADJ else self.parts[1][(f - ADJ, *key[1:])]

    def __setitem__(self, key, value):
        f = key[0]
        if f < ADJ:
            self.parts[0][key] = value
        else:
            self.parts[1][(f - ADJ, *key[1:])] = value


def window_kernel(
    cz, ring_f_in, ring_w_in, strips, from_a, from_b, own, final, image_lam, image_mu, ring_f, ring_w,
    packed, keep, images, speeds, sems,
):
    cy, lanes = own.shape[2], own.shape[3]
    layers = cz + 2 * HALO
    ring_rows = ring_f.shape[2]
    ring = Ring(ring_f, ring_w)
    for f in range(FIELDS):
        ring[f, layers, 0:cy, :] = strips[f]

    def put_row(f, z, y, value):
        ring[f, z, y : y + 1, :] = value

    unpack_rows(cz, cy, from_a, from_b, packed, put_row)

    lane = lax.broadcasted_iota(jnp.int32, (ring_rows, lanes), 1)
    first_lane, last_lane = lane == 0, lane == lanes - 1
    edge = layers

    def at(f, z):
        return ring[f, z]

    def x_next(f, z):
        value = at(f, z)
        if z == edge:
            return pltpu.roll(value, lanes - 1, 1)
        beyond = pltpu.roll(at(f, edge), (lanes - 1 - (8 * z + 2)) % lanes, 1)
        return jnp.where(last_lane, beyond, pltpu.roll(value, lanes - 1, 1))

    def x_prev(f, z):
        value = at(f, z)
        if z == edge:
            return pltpu.roll(value, 1, 1)
        beyond = pltpu.roll(at(f, edge), (lanes - (8 * z + 5)) % lanes, 1)
        return jnp.where(first_lane, beyond, pltpu.roll(value, 1, 1))

    def y_next(f, z):
        return pltpu.roll(at(f, z), ring_rows - 1, 0)

    def y_prev(f, z):
        return pltpu.roll(at(f, z), 1, 0)

    def z_next(f, z):
        return pltpu.roll(at(f, edge), lanes - 8, 1) if z == edge else at(f, z + 1)

    def z_prev(f, z):
        return pltpu.roll(at(f, edge), 8, 1) if z == edge else at(f, z - 1)

    def velocity_rates(base, z, want):
        buoy = at(BUOY, z)
        sxx, syy, szz = (functools.partial(at, base + f) for f in (SXX, SYY, SZZ))
        sxy, sxz, syz = (functools.partial(at, base + f) for f in (SXY, SXZ, SYZ))
        out = {}
        if VX in want:
            out[VX] = buoy * (
                (x_next(base + SXX, z) - sxx(z)) + (sxy(z) - y_prev(base + SXY, z)) + (sxz(z) - z_prev(base + SXZ, z))
            )
        if VY in want:
            out[VY] = buoy * (
                (sxy(z) - x_prev(base + SXY, z)) + (y_next(base + SYY, z) - syy(z)) + (syz(z) - z_prev(base + SYZ, z))
            )
        if VZ in want:
            out[VZ] = buoy * (
                (sxz(z) - x_prev(base + SXZ, z)) + (syz(z) - y_prev(base + SYZ, z)) + (z_next(base + SZZ, z) - szz(z))
            )
        return out

    def stress_rates(base, z, want):
        lam, mu = at(LAM, z), at(MU, z)
        vx, vy, vz = at(base + VX, z), at(base + VY, z), at(base + VZ, z)
        out = {}
        if SXX in want:
            exx = vx - x_prev(base + VX, z)
            eyy = vy - y_prev(base + VY, z)
            ezz = vz - z_prev(base + VZ, z)
            common = lam * (exx + eyy + ezz)
            twice = 2.0 * mu
            out[SXX] = common + twice * exx
            out[SYY] = common + twice * eyy
            out[SZZ] = common + twice * ezz
        if SXY in want:
            out[SXY] = mu * ((y_next(base + VX, z) - vx) + (x_next(base + VY, z) - vy))
        if SXZ in want:
            out[SXZ] = mu * ((z_next(base + VX, z) - vx) + (x_next(base + VZ, z) - vz))
            out[SYZ] = mu * ((z_next(base + VY, z) - vy) + (y_next(base + VZ, z) - vz))
        return out

    def spread(ranges):
        for z in list(range(layers)) + [edge]:
            want = {f for f, (a, b) in ranges.items() if z == edge or a <= z < b}
            if want:
                yield z, want

    def velocity_step(base, sign, ranges):
        for z, want in spread(ranges):
            for f, rate in velocity_rates(base, z, want).items():
                ring[base + f, z] = at(base + f, z) + rate if sign > 0 else at(base + f, z) - rate

    def stress_step(base, sign, ranges, before=None, after=None):
        for z, want in spread(ranges):
            for f, rate in stress_rates(base, z, want).items():
                value, normal = at(base + f, z), f in (SXX, SYY, SZZ)
                if before is not None and normal:
                    value = value + at(before, z)
                value = value + rate if sign > 0 else value - rate
                if after is not None and normal:
                    value = value + at(after, z)
                ring[base + f, z] = value

    def terms(f, a):
        term_lam = (f[0] + f[1] + f[2]) * (a[0] + a[1] + a[2])
        term_mu = f[0] * a[0] + f[1] * a[1] + f[2] * a[2] + 2.0 * (f[3] * a[3] + f[4] * a[4] + f[5] * a[5])
        return term_lam, term_mu

    inner = (HALO, HALO + cz)
    n = layers
    stress_step(ADJ, -1, {SXX: (1, n), SXY: (0, n), SXZ: (0, n - 1)})
    velocity_step(FWD, 1, {VX: (1, n), VY: (1, n), VZ: (0, n - 1)})
    stress_step(FWD, 1, {SXX: (1, n - 1), SXY: (1, n - 1), SXZ: (1, n - 1)}, after=SRC)
    for z in range(*inner):
        f = [ring[FWD + s, z, 0:cy, :] for s in range(SXX, SYZ + 1)]
        a = [ring[ADJ + s, z, 0:cy, :] for s in range(SXX, SYZ + 1)]
        a = [value + ring[INJ, z, 0:cy, :] for value in a[:3]] + a[3:]
        keep[0, z - HALO], keep[1, z - HALO] = terms(f, a)
    velocity_step(FWD, 1, {VX: (2, n - 1), VY: (2, n - 1), VZ: (1, n - 2)})
    everything = set(range(SXX, SYZ + 1))
    for z in range(*inner):
        rates = stress_rates(FWD, z, everything)
        f = []
        for s in range(SXX, SYZ + 1):
            value = (at(FWD + s, z) + rates[s])[0:cy, :]
            f.append(value + own[SRC - ADJ + 1, z - HALO] if s <= SZZ else value)
        a = [own[s, z - HALO] for s in range(SXX, SYZ + 1)]
        term_lam, term_mu = terms(f, a)
        images[0, z - HALO] = term_lam + keep[0, z - HALO]
        images[1, z - HALO] = term_mu + keep[1, z - HALO]
    moves = copies(sems, (images.at[0], image_lam), (images.at[1], image_mu))
    velocity_step(ADJ, -1, {VX: (1, n - 1), VY: (1, n - 1), VZ: (1, n - 1)})
    stress_step(ADJ, -1, {SXX: (2, n - 1), SXY: (1, n - 1), SXZ: (1, n - 2)}, before=INJ)
    stresses = ring_w.at[pl.ds(SXX, SYZ + 1 - SXX), pl.ds(HALO, cz), pl.ds(0, cy)]
    moves += copies(sems.at[pl.ds(2, 1)], (stresses, final.at[pl.ds(SXX, SYZ + 1 - SXX)]))
    for z in range(*inner):
        rates = velocity_rates(ADJ, z, {VX, VY, VZ})
        for f in (VX, VY, VZ):
            speeds[f, z - HALO] = (at(ADJ + f, z) - rates[f])[0:cy, :]
    moves += copies(sems.at[pl.ds(3, 1)], (speeds, final.at[pl.ds(VX, VZ + 1 - VX)]))
    for move in moves:
        move.wait()


def swap_pairs(count, first):
    pairs = [(i + d, i + 1 - d) for i in range(first, count - 1, 2) for d in (0, 1)]
    return pairs + [(i, i) for i in range(count) if i not in dict(pairs)]


def swapped(value_a, value_b, axis):
    count = lax.axis_size(axis)
    got_a = lax.ppermute(value_a, axis, swap_pairs(count, 0))
    return got_a, None if value_b is None else lax.ppermute(value_b, axis, swap_pairs(count, 1))


def stay(value, spec):
    return pltpu.with_memory_space_constraint(value, pltpu.HBM) if spec.memory_space == pl.ANY else value


def kernel_call(body, args, in_specs, out_shape, scratch_shapes=(), aliases=None, out_specs=None):
    here = [a is not None for a in args]
    there = [o is not None for o in out_shape]

    def run(*refs):
        refs = iter(refs)
        full = [next(refs) if h else None for h in here + there]
        body(*full, *refs)

    out = iter(
        pl.pallas_call(
            run,
            out_shape=tuple(o for o in out_shape if o is not None),
            in_specs=[s for s, h in zip(in_specs, here) if h],
            out_specs=out_specs or tuple(vmem() for h in there if h),
            scratch_shapes=list(scratch_shapes),
            input_output_aliases=aliases or {},
            compiler_params=pltpu.CompilerParams(vmem_limit_bytes=VMEM_LIMIT),
        )(*[stay(a, s) for a, s in zip(args, in_specs) if a is not None])
    )
    return tuple(next(out) if h else None for h in there)


def on_device(
    checkpoint_store,
    holder_peer,
    holder_slot,
    adjoint_state,
    lame_lambda,
    lame_mu,
    buoyancy,
    source_cell,
    wavelet,
    receiver_cell,
    traces,
    plan,
):
    cz, cy, cx = lame_mu.shape
    layers = cz + 2 * HALO
    bf16, f32 = jnp.bfloat16, jnp.float32
    store = checkpoint_store.reshape(-1, cy, cx)
    tiles = store.shape[0]
    peer, slot = holder_peer[0, 0], holder_slot[0, 0]
    source, receiver = source_cell.reshape(1, -1), receiver_cell.reshape(1, -1)
    traces = traces.reshape(traces.shape[-2:])
    holders = lax.axis_size("gz")
    assert holders == 4
    near, far = face_counts(cz)
    face = 2 * near + far
    half = tiles // 2

    def shape(*dims, dtype=f32):
        return jax.ShapeDtypeStruct(dims, dtype)

    wide_x = lax.axis_size("gx") > 2
    chip = lax.ppermute(store, "gz", [(i, i ^ 2) for i in range(holders)])
    to_core, to_far, own = kernel_call(
        functools.partial(start_kernel, cz),
        (store, adjoint_state, lame_lambda, lame_mu, buoyancy, source, wavelet, receiver, traces, plan),
        [hbm()] * 10,
        (shape(tiles + face, cy, cx, dtype=bf16), shape(max(face, half) + PAD, cy, cx, dtype=bf16), shape(15, cz, cy, cx)),
        [
            pltpu.VMEM(receiver.shape, jnp.int32),
            pltpu.VMEM(traces.shape, f32),
            pltpu.SMEM(source.shape, jnp.int32),
            pltpu.SMEM(wavelet.shape, f32),
            pltpu.SMEM(plan.shape, jnp.int32),
            pltpu.SemaphoreType.DMA((10,)),
        ],
    )
    core = lax.ppermute(to_core, "gz", [(i, i ^ 1) for i in range(holders)])
    gy = lax.axis_size("gy")
    across = {
        (i, c): (i, 3 - c) if c in (1, 2) else (i ^ 1, c)
        for i in range(gy) for c in range(holders)
    }
    far_face = lax.ppermute(
        to_far, ("gy", "gz"), [(a[0] * holders + a[1], b[0] * holders + b[1]) for a, b in across.items()]
    )
    both = [lax.ppermute(part, "gz", [(i, i ^ 1) for i in range(holders)]) for part in (chip[:half], chip[half:])]

    x_send = shape(x_tiles(), cy, cx, dtype=bf16)
    ring_f, ring_w, x_a, x_b = kernel_call(
        functools.partial(column_kernel, cz),
        (store, core, chip, *both, far_face, peer, slot, own),
        [hbm()] + [vmem()] * 5 + [hbm()] * 2 + [vmem()],
        (
            shape(ADJ, layers + 1, 2 * cy, cx),
            shape(FIELDS - ADJ, layers + 1, 2 * cy, cx),
            x_send,
            x_send if wide_x else None,
        ),
        [
            pltpu.VMEM((holders, tiles, cy, cx), bf16),
            pltpu.SMEM(peer.shape, jnp.int32),
            pltpu.SMEM(slot.shape, jnp.int32),
            pltpu.SemaphoreType.DMA((7,)),
        ],
    )
    from_a, from_b = swapped(x_a, x_b, "gx")

    y_send = shape(row_tiles(cz, cy), cy, cx, dtype=bf16)
    row_scratch = pltpu.VMEM((2, max(sum(row_counts(cz, cy, up)) for up in (True, False)), 8, cx), f32)
    strips, y_a, y_b = kernel_call(
        functools.partial(rows_kernel, cz),
        (ring_f, ring_w, from_a, from_b),
        [vmem()] * 4,
        (shape(FIELDS, cy, cx), y_send, y_send),
        [row_scratch],
    )
    turns = [[], []]
    for turn, pairs in enumerate(turns):
        for c in range(holders):
            first = (c + turn) % 2
            change = dict(swap_pairs(gy, first))
            pairs.extend((i * holders + c, (i * holders + (c ^ 2)) if j == i else (j * holders + c)) for i, j in change.items())
    from_a = lax.ppermute(y_a, ("gy", "gz"), turns[0])
    from_b = lax.ppermute(y_b, ("gy", "gz"), turns[1])

    result = kernel_call(
        functools.partial(window_kernel, cz),
        (ring_f, ring_w, strips, from_a, from_b, own),
        [vmem()] * 6,
        (
            shape(9, cz, cy, cx),
            shape(cz, cy, cx),
            shape(cz, cy, cx),
            shape(*ring_f.shape),
            shape(*ring_w.shape),
        ),
        [
            row_scratch,
            pltpu.VMEM((2, cz, cy, cx), f32),
            pltpu.VMEM((2, cz, cy, cx), f32),
            pltpu.VMEM((3, cz, cy, cx), f32),
            pltpu.SemaphoreType.DMA((4,)),
        ],
        {0: 3, 1: 4},
        (hbm(),) * 3 + (vmem(),) * 2,
    )
    return result[:3]


def solution(mesh):
    return jax.shard_map(
        on_device,
        mesh=mesh,
        in_specs=(
            P("gz", None, None, "gy", "gx"),
            P("gx", "gy", None, None),
            P("gx", "gy", None, None),
            P(None, "gz", "gy", "gx"),
            P("gz", "gy", "gx"),
            P("gz", "gy", "gx"),
            P("gz", "gy", "gx"),
            P("gz", "gy", "gx", None),
            P(),
            P("gz", "gy", "gx", None),
            P("gz", "gy", "gx", None, None),
            P(),
        ),
        out_specs=(P(None, "gz", "gy", "gx"), P("gz", "gy", "gx"), P("gz", "gy", "gx")),
        check_vma=False,
    )
```

```python
import functools

import jax
import jax.numpy as jnp
from jax import lax
from jax.experimental import pallas as pl
from jax.experimental.pallas import tpu as pltpu
from jax.sharding import PartitionSpec as P

VX, VY, VZ, SXX, SYY, SZZ, SXY, SXZ, SYZ = range(9)
FWD, ADJ, BUOY, LAM, MU, INJ, SRC = 0, 9, 18, 19, 20, 21, 22
FIELDS = 23
HALO = 2

ADJ_Z = {VX: (2, 2), VY: (2, 2), VZ: (2, 2), SXX: (1, 1), SYY: (1, 1), SZZ: (1, 2), SXY: (1, 1), SXZ: (2, 1), SYZ: (2, 1)}
OTHER_Z = {BUOY: (2, 2), LAM: (1, 2), MU: (2, 2), INJ: (0, 1), SRC: (1, 1)}
F32_Z = {**{ADJ + f: c for f, c in ADJ_Z.items()}, **OTHER_Z}

Y_ROWS = {
    FWD + VX: (None, (2, -1, 1), (1, -1, 1), (2, -2, 0)),
    FWD + VY: ((2, -2, 0), (1, -1, 1), (2, -1, 1), None),
    FWD + VZ: (None, (1, -2, 1), (1, -1, 1), (2, -2, 0)),
    FWD + SXX: (None, (2, -1, 1), (1, -1, 1), (2, -2, 1)),
    FWD + SYY: ((2, -2, 0), (1, -1, 1), (1, 0, 1), (2, -1, 1)),
    FWD + SZZ: (None, (1, -1, 1), (1, 0, 1), (2, -1, 0)),
    FWD + SXY: ((2, -1, 1), (1, 0, 1), (1, -1, 1), (2, -2, 0)),
    FWD + SXZ: (None, (1, -1, 1), (0, -1, 1), (1, -2, 1)),
    FWD + SYZ: ((1, -2, 1), (0, -1, 1), (1, -1, 1), (2, -2, 0)),
    ADJ + VX: ((2, -2, 0), (1, -1, 1), (1, -1, 1), (2, -2, 1)),
    ADJ + VY: ((2, -1, 1), (1, 0, 1), (1, -1, 1), (2, -2, 0)),
    ADJ + VZ: ((2, -2, 0), (1, -1, 1), (0, -1, 1), (1, -2, 0)),
    ADJ + SXX: (None, (2, -2, 1), (2, -2, 1), None),
    ADJ + SYY: (None, (2, -1, 1), (1, -1, 1), (2, -2, 0)),
    ADJ + SZZ: (None, (2, -1, 0), (1, -1, 0), None),
    ADJ + SXY: ((2, -2, 0), (1, -1, 1), (2, -2, 1), None),
    ADJ + SXZ: (None, (1, -2, 1), (1, -2, 1), None),
    ADJ + SYZ: ((2, -2, 0), (1, -1, 1), (1, -2, 0), None),
    BUOY: ((2, -2, 0), (1, -1, 1), (1, -1, 1), (2, -2, 0)),
    LAM: (None, (2, -1, 1), (1, -1, 1), (2, -2, 0)),
    MU: ((2, -2, 0), (1, -1, 1), (1, -1, 1), (2, -2, 0)),
    INJ: (None, None, (2, -2, 0), None),
    SRC: (None, (2, -2, 0), (2, -1, 1), None),
}

EXACT_ROWS = {-1: (ADJ + VY, ADJ + SXY, ADJ + SYZ, BUOY, SRC), 0: (ADJ + SYY, LAM, INJ, SRC)}

PAD = 1
VMEM_LIMIT = 48 * 1024 * 1024


def vmem():
    return pl.BlockSpec(memory_space=pltpu.VMEM)


def hbm():
    return pl.BlockSpec(memory_space=pl.ANY)


def faces(cz, up):
    near, far = [], []
    for f in sorted(F32_Z):
        before, after = F32_Z[f]
        depth = before if up else after
        for d in range(depth):
            layer = cz - 1 - d if up else d
            (far if d else near).append((f, layer, HALO - 1 - d if up else HALO + cz + d))
    return near, far


def face_counts(cz):
    sides = [faces(cz, up) for up in (True, False)]
    return max(len(s[0]) for s in sides), max(len(s[1]) for s in sides)


def y_rows(cz, cy, up):
    layers = cz + 2 * HALO
    narrow, wide, strip = [], [], []
    for f in sorted(Y_ROWS):
        for offset in (-1, -2) if up else (0, 1):
            spec = Y_ROWS[f][offset + HALO]
            if spec is None:
                continue
            source = cy + offset if up else offset
            target = 2 * cy + offset if up else cy + offset
            exact = f in EXACT_ROWS.get(offset, ())
            (wide if exact else narrow).extend((f, z, source, target) for z in range(spec[0], layers + spec[1]))
            if spec[2]:
                strip.append((f, layers, source, target))
    return narrow, wide, strip


def row_counts(cz, cy, up):
    return tuple(-(-len(rows) // 8) for rows in y_rows(cz, cy, up))


def row_tiles(cz, cy):
    sides = [row_counts(cz, cy, up) for up in (True, False)]
    return max(n + 2 * w + c for n, w, c in sides), max(c for _, _, c in sides)


def split(value):
    high = value.astype(jnp.bfloat16)
    low = (value - high.astype(jnp.float32)).astype(jnp.bfloat16)
    return high, low


def joined(high, low):
    return high.astype(jnp.float32) + low.astype(jnp.float32)


def even_mask(axes, shape):
    total = sum(lax.axis_index(a) for a in ((axes,) if isinstance(axes, str) else axes))
    return jnp.full(shape, lax.rem(total, 2), jnp.int32) == 0


def has_neighbours(axis):
    index = lax.axis_index(axis)
    return (index > 0).astype(jnp.float32), (index < lax.axis_size(axis) - 1).astype(jnp.float32)


def copies(sems, *pairs):
    out = [pltpu.make_async_copy(source, target, sems.at[i]) for i, (source, target) in enumerate(pairs)]
    for copy in out:
        copy.start()
    return out


def pack_rows(cz, cy, row_of, packed, sends, diagonals):
    coded, corners = [], []
    for side, up in enumerate((True, False)):
        narrow, wide, strip = row_counts(cz, cy, up)
        for base, listed in zip((0, narrow, narrow + wide), y_rows(cz, cy, up)):
            for r, (f, z, y, _) in enumerate(listed):
                packed[side, base + r // 8, r % 8 : r % 8 + 1, :] = row_of(f, z, y)
        rest = [split(packed[side, narrow + t])[1].astype(jnp.float32) for t in range(wide)]
        coded.append([packed[side, t] for t in range(narrow + wide + strip)] + rest)
        corners.append([packed[side, narrow + wide + t] for t in range(strip)])
    even = even_mask(("gy", "gz"), packed.shape[2:])
    for outs, tiles in ((sends, coded), (diagonals, corners)):
        for t in range(outs[0].shape[0]):
            up, down = (side[min(t, len(side) - 1)] for side in tiles)
            outs[0][t] = jnp.where(even, up, down).astype(jnp.bfloat16)
            outs[1][t] = jnp.where(even, down, up).astype(jnp.bfloat16)


def unpack_rows(cz, cy, got, diagonals, packed, put_row):
    lanes = packed.shape[3]
    has_lower, has_upper = has_neighbours("gy")
    has_left, has_right = has_neighbours("gx")
    even = even_mask(("gy", "gz"), packed.shape[2:])
    even_x = even_mask("gx", packed.shape[2:])
    pair = lax.broadcasted_iota(jnp.int32, packed.shape[2:], 1) % 8 // 2
    for side, (up, keep) in enumerate(((True, has_lower), (False, has_upper))):
        narrow, wide, strip = row_counts(cz, cy, up)

        def of(two, t):
            a, b = two[0][t].astype(jnp.float32), two[1][t].astype(jnp.float32)
            return (jnp.where(even, b, a) if up else jnp.where(even, a, b)) * keep

        for t in range(narrow + wide + strip):
            value = of(got, t)
            if narrow <= t < narrow + wide:
                value = value + of(got, wide + strip + t)
            if t >= narrow + wide:
                for turn, two in enumerate(diagonals):
                    corner = of(two, t - narrow - wide)
                    right = jnp.where(pair == 1, pltpu.roll(corner * has_right, lanes - 4, 1), 0.0)
                    left = jnp.where(pair == 2, pltpu.roll(corner * has_left, 4, 1), 0.0)
                    value = value + (jnp.where(even_x, left, right) if turn else jnp.where(even_x, right, left))
            packed[side, t] = value
        for base, listed in zip((0, narrow, narrow + wide), y_rows(cz, cy, up)):
            for r, (f, z, _, y) in enumerate(listed):
                put_row(f, z, y, packed[side, base + r // 8, r % 8 : r % 8 + 1, :])


def start_kernel(
    cz, store, adjoint, lam, mu, buoy, source, wavelet, receiver, traces, plan, peer, slot,
    near_out, far_out, own, peer_out, slot_out, cells, samples, spots, wave, steps, sems,
):
    cy, lanes = own.shape[2], own.shape[3]
    rows = cz * cy
    tiles = store.shape[0]
    small = copies(sems, (plan, steps), (wavelet, wave), (source, spots), (receiver, cells), (traces, samples))
    large = copies(
        sems.at[pl.ds(len(small), 7)],
        (adjoint, own.at[pl.ds(0, 9)]),
        (buoy, own.at[BUOY - ADJ]),
        (lam, own.at[LAM - ADJ]),
        (mu, own.at[MU - ADJ]),
        (store, near_out.at[pl.ds(0, tiles)]),
        (peer, peer_out),
        (slot, slot_out),
    )
    for copy in small:
        copy.wait()
    listed = cells[...]
    count = listed.shape[1]
    row_hot = (lax.broadcasted_iota(jnp.int32, (rows, count), 0) == listed // lanes).astype(jnp.float32)
    lane_hit = lax.broadcasted_iota(jnp.int32, (lanes, count), 0) == listed % lanes
    injected = []
    for step in (1, 0):
        sample = samples[pl.ds(steps[step], 1), :]
        field = lax.dot_general(
            row_hot,
            jnp.where(lane_hit, sample, 0.0),
            (((1,), (1,)), ((), ())),
            precision=lax.Precision.HIGHEST,
            preferred_element_type=jnp.float32,
        )
        injected.append(field.reshape(cz, cy, lanes))
    own[INJ - ADJ] = injected[1]
    flat = lax.broadcasted_iota(jnp.int32, (rows, lanes), 0) * lanes + lax.broadcasted_iota(jnp.int32, (rows, lanes), 1)
    for step in range(2):
        value = wave[steps[step]]
        field = jnp.zeros((rows, lanes), jnp.float32)
        for j in range(source.shape[1]):
            field = field + jnp.where(flat == spots[0, j], value, 0.0)
        own[SRC - ADJ + step] = field.reshape(cz, cy, lanes)
    for copy in large:
        copy.wait()
    for f in (SXX, SYY, SZZ):
        own[f] = own[f] + injected[0]

    even = even_mask("gz", (cy, lanes))
    near, far = face_counts(cz)
    up, down = faces(cz, True), faces(cz, False)
    zero = jnp.zeros((cy, lanes), jnp.float32)

    def tile(side, i):
        return own[side[i][0] - ADJ, side[i][1]] if i < len(side) else zero

    for i in range(near):
        above, below = tile(up[0], i), tile(down[0], i)
        for out, base, value in (
            (near_out, tiles, jnp.where(even, above, below)),
            (far_out, 0, jnp.where(even, below, above)),
        ):
            out[base + i], out[base + near + i] = split(value)
    for i in range(far):
        above, below = tile(up[1], i), tile(down[1], i)
        near_out[tiles + 2 * near + i] = jnp.where(even, above, below).astype(jnp.bfloat16)
        far_out[2 * near + i] = jnp.where(even, below, above).astype(jnp.bfloat16)
    for i in range(2 * near + far, far_out.shape[0]):
        far_out[i] = zero.astype(jnp.bfloat16)


def strip_of(main, layers):
    cy, lanes = main(0).shape
    lane = lax.broadcasted_iota(jnp.int32, (cy, lanes), 1)
    position = lane % 8
    group = lane // 8
    tile = jnp.zeros((cy, lanes), jnp.float32)
    for z in range(layers):
        tail = pltpu.roll(main(z), (8 * z + 2) % lanes, 1)
        head = pltpu.roll(main(z), (8 * z + 6) % lanes, 1)
        here = group == z
        tile = jnp.where(here & (position < 2), tail, jnp.where(here & (position >= 6), head, tile))
    return tile


def column_kernel(
    cz, mine, core, chip, both_a, both_b, far, peer, slot, own,
    ring_f, ring, x_a, x_b, y_a, y_b, corner_a, corner_b, packed, peers, slots, sems,
):
    cy, lanes = own.shape[2], own.shape[3]
    layers = cz + 2 * HALO
    ring_rows = ring.shape[2]
    tiles = chip.shape[0]
    half = both_a.shape[0]
    me = lax.axis_index("gz")
    count = lax.axis_size("gz")
    moves = copies(sems, (peer, peers), (slot, slots))
    near, _ = face_counts(cz)
    even = even_mask("gz", (cy, lanes))
    has_below, has_above = has_neighbours("gz")
    zero = jnp.zeros((cy, lanes), jnp.float32)
    for f in range(ring.shape[0]):
        for z in range(cz):
            ring[f, HALO + z, 0:cy, :] = own[f, z]
    filled = set()
    for up in (True, False):
        for depth, listed in enumerate(faces(cz, up)):
            for i, (f, _, z) in enumerate(listed):
                values = []
                for ref, base in ((core, tiles), (far, 0)):
                    if depth == 0:
                        values.append(joined(ref[base + i], ref[base + near + i]))
                    else:
                        values.append(ref[base + 2 * near + i].astype(jnp.float32))
                value = jnp.where(even, values[1], values[0]) if up else jnp.where(even, values[0], values[1])
                ring[f - ADJ, z, 0:cy, :] = value * (has_below if up else has_above)
                filled.add((f - ADJ, z))
    for f in range(ring.shape[0]):
        for z in (0, 1, layers - 2, layers - 1):
            if (f, z) not in filled:
                ring[f, z, 0:cy, :] = zero
        ring[f, layers, 0:cy, :] = strip_of(lambda z: ring[f, z, 0:cy, :], layers)
        for z in range(layers + 1):
            ring[f, z, cy:ring_rows, :] = jnp.zeros((ring_rows - cy, lanes), jnp.float32)
    for f in range(ring_f.shape[0]):
        for z in range(layers + 1):
            ring_f[f, z, cy:ring_rows, :] = jnp.zeros((ring_rows - cy, lanes), jnp.float32)
    strip = [ring[f, layers, 0:cy, :] for f in range(ring.shape[0])]
    for move in moves:
        move.wait()
    below, above = jnp.maximum(me - 1, 0), jnp.minimum(me + 1, count - 1)
    for z in range(layers):
        if z < HALO:
            brick, piece, keep = below, cz - HALO + z, has_below
        elif z < HALO + cz:
            brick, piece, keep = me, z - HALO, None
        else:
            brick, piece, keep = above, z - HALO - cz, has_above
        row = slots[brick, piece] * 9
        hops = jnp.full((cy, lanes), peers[brick, piece] ^ me, jnp.int32)
        late = jnp.full((cy, lanes), row, jnp.int32) >= half
        row_a, row_b = jnp.minimum(row, half - 9), jnp.maximum(row - half, 0)
        for f in range(9):
            parts = (mine[row + f], core[row + f], chip[row + f], both_a[row_a + f], both_b[row_b + f])
            parts = [part.astype(jnp.float32) for part in parts]
            value = jnp.where(late, parts[4], parts[3])
            value = jnp.where(hops < 2, jnp.where(hops == 1, parts[1], parts[0]), jnp.where(hops == 2, parts[2], value))
            ring_f[f, z, 0:cy, :] = value if keep is None else value * keep
    for f in range(9):
        ring_f[f, layers, 0:cy, :] = strip_of(lambda z: ring_f[f, z, 0:cy, :], layers)
    strip = [ring_f[f, layers, 0:cy, :] for f in range(9)] + strip
    position = lax.broadcasted_iota(jnp.int32, (cy, lanes), 1) % 8
    even_x = even_mask("gx", (cy, lanes))
    for out, tail_from_even in ((x_a, True), (x_b, False)):
        if out is None:
            continue
        place = 0
        for fields, narrow in ((range(ADJ), True), (range(ADJ, FIELDS), False)):
            quads = [fields[i : i + 4] for i in range(0, len(fields), 4)]
            for i, quad in enumerate(quads):
                tile = zero
                for g, f in enumerate(quad):
                    tail, head = strip[f], pltpu.roll(strip[f], lanes - 6, 1)
                    value = jnp.where(even_x, tail, head) if tail_from_even else jnp.where(even_x, head, tail)
                    value = value if g == 0 else pltpu.roll(value, 2 * g, 1)
                    tile = jnp.where(position // 2 == g, value, tile)
                high, low = split(tile)
                out[place + i] = high
                if not narrow:
                    out[place + len(quads) + i] = low
            place += len(quads) if narrow else 2 * len(quads)

    def row_of(f, z, y):
        return ring_f[f, z, y : y + 1, :] if f < ADJ else ring[f - ADJ, z, y : y + 1, :]

    pack_rows(cz, cy, row_of, packed, (y_a, y_b), (corner_a, corner_b))


def x_tiles():
    return -(-ADJ // 4) + 2 * -(-(FIELDS - ADJ) // 4)


class Ring:
    def __init__(self, ring_f, ring_w):
        self.parts = ring_f, ring_w

    def __getitem__(self, key):
        f = key[0]
        return self.parts[0][key] if f < ADJ else self.parts[1][(f - ADJ, *key[1:])]

    def __setitem__(self, key, value):
        f = key[0]
        if f < ADJ:
            self.parts[0][key] = value
        else:
            self.parts[1][(f - ADJ, *key[1:])] = value


def window_kernel(
    cz, ring_f_in, ring_w_in, x_a, x_b, y_a, y_b, corner_aa, corner_ab, corner_ba, corner_bb, own,
    final, image_lam, image_mu, ring_f, ring_w, packed, keep, images, speeds, sems,
):
    cy, lanes = own.shape[2], own.shape[3]
    layers = cz + 2 * HALO
    ring_rows = ring_f.shape[2]
    ring = Ring(ring_f, ring_w)
    pair = lax.broadcasted_iota(jnp.int32, (cy, lanes), 1) % 8 // 2
    even_x = even_mask("gx", (cy, lanes))
    has_left, has_right = has_neighbours("gx")
    zero = jnp.zeros((cy, lanes), jnp.float32)
    place = 0
    for fields, narrow in ((range(ADJ), True), (range(ADJ, FIELDS), False)):
        quads = [fields[i : i + 4] for i in range(0, len(fields), 4)]
        for i, quad in enumerate(quads):
            got = []
            for ref in (x_a, x_b):
                if ref is None:
                    got.append(zero)
                elif narrow:
                    got.append(ref[place + i].astype(jnp.float32))
                else:
                    got.append(joined(ref[place + i], ref[place + len(quads) + i]))
            right = jnp.where(even_x, got[0], got[1]) * has_right
            left = jnp.where(even_x, got[1], got[0]) * has_left
            for g, f in enumerate(quad):
                tile = jnp.where(pair == 1, pltpu.roll(right, (2 - 2 * g) % lanes, 1), ring[f, layers, 0:cy, :])
                ring[f, layers, 0:cy, :] = jnp.where(pair == 2, pltpu.roll(left, (4 - 2 * g) % lanes, 1), tile)
        place += len(quads) if narrow else 2 * len(quads)

    def put_row(f, z, y, value):
        ring[f, z, y : y + 1, :] = value

    diagonals = [two for two in ((corner_aa, corner_ab), (corner_ba, corner_bb)) if two[0] is not None]
    unpack_rows(cz, cy, (y_a, y_b), diagonals, packed, put_row)

    lane = lax.broadcasted_iota(jnp.int32, (ring_rows, lanes), 1)
    first_lane, last_lane = lane == 0, lane == lanes - 1
    edge = layers

    def at(f, z):
        return ring[f, z]

    def x_next(f, z):
        value = at(f, z)
        if z == edge:
            return pltpu.roll(value, lanes - 1, 1)
        beyond = pltpu.roll(at(f, edge), (lanes - 1 - (8 * z + 2)) % lanes, 1)
        return jnp.where(last_lane, beyond, pltpu.roll(value, lanes - 1, 1))

    def x_prev(f, z):
        value = at(f, z)
        if z == edge:
            return pltpu.roll(value, 1, 1)
        beyond = pltpu.roll(at(f, edge), (lanes - (8 * z + 5)) % lanes, 1)
        return jnp.where(first_lane, beyond, pltpu.roll(value, 1, 1))

    def y_next(f, z):
        return pltpu.roll(at(f, z), ring_rows - 1, 0)

    def y_prev(f, z):
        return pltpu.roll(at(f, z), 1, 0)

    def z_next(f, z):
        return pltpu.roll(at(f, edge), lanes - 8, 1) if z == edge else at(f, z + 1)

    def z_prev(f, z):
        return pltpu.roll(at(f, edge), 8, 1) if z == edge else at(f, z - 1)

    def velocity_rates(base, z, want):
        buoy = at(BUOY, z)
        sxx, syy, szz = (functools.partial(at, base + f) for f in (SXX, SYY, SZZ))
        sxy, sxz, syz = (functools.partial(at, base + f) for f in (SXY, SXZ, SYZ))
        out = {}
        if VX in want:
            out[VX] = buoy * (
                (x_next(base + SXX, z) - sxx(z)) + (sxy(z) - y_prev(base + SXY, z)) + (sxz(z) - z_prev(base + SXZ, z))
            )
        if VY in want:
            out[VY] = buoy * (
                (sxy(z) - x_prev(base + SXY, z)) + (y_next(base + SYY, z) - syy(z)) + (syz(z) - z_prev(base + SYZ, z))
            )
        if VZ in want:
            out[VZ] = buoy * (
                (sxz(z) - x_prev(base + SXZ, z)) + (syz(z) - y_prev(base + SYZ, z)) + (z_next(base + SZZ, z) - szz(z))
            )
        return out

    def stress_rates(base, z, want):
        lam, mu = at(LAM, z), at(MU, z)
        vx, vy, vz = at(base + VX, z), at(base + VY, z), at(base + VZ, z)
        out = {}
        if SXX in want:
            exx = vx - x_prev(base + VX, z)
            eyy = vy - y_prev(base + VY, z)
            ezz = vz - z_prev(base + VZ, z)
            common = lam * (exx + eyy + ezz)
            twice = 2.0 * mu
            out[SXX] = common + twice * exx
            out[SYY] = common + twice * eyy
            out[SZZ] = common + twice * ezz
        if SXY in want:
            out[SXY] = mu * ((y_next(base + VX, z) - vx) + (x_next(base + VY, z) - vy))
        if SXZ in want:
            out[SXZ] = mu * ((z_next(base + VX, z) - vx) + (x_next(base + VZ, z) - vz))
            out[SYZ] = mu * ((z_next(base + VY, z) - vy) + (y_next(base + VZ, z) - vz))
        return out

    def spread(ranges):
        for z in list(range(layers)) + [edge]:
            want = {f for f, (a, b) in ranges.items() if z == edge or a <= z < b}
            if want:
                yield z, want

    def velocity_step(base, sign, ranges):
        for z, want in spread(ranges):
            for f, rate in velocity_rates(base, z, want).items():
                ring[base + f, z] = at(base + f, z) + rate if sign > 0 else at(base + f, z) - rate

    def stress_step(base, sign, ranges, before=None, after=None):
        for z, want in spread(ranges):
            for f, rate in stress_rates(base, z, want).items():
                value, normal = at(base + f, z), f in (SXX, SYY, SZZ)
                if before is not None and normal:
                    value = value + at(before, z)
                value = value + rate if sign > 0 else value - rate
                if after is not None and normal:
                    value = value + at(after, z)
                ring[base + f, z] = value

    def terms(f, a):
        term_lam = (f[0] + f[1] + f[2]) * (a[0] + a[1] + a[2])
        term_mu = f[0] * a[0] + f[1] * a[1] + f[2] * a[2] + 2.0 * (f[3] * a[3] + f[4] * a[4] + f[5] * a[5])
        return term_lam, term_mu

    inner = (HALO, HALO + cz)
    n = layers
    stress_step(ADJ, -1, {SXX: (1, n), SXY: (0, n), SXZ: (0, n - 1)})
    velocity_step(FWD, 1, {VX: (1, n), VY: (1, n), VZ: (0, n - 1)})
    stress_step(FWD, 1, {SXX: (1, n - 1), SXY: (1, n - 1), SXZ: (1, n - 1)}, after=SRC)
    for z in range(*inner):
        f = [ring[FWD + s, z, 0:cy, :] for s in range(SXX, SYZ + 1)]
        a = [ring[ADJ + s, z, 0:cy, :] for s in range(SXX, SYZ + 1)]
        a = [value + ring[INJ, z, 0:cy, :] for value in a[:3]] + a[3:]
        keep[0, z - HALO], keep[1, z - HALO] = terms(f, a)
    velocity_step(FWD, 1, {VX: (2, n - 1), VY: (2, n - 1), VZ: (1, n - 2)})
    everything = set(range(SXX, SYZ + 1))
    for z in range(*inner):
        rates = stress_rates(FWD, z, everything)
        f = []
        for s in range(SXX, SYZ + 1):
            value = (at(FWD + s, z) + rates[s])[0:cy, :]
            f.append(value + own[SRC - ADJ + 1, z - HALO] if s <= SZZ else value)
        a = [own[s, z - HALO] for s in range(SXX, SYZ + 1)]
        term_lam, term_mu = terms(f, a)
        images[0, z - HALO] = term_lam + keep[0, z - HALO]
        images[1, z - HALO] = term_mu + keep[1, z - HALO]
    moves = copies(sems, (images.at[0], image_lam), (images.at[1], image_mu))
    velocity_step(ADJ, -1, {VX: (1, n - 1), VY: (1, n - 1), VZ: (1, n - 1)})
    stress_step(ADJ, -1, {SXX: (2, n - 1), SXY: (1, n - 1), SXZ: (1, n - 2)}, before=INJ)
    stresses = ring_w.at[pl.ds(SXX, SYZ + 1 - SXX), pl.ds(HALO, cz), pl.ds(0, cy)]
    moves += copies(sems.at[pl.ds(2, 1)], (stresses, final.at[pl.ds(SXX, SYZ + 1 - SXX)]))
    for z in range(*inner):
        rates = velocity_rates(ADJ, z, {VX, VY, VZ})
        for f in (VX, VY, VZ):
            speeds[f, z - HALO] = (at(ADJ + f, z) - rates[f])[0:cy, :]
    moves += copies(sems.at[pl.ds(3, 1)], (speeds, final.at[pl.ds(VX, VZ + 1 - VX)]))
    for move in moves:
        move.wait()


def swap_pairs(count, first):
    pairs = [(i + d, i + 1 - d) for i in range(first, count - 1, 2) for d in (0, 1)]
    return pairs + [(i, i) for i in range(count) if i not in dict(pairs)]


def swapped(value_a, value_b, axis):
    count = lax.axis_size(axis)
    got_a = lax.ppermute(value_a, axis, swap_pairs(count, 0))
    return got_a, None if value_b is None else lax.ppermute(value_b, axis, swap_pairs(count, 1))


def stay(value, spec):
    return pltpu.with_memory_space_constraint(value, pltpu.HBM) if spec.memory_space == pl.ANY else value


def kernel_call(body, args, in_specs, out_shape, scratch_shapes=(), aliases=None, out_specs=None):
    here = [a is not None for a in args]
    there = [o is not None for o in out_shape]

    def run(*refs):
        refs = iter(refs)
        full = [next(refs) if h else None for h in here + there]
        body(*full, *refs)

    out = iter(
        pl.pallas_call(
            run,
            out_shape=tuple(o for o in out_shape if o is not None),
            in_specs=[s for s, h in zip(in_specs, here) if h],
            out_specs=out_specs or tuple(vmem() for h in there if h),
            scratch_shapes=list(scratch_shapes),
            input_output_aliases=aliases or {},
            compiler_params=pltpu.CompilerParams(vmem_limit_bytes=VMEM_LIMIT),
        )(*[stay(a, s) for a, s in zip(args, in_specs) if a is not None])
    )
    return tuple(next(out) if h else None for h in there)


def on_device(
    checkpoint_store,
    holder_peer,
    holder_slot,
    adjoint_state,
    lame_lambda,
    lame_mu,
    buoyancy,
    source_cell,
    wavelet,
    receiver_cell,
    traces,
    plan,
):
    cz, cy, cx = lame_mu.shape
    layers = cz + 2 * HALO
    bf16, f32 = jnp.bfloat16, jnp.float32
    store = checkpoint_store.reshape(-1, cy, cx)
    tiles = store.shape[0]
    peer, slot = holder_peer[0, 0], holder_slot[0, 0]
    source, receiver = source_cell.reshape(1, -1), receiver_cell.reshape(1, -1)
    traces = traces.reshape(traces.shape[-2:])
    holders = lax.axis_size("gz")
    assert holders == 4
    near, far = face_counts(cz)
    face = 2 * near + far
    half = tiles // 2

    def shape(*dims, dtype=f32):
        return jax.ShapeDtypeStruct(dims, dtype)

    wide_x = lax.axis_size("gx") > 2
    chip = lax.ppermute(store, "gz", [(i, i ^ 2) for i in range(holders)])
    to_core, to_far, own, peer, slot = kernel_call(
        functools.partial(start_kernel, cz),
        (store, adjoint_state, lame_lambda, lame_mu, buoyancy, source, wavelet, receiver, traces, plan, peer, slot),
        [hbm()] * 12,
        (shape(tiles + face, cy, cx, dtype=bf16), shape(max(face, half) + PAD, cy, cx, dtype=bf16), shape(15, cz, cy, cx),
         shape(*peer.shape, dtype=jnp.int32), shape(*slot.shape, dtype=jnp.int32)),
        [
            pltpu.VMEM(receiver.shape, jnp.int32),
            pltpu.VMEM(traces.shape, f32),
            pltpu.SMEM(source.shape, jnp.int32),
            pltpu.SMEM(wavelet.shape, f32),
            pltpu.SMEM(plan.shape, jnp.int32),
            pltpu.SemaphoreType.DMA((12,)),
        ],
    )
    core = lax.ppermute(to_core, "gz", [(i, i ^ 1) for i in range(holders)])
    gy = lax.axis_size("gy")
    across = {
        (i, c): (i, 3 - c) if c in (1, 2) else (i ^ 1, c)
        for i in range(gy) for c in range(holders)
    }
    far_face = lax.ppermute(
        to_far, ("gy", "gz"), [(a[0] * holders + a[1], b[0] * holders + b[1]) for a, b in across.items()]
    )
    both = [lax.ppermute(part, "gz", [(i, i ^ 1) for i in range(holders)]) for part in (chip[:half], chip[half:])]

    x_send = shape(x_tiles(), cy, cx, dtype=bf16)
    y_size, corner_size = row_tiles(cz, cy)
    y_send, corner_send = shape(y_size, cy, cx, dtype=bf16), shape(corner_size, cy, cx, dtype=bf16)
    row_scratch = pltpu.VMEM((2, max(sum(row_counts(cz, cy, up)) for up in (True, False)), 8, cx), f32)
    ring_f, ring_w, x_a, x_b, y_a, y_b, corner_a, corner_b = kernel_call(
        functools.partial(column_kernel, cz),
        (to_core, core, chip, *both, far_face, peer, slot, own),
        [vmem()] * 9,
        (
            shape(ADJ, layers + 1, 2 * cy, cx),
            shape(FIELDS - ADJ, layers + 1, 2 * cy, cx),
            x_send,
            x_send if wide_x else None,
            y_send,
            y_send,
            corner_send,
            corner_send,
        ),
        [
            row_scratch,
            pltpu.SMEM(peer.shape, jnp.int32),
            pltpu.SMEM(slot.shape, jnp.int32),
            pltpu.SemaphoreType.DMA((2,)),
        ],
    )
    axes = ("gx", "gy", "gz")
    gx = lax.axis_size("gx")

    def partner(i, j, c, x_turn, y_turn):
        if x_turn is not None:
            i = dict(swap_pairs(gx, x_turn))[i]
        if y_turn is not None:
            other = dict(swap_pairs(gy, (c + y_turn) % 2))[j]
            j, c = (j, c ^ 2) if other == j else (other, c)
        return (i * gy + j) * holders + c

    def swap(value, x_turn, y_turn):
        if value is None:
            return None
        pairs = [
            ((i * gy + j) * holders + c, partner(i, j, c, x_turn, y_turn))
            for i in range(gx) for j in range(gy) for c in range(holders)
        ]
        return lax.ppermute(value, axes, pairs)

    x_turns = (0, 1) if wide_x else (0,)
    corners = [swap(v, t, u) for t in x_turns for u, v in enumerate((corner_a, corner_b))]
    corners += [None] * (4 - len(corners))
    result = kernel_call(
        functools.partial(window_kernel, cz),
        (
            ring_f, ring_w, swap(x_a, 0, None), swap(x_b, 1, None), swap(y_a, None, 0), swap(y_b, None, 1),
            *corners, own,
        ),
        [vmem()] * 11,
        (
            shape(9, cz, cy, cx),
            shape(cz, cy, cx),
            shape(cz, cy, cx),
            shape(*ring_f.shape),
            shape(*ring_w.shape),
        ),
        [
            row_scratch,
            pltpu.VMEM((2, cz, cy, cx), f32),
            pltpu.VMEM((2, cz, cy, cx), f32),
            pltpu.VMEM((3, cz, cy, cx), f32),
            pltpu.SemaphoreType.DMA((4,)),
        ],
        {0: 3, 1: 4},
        (hbm(),) * 3 + (vmem(),) * 2,
    )
    return result[:3]


def solution(mesh):
    return jax.shard_map(
        on_device,
        mesh=mesh,
        in_specs=(
            P("gz", None, None, "gy", "gx"),
            P("gx", "gy", None, None),
            P("gx", "gy", None, None),
            P(None, "gz", "gy", "gx"),
            P("gz", "gy", "gx"),
            P("gz", "gy", "gx"),
            P("gz", "gy", "gx"),
            P("gz", "gy", "gx", None),
            P(),
            P("gz", "gy", "gx", None),
            P("gz", "gy", "gx", None, None),
            P(),
        ),
        out_specs=(P(None, "gz", "gy", "gx"), P("gz", "gy", "gx"), P("gz", "gy", "gx")),
        check_vma=False,
    )
```

```python
import functools

import jax
import jax.numpy as jnp
from jax import lax
from jax.experimental import pallas as pl
from jax.experimental.pallas import tpu as pltpu
from jax.sharding import PartitionSpec as P

VX, VY, VZ, SXX, SYY, SZZ, SXY, SXZ, SYZ = range(9)
FWD, ADJ, BUOY, LAM, MU, INJ, SRC = 0, 9, 18, 19, 20, 21, 22
FIELDS = 23
HALO = 2

ADJ_Z = {VX: (2, 2), VY: (2, 2), VZ: (2, 2), SXX: (1, 1), SYY: (1, 1), SZZ: (1, 2), SXY: (1, 1), SXZ: (2, 1), SYZ: (2, 1)}
OTHER_Z = {BUOY: (2, 2), LAM: (1, 2), MU: (2, 2), INJ: (0, 1), SRC: (1, 1)}
F32_Z = {**{ADJ + f: c for f, c in ADJ_Z.items()}, **OTHER_Z}

Y_ROWS = {
    FWD + VX: (None, (2, -1, 1), (1, -1, 1), (2, -2, 0)),
    FWD + VY: ((2, -2, 0), (1, -1, 1), (2, -1, 1), None),
    FWD + VZ: (None, (1, -2, 1), (1, -1, 1), (2, -2, 0)),
    FWD + SXX: (None, (2, -1, 1), (1, -1, 1), (2, -2, 1)),
    FWD + SYY: ((2, -2, 0), (1, -1, 1), (1, 0, 1), (2, -1, 1)),
    FWD + SZZ: (None, (1, -1, 1), (1, 0, 1), (2, -1, 0)),
    FWD + SXY: ((2, -1, 1), (1, 0, 1), (1, -1, 1), (2, -2, 0)),
    FWD + SXZ: (None, (1, -1, 1), (0, -1, 1), (1, -2, 1)),
    FWD + SYZ: ((1, -2, 1), (0, -1, 1), (1, -1, 1), (2, -2, 0)),
    ADJ + VX: ((2, -2, 0), (1, -1, 1), (1, -1, 1), (2, -2, 1)),
    ADJ + VY: ((2, -1, 1), (1, 0, 1), (1, -1, 1), (2, -2, 0)),
    ADJ + VZ: ((2, -2, 0), (1, -1, 1), (0, -1, 1), (1, -2, 0)),
    ADJ + SXX: (None, (2, -2, 1), (2, -2, 1), None),
    ADJ + SYY: (None, (2, -1, 1), (1, -1, 1), (2, -2, 0)),
    ADJ + SZZ: (None, (2, -1, 0), (1, -1, 0), None),
    ADJ + SXY: ((2, -2, 0), (1, -1, 1), (2, -2, 1), None),
    ADJ + SXZ: (None, (1, -2, 1), (1, -2, 1), None),
    ADJ + SYZ: ((2, -2, 0), (1, -1, 1), (1, -2, 0), None),
    BUOY: ((2, -2, 0), (1, -1, 1), (1, -1, 1), (2, -2, 0)),
    LAM: (None, (2, -1, 1), (1, -1, 1), (2, -2, 0)),
    MU: ((2, -2, 0), (1, -1, 1), (1, -1, 1), (2, -2, 0)),
    INJ: (None, None, (2, -2, 0), None),
    SRC: (None, (2, -2, 0), (2, -1, 1), None),
}

EXACT_ROWS = {-1: (ADJ + VY, ADJ + SXY, ADJ + SYZ, BUOY, SRC), 0: (ADJ + SYY, LAM, INJ, SRC)}

PAD = 1
VMEM_LIMIT = 48 * 1024 * 1024


def vmem():
    return pl.BlockSpec(memory_space=pltpu.VMEM)


def hbm():
    return pl.BlockSpec(memory_space=pl.ANY)


def faces(cz, up):
    near, far = [], []
    for f in sorted(F32_Z):
        before, after = F32_Z[f]
        depth = before if up else after
        for d in range(depth):
            layer = cz - 1 - d if up else d
            (far if d else near).append((f, layer, HALO - 1 - d if up else HALO + cz + d))
    return near, far


def face_counts(cz):
    sides = [faces(cz, up) for up in (True, False)]
    return max(len(s[0]) for s in sides), max(len(s[1]) for s in sides)


def y_rows(cz, cy, up):
    layers = cz + 2 * HALO
    narrow, wide, strip = [], [], []
    for f in sorted(Y_ROWS):
        for offset in (-1, -2) if up else (0, 1):
            spec = Y_ROWS[f][offset + HALO]
            if spec is None:
                continue
            source = cy + offset if up else offset
            target = 2 * cy + offset if up else cy + offset
            exact = f in EXACT_ROWS.get(offset, ())
            (wide if exact else narrow).extend((f, z, source, target) for z in range(spec[0], layers + spec[1]))
            if spec[2]:
                strip.append((f, layers, source, target))
    return narrow, wide, strip


def row_counts(cz, cy, up):
    return tuple(-(-len(rows) // 8) for rows in y_rows(cz, cy, up))


def row_tiles(cz, cy):
    sides = [row_counts(cz, cy, up) for up in (True, False)]
    return max(c for _, _, c in sides), max(n + 2 * w for n, w, _ in sides)


def split(value):
    high = value.astype(jnp.bfloat16)
    low = (value - high.astype(jnp.float32)).astype(jnp.bfloat16)
    return high, low


def joined(high, low):
    return high.astype(jnp.float32) + low.astype(jnp.float32)


def even_mask(axes, shape):
    total = sum(lax.axis_index(a) for a in ((axes,) if isinstance(axes, str) else axes))
    return jnp.full(shape, lax.rem(total, 2), jnp.int32) == 0


def has_neighbours(axis):
    index = lax.axis_index(axis)
    return (index > 0).astype(jnp.float32), (index < lax.axis_size(axis) - 1).astype(jnp.float32)


def copies(sems, *pairs):
    out = [pltpu.make_async_copy(source, target, sems.at[i]) for i, (source, target) in enumerate(pairs)]
    for copy in out:
        copy.start()
    return out


def scatter_rows(packed, listed, row_of):
    for r, (f, z, y, _) in enumerate(listed):
        packed[r // 8, r % 8 : r % 8 + 1, :] = row_of(f, z, y)


def pack_tiles(sides, sends, first, count):
    even = even_mask(("gy", "gz"), sends[0].shape[1:])
    for t in range(count):
        up, down = (side[min(t, len(side) - 1)] for side in sides)
        sends[0][first + t] = jnp.where(even, up, down).astype(jnp.bfloat16)
        sends[1][first + t] = jnp.where(even, down, up).astype(jnp.bfloat16)


def layer_rows_kernel(cz, ring_f, ring_w, send_a, send_b, packed):
    cy = ring_f.shape[2] // 2
    strip_tiles, tiles = row_tiles(cz, cy)

    def row_of(f, z, y):
        return ring_f[f, z, y : y + 1, :] if f < ADJ else ring_w[f - ADJ, z, y : y + 1, :]

    sides = []
    for side, up in enumerate((True, False)):
        narrow, wide, _ = y_rows(cz, cy, up)
        n, w, _ = row_counts(cz, cy, up)
        scatter_rows(packed.at[side], narrow, row_of)
        scatter_rows(packed.at[side, pl.ds(n, w)], wide, row_of)
        rest = [split(packed[side, n + t])[1].astype(jnp.float32) for t in range(w)]
        sides.append([packed[side, t] for t in range(n + w)] + rest)
    pack_tiles(sides, (send_a, send_b), strip_tiles, tiles)


def unpack_rows(cz, cy, got, packed, put_row):
    has_lower, has_upper = has_neighbours("gy")
    even = even_mask(("gy", "gz"), packed.shape[2:])
    strip_tiles, _ = row_tiles(cz, cy)
    for side, (up, keep) in enumerate(((True, has_lower), (False, has_upper))):
        narrow, wide, strip = y_rows(cz, cy, up)
        n, w, c = row_counts(cz, cy, up)

        def of(t):
            a, b = got[0][t].astype(jnp.float32), got[1][t].astype(jnp.float32)
            return (jnp.where(even, b, a) if up else jnp.where(even, a, b)) * keep

        for t in range(n + w):
            value = of(strip_tiles + t)
            packed[side, t] = value if t < n else value + of(strip_tiles + w + t)
        for t in range(c):
            packed[side, n + w + t] = of(t)
        for base, listed in ((0, narrow), (n, wide), (n + w, strip)):
            for r, (f, z, _, y) in enumerate(listed):
                put_row(f, z, y, packed[side, base + r // 8, r % 8 : r % 8 + 1, :])


def start_kernel(
    cz, store, adjoint, lam, mu, buoy, source, wavelet, receiver, traces, plan, peer, slot,
    near_out, far_out, own, peer_out, slot_out, cells, samples, spots, wave, steps, sems,
):
    cy, lanes = own.shape[2], own.shape[3]
    rows = cz * cy
    tiles = store.shape[0]
    small = copies(sems, (plan, steps), (wavelet, wave), (source, spots), (receiver, cells), (traces, samples))
    large = copies(
        sems.at[pl.ds(len(small), 7)],
        (adjoint, own.at[pl.ds(0, 9)]),
        (buoy, own.at[BUOY - ADJ]),
        (lam, own.at[LAM - ADJ]),
        (mu, own.at[MU - ADJ]),
        (store, near_out.at[pl.ds(0, tiles)]),
        (peer, peer_out),
        (slot, slot_out),
    )
    for copy in small:
        copy.wait()
    listed = cells[...]
    count = listed.shape[1]
    row_hot = (lax.broadcasted_iota(jnp.int32, (rows, count), 0) == listed // lanes).astype(jnp.float32)
    lane_hit = lax.broadcasted_iota(jnp.int32, (lanes, count), 0) == listed % lanes
    injected = []
    for step in (1, 0):
        sample = samples[pl.ds(steps[step], 1), :]
        field = lax.dot_general(
            row_hot,
            jnp.where(lane_hit, sample, 0.0),
            (((1,), (1,)), ((), ())),
            precision=lax.Precision.HIGHEST,
            preferred_element_type=jnp.float32,
        )
        injected.append(field.reshape(cz, cy, lanes))
    own[INJ - ADJ] = injected[1]
    flat = lax.broadcasted_iota(jnp.int32, (rows, lanes), 0) * lanes + lax.broadcasted_iota(jnp.int32, (rows, lanes), 1)
    for step in range(2):
        value = wave[steps[step]]
        field = jnp.zeros((rows, lanes), jnp.float32)
        for j in range(source.shape[1]):
            field = field + jnp.where(flat == spots[0, j], value, 0.0)
        own[SRC - ADJ + step] = field.reshape(cz, cy, lanes)
    for copy in large:
        copy.wait()
    for f in (SXX, SYY, SZZ):
        own[f] = own[f] + injected[0]

    even = even_mask("gz", (cy, lanes))
    near, far = face_counts(cz)
    up, down = faces(cz, True), faces(cz, False)
    zero = jnp.zeros((cy, lanes), jnp.float32)

    def tile(side, i):
        return own[side[i][0] - ADJ, side[i][1]] if i < len(side) else zero

    for i in range(near):
        above, below = tile(up[0], i), tile(down[0], i)
        for out, base, value in (
            (near_out, tiles, jnp.where(even, above, below)),
            (far_out, 0, jnp.where(even, below, above)),
        ):
            out[base + i], out[base + near + i] = split(value)
    for i in range(far):
        above, below = tile(up[1], i), tile(down[1], i)
        near_out[tiles + 2 * near + i] = jnp.where(even, above, below).astype(jnp.bfloat16)
        far_out[2 * near + i] = jnp.where(even, below, above).astype(jnp.bfloat16)
    for i in range(2 * near + far, far_out.shape[0]):
        far_out[i] = zero.astype(jnp.bfloat16)


def strip_part(tile, main, listed):
    lanes = tile.shape[1]
    lane = lax.broadcasted_iota(jnp.int32, tile.shape, 1)
    for z in listed:
        tile = jnp.where((lane >= 8 * z) & (lane < 8 * z + 4), pltpu.roll(main(z), (8 * z + 2) % lanes, 1), tile)
    return tile


def strip_whole(tile):
    position = lax.broadcasted_iota(jnp.int32, tile.shape, 1) % 8
    return jnp.where(position < 2, tile, jnp.where(position >= 6, pltpu.roll(tile, 4, 1), 0.0))


def frame_kernel(cz, own, ring_f, ring):
    cy, lanes = own.shape[2], own.shape[3]
    layers = cz + 2 * HALO
    ring_rows = ring.shape[2]
    zero = jnp.zeros((cy, lanes), jnp.float32)
    beyond = jnp.zeros((ring_rows - cy, lanes), jnp.float32)
    filled = {(f - ADJ, z) for up in (True, False) for listed in faces(cz, up) for f, _, z in listed}
    for f in range(ring.shape[0]):
        for z in range(cz):
            ring[f, HALO + z, 0:cy, :] = own[f, z]
        for z in (0, 1, layers - 2, layers - 1):
            if (f, z) not in filled:
                ring[f, z, 0:cy, :] = zero
        ring[f, layers, 0:cy, :] = strip_part(zero, lambda z: own[f, z - HALO], range(HALO, HALO + cz))
        for z in range(layers + 1):
            ring[f, z, cy:ring_rows, :] = beyond
    for f in range(ring_f.shape[0]):
        for z in range(layers + 1):
            ring_f[f, z, cy:ring_rows, :] = beyond


def column_kernel(
    cz, mine, core, chip, both_a, both_b, far, peer, slot, ring_f_in, ring_w_in,
    ring_f, ring, x_a, x_b, peers, slots, sems,
):
    cy, lanes = chip.shape[1], chip.shape[2]
    layers = cz + 2 * HALO
    tiles = chip.shape[0]
    half = both_a.shape[0]
    me = lax.axis_index("gz")
    count = lax.axis_size("gz")
    moves = copies(sems, (peer, peers), (slot, slots))
    near, _ = face_counts(cz)
    even = even_mask("gz", (cy, lanes))
    has_below, has_above = has_neighbours("gz")
    zero = jnp.zeros((cy, lanes), jnp.float32)
    filled = {}
    for up in (True, False):
        for depth, listed in enumerate(faces(cz, up)):
            for i, (f, _, z) in enumerate(listed):
                values = []
                for ref, base in ((core, tiles), (far, 0)):
                    if depth == 0:
                        values.append(joined(ref[base + i], ref[base + near + i]))
                    else:
                        values.append(ref[base + 2 * near + i].astype(jnp.float32))
                value = jnp.where(even, values[1], values[0]) if up else jnp.where(even, values[0], values[1])
                value = value * (has_below if up else has_above)
                ring[f - ADJ, z, 0:cy, :] = value
                filled.setdefault(f - ADJ, {})[z] = value
    strip = []
    for f in range(ring.shape[0]):
        there = filled.get(f, {})
        tile = strip_whole(strip_part(ring[f, layers, 0:cy, :], lambda z: there[z], sorted(there)))
        ring[f, layers, 0:cy, :] = tile
        strip.append(tile)
    for move in moves:
        move.wait()
    below, above = jnp.maximum(me - 1, 0), jnp.minimum(me + 1, count - 1)
    for z in range(layers):
        if z < HALO:
            brick, piece, keep = below, cz - HALO + z, has_below
        elif z < HALO + cz:
            brick, piece, keep = me, z - HALO, None
        else:
            brick, piece, keep = above, z - HALO - cz, has_above
        row = slots[brick, piece] * 9
        hops = jnp.full((cy, lanes), peers[brick, piece] ^ me, jnp.int32)
        late = jnp.full((cy, lanes), row, jnp.int32) >= half
        row_a, row_b = jnp.minimum(row, half - 9), jnp.maximum(row - half, 0)
        for f in range(9):
            parts = (mine[row + f], core[row + f], chip[row + f], both_a[row_a + f], both_b[row_b + f])
            parts = [part.astype(jnp.float32) for part in parts]
            value = jnp.where(late, parts[4], parts[3])
            value = jnp.where(hops < 2, jnp.where(hops == 1, parts[1], parts[0]), jnp.where(hops == 2, parts[2], value))
            ring_f[f, z, 0:cy, :] = value if keep is None else value * keep
    for f in range(9):
        ring_f[f, layers, 0:cy, :] = strip_whole(strip_part(zero, lambda z: ring_f[f, z, 0:cy, :], range(layers)))
    strip = [ring_f[f, layers, 0:cy, :] for f in range(9)] + strip
    position = lax.broadcasted_iota(jnp.int32, (cy, lanes), 1) % 8
    even_x = even_mask("gx", (cy, lanes))
    for out, tail_from_even in ((x_a, True), (x_b, False)):
        if out is None:
            continue
        place = 0
        for fields, narrow in ((range(ADJ), True), (range(ADJ, FIELDS), False)):
            quads = [fields[i : i + 4] for i in range(0, len(fields), 4)]
            for i, quad in enumerate(quads):
                tile = zero
                for g, f in enumerate(quad):
                    tail, head = strip[f], pltpu.roll(strip[f], lanes - 6, 1)
                    value = jnp.where(even_x, tail, head) if tail_from_even else jnp.where(even_x, head, tail)
                    value = value if g == 0 else pltpu.roll(value, 2 * g, 1)
                    tile = jnp.where(position // 2 == g, value, tile)
                high, low = split(tile)
                out[place + i] = high
                if not narrow:
                    out[place + len(quads) + i] = low
            place += len(quads) if narrow else 2 * len(quads)


def x_tiles():
    return -(-ADJ // 4) + 2 * -(-(FIELDS - ADJ) // 4)


class Ring:
    def __init__(self, ring_f, ring_w):
        self.parts = ring_f, ring_w

    def __getitem__(self, key):
        f = key[0]
        return self.parts[0][key] if f < ADJ else self.parts[1][(f - ADJ, *key[1:])]

    def __setitem__(self, key, value):
        f = key[0]
        if f < ADJ:
            self.parts[0][key] = value
        else:
            self.parts[1][(f - ADJ, *key[1:])] = value


def strip_rows_kernel(cz, ring_f, ring_w, x_a, x_b, y_a_in, y_b_in, strips, y_a, y_b, packed):
    cy, lanes = strips.shape[1], strips.shape[2]
    layers = cz + 2 * HALO
    pair = lax.broadcasted_iota(jnp.int32, (cy, lanes), 1) % 8 // 2
    even_x = even_mask("gx", (cy, lanes))
    has_left, has_right = has_neighbours("gx")
    zero = jnp.zeros((cy, lanes), jnp.float32)
    place = 0
    for fields, narrow in ((range(ADJ), True), (range(ADJ, FIELDS), False)):
        quads = [fields[i : i + 4] for i in range(0, len(fields), 4)]
        for i, quad in enumerate(quads):
            got = []
            for ref in (x_a, x_b):
                if ref is None:
                    got.append(zero)
                elif narrow:
                    got.append(ref[place + i].astype(jnp.float32))
                else:
                    got.append(joined(ref[place + i], ref[place + len(quads) + i]))
            right = jnp.where(even_x, got[0], got[1]) * has_right
            left = jnp.where(even_x, got[1], got[0]) * has_left
            for g, f in enumerate(quad):
                strip = ring_f[f, layers, 0:cy, :] if f < ADJ else ring_w[f - ADJ, layers, 0:cy, :]
                tile = jnp.where(pair == 1, pltpu.roll(right, (2 - 2 * g) % lanes, 1), strip)
                strips[f] = jnp.where(pair == 2, pltpu.roll(left, (4 - 2 * g) % lanes, 1), tile)
        place += len(quads) if narrow else 2 * len(quads)
    sides = []
    for side, up in enumerate((True, False)):
        scatter_rows(packed.at[side], y_rows(cz, cy, up)[2], lambda f, z, y: strips[f, y : y + 1, :])
        sides.append([packed[side, t] for t in range(row_counts(cz, cy, up)[2])])
    pack_tiles(sides, (y_a, y_b), 0, packed.shape[1])


def window_kernel(
    cz, ring_f_in, ring_w_in, strips, y_a, y_b, own,
    final, image_lam, image_mu, ring_f, ring_w, packed, keep, images, speeds, sems,
):
    cy, lanes = own.shape[2], own.shape[3]
    layers = cz + 2 * HALO
    ring_rows = ring_f.shape[2]
    ring = Ring(ring_f, ring_w)
    for f in range(FIELDS):
        ring[f, layers, 0:cy, :] = strips[f]

    def put_row(f, z, y, value):
        ring[f, z, y : y + 1, :] = value

    unpack_rows(cz, cy, (y_a, y_b), packed, put_row)

    lane = lax.broadcasted_iota(jnp.int32, (ring_rows, lanes), 1)
    first_lane, last_lane = lane == 0, lane == lanes - 1
    edge = layers

    def at(f, z):
        return ring[f, z]

    def x_next(f, z):
        value = at(f, z)
        if z == edge:
            return pltpu.roll(value, lanes - 1, 1)
        beyond = pltpu.roll(at(f, edge), (lanes - 1 - (8 * z + 2)) % lanes, 1)
        return jnp.where(last_lane, beyond, pltpu.roll(value, lanes - 1, 1))

    def x_prev(f, z):
        value = at(f, z)
        if z == edge:
            return pltpu.roll(value, 1, 1)
        beyond = pltpu.roll(at(f, edge), (lanes - (8 * z + 5)) % lanes, 1)
        return jnp.where(first_lane, beyond, pltpu.roll(value, 1, 1))

    def y_next(f, z):
        return pltpu.roll(at(f, z), ring_rows - 1, 0)

    def y_prev(f, z):
        return pltpu.roll(at(f, z), 1, 0)

    def z_next(f, z):
        return pltpu.roll(at(f, edge), lanes - 8, 1) if z == edge else at(f, z + 1)

    def z_prev(f, z):
        return pltpu.roll(at(f, edge), 8, 1) if z == edge else at(f, z - 1)

    def velocity_rates(base, z, want):
        buoy = at(BUOY, z)
        sxx, syy, szz = (functools.partial(at, base + f) for f in (SXX, SYY, SZZ))
        sxy, sxz, syz = (functools.partial(at, base + f) for f in (SXY, SXZ, SYZ))
        out = {}
        if VX in want:
            out[VX] = buoy * (
                (x_next(base + SXX, z) - sxx(z)) + (sxy(z) - y_prev(base + SXY, z)) + (sxz(z) - z_prev(base + SXZ, z))
            )
        if VY in want:
            out[VY] = buoy * (
                (sxy(z) - x_prev(base + SXY, z)) + (y_next(base + SYY, z) - syy(z)) + (syz(z) - z_prev(base + SYZ, z))
            )
        if VZ in want:
            out[VZ] = buoy * (
                (sxz(z) - x_prev(base + SXZ, z)) + (syz(z) - y_prev(base + SYZ, z)) + (z_next(base + SZZ, z) - szz(z))
            )
        return out

    def stress_rates(base, z, want):
        lam, mu = at(LAM, z), at(MU, z)
        vx, vy, vz = at(base + VX, z), at(base + VY, z), at(base + VZ, z)
        out = {}
        if SXX in want:
            exx = vx - x_prev(base + VX, z)
            eyy = vy - y_prev(base + VY, z)
            ezz = vz - z_prev(base + VZ, z)
            common = lam * (exx + eyy + ezz)
            twice = 2.0 * mu
            out[SXX] = common + twice * exx
            out[SYY] = common + twice * eyy
            out[SZZ] = common + twice * ezz
        if SXY in want:
            out[SXY] = mu * ((y_next(base + VX, z) - vx) + (x_next(base + VY, z) - vy))
        if SXZ in want:
            out[SXZ] = mu * ((z_next(base + VX, z) - vx) + (x_next(base + VZ, z) - vz))
            out[SYZ] = mu * ((z_next(base + VY, z) - vy) + (y_next(base + VZ, z) - vz))
        return out

    def spread(ranges):
        for z in list(range(layers)) + [edge]:
            want = {f for f, (a, b) in ranges.items() if z == edge or a <= z < b}
            if want:
                yield z, want

    def velocity_step(base, sign, ranges):
        for z, want in spread(ranges):
            for f, rate in velocity_rates(base, z, want).items():
                ring[base + f, z] = at(base + f, z) + rate if sign > 0 else at(base + f, z) - rate

    def stress_step(base, sign, ranges, before=None, after=None):
        for z, want in spread(ranges):
            for f, rate in stress_rates(base, z, want).items():
                value, normal = at(base + f, z), f in (SXX, SYY, SZZ)
                if before is not None and normal:
                    value = value + at(before, z)
                value = value + rate if sign > 0 else value - rate
                if after is not None and normal:
                    value = value + at(after, z)
                ring[base + f, z] = value

    def terms(f, a):
        term_lam = (f[0] + f[1] + f[2]) * (a[0] + a[1] + a[2])
        term_mu = f[0] * a[0] + f[1] * a[1] + f[2] * a[2] + 2.0 * (f[3] * a[3] + f[4] * a[4] + f[5] * a[5])
        return term_lam, term_mu

    inner = (HALO, HALO + cz)
    n = layers
    stress_step(ADJ, -1, {SXX: (1, n), SXY: (0, n), SXZ: (0, n - 1)})
    velocity_step(FWD, 1, {VX: (1, n), VY: (1, n), VZ: (0, n - 1)})
    stress_step(FWD, 1, {SXX: (1, n - 1), SXY: (1, n - 1), SXZ: (1, n - 1)}, after=SRC)
    for z in range(*inner):
        f = [ring[FWD + s, z, 0:cy, :] for s in range(SXX, SYZ + 1)]
        a = [ring[ADJ + s, z, 0:cy, :] for s in range(SXX, SYZ + 1)]
        a = [value + ring[INJ, z, 0:cy, :] for value in a[:3]] + a[3:]
        keep[0, z - HALO], keep[1, z - HALO] = terms(f, a)
    velocity_step(FWD, 1, {VX: (2, n - 1), VY: (2, n - 1), VZ: (1, n - 2)})
    everything = set(range(SXX, SYZ + 1))
    for z in range(*inner):
        rates = stress_rates(FWD, z, everything)
        f = []
        for s in range(SXX, SYZ + 1):
            value = (at(FWD + s, z) + rates[s])[0:cy, :]
            f.append(value + own[SRC - ADJ + 1, z - HALO] if s <= SZZ else value)
        a = [own[s, z - HALO] for s in range(SXX, SYZ + 1)]
        term_lam, term_mu = terms(f, a)
        images[0, z - HALO] = term_lam + keep[0, z - HALO]
        images[1, z - HALO] = term_mu + keep[1, z - HALO]
    moves = copies(sems, (images.at[0], image_lam), (images.at[1], image_mu))
    velocity_step(ADJ, -1, {VX: (1, n - 1), VY: (1, n - 1), VZ: (1, n - 1)})
    stress_step(ADJ, -1, {SXX: (2, n - 1), SXY: (1, n - 1), SXZ: (1, n - 2)}, before=INJ)
    stresses = ring_w.at[pl.ds(SXX, SYZ + 1 - SXX), pl.ds(HALO, cz), pl.ds(0, cy)]
    moves += copies(sems.at[pl.ds(2, 1)], (stresses, final.at[pl.ds(SXX, SYZ + 1 - SXX)]))
    for z in range(*inner):
        rates = velocity_rates(ADJ, z, {VX, VY, VZ})
        for f in (VX, VY, VZ):
            speeds[f, z - HALO] = (at(ADJ + f, z) - rates[f])[0:cy, :]
    moves += copies(sems.at[pl.ds(3, 1)], (speeds, final.at[pl.ds(VX, VZ + 1 - VX)]))
    for move in moves:
        move.wait()


def swap_pairs(count, first):
    pairs = [(i + d, i + 1 - d) for i in range(first, count - 1, 2) for d in (0, 1)]
    return pairs + [(i, i) for i in range(count) if i not in dict(pairs)]


def swapped(value_a, value_b, axis):
    count = lax.axis_size(axis)
    got_a = lax.ppermute(value_a, axis, swap_pairs(count, 0))
    return got_a, None if value_b is None else lax.ppermute(value_b, axis, swap_pairs(count, 1))


def stay(value, spec):
    return pltpu.with_memory_space_constraint(value, pltpu.HBM) if spec.memory_space == pl.ANY else value


def kernel_call(body, args, in_specs, out_shape, scratch_shapes=(), aliases=None, out_specs=None):
    here = [a is not None for a in args]
    there = [o is not None for o in out_shape]

    def run(*refs):
        refs = iter(refs)
        full = [next(refs) if h else None for h in here + there]
        body(*full, *refs)

    out = iter(
        pl.pallas_call(
            run,
            out_shape=tuple(o for o in out_shape if o is not None),
            in_specs=[s for s, h in zip(in_specs, here) if h],
            out_specs=out_specs or tuple(vmem() for h in there if h),
            scratch_shapes=list(scratch_shapes),
            input_output_aliases=aliases or {},
            compiler_params=pltpu.CompilerParams(vmem_limit_bytes=VMEM_LIMIT),
        )(*[stay(a, s) for a, s in zip(args, in_specs) if a is not None])
    )
    return tuple(next(out) if h else None for h in there)


def on_device(
    checkpoint_store,
    holder_peer,
    holder_slot,
    adjoint_state,
    lame_lambda,
    lame_mu,
    buoyancy,
    source_cell,
    wavelet,
    receiver_cell,
    traces,
    plan,
):
    cz, cy, cx = lame_mu.shape
    layers = cz + 2 * HALO
    bf16, f32 = jnp.bfloat16, jnp.float32
    store = checkpoint_store.reshape(-1, cy, cx)
    tiles = store.shape[0]
    peer, slot = holder_peer[0, 0], holder_slot[0, 0]
    source, receiver = source_cell.reshape(1, -1), receiver_cell.reshape(1, -1)
    traces = traces.reshape(traces.shape[-2:])
    holders = lax.axis_size("gz")
    assert holders == 4
    near, far = face_counts(cz)
    face = 2 * near + far
    half = tiles // 2

    def shape(*dims, dtype=f32):
        return jax.ShapeDtypeStruct(dims, dtype)

    wide_x = lax.axis_size("gx") > 2
    chip = lax.ppermute(store, "gz", [(i, i ^ 2) for i in range(holders)])
    to_core, to_far, own, peer, slot = kernel_call(
        functools.partial(start_kernel, cz),
        (store, adjoint_state, lame_lambda, lame_mu, buoyancy, source, wavelet, receiver, traces, plan, peer, slot),
        [hbm()] * 12,
        (shape(tiles + face, cy, cx, dtype=bf16), shape(max(face, half) + PAD, cy, cx, dtype=bf16), shape(15, cz, cy, cx),
         shape(*peer.shape, dtype=jnp.int32), shape(*slot.shape, dtype=jnp.int32)),
        [
            pltpu.VMEM(receiver.shape, jnp.int32),
            pltpu.VMEM(traces.shape, f32),
            pltpu.SMEM(source.shape, jnp.int32),
            pltpu.SMEM(wavelet.shape, f32),
            pltpu.SMEM(plan.shape, jnp.int32),
            pltpu.SemaphoreType.DMA((12,)),
        ],
    )
    core = lax.ppermute(to_core, "gz", [(i, i ^ 1) for i in range(holders)])
    gy = lax.axis_size("gy")
    across = {
        (i, c): (i, 3 - c) if c in (1, 2) else (i ^ 1, c)
        for i in range(gy) for c in range(holders)
    }
    far_face = lax.ppermute(
        to_far, ("gy", "gz"), [(a[0] * holders + a[1], b[0] * holders + b[1]) for a, b in across.items()]
    )
    both = [lax.ppermute(part, "gz", [(i, i ^ 1) for i in range(holders)]) for part in (chip[:half], chip[half:])]

    ring_f, ring_w = kernel_call(
        functools.partial(frame_kernel, cz),
        (own,),
        [vmem()],
        (shape(ADJ, layers + 1, 2 * cy, cx), shape(FIELDS - ADJ, layers + 1, 2 * cy, cx)),
    )
    x_send = shape(x_tiles(), cy, cx, dtype=bf16)
    ring_f, ring_w, x_a, x_b = kernel_call(
        functools.partial(column_kernel, cz),
        (to_core, core, chip, *both, far_face, peer, slot, ring_f, ring_w),
        [vmem()] * 10,
        (shape(*ring_f.shape), shape(*ring_w.shape), x_send, x_send if wide_x else None),
        [
            pltpu.SMEM(peer.shape, jnp.int32),
            pltpu.SMEM(slot.shape, jnp.int32),
            pltpu.SemaphoreType.DMA((2,)),
        ],
        {8: 0, 9: 1},
    )
    axes = ("gx", "gy", "gz")
    gx = lax.axis_size("gx")

    def partner(i, j, c, x_turn, y_turn):
        if x_turn is not None:
            i = dict(swap_pairs(gx, x_turn))[i]
        if y_turn is not None:
            other = dict(swap_pairs(gy, (c + y_turn) % 2))[j]
            j, c = (j, c ^ 2) if other == j else (other, c)
        return (i * gy + j) * holders + c

    def swap(value, x_turn, y_turn):
        if value is None:
            return None
        pairs = [
            ((i * gy + j) * holders + c, partner(i, j, c, x_turn, y_turn))
            for i in range(gx) for j in range(gy) for c in range(holders)
        ]
        return lax.ppermute(value, axes, pairs)

    strip_tiles, tiles = row_tiles(cz, cy)
    y_send = shape(strip_tiles + tiles, cy, cx, dtype=bf16)
    scratch_tiles = max(sum(row_counts(cz, cy, up)) for up in (True, False))
    y_a, y_b = kernel_call(
        functools.partial(layer_rows_kernel, cz),
        (ring_f, ring_w),
        [vmem()] * 2,
        (y_send, y_send),
        [pltpu.VMEM((2, scratch_tiles, 8, cx), f32)],
    )
    strips, y_a, y_b = kernel_call(
        functools.partial(strip_rows_kernel, cz),
        (ring_f, ring_w, swap(x_a, 0, None), swap(x_b, 1, None), y_a, y_b),
        [vmem()] * 6,
        (shape(FIELDS, cy, cx), y_send, y_send),
        [pltpu.VMEM((2, strip_tiles, 8, cx), f32)],
        {4 if wide_x else 3: 1, 5 if wide_x else 4: 2},
    )
    result = kernel_call(
        functools.partial(window_kernel, cz),
        (ring_f, ring_w, strips, swap(y_a, None, 0), swap(y_b, None, 1), own),
        [vmem()] * 6,
        (
            shape(9, cz, cy, cx),
            shape(cz, cy, cx),
            shape(cz, cy, cx),
            shape(*ring_f.shape),
            shape(*ring_w.shape),
        ),
        [
            pltpu.VMEM((2, scratch_tiles, 8, cx), f32),
            pltpu.VMEM((2, cz, cy, cx), f32),
            pltpu.VMEM((2, cz, cy, cx), f32),
            pltpu.VMEM((3, cz, cy, cx), f32),
            pltpu.SemaphoreType.DMA((4,)),
        ],
        {0: 3, 1: 4},
        (hbm(),) * 3 + (vmem(),) * 2,
    )
    return result[:3]


def solution(mesh):
    return jax.shard_map(
        on_device,
        mesh=mesh,
        in_specs=(
            P("gz", None, None, "gy", "gx"),
            P("gx", "gy", None, None),
            P("gx", "gy", None, None),
            P(None, "gz", "gy", "gx"),
            P("gz", "gy", "gx"),
            P("gz", "gy", "gx"),
            P("gz", "gy", "gx"),
            P("gz", "gy", "gx", None),
            P(),
            P("gz", "gy", "gx", None),
            P("gz", "gy", "gx", None, None),
            P(),
        ),
        out_specs=(P(None, "gz", "gy", "gx"), P("gz", "gy", "gx"), P("gz", "gy", "gx")),
        check_vma=False,
    )
```

```python
import functools

import jax
import jax.numpy as jnp
from jax import lax
from jax.experimental import pallas as pl
from jax.experimental.pallas import tpu as pltpu
from jax.sharding import PartitionSpec as P

VX, VY, VZ, SXX, SYY, SZZ, SXY, SXZ, SYZ = range(9)
FWD, ADJ, BUOY, LAM, MU, INJ, SRC = 0, 9, 18, 19, 20, 21, 22
FIELDS = 23
HALO = 2

ADJ_Z = {VX: (2, 2), VY: (2, 2), VZ: (2, 2), SXX: (1, 1), SYY: (1, 1), SZZ: (1, 2), SXY: (1, 1), SXZ: (2, 1), SYZ: (2, 1)}
OTHER_Z = {BUOY: (2, 2), LAM: (1, 2), MU: (2, 2), INJ: (0, 1), SRC: (1, 1)}
F32_Z = {**{ADJ + f: c for f, c in ADJ_Z.items()}, **OTHER_Z}

Y_ROWS = {
    FWD + VX: (None, (2, -1, 1), (1, -1, 1), (2, -2, 0)),
    FWD + VY: ((2, -2, 0), (1, -1, 1), (2, -1, 1), None),
    FWD + VZ: (None, (1, -2, 1), (1, -1, 1), (2, -2, 0)),
    FWD + SXX: (None, (2, -1, 1), (1, -1, 1), (2, -2, 1)),
    FWD + SYY: ((2, -2, 0), (1, -1, 1), (1, 0, 1), (2, -1, 1)),
    FWD + SZZ: (None, (1, -1, 1), (1, 0, 1), (2, -1, 0)),
    FWD + SXY: ((2, -1, 1), (1, 0, 1), (1, -1, 1), (2, -2, 0)),
    FWD + SXZ: (None, (1, -1, 1), (0, -1, 1), (1, -2, 1)),
    FWD + SYZ: ((1, -2, 1), (0, -1, 1), (1, -1, 1), (2, -2, 0)),
    ADJ + VX: ((2, -2, 0), (1, -1, 1), (1, -1, 1), (2, -2, 1)),
    ADJ + VY: ((2, -1, 1), (1, 0, 1), (1, -1, 1), (2, -2, 0)),
    ADJ + VZ: ((2, -2, 0), (1, -1, 1), (0, -1, 1), (1, -2, 0)),
    ADJ + SXX: (None, (2, -2, 1), (2, -2, 1), None),
    ADJ + SYY: (None, (2, -1, 1), (1, -1, 1), (2, -2, 0)),
    ADJ + SZZ: (None, (2, -1, 0), (1, -1, 0), None),
    ADJ + SXY: ((2, -2, 0), (1, -1, 1), (2, -2, 1), None),
    ADJ + SXZ: (None, (1, -2, 1), (1, -2, 1), None),
    ADJ + SYZ: ((2, -2, 0), (1, -1, 1), (1, -2, 0), None),
    BUOY: ((2, -2, 0), (1, -1, 1), (1, -1, 1), (2, -2, 0)),
    LAM: (None, (2, -1, 1), (1, -1, 1), (2, -2, 0)),
    MU: ((2, -2, 0), (1, -1, 1), (1, -1, 1), (2, -2, 0)),
    INJ: (None, None, (2, -2, 0), None),
    SRC: (None, (2, -2, 0), (2, -1, 1), None),
}

EXACT_ROWS = {-1: (ADJ + VY, ADJ + SXY, ADJ + SYZ, BUOY, SRC), 0: (ADJ + SYY, LAM, INJ, SRC)}

PAD = 1
VMEM_LIMIT = 48 * 1024 * 1024


def vmem():
    return pl.BlockSpec(memory_space=pltpu.VMEM)


def hbm():
    return pl.BlockSpec(memory_space=pl.ANY)


def faces(cz, up):
    near, far = [], []
    for f in sorted(F32_Z):
        before, after = F32_Z[f]
        depth = before if up else after
        for d in range(depth):
            layer = cz - 1 - d if up else d
            (far if d else near).append((f, layer, HALO - 1 - d if up else HALO + cz + d))
    return near, far


def face_counts(cz):
    sides = [faces(cz, up) for up in (True, False)]
    return max(len(s[0]) for s in sides), max(len(s[1]) for s in sides)


def y_rows(cz, cy, up):
    layers = cz + 2 * HALO
    narrow, wide, strip = [], [], []
    for f in sorted(Y_ROWS):
        for offset in (-1, -2) if up else (0, 1):
            spec = Y_ROWS[f][offset + HALO]
            if spec is None:
                continue
            source = cy + offset if up else offset
            target = cy - HALO + offset if up else HALO + offset
            exact = f in EXACT_ROWS.get(offset, ())
            (wide if exact else narrow).extend((f, z, source, target) for z in range(spec[0], layers + spec[1]))
            if spec[2]:
                strip.append((f, layers, source, target))
    return narrow, wide, strip


def row_counts(cz, cy, up):
    return tuple(-(-len(rows) // 8) for rows in y_rows(cz, cy, up))


def row_tiles(cz, cy):
    sides = [row_counts(cz, cy, up) for up in (True, False)]
    return max(c for _, _, c in sides), max(n + 2 * w for n, w, _ in sides)


def split(value):
    high = value.astype(jnp.bfloat16)
    low = (value - high.astype(jnp.float32)).astype(jnp.bfloat16)
    return high, low


def joined(high, low):
    return high.astype(jnp.float32) + low.astype(jnp.float32)


def even_mask(axes, shape):
    total = sum(lax.axis_index(a) for a in ((axes,) if isinstance(axes, str) else axes))
    return jnp.full(shape, lax.rem(total, 2), jnp.int32) == 0


def has_neighbours(axis):
    index = lax.axis_index(axis)
    return (index > 0).astype(jnp.float32), (index < lax.axis_size(axis) - 1).astype(jnp.float32)


def copies(sems, *pairs):
    out = [pltpu.make_async_copy(source, target, sems.at[i]) for i, (source, target) in enumerate(pairs)]
    for copy in out:
        copy.start()
    return out


def scatter_rows(packed, listed, row_of):
    for r, (f, z, y, _) in enumerate(listed):
        packed[r // 8, r % 8 : r % 8 + 1, :] = row_of(f, z, y)


def pack_tiles(sides, sends, first, count):
    even = even_mask(("gy", "gz"), sends[0].shape[1:])
    for t in range(count):
        up, down = (side[min(t, len(side) - 1)] for side in sides)
        sends[0][first + t] = jnp.where(even, up, down).astype(jnp.bfloat16)
        sends[1][first + t] = jnp.where(even, down, up).astype(jnp.bfloat16)


def layer_rows_kernel(cz, ring_f, ring_w, send_a, send_b, packed):
    cy = ring_f.shape[2]
    strip_tiles, tiles = row_tiles(cz, cy)

    def row_of(f, z, y):
        return ring_f[f, z, y : y + 1, :] if f < ADJ else ring_w[f - ADJ, z, y : y + 1, :]

    sides = []
    for side, up in enumerate((True, False)):
        narrow, wide, _ = y_rows(cz, cy, up)
        n, w, _ = row_counts(cz, cy, up)
        scatter_rows(packed.at[side], narrow, row_of)
        scatter_rows(packed.at[side, pl.ds(n, w)], wide, row_of)
        rest = [split(packed[side, n + t])[1].astype(jnp.float32) for t in range(w)]
        sides.append([packed[side, t] for t in range(n + w)] + rest)
    pack_tiles(sides, (send_a, send_b), strip_tiles, tiles)


def unpack_rows(cz, cy, got, packed, put_row):
    has_lower, has_upper = has_neighbours("gy")
    even = even_mask(("gy", "gz"), packed.shape[2:])
    strip_tiles, _ = row_tiles(cz, cy)
    for side, (up, keep) in enumerate(((True, has_lower), (False, has_upper))):
        narrow, wide, strip = y_rows(cz, cy, up)
        n, w, c = row_counts(cz, cy, up)

        def of(t):
            a, b = got[0][t].astype(jnp.float32), got[1][t].astype(jnp.float32)
            return (jnp.where(even, b, a) if up else jnp.where(even, a, b)) * keep

        for t in range(n + w):
            value = of(strip_tiles + t)
            packed[side, t] = value if t < n else value + of(strip_tiles + w + t)
        for t in range(c):
            packed[side, n + w + t] = of(t)
        for base, listed in ((0, narrow), (n, wide), (n + w, strip)):
            for r, (f, z, _, y) in enumerate(listed):
                put_row(f, z, y, packed[side, base + r // 8, r % 8 : r % 8 + 1, :])


def start_kernel(
    cz, store, adjoint, lam, mu, buoy, source, wavelet, receiver, traces, plan, peer, slot,
    near_out, far_out, own, peer_out, slot_out, cells, samples, spots, wave, steps, sems,
):
    cy, lanes = own.shape[2], own.shape[3]
    rows = cz * cy
    tiles = store.shape[0]
    small = copies(sems, (plan, steps), (wavelet, wave), (source, spots), (receiver, cells), (traces, samples))
    large = copies(
        sems.at[pl.ds(len(small), 7)],
        (adjoint, own.at[pl.ds(0, 9)]),
        (buoy, own.at[BUOY - ADJ]),
        (lam, own.at[LAM - ADJ]),
        (mu, own.at[MU - ADJ]),
        (store, near_out.at[pl.ds(0, tiles)]),
        (peer, peer_out),
        (slot, slot_out),
    )
    for copy in small:
        copy.wait()
    listed = cells[...]
    count = listed.shape[1]
    row_hot = (lax.broadcasted_iota(jnp.int32, (rows, count), 0) == listed // lanes).astype(jnp.float32)
    lane_hit = lax.broadcasted_iota(jnp.int32, (lanes, count), 0) == listed % lanes
    injected = []
    for step in (1, 0):
        sample = samples[pl.ds(steps[step], 1), :]
        field = lax.dot_general(
            row_hot,
            jnp.where(lane_hit, sample, 0.0),
            (((1,), (1,)), ((), ())),
            precision=lax.Precision.HIGHEST,
            preferred_element_type=jnp.float32,
        )
        injected.append(field.reshape(cz, cy, lanes))
    own[INJ - ADJ] = injected[1]
    flat = lax.broadcasted_iota(jnp.int32, (rows, lanes), 0) * lanes + lax.broadcasted_iota(jnp.int32, (rows, lanes), 1)
    for step in range(2):
        value = wave[steps[step]]
        field = jnp.zeros((rows, lanes), jnp.float32)
        for j in range(source.shape[1]):
            field = field + jnp.where(flat == spots[0, j], value, 0.0)
        own[SRC - ADJ + step] = field.reshape(cz, cy, lanes)
    for copy in large:
        copy.wait()
    for f in (SXX, SYY, SZZ):
        own[f] = own[f] + injected[0]

    even = even_mask("gz", (cy, lanes))
    near, far = face_counts(cz)
    up, down = faces(cz, True), faces(cz, False)
    zero = jnp.zeros((cy, lanes), jnp.float32)

    def tile(side, i):
        return own[side[i][0] - ADJ, side[i][1]] if i < len(side) else zero

    for i in range(near):
        above, below = tile(up[0], i), tile(down[0], i)
        for out, base, value in (
            (near_out, tiles, jnp.where(even, above, below)),
            (far_out, 0, jnp.where(even, below, above)),
        ):
            out[base + i], out[base + near + i] = split(value)
    for i in range(far):
        above, below = tile(up[1], i), tile(down[1], i)
        near_out[tiles + 2 * near + i] = jnp.where(even, above, below).astype(jnp.bfloat16)
        far_out[2 * near + i] = jnp.where(even, below, above).astype(jnp.bfloat16)
    for i in range(2 * near + far, far_out.shape[0]):
        far_out[i] = zero.astype(jnp.bfloat16)


def strip_part(tile, main, listed):
    lanes = tile.shape[1]
    lane = lax.broadcasted_iota(jnp.int32, tile.shape, 1)
    for z in listed:
        tile = jnp.where((lane >= 8 * z) & (lane < 8 * z + 4), pltpu.roll(main(z), (8 * z + 2) % lanes, 1), tile)
    return tile


def strip_whole(tile):
    position = lax.broadcasted_iota(jnp.int32, tile.shape, 1) % 8
    return jnp.where(position < 2, tile, jnp.where(position >= 6, pltpu.roll(tile, 4, 1), 0.0))


def frame_kernel(cz, own, ring):
    cy, lanes = own.shape[2], own.shape[3]
    layers = cz + 2 * HALO
    zero = jnp.zeros((cy, lanes), jnp.float32)
    filled = {(f - ADJ, z) for up in (True, False) for listed in faces(cz, up) for f, _, z in listed}
    for f in range(ring.shape[0]):
        for z in range(cz):
            ring[f, HALO + z] = own[f, z]
        for z in (0, 1, layers - 2, layers - 1):
            if (f, z) not in filled:
                ring[f, z] = zero
        ring[f, layers] = strip_part(zero, lambda z: own[f, z - HALO], range(HALO, HALO + cz))


def column_kernel(
    cz, mine, core, chip, both_a, both_b, far, peer, slot, ring_w_in,
    ring_f, ring, x_a, x_b, peers, slots, sems,
):
    cy, lanes = chip.shape[1], chip.shape[2]
    layers = cz + 2 * HALO
    tiles = chip.shape[0]
    half = both_a.shape[0]
    me = lax.axis_index("gz")
    count = lax.axis_size("gz")
    moves = copies(sems, (peer, peers), (slot, slots))
    near, _ = face_counts(cz)
    even = even_mask("gz", (cy, lanes))
    has_below, has_above = has_neighbours("gz")
    zero = jnp.zeros((cy, lanes), jnp.float32)
    filled = {}
    for up in (True, False):
        for depth, listed in enumerate(faces(cz, up)):
            for i, (f, _, z) in enumerate(listed):
                values = []
                for ref, base in ((core, tiles), (far, 0)):
                    if depth == 0:
                        values.append(joined(ref[base + i], ref[base + near + i]))
                    else:
                        values.append(ref[base + 2 * near + i].astype(jnp.float32))
                value = jnp.where(even, values[1], values[0]) if up else jnp.where(even, values[0], values[1])
                value = value * (has_below if up else has_above)
                ring[f - ADJ, z] = value
                filled.setdefault(f - ADJ, {})[z] = value
    strip = []
    for f in range(ring.shape[0]):
        there = filled.get(f, {})
        tile = strip_whole(strip_part(ring[f, layers], lambda z: there[z], sorted(there)))
        ring[f, layers] = tile
        strip.append(tile)
    for move in moves:
        move.wait()
    below, above = jnp.maximum(me - 1, 0), jnp.minimum(me + 1, count - 1)
    for z in range(layers):
        if z < HALO:
            brick, piece, keep = below, cz - HALO + z, has_below
        elif z < HALO + cz:
            brick, piece, keep = me, z - HALO, None
        else:
            brick, piece, keep = above, z - HALO - cz, has_above
        row = slots[brick, piece] * 9
        hops = jnp.full((cy, lanes), peers[brick, piece] ^ me, jnp.int32)
        late = jnp.full((cy, lanes), row, jnp.int32) >= half
        row_a, row_b = jnp.minimum(row, half - 9), jnp.maximum(row - half, 0)
        for f in range(9):
            parts = (mine[row + f], core[row + f], chip[row + f], both_a[row_a + f], both_b[row_b + f])
            parts = [part.astype(jnp.float32) for part in parts]
            value = jnp.where(late, parts[4], parts[3])
            value = jnp.where(hops < 2, jnp.where(hops == 1, parts[1], parts[0]), jnp.where(hops == 2, parts[2], value))
            ring_f[f, z] = value if keep is None else value * keep
    for f in range(9):
        ring_f[f, layers] = strip_whole(strip_part(zero, lambda z: ring_f[f, z], range(layers)))
    strip = [ring_f[f, layers] for f in range(9)] + strip
    position = lax.broadcasted_iota(jnp.int32, (cy, lanes), 1) % 8
    even_x = even_mask("gx", (cy, lanes))
    for out, tail_from_even in ((x_a, True), (x_b, False)):
        if out is None:
            continue
        place = 0
        for fields, narrow in ((range(ADJ), True), (range(ADJ, FIELDS), False)):
            quads = [fields[i : i + 4] for i in range(0, len(fields), 4)]
            for i, quad in enumerate(quads):
                tile = zero
                for g, f in enumerate(quad):
                    tail, head = strip[f], pltpu.roll(strip[f], lanes - 6, 1)
                    value = jnp.where(even_x, tail, head) if tail_from_even else jnp.where(even_x, head, tail)
                    value = value if g == 0 else pltpu.roll(value, 2 * g, 1)
                    tile = jnp.where(position // 2 == g, value, tile)
                high, low = split(tile)
                out[place + i] = high
                if not narrow:
                    out[place + len(quads) + i] = low
            place += len(quads) if narrow else 2 * len(quads)


def x_tiles():
    return -(-ADJ // 4) + 2 * -(-(FIELDS - ADJ) // 4)


def strip_rows_kernel(cz, ring_f, ring_w, x_a, x_b, y_a_in, y_b_in, strips, y_a, y_b, packed):
    cy, lanes = strips.shape[1], strips.shape[2]
    layers = cz + 2 * HALO
    pair = lax.broadcasted_iota(jnp.int32, (cy, lanes), 1) % 8 // 2
    even_x = even_mask("gx", (cy, lanes))
    has_left, has_right = has_neighbours("gx")
    zero = jnp.zeros((cy, lanes), jnp.float32)
    place = 0
    for fields, narrow in ((range(ADJ), True), (range(ADJ, FIELDS), False)):
        quads = [fields[i : i + 4] for i in range(0, len(fields), 4)]
        for i, quad in enumerate(quads):
            got = []
            for ref in (x_a, x_b):
                if ref is None:
                    got.append(zero)
                elif narrow:
                    got.append(ref[place + i].astype(jnp.float32))
                else:
                    got.append(joined(ref[place + i], ref[place + len(quads) + i]))
            right = jnp.where(even_x, got[0], got[1]) * has_right
            left = jnp.where(even_x, got[1], got[0]) * has_left
            for g, f in enumerate(quad):
                strip = ring_f[f, layers] if f < ADJ else ring_w[f - ADJ, layers]
                tile = jnp.where(pair == 1, pltpu.roll(right, (2 - 2 * g) % lanes, 1), strip)
                strips[f] = jnp.where(pair == 2, pltpu.roll(left, (4 - 2 * g) % lanes, 1), tile)
        place += len(quads) if narrow else 2 * len(quads)
    sides = []
    for side, up in enumerate((True, False)):
        scatter_rows(packed.at[side], y_rows(cz, cy, up)[2], lambda f, z, y: strips[f, y : y + 1, :])
        sides.append([packed[side, t] for t in range(row_counts(cz, cy, up)[2])])
    pack_tiles(sides, (y_a, y_b), 0, packed.shape[1])


STAGE = {"fv": 0, "fs": 3, "fw": 9, "as": 12, "av": 18, "at": 21}
STAGES = 27
NORMAL = (SXX, SYY, SZZ)
STRESS = range(SXX, SYZ + 1)


def window(cz, base, stage, after, before, put):
    layers = cz + 2 * HALO
    edge = layers
    cy, lanes = stage.shape[2], stage.shape[3]
    lane = lax.broadcasted_iota(jnp.int32, (cy, lanes), 1)
    first_lane, last_lane = lane == 0, lane == lanes - 1
    inner = range(HALO, HALO + cz)

    def start(field):
        return lambda z: base(field, z)

    def kept(name, field):
        index = STAGE[name] + field
        return lambda z: stage[index, z]

    def x_next(of, z):
        value = pltpu.roll(of(z), lanes - 1, 1)
        if z == edge:
            return value
        return jnp.where(last_lane, pltpu.roll(of(edge), (lanes - 1 - (8 * z + 2)) % lanes, 1), value)

    def x_prev(of, z):
        value = pltpu.roll(of(z), 1, 1)
        if z == edge:
            return value
        return jnp.where(first_lane, pltpu.roll(of(edge), (lanes - (8 * z + 5)) % lanes, 1), value)

    def z_next(of, z):
        return pltpu.roll(of(edge), lanes - 8, 1) if z == edge else of(z + 1)

    def z_prev(of, z):
        return pltpu.roll(of(edge), 8, 1) if z == edge else of(z - 1)

    def velocity_rates(k, s, z, want):
        buoy = base(BUOY, z)
        sxx, syy, szz, sxy, sxz, syz = s
        out = {}
        if VX in want:
            xy = sxy(z)
            out[VX] = buoy * (
                (x_next(sxx, z) - sxx(z)) + (xy - before(k, 0, z, xy)) + (sxz(z) - z_prev(sxz, z))
            )
        if VY in want:
            yy = syy(z)
            out[VY] = buoy * (
                (sxy(z) - x_prev(sxy, z)) + (after(k, 1, z, yy) - yy) + (syz(z) - z_prev(syz, z))
            )
        if VZ in want:
            yz = syz(z)
            out[VZ] = buoy * (
                (sxz(z) - x_prev(sxz, z)) + (yz - before(k, 2, z, yz)) + (z_next(szz, z) - szz(z))
            )
        return out

    def stress_rates(k, v, z, want):
        lam, mu = base(LAM, z), base(MU, z)
        of_x, of_y, of_z = v
        vx, vy, vz = of_x(z), of_y(z), of_z(z)
        out = {}
        if SXX in want:
            exx = vx - x_prev(of_x, z)
            eyy = vy - before(k, 0, z, vy)
            ezz = vz - z_prev(of_z, z)
            common = lam * (exx + eyy + ezz)
            twice = 2.0 * mu
            out[SXX] = common + twice * exx
            out[SYY] = common + twice * eyy
            out[SZZ] = common + twice * ezz
        if SXY in want:
            out[SXY] = mu * ((after(k, 1, z, vx) - vx) + (x_next(of_y, z) - vy))
        if SXZ in want:
            out[SXZ] = mu * ((z_next(of_x, z) - vx) + (x_next(of_z, z) - vz))
            out[SYZ] = mu * ((z_next(of_y, z) - vy) + (after(k, 2, z, vz) - vz))
        return out

    def spread(ranges):
        for z in range(layers + 1):
            want = {f for f, (a, b) in ranges.items() if z == edge or a <= z < b}
            if want:
                yield z, want

    def velocity_step(k, name, v, s, sign, ranges):
        for z, want in spread(ranges):
            for f, rate in velocity_rates(k, s, z, want).items():
                stage[STAGE[name] + f, z] = v[f](z) + rate if sign > 0 else v[f](z) - rate
        return [kept(name, f) for f in (VX, VY, VZ)]

    def stress_step(k, name, v, s, sign, ranges, ahead=None, behind=None):
        for z, want in spread(ranges):
            for f, rate in stress_rates(k, v, z, want).items():
                value = s[f - SXX](z)
                if ahead is not None and f in NORMAL:
                    value = value + base(ahead, z)
                value = value + rate if sign > 0 else value - rate
                if behind is not None and f in NORMAL:
                    value = value + base(behind, z)
                stage[STAGE[name] + f - SXX, z] = value
        return [kept(name, f - SXX) for f in STRESS]

    def terms(f, a):
        term_lam = (f[0] + f[1] + f[2]) * (a[0] + a[1] + a[2])
        term_mu = f[0] * a[0] + f[1] * a[1] + f[2] * a[2] + 2.0 * (f[3] * a[3] + f[4] * a[4] + f[5] * a[5])
        return term_lam, term_mu

    n = layers
    fv, fs = [start(FWD + f) for f in (VX, VY, VZ)], [start(FWD + f) for f in STRESS]
    av, first = [start(ADJ + f) for f in (VX, VY, VZ)], [start(ADJ + f) for f in STRESS]
    a_s = stress_step(0, "as", av, first, -1, {SXX: (1, n), SXY: (0, n), SXZ: (0, n - 1)})
    fv = velocity_step(1, "fv", fv, fs, 1, {VX: (1, n), VY: (1, n), VZ: (0, n - 1)})
    fs = stress_step(2, "fs", fv, fs, 1, {SXX: (1, n - 1), SXY: (1, n - 1), SXZ: (1, n - 1)}, behind=SRC)
    fv = velocity_step(3, "fw", fv, fs, 1, {VX: (2, n - 1), VY: (2, n - 1), VZ: (1, n - 2)})
    for z in inner:
        rates = stress_rates(4, fv, z, set(STRESS))
        now = [of(z) for of in fs]
        later = [now[s - SXX] + rates[s] + (base(FIELDS, z) if s in NORMAL else 0.0) for s in STRESS]
        lam_late, mu_late = terms(later, [of(z) for of in first])
        with_traces = [of(z) + (base(INJ, z) if s in NORMAL else 0.0) for s, of in zip(STRESS, a_s)]
        lam_early, mu_early = terms(now, with_traces)
        put(9, z - HALO, lam_late + lam_early)
        put(10, z - HALO, mu_late + mu_early)
    av = velocity_step(5, "av", av, a_s, -1, {VX: (1, n - 1), VY: (1, n - 1), VZ: (1, n - 1)})
    a_s = stress_step(6, "at", av, a_s, -1, {SXX: (2, n - 1), SXY: (1, n - 1), SXZ: (1, n - 2)}, ahead=INJ)
    for s, of in zip(STRESS, a_s):
        for z in inner:
            put(s, z - HALO, of(z))
    for z in inner:
        rates = velocity_rates(7, a_s, z, {VX, VY, VZ})
        for f in (VX, VY, VZ):
            put(f, z - HALO, av[f](z) - rates[f])


def middle_kernel(cz, ring_f, ring_w, strips, own, edges, sides, middle, stage):
    cy, lanes = own.shape[2], own.shape[3]
    layers = cz + 2 * HALO

    def base(f, z):
        if f == FIELDS:
            return own[f - ADJ, z - HALO]
        if z == layers:
            return strips[f]
        return ring_f[f, z] if f < ADJ else ring_w[f - ADJ, z]

    row = lax.broadcasted_iota(jnp.int32, (cy, lanes), 0)
    for f in range(FIELDS + 1):
        for z in range(HALO, HALO + cz) if f == FIELDS else range(layers + 1):
            tile = base(f, z)
            tail, head = pltpu.roll(tile, HALO, 0), pltpu.roll(tile, cy - HALO, 0)
            edges[f, z] = jnp.where(row < HALO, tail, jnp.where(row >= cy - HALO, head, 0.0))

    def after(k, j, z, tile):
        sides[k, j, z] = pltpu.roll(tile, cy - 1 - HALO, 0)
        return pltpu.roll(tile, cy - 1, 0)

    def before(k, j, z, tile):
        sides[k, j, z] = pltpu.roll(tile, HALO + 1, 0)
        return pltpu.roll(tile, 1, 0)

    def put(i, z, value):
        middle[i, z] = value

    window(cz, base, stage, after, before, put)


def edge_kernel(
    cz, edges_in, sides, middle, y_a, y_b, final, image_lam, image_mu, edges, packed, stage, result, sems
):
    cy, lanes = middle.shape[2], middle.shape[3]

    def put_row(f, z, y, value):
        edges[f, z, y : y + 1, :] = value

    unpack_rows(cz, cy, (y_a, y_b), packed, put_row)
    row = lax.broadcasted_iota(jnp.int32, (cy, lanes), 0)

    def after(k, j, z, tile):
        return jnp.where(row == cy - 1, sides[k, j, z], pltpu.roll(tile, cy - 1, 0))

    def before(k, j, z, tile):
        return jnp.where(row == 0, sides[k, j, z], pltpu.roll(tile, 1, 0))

    moves = []

    def put(i, z, value):
        tail, head = pltpu.roll(value, HALO, 0), pltpu.roll(value, cy - HALO, 0)
        result[i, z] = jnp.where(row < HALO, tail, jnp.where(row >= cy - HALO, head, middle[i, z]))
        if z == cz - 1:
            if i == 10:
                moves.extend(copies(sems, (result.at[9], image_lam), (result.at[10], image_mu)))
            if i == SYZ:
                part = pl.ds(SXX, SYZ + 1 - SXX)
                moves.extend(copies(sems.at[pl.ds(2, 1)], (result.at[part], final.at[part])))
            if i == VZ:
                part = pl.ds(VX, VZ + 1 - VX)
                moves.extend(copies(sems.at[pl.ds(3, 1)], (result.at[part], final.at[part])))

    window(cz, lambda f, z: edges[f, z], stage, after, before, put)
    for move in moves:
        move.wait()


def swap_pairs(count, first):
    pairs = [(i + d, i + 1 - d) for i in range(first, count - 1, 2) for d in (0, 1)]
    return pairs + [(i, i) for i in range(count) if i not in dict(pairs)]


def swapped(value_a, value_b, axis):
    count = lax.axis_size(axis)
    got_a = lax.ppermute(value_a, axis, swap_pairs(count, 0))
    return got_a, None if value_b is None else lax.ppermute(value_b, axis, swap_pairs(count, 1))


def stay(value, spec):
    return pltpu.with_memory_space_constraint(value, pltpu.HBM) if spec.memory_space == pl.ANY else value


def kernel_call(body, args, in_specs, out_shape, scratch_shapes=(), aliases=None, out_specs=None):
    here = [a is not None for a in args]
    there = [o is not None for o in out_shape]

    def run(*refs):
        refs = iter(refs)
        full = [next(refs) if h else None for h in here + there]
        body(*full, *refs)

    out = iter(
        pl.pallas_call(
            run,
            out_shape=tuple(o for o in out_shape if o is not None),
            in_specs=[s for s, h in zip(in_specs, here) if h],
            out_specs=out_specs or tuple(vmem() for h in there if h),
            scratch_shapes=list(scratch_shapes),
            input_output_aliases=aliases or {},
            compiler_params=pltpu.CompilerParams(vmem_limit_bytes=VMEM_LIMIT),
        )(*[stay(a, s) for a, s in zip(args, in_specs) if a is not None])
    )
    return tuple(next(out) if h else None for h in there)


def on_device(
    checkpoint_store,
    holder_peer,
    holder_slot,
    adjoint_state,
    lame_lambda,
    lame_mu,
    buoyancy,
    source_cell,
    wavelet,
    receiver_cell,
    traces,
    plan,
):
    cz, cy, cx = lame_mu.shape
    layers = cz + 2 * HALO
    bf16, f32 = jnp.bfloat16, jnp.float32
    store = checkpoint_store.reshape(-1, cy, cx)
    tiles = store.shape[0]
    peer, slot = holder_peer[0, 0], holder_slot[0, 0]
    source, receiver = source_cell.reshape(1, -1), receiver_cell.reshape(1, -1)
    traces = traces.reshape(traces.shape[-2:])
    holders = lax.axis_size("gz")
    assert holders == 4
    near, far = face_counts(cz)
    face = 2 * near + far
    half = tiles // 2

    def shape(*dims, dtype=f32):
        return jax.ShapeDtypeStruct(dims, dtype)

    wide_x = lax.axis_size("gx") > 2
    chip = lax.ppermute(store, "gz", [(i, i ^ 2) for i in range(holders)])
    to_core, to_far, own, peer, slot = kernel_call(
        functools.partial(start_kernel, cz),
        (store, adjoint_state, lame_lambda, lame_mu, buoyancy, source, wavelet, receiver, traces, plan, peer, slot),
        [hbm()] * 12,
        (shape(tiles + face, cy, cx, dtype=bf16), shape(max(face, half) + PAD, cy, cx, dtype=bf16), shape(15, cz, cy, cx),
         shape(*peer.shape, dtype=jnp.int32), shape(*slot.shape, dtype=jnp.int32)),
        [
            pltpu.VMEM(receiver.shape, jnp.int32),
            pltpu.VMEM(traces.shape, f32),
            pltpu.SMEM(source.shape, jnp.int32),
            pltpu.SMEM(wavelet.shape, f32),
            pltpu.SMEM(plan.shape, jnp.int32),
            pltpu.SemaphoreType.DMA((12,)),
        ],
    )
    core = lax.ppermute(to_core, "gz", [(i, i ^ 1) for i in range(holders)])
    gy = lax.axis_size("gy")
    across = {
        (i, c): (i, 3 - c) if c in (1, 2) else (i ^ 1, c)
        for i in range(gy) for c in range(holders)
    }
    far_face = lax.ppermute(
        to_far, ("gy", "gz"), [(a[0] * holders + a[1], b[0] * holders + b[1]) for a, b in across.items()]
    )
    both = [lax.ppermute(part, "gz", [(i, i ^ 1) for i in range(holders)]) for part in (chip[:half], chip[half:])]

    (ring_w,) = kernel_call(
        functools.partial(frame_kernel, cz), (own,), [vmem()], (shape(FIELDS - ADJ, layers + 1, cy, cx),)
    )
    x_send = shape(x_tiles(), cy, cx, dtype=bf16)
    ring_f, ring_w, x_a, x_b = kernel_call(
        functools.partial(column_kernel, cz),
        (to_core, core, chip, *both, far_face, peer, slot, ring_w),
        [vmem()] * 9,
        (shape(ADJ, layers + 1, cy, cx), shape(*ring_w.shape), x_send, x_send if wide_x else None),
        [
            pltpu.SMEM(peer.shape, jnp.int32),
            pltpu.SMEM(slot.shape, jnp.int32),
            pltpu.SemaphoreType.DMA((2,)),
        ],
        {8: 1},
    )
    axes = ("gx", "gy", "gz")
    gx = lax.axis_size("gx")

    def partner(i, j, c, x_turn, y_turn):
        if x_turn is not None:
            i = dict(swap_pairs(gx, x_turn))[i]
        if y_turn is not None:
            other = dict(swap_pairs(gy, (c + y_turn) % 2))[j]
            j, c = (j, c ^ 2) if other == j else (other, c)
        return (i * gy + j) * holders + c

    def swap(value, x_turn, y_turn):
        if value is None:
            return None
        pairs = [
            ((i * gy + j) * holders + c, partner(i, j, c, x_turn, y_turn))
            for i in range(gx) for j in range(gy) for c in range(holders)
        ]
        return lax.ppermute(value, axes, pairs)

    strip_tiles, tiles = row_tiles(cz, cy)
    y_send = shape(strip_tiles + tiles, cy, cx, dtype=bf16)
    scratch_tiles = max(sum(row_counts(cz, cy, up)) for up in (True, False))
    y_a, y_b = kernel_call(
        functools.partial(layer_rows_kernel, cz),
        (ring_f, ring_w),
        [vmem()] * 2,
        (y_send, y_send),
        [pltpu.VMEM((2, scratch_tiles, 8, cx), f32)],
    )
    strips, y_a, y_b = kernel_call(
        functools.partial(strip_rows_kernel, cz),
        (ring_f, ring_w, swap(x_a, 0, None), swap(x_b, 1, None), y_a, y_b),
        [vmem()] * 6,
        (shape(FIELDS, cy, cx), y_send, y_send),
        [pltpu.VMEM((2, strip_tiles, 8, cx), f32)],
        {4 if wide_x else 3: 1, 5 if wide_x else 4: 2},
    )
    edges, sides, middle = kernel_call(
        functools.partial(middle_kernel, cz),
        (ring_f, ring_w, strips, own),
        [vmem()] * 4,
        (
            shape(FIELDS + 1, layers + 1, cy, cx),
            shape(8, 3, layers + 1, cy, cx),
            shape(11, cz, cy, cx),
        ),
        [pltpu.VMEM((STAGES, layers + 1, cy, cx), f32)],
    )
    result = kernel_call(
        functools.partial(edge_kernel, cz),
        (edges, sides, middle, swap(y_a, None, 0), swap(y_b, None, 1)),
        [vmem()] * 5,
        (shape(9, cz, cy, cx), shape(cz, cy, cx), shape(cz, cy, cx), shape(*edges.shape)),
        [
            pltpu.VMEM((2, scratch_tiles, 8, cx), f32),
            pltpu.VMEM((STAGES, layers + 1, cy, cx), f32),
            pltpu.VMEM((11, cz, cy, cx), f32),
            pltpu.SemaphoreType.DMA((4,)),
        ],
        {0: 3},
        (hbm(),) * 3 + (vmem(),),
    )
    return result[:3]


def solution(mesh):
    return jax.shard_map(
        on_device,
        mesh=mesh,
        in_specs=(
            P("gz", None, None, "gy", "gx"),
            P("gx", "gy", None, None),
            P("gx", "gy", None, None),
            P(None, "gz", "gy", "gx"),
            P("gz", "gy", "gx"),
            P("gz", "gy", "gx"),
            P("gz", "gy", "gx"),
            P("gz", "gy", "gx", None),
            P(),
            P("gz", "gy", "gx", None),
            P("gz", "gy", "gx", None, None),
            P(),
        ),
        out_specs=(P(None, "gz", "gy", "gx"), P("gz", "gy", "gx"), P("gz", "gy", "gx")),
        check_vma=False,
    )
```

```python
import functools

import jax
import jax.numpy as jnp
from jax import lax
from jax.experimental import pallas as pl
from jax.experimental.pallas import tpu as pltpu
from jax.sharding import PartitionSpec as P

VX, VY, VZ, SXX, SYY, SZZ, SXY, SXZ, SYZ = range(9)
FWD, ADJ, BUOY, LAM, MU, INJ, SRC = 0, 9, 18, 19, 20, 21, 22
FIELDS = 23
HALO = 2

ADJ_Z = {VX: (2, 2), VY: (2, 2), VZ: (2, 2), SXX: (1, 1), SYY: (1, 1), SZZ: (1, 2), SXY: (1, 1), SXZ: (2, 1), SYZ: (2, 1)}
OTHER_Z = {BUOY: (2, 2), LAM: (1, 2), MU: (2, 2), INJ: (0, 1), SRC: (1, 1)}
F32_Z = {**{ADJ + f: c for f, c in ADJ_Z.items()}, **OTHER_Z}

Y_ROWS = {
    FWD + VX: (None, (2, -1, 1), (1, -1, 1), (2, -2, 0)),
    FWD + VY: ((2, -2, 0), (1, -1, 1), (2, -1, 1), None),
    FWD + VZ: (None, (1, -2, 1), (1, -1, 1), (2, -2, 0)),
    FWD + SXX: (None, (2, -1, 1), (1, -1, 1), (2, -2, 1)),
    FWD + SYY: ((2, -2, 0), (1, -1, 1), (1, 0, 1), (2, -1, 1)),
    FWD + SZZ: (None, (1, -1, 1), (1, 0, 1), (2, -1, 0)),
    FWD + SXY: ((2, -1, 1), (1, 0, 1), (1, -1, 1), (2, -2, 0)),
    FWD + SXZ: (None, (1, -1, 1), (0, -1, 1), (1, -2, 1)),
    FWD + SYZ: ((1, -2, 1), (0, -1, 1), (1, -1, 1), (2, -2, 0)),
    ADJ + VX: ((2, -2, 0), (1, -1, 1), (1, -1, 1), (2, -2, 1)),
    ADJ + VY: ((2, -1, 1), (1, 0, 1), (1, -1, 1), (2, -2, 0)),
    ADJ + VZ: ((2, -2, 0), (1, -1, 1), (0, -1, 1), (1, -2, 0)),
    ADJ + SXX: (None, (2, -2, 1), (2, -2, 1), None),
    ADJ + SYY: (None, (2, -1, 1), (1, -1, 1), (2, -2, 0)),
    ADJ + SZZ: (None, (2, -1, 0), (1, -1, 0), None),
    ADJ + SXY: ((2, -2, 0), (1, -1, 1), (2, -2, 1), None),
    ADJ + SXZ: (None, (1, -2, 1), (1, -2, 1), None),
    ADJ + SYZ: ((2, -2, 0), (1, -1, 1), (1, -2, 0), None),
    BUOY: ((2, -2, 0), (1, -1, 1), (1, -1, 1), (2, -2, 0)),
    LAM: (None, (2, -1, 1), (1, -1, 1), (2, -2, 0)),
    MU: ((2, -2, 0), (1, -1, 1), (1, -1, 1), (2, -2, 0)),
    INJ: (None, None, (2, -2, 0), None),
    SRC: (None, (2, -2, 0), (2, -1, 1), None),
}

EXACT_ROWS = {-1: (ADJ + VY, ADJ + SXY, ADJ + SYZ, BUOY, SRC), 0: (ADJ + SYY, LAM, INJ, SRC)}

PAD = 1
VMEM_LIMIT = 48 * 1024 * 1024


def vmem():
    return pl.BlockSpec(memory_space=pltpu.VMEM)


def hbm():
    return pl.BlockSpec(memory_space=pl.ANY)


def faces(cz, up):
    near, far = [], []
    for f in sorted(F32_Z):
        before, after = F32_Z[f]
        depth = before if up else after
        for d in range(depth):
            layer = cz - 1 - d if up else d
            (far if d else near).append((f, layer, HALO - 1 - d if up else HALO + cz + d))
    return near, far


def face_counts(cz):
    sides = [faces(cz, up) for up in (True, False)]
    return max(len(s[0]) for s in sides), max(len(s[1]) for s in sides)


def y_rows(cz, cy, up):
    layers = cz + 2 * HALO
    narrow, wide, strip = [], [], []
    for f in sorted(Y_ROWS):
        for offset in (-1, -2) if up else (0, 1):
            spec = Y_ROWS[f][offset + HALO]
            if spec is None:
                continue
            source = cy + offset if up else offset
            target = cy - HALO + offset if up else HALO + offset
            exact = f in EXACT_ROWS.get(offset, ())
            (wide if exact else narrow).extend((f, z, source, target) for z in range(spec[0], layers + spec[1]))
            if spec[2]:
                strip.append((f, layers, source, target))
    return narrow, wide, strip


def row_counts(cz, cy, up):
    return tuple(-(-len(rows) // 8) for rows in y_rows(cz, cy, up))


def row_tiles(cz, cy):
    sides = [row_counts(cz, cy, up) for up in (True, False)]
    return max(c for _, _, c in sides), max(n + 2 * w for n, w, _ in sides)


def split(value):
    high = value.astype(jnp.bfloat16)
    low = (value - high.astype(jnp.float32)).astype(jnp.bfloat16)
    return high, low


def joined(high, low):
    return high.astype(jnp.float32) + low.astype(jnp.float32)


def even_mask(axes, shape):
    total = sum(lax.axis_index(a) for a in ((axes,) if isinstance(axes, str) else axes))
    return jnp.full(shape, lax.rem(total, 2), jnp.int32) == 0


def has_neighbours(axis):
    index = lax.axis_index(axis)
    return (index > 0).astype(jnp.float32), (index < lax.axis_size(axis) - 1).astype(jnp.float32)


def copies(sems, *pairs):
    out = [pltpu.make_async_copy(source, target, sems.at[i]) for i, (source, target) in enumerate(pairs)]
    for copy in out:
        copy.start()
    return out


def scatter_rows(packed, listed, row_of):
    for r, (f, z, y, _) in enumerate(listed):
        packed[r // 8, r % 8 : r % 8 + 1, :] = row_of(f, z, y)


def pack_tiles(sides, sends, first, count):
    even = even_mask(("gy", "gz"), sends[0].shape[1:])
    for t in range(count):
        up, down = (side[min(t, len(side) - 1)] for side in sides)
        sends[0][first + t] = jnp.where(even, up, down).astype(jnp.bfloat16)
        sends[1][first + t] = jnp.where(even, down, up).astype(jnp.bfloat16)


def layer_rows_kernel(cz, ring_f, ring_w, send_a, send_b, packed):
    cy = ring_f.shape[2]
    strip_tiles, tiles = row_tiles(cz, cy)

    def row_of(f, z, y):
        return ring_f[f, z, y : y + 1, :] if f < ADJ else ring_w[f - ADJ, z, y : y + 1, :]

    sides = []
    for side, up in enumerate((True, False)):
        narrow, wide, _ = y_rows(cz, cy, up)
        n, w, _ = row_counts(cz, cy, up)
        scatter_rows(packed.at[side], narrow, row_of)
        scatter_rows(packed.at[side, pl.ds(n, w)], wide, row_of)
        rest = [split(packed[side, n + t])[1].astype(jnp.float32) for t in range(w)]
        sides.append([packed[side, t] for t in range(n + w)] + rest)
    pack_tiles(sides, (send_a, send_b), strip_tiles, tiles)


def unpack_rows(cz, cy, first, message, packed, edges):
    has_lower, has_upper = has_neighbours("gy")
    strip_tiles, _ = row_tiles(cz, cy)
    parity = lax.rem(lax.axis_index("gy") + lax.axis_index("gz"), 2)

    def side(up, keep):
        narrow, wide, strip = y_rows(cz, cy, up)
        n, w, c = row_counts(cz, cy, up)
        for t in range(n + w):
            value = message[strip_tiles + t].astype(jnp.float32)
            if t >= n:
                value = value + message[strip_tiles + w + t].astype(jnp.float32)
            packed[t] = value * keep
        for t in range(c):
            packed[n + w + t] = message[t].astype(jnp.float32) * keep
        for base, listed in ((0, narrow), (n, wide), (n + w, strip)):
            for r, (f, z, _, y) in enumerate(listed):
                edges[f, z, y : y + 1, :] = packed[base + r // 8, r % 8 : r % 8 + 1, :]

    @pl.when(parity == (1 if first else 0))
    def _():
        side(True, has_lower)

    @pl.when(parity == (0 if first else 1))
    def _():
        side(False, has_upper)


def first_rows_kernel(cz, message, edges_in, edges, packed):
    unpack_rows(cz, edges.shape[2], True, message, packed, edges)


def start_kernel(
    cz, store, adjoint, lam, mu, buoy, source, wavelet, receiver, traces, plan, peer, slot,
    near_out, far_out, own, peer_out, slot_out, cells, samples, spots, wave, steps, sems,
):
    cy, lanes = own.shape[2], own.shape[3]
    rows = cz * cy
    tiles = store.shape[0]
    small = copies(sems, (plan, steps), (wavelet, wave), (source, spots), (receiver, cells), (traces, samples))
    large = copies(
        sems.at[pl.ds(len(small), 7)],
        (adjoint, own.at[pl.ds(0, 9)]),
        (buoy, own.at[BUOY - ADJ]),
        (lam, own.at[LAM - ADJ]),
        (mu, own.at[MU - ADJ]),
        (store, near_out.at[pl.ds(0, tiles)]),
        (peer, peer_out),
        (slot, slot_out),
    )
    for copy in small:
        copy.wait()
    listed = cells[...]
    count = listed.shape[1]
    row_hot = (lax.broadcasted_iota(jnp.int32, (rows, count), 0) == listed // lanes).astype(jnp.float32)
    lane_hit = lax.broadcasted_iota(jnp.int32, (lanes, count), 0) == listed % lanes
    injected = []
    for step in (1, 0):
        sample = samples[pl.ds(steps[step], 1), :]
        field = lax.dot_general(
            row_hot,
            jnp.where(lane_hit, sample, 0.0),
            (((1,), (1,)), ((), ())),
            precision=lax.Precision.HIGHEST,
            preferred_element_type=jnp.float32,
        )
        injected.append(field.reshape(cz, cy, lanes))
    own[INJ - ADJ] = injected[1]
    flat = lax.broadcasted_iota(jnp.int32, (rows, lanes), 0) * lanes + lax.broadcasted_iota(jnp.int32, (rows, lanes), 1)
    for step in range(2):
        value = wave[steps[step]]
        field = jnp.zeros((rows, lanes), jnp.float32)
        for j in range(source.shape[1]):
            field = field + jnp.where(flat == spots[0, j], value, 0.0)
        own[SRC - ADJ + step] = field.reshape(cz, cy, lanes)
    for copy in large:
        copy.wait()
    for f in (SXX, SYY, SZZ):
        own[f] = own[f] + injected[0]

    even = even_mask("gz", (cy, lanes))
    near, far = face_counts(cz)
    up, down = faces(cz, True), faces(cz, False)
    zero = jnp.zeros((cy, lanes), jnp.float32)

    def tile(side, i):
        return own[side[i][0] - ADJ, side[i][1]] if i < len(side) else zero

    for i in range(near):
        above, below = tile(up[0], i), tile(down[0], i)
        for out, base, value in (
            (near_out, tiles, jnp.where(even, above, below)),
            (far_out, 0, jnp.where(even, below, above)),
        ):
            out[base + i], out[base + near + i] = split(value)
    for i in range(far):
        above, below = tile(up[1], i), tile(down[1], i)
        near_out[tiles + 2 * near + i] = jnp.where(even, above, below).astype(jnp.bfloat16)
        far_out[2 * near + i] = jnp.where(even, below, above).astype(jnp.bfloat16)
    for i in range(2 * near + far, far_out.shape[0]):
        far_out[i] = zero.astype(jnp.bfloat16)


def strip_part(tile, main, listed):
    lanes = tile.shape[1]
    lane = lax.broadcasted_iota(jnp.int32, tile.shape, 1)
    for z in listed:
        tile = jnp.where((lane >= 8 * z) & (lane < 8 * z + 4), pltpu.roll(main(z), (8 * z + 2) % lanes, 1), tile)
    return tile


def strip_whole(tile):
    position = lax.broadcasted_iota(jnp.int32, tile.shape, 1) % 8
    return jnp.where(position < 2, tile, jnp.where(position >= 6, pltpu.roll(tile, 4, 1), 0.0))


def frame_kernel(cz, own, ring):
    cy, lanes = own.shape[2], own.shape[3]
    layers = cz + 2 * HALO
    zero = jnp.zeros((cy, lanes), jnp.float32)
    filled = {(f - ADJ, z) for up in (True, False) for listed in faces(cz, up) for f, _, z in listed}
    for f in range(ring.shape[0]):
        for z in range(cz):
            ring[f, HALO + z] = own[f, z]
        for z in (0, 1, layers - 2, layers - 1):
            if (f, z) not in filled:
                ring[f, z] = zero
        ring[f, layers] = strip_part(zero, lambda z: own[f, z - HALO], range(HALO, HALO + cz))


def column_kernel(
    cz, mine, core, chip, both_a, both_b, far, peer, slot, ring_w_in,
    ring_f, ring, x_a, x_b, peers, slots, sems,
):
    cy, lanes = chip.shape[1], chip.shape[2]
    layers = cz + 2 * HALO
    tiles = chip.shape[0]
    half = both_a.shape[0]
    me = lax.axis_index("gz")
    count = lax.axis_size("gz")
    moves = copies(sems, (peer, peers), (slot, slots))
    near, _ = face_counts(cz)
    even = even_mask("gz", (cy, lanes))
    has_below, has_above = has_neighbours("gz")
    zero = jnp.zeros((cy, lanes), jnp.float32)
    filled = {}
    for up in (True, False):
        for depth, listed in enumerate(faces(cz, up)):
            for i, (f, _, z) in enumerate(listed):
                values = []
                for ref, base in ((core, tiles), (far, 0)):
                    if depth == 0:
                        values.append(joined(ref[base + i], ref[base + near + i]))
                    else:
                        values.append(ref[base + 2 * near + i].astype(jnp.float32))
                value = jnp.where(even, values[1], values[0]) if up else jnp.where(even, values[0], values[1])
                value = value * (has_below if up else has_above)
                ring[f - ADJ, z] = value
                filled.setdefault(f - ADJ, {})[z] = value
    strip = []
    for f in range(ring.shape[0]):
        there = filled.get(f, {})
        tile = strip_whole(strip_part(ring[f, layers], lambda z: there[z], sorted(there)))
        ring[f, layers] = tile
        strip.append(tile)
    for move in moves:
        move.wait()
    below, above = jnp.maximum(me - 1, 0), jnp.minimum(me + 1, count - 1)
    for z in range(layers):
        if z < HALO:
            brick, piece, keep = below, cz - HALO + z, has_below
        elif z < HALO + cz:
            brick, piece, keep = me, z - HALO, None
        else:
            brick, piece, keep = above, z - HALO - cz, has_above
        row = slots[brick, piece] * 9
        hops = jnp.full((cy, lanes), peers[brick, piece] ^ me, jnp.int32)
        late = jnp.full((cy, lanes), row, jnp.int32) >= half
        row_a, row_b = jnp.minimum(row, half - 9), jnp.maximum(row - half, 0)
        for f in range(9):
            parts = (mine[row + f], core[row + f], chip[row + f], both_a[row_a + f], both_b[row_b + f])
            parts = [part.astype(jnp.float32) for part in parts]
            value = jnp.where(late, parts[4], parts[3])
            value = jnp.where(hops < 2, jnp.where(hops == 1, parts[1], parts[0]), jnp.where(hops == 2, parts[2], value))
            ring_f[f, z] = value if keep is None else value * keep
    for f in range(9):
        ring_f[f, layers] = strip_whole(strip_part(zero, lambda z: ring_f[f, z], range(layers)))
    strip = [ring_f[f, layers] for f in range(9)] + strip
    position = lax.broadcasted_iota(jnp.int32, (cy, lanes), 1) % 8
    even_x = even_mask("gx", (cy, lanes))
    for out, tail_from_even in ((x_a, True), (x_b, False)):
        if out is None:
            continue
        place = 0
        for fields, narrow in ((range(ADJ), True), (range(ADJ, FIELDS), False)):
            quads = [fields[i : i + 4] for i in range(0, len(fields), 4)]
            for i, quad in enumerate(quads):
                tile = zero
                for g, f in enumerate(quad):
                    tail, head = strip[f], pltpu.roll(strip[f], lanes - 6, 1)
                    value = jnp.where(even_x, tail, head) if tail_from_even else jnp.where(even_x, head, tail)
                    value = value if g == 0 else pltpu.roll(value, 2 * g, 1)
                    tile = jnp.where(position // 2 == g, value, tile)
                high, low = split(tile)
                out[place + i] = high
                if not narrow:
                    out[place + len(quads) + i] = low
            place += len(quads) if narrow else 2 * len(quads)


def x_tiles():
    return -(-ADJ // 4) + 2 * -(-(FIELDS - ADJ) // 4)


def strip_rows_kernel(cz, ring_f, ring_w, x_a, x_b, y_a_in, y_b_in, strips, y_a, y_b, packed):
    cy, lanes = strips.shape[1], strips.shape[2]
    layers = cz + 2 * HALO
    pair = lax.broadcasted_iota(jnp.int32, (cy, lanes), 1) % 8 // 2
    even_x = even_mask("gx", (cy, lanes))
    has_left, has_right = has_neighbours("gx")
    zero = jnp.zeros((cy, lanes), jnp.float32)
    place = 0
    for fields, narrow in ((range(ADJ), True), (range(ADJ, FIELDS), False)):
        quads = [fields[i : i + 4] for i in range(0, len(fields), 4)]
        for i, quad in enumerate(quads):
            got = []
            for ref in (x_a, x_b):
                if ref is None:
                    got.append(zero)
                elif narrow:
                    got.append(ref[place + i].astype(jnp.float32))
                else:
                    got.append(joined(ref[place + i], ref[place + len(quads) + i]))
            right = jnp.where(even_x, got[0], got[1]) * has_right
            left = jnp.where(even_x, got[1], got[0]) * has_left
            for g, f in enumerate(quad):
                strip = ring_f[f, layers] if f < ADJ else ring_w[f - ADJ, layers]
                tile = jnp.where(pair == 1, pltpu.roll(right, (2 - 2 * g) % lanes, 1), strip)
                strips[f] = jnp.where(pair == 2, pltpu.roll(left, (4 - 2 * g) % lanes, 1), tile)
        place += len(quads) if narrow else 2 * len(quads)
    sides = []
    for side, up in enumerate((True, False)):
        scatter_rows(packed.at[side], y_rows(cz, cy, up)[2], lambda f, z, y: strips[f, y : y + 1, :])
        sides.append([packed[side, t] for t in range(row_counts(cz, cy, up)[2])])
    pack_tiles(sides, (y_a, y_b), 0, packed.shape[1])


STAGE = {"fv": 0, "fs": 3, "fw": 9, "as": 12, "av": 18, "at": 21}
STAGES = 27
NORMAL = (SXX, SYY, SZZ)
STRESS = range(SXX, SYZ + 1)


def window(cz, base, stage, after, before, put):
    layers = cz + 2 * HALO
    edge = layers
    cy, lanes = stage.shape[2], stage.shape[3]
    lane = lax.broadcasted_iota(jnp.int32, (cy, lanes), 1)
    first_lane, last_lane = lane == 0, lane == lanes - 1
    inner = range(HALO, HALO + cz)

    def start(field):
        return lambda z: base(field, z)

    def kept(name, field):
        index = STAGE[name] + field
        return lambda z: stage[index, z]

    def x_next(of, z):
        value = pltpu.roll(of(z), lanes - 1, 1)
        if z == edge:
            return value
        return jnp.where(last_lane, pltpu.roll(of(edge), (lanes - 1 - (8 * z + 2)) % lanes, 1), value)

    def x_prev(of, z):
        value = pltpu.roll(of(z), 1, 1)
        if z == edge:
            return value
        return jnp.where(first_lane, pltpu.roll(of(edge), (lanes - (8 * z + 5)) % lanes, 1), value)

    def z_next(of, z):
        return pltpu.roll(of(edge), lanes - 8, 1) if z == edge else of(z + 1)

    def z_prev(of, z):
        return pltpu.roll(of(edge), 8, 1) if z == edge else of(z - 1)

    def velocity_rates(k, s, z, want):
        buoy = base(BUOY, z)
        sxx, syy, szz, sxy, sxz, syz = s
        out = {}
        if VX in want:
            xy = sxy(z)
            out[VX] = buoy * (
                (x_next(sxx, z) - sxx(z)) + (xy - before(k, 0, z, xy)) + (sxz(z) - z_prev(sxz, z))
            )
        if VY in want:
            yy = syy(z)
            out[VY] = buoy * (
                (sxy(z) - x_prev(sxy, z)) + (after(k, 1, z, yy) - yy) + (syz(z) - z_prev(syz, z))
            )
        if VZ in want:
            yz = syz(z)
            out[VZ] = buoy * (
                (sxz(z) - x_prev(sxz, z)) + (yz - before(k, 2, z, yz)) + (z_next(szz, z) - szz(z))
            )
        return out

    def stress_rates(k, v, z, want):
        lam, mu = base(LAM, z), base(MU, z)
        of_x, of_y, of_z = v
        vx, vy, vz = of_x(z), of_y(z), of_z(z)
        out = {}
        if SXX in want:
            exx = vx - x_prev(of_x, z)
            eyy = vy - before(k, 0, z, vy)
            ezz = vz - z_prev(of_z, z)
            common = lam * (exx + eyy + ezz)
            twice = 2.0 * mu
            out[SXX] = common + twice * exx
            out[SYY] = common + twice * eyy
            out[SZZ] = common + twice * ezz
        if SXY in want:
            out[SXY] = mu * ((after(k, 1, z, vx) - vx) + (x_next(of_y, z) - vy))
        if SXZ in want:
            out[SXZ] = mu * ((z_next(of_x, z) - vx) + (x_next(of_z, z) - vz))
            out[SYZ] = mu * ((z_next(of_y, z) - vy) + (after(k, 2, z, vz) - vz))
        return out

    def spread(ranges):
        for z in range(layers + 1):
            want = {f for f, (a, b) in ranges.items() if z == edge or a <= z < b}
            if want:
                yield z, want

    def velocity_step(k, name, v, s, sign, ranges):
        for z, want in spread(ranges):
            for f, rate in velocity_rates(k, s, z, want).items():
                stage[STAGE[name] + f, z] = v[f](z) + rate if sign > 0 else v[f](z) - rate
        return [kept(name, f) for f in (VX, VY, VZ)]

    def stress_step(k, name, v, s, sign, ranges, ahead=None, behind=None):
        for z, want in spread(ranges):
            for f, rate in stress_rates(k, v, z, want).items():
                value = s[f - SXX](z)
                if ahead is not None and f in NORMAL:
                    value = value + base(ahead, z)
                value = value + rate if sign > 0 else value - rate
                if behind is not None and f in NORMAL:
                    value = value + base(behind, z)
                stage[STAGE[name] + f - SXX, z] = value
        return [kept(name, f - SXX) for f in STRESS]

    def terms(f, a):
        term_lam = (f[0] + f[1] + f[2]) * (a[0] + a[1] + a[2])
        term_mu = f[0] * a[0] + f[1] * a[1] + f[2] * a[2] + 2.0 * (f[3] * a[3] + f[4] * a[4] + f[5] * a[5])
        return term_lam, term_mu

    n = layers
    fv, fs = [start(FWD + f) for f in (VX, VY, VZ)], [start(FWD + f) for f in STRESS]
    av, first = [start(ADJ + f) for f in (VX, VY, VZ)], [start(ADJ + f) for f in STRESS]
    a_s = stress_step(0, "as", av, first, -1, {SXX: (1, n), SXY: (0, n), SXZ: (0, n - 1)})
    fv = velocity_step(1, "fv", fv, fs, 1, {VX: (1, n), VY: (1, n), VZ: (0, n - 1)})
    fs = stress_step(2, "fs", fv, fs, 1, {SXX: (1, n - 1), SXY: (1, n - 1), SXZ: (1, n - 1)}, behind=SRC)
    fv = velocity_step(3, "fw", fv, fs, 1, {VX: (2, n - 1), VY: (2, n - 1), VZ: (1, n - 2)})
    for z in inner:
        rates = stress_rates(4, fv, z, set(STRESS))
        now = [of(z) for of in fs]
        later = [now[s - SXX] + rates[s] + (base(FIELDS, z) if s in NORMAL else 0.0) for s in STRESS]
        lam_late, mu_late = terms(later, [of(z) for of in first])
        with_traces = [of(z) + (base(INJ, z) if s in NORMAL else 0.0) for s, of in zip(STRESS, a_s)]
        lam_early, mu_early = terms(now, with_traces)
        put(9, z - HALO, lam_late + lam_early)
        put(10, z - HALO, mu_late + mu_early)
    av = velocity_step(5, "av", av, a_s, -1, {VX: (1, n - 1), VY: (1, n - 1), VZ: (1, n - 1)})
    a_s = stress_step(6, "at", av, a_s, -1, {SXX: (2, n - 1), SXY: (1, n - 1), SXZ: (1, n - 2)}, ahead=INJ)
    for s, of in zip(STRESS, a_s):
        for z in inner:
            put(s, z - HALO, of(z))
    for z in inner:
        rates = velocity_rates(7, a_s, z, {VX, VY, VZ})
        for f in (VX, VY, VZ):
            put(f, z - HALO, av[f](z) - rates[f])


def middle_kernel(cz, ring_f, ring_w, strips, own, edges, sides, middle, stage):
    cy, lanes = own.shape[2], own.shape[3]
    layers = cz + 2 * HALO

    def base(f, z):
        if f == FIELDS:
            return own[f - ADJ, z - HALO]
        if z == layers:
            return strips[f]
        return ring_f[f, z] if f < ADJ else ring_w[f - ADJ, z]

    row = lax.broadcasted_iota(jnp.int32, (cy, lanes), 0)
    for f in range(FIELDS + 1):
        for z in range(HALO, HALO + cz) if f == FIELDS else range(layers + 1):
            tile = base(f, z)
            tail, head = pltpu.roll(tile, HALO, 0), pltpu.roll(tile, cy - HALO, 0)
            edges[f, z] = jnp.where(row < HALO, tail, jnp.where(row >= cy - HALO, head, 0.0))

    def after(k, j, z, tile):
        sides[k, j, z] = pltpu.roll(tile, cy - 1 - HALO, 0)
        return pltpu.roll(tile, cy - 1, 0)

    def before(k, j, z, tile):
        sides[k, j, z] = pltpu.roll(tile, HALO + 1, 0)
        return pltpu.roll(tile, 1, 0)

    def put(i, z, value):
        middle[i, z] = value

    window(cz, base, stage, after, before, put)


def edge_kernel(
    cz, edges_in, sides, middle, message, final, image_lam, image_mu, edges, packed, stage, result, sems
):
    cy, lanes = middle.shape[2], middle.shape[3]

    unpack_rows(cz, cy, False, message, packed, edges)
    row = lax.broadcasted_iota(jnp.int32, (cy, lanes), 0)

    def after(k, j, z, tile):
        return jnp.where(row == cy - 1, sides[k, j, z], pltpu.roll(tile, cy - 1, 0))

    def before(k, j, z, tile):
        return jnp.where(row == 0, sides[k, j, z], pltpu.roll(tile, 1, 0))

    moves = []

    def put(i, z, value):
        tail, head = pltpu.roll(value, HALO, 0), pltpu.roll(value, cy - HALO, 0)
        result[i, z] = jnp.where(row < HALO, tail, jnp.where(row >= cy - HALO, head, middle[i, z]))
        if z == cz - 1:
            if i == 10:
                moves.extend(copies(sems, (result.at[9], image_lam), (result.at[10], image_mu)))
            if i == SYZ:
                part = pl.ds(SXX, SYZ + 1 - SXX)
                moves.extend(copies(sems.at[pl.ds(2, 1)], (result.at[part], final.at[part])))
            if i == VZ:
                part = pl.ds(VX, VZ + 1 - VX)
                moves.extend(copies(sems.at[pl.ds(3, 1)], (result.at[part], final.at[part])))

    window(cz, lambda f, z: edges[f, z], stage, after, before, put)
    for move in moves:
        move.wait()


def swap_pairs(count, first):
    pairs = [(i + d, i + 1 - d) for i in range(first, count - 1, 2) for d in (0, 1)]
    return pairs + [(i, i) for i in range(count) if i not in dict(pairs)]


def swapped(value_a, value_b, axis):
    count = lax.axis_size(axis)
    got_a = lax.ppermute(value_a, axis, swap_pairs(count, 0))
    return got_a, None if value_b is None else lax.ppermute(value_b, axis, swap_pairs(count, 1))


def stay(value, spec):
    return pltpu.with_memory_space_constraint(value, pltpu.HBM) if spec.memory_space == pl.ANY else value


def kernel_call(body, args, in_specs, out_shape, scratch_shapes=(), aliases=None, out_specs=None):
    here = [a is not None for a in args]
    there = [o is not None for o in out_shape]

    def run(*refs):
        refs = iter(refs)
        full = [next(refs) if h else None for h in here + there]
        body(*full, *refs)

    out = iter(
        pl.pallas_call(
            run,
            out_shape=tuple(o for o in out_shape if o is not None),
            in_specs=[s for s, h in zip(in_specs, here) if h],
            out_specs=out_specs or tuple(vmem() for h in there if h),
            scratch_shapes=list(scratch_shapes),
            input_output_aliases=aliases or {},
            compiler_params=pltpu.CompilerParams(vmem_limit_bytes=VMEM_LIMIT),
        )(*[stay(a, s) for a, s in zip(args, in_specs) if a is not None])
    )
    return tuple(next(out) if h else None for h in there)


def on_device(
    checkpoint_store,
    holder_peer,
    holder_slot,
    adjoint_state,
    lame_lambda,
    lame_mu,
    buoyancy,
    source_cell,
    wavelet,
    receiver_cell,
    traces,
    plan,
):
    cz, cy, cx = lame_mu.shape
    layers = cz + 2 * HALO
    bf16, f32 = jnp.bfloat16, jnp.float32
    store = checkpoint_store.reshape(-1, cy, cx)
    tiles = store.shape[0]
    peer, slot = holder_peer[0, 0], holder_slot[0, 0]
    source, receiver = source_cell.reshape(1, -1), receiver_cell.reshape(1, -1)
    traces = traces.reshape(traces.shape[-2:])
    holders = lax.axis_size("gz")
    assert holders == 4
    near, far = face_counts(cz)
    face = 2 * near + far
    half = tiles // 2

    def shape(*dims, dtype=f32):
        return jax.ShapeDtypeStruct(dims, dtype)

    wide_x = lax.axis_size("gx") > 2
    chip = lax.ppermute(store, "gz", [(i, i ^ 2) for i in range(holders)])
    to_core, to_far, own, peer, slot = kernel_call(
        functools.partial(start_kernel, cz),
        (store, adjoint_state, lame_lambda, lame_mu, buoyancy, source, wavelet, receiver, traces, plan, peer, slot),
        [hbm()] * 12,
        (shape(tiles + face, cy, cx, dtype=bf16), shape(max(face, half) + PAD, cy, cx, dtype=bf16), shape(15, cz, cy, cx),
         shape(*peer.shape, dtype=jnp.int32), shape(*slot.shape, dtype=jnp.int32)),
        [
            pltpu.VMEM(receiver.shape, jnp.int32),
            pltpu.VMEM(traces.shape, f32),
            pltpu.SMEM(source.shape, jnp.int32),
            pltpu.SMEM(wavelet.shape, f32),
            pltpu.SMEM(plan.shape, jnp.int32),
            pltpu.SemaphoreType.DMA((12,)),
        ],
    )
    core = lax.ppermute(to_core, "gz", [(i, i ^ 1) for i in range(holders)])
    gy = lax.axis_size("gy")
    across = {
        (i, c): (i, 3 - c) if c in (1, 2) else (i ^ 1, c)
        for i in range(gy) for c in range(holders)
    }
    far_face = lax.ppermute(
        to_far, ("gy", "gz"), [(a[0] * holders + a[1], b[0] * holders + b[1]) for a, b in across.items()]
    )
    both = [lax.ppermute(part, "gz", [(i, i ^ 1) for i in range(holders)]) for part in (chip[:half], chip[half:])]

    (ring_w,) = kernel_call(
        functools.partial(frame_kernel, cz), (own,), [vmem()], (shape(FIELDS - ADJ, layers + 1, cy, cx),)
    )
    x_send = shape(x_tiles(), cy, cx, dtype=bf16)
    ring_f, ring_w, x_a, x_b = kernel_call(
        functools.partial(column_kernel, cz),
        (to_core, core, chip, *both, far_face, peer, slot, ring_w),
        [vmem()] * 9,
        (shape(ADJ, layers + 1, cy, cx), shape(*ring_w.shape), x_send, x_send if wide_x else None),
        [
            pltpu.SMEM(peer.shape, jnp.int32),
            pltpu.SMEM(slot.shape, jnp.int32),
            pltpu.SemaphoreType.DMA((2,)),
        ],
        {8: 1},
    )
    axes = ("gx", "gy", "gz")
    gx = lax.axis_size("gx")

    def partner(i, j, c, x_turn, y_turn):
        if x_turn is not None:
            i = dict(swap_pairs(gx, x_turn))[i]
        if y_turn is not None:
            other = dict(swap_pairs(gy, (c + y_turn) % 2))[j]
            i, j = (i ^ 1, j) if other == j else (i, other)
        return (i * gy + j) * holders + c

    def swap(value, x_turn, y_turn):
        if value is None:
            return None
        pairs = [
            ((i * gy + j) * holders + c, partner(i, j, c, x_turn, y_turn))
            for i in range(gx) for j in range(gy) for c in range(holders)
        ]
        return lax.ppermute(value, axes, pairs)

    strip_tiles, tiles = row_tiles(cz, cy)
    y_send = shape(strip_tiles + tiles, cy, cx, dtype=bf16)
    scratch_tiles = max(sum(row_counts(cz, cy, up)) for up in (True, False))
    y_a, y_b = kernel_call(
        functools.partial(layer_rows_kernel, cz),
        (ring_f, ring_w),
        [vmem()] * 2,
        (y_send, y_send),
        [pltpu.VMEM((2, scratch_tiles, 8, cx), f32)],
    )
    strips, y_a, y_b = kernel_call(
        functools.partial(strip_rows_kernel, cz),
        (ring_f, ring_w, swap(x_a, 0, None), swap(x_b, 1, None), y_a, y_b),
        [vmem()] * 6,
        (shape(FIELDS, cy, cx), y_send, y_send),
        [pltpu.VMEM((2, strip_tiles, 8, cx), f32)],
        {4 if wide_x else 3: 1, 5 if wide_x else 4: 2},
    )
    edges, sides, middle = kernel_call(
        functools.partial(middle_kernel, cz),
        (ring_f, ring_w, strips, own),
        [vmem()] * 4,
        (
            shape(FIELDS + 1, layers + 1, cy, cx),
            shape(8, 3, layers + 1, cy, cx),
            shape(11, cz, cy, cx),
        ),
        [pltpu.VMEM((STAGES, layers + 1, cy, cx), f32)],
    )
    row_scratch = pltpu.VMEM((scratch_tiles, 8, cx), f32)
    (edges,) = kernel_call(
        functools.partial(first_rows_kernel, cz),
        (swap(y_a, None, 0), edges),
        [vmem()] * 2,
        (shape(*edges.shape),),
        [row_scratch],
        {1: 0},
    )
    result = kernel_call(
        functools.partial(edge_kernel, cz),
        (edges, sides, middle, swap(y_b, None, 1)),
        [vmem()] * 4,
        (shape(9, cz, cy, cx), shape(cz, cy, cx), shape(cz, cy, cx), shape(*edges.shape)),
        [
            row_scratch,
            pltpu.VMEM((STAGES, layers + 1, cy, cx), f32),
            pltpu.VMEM((11, cz, cy, cx), f32),
            pltpu.SemaphoreType.DMA((4,)),
        ],
        {0: 3},
        (hbm(),) * 3 + (vmem(),),
    )
    return result[:3]


def solution(mesh):
    return jax.shard_map(
        on_device,
        mesh=mesh,
        in_specs=(
            P("gz", None, None, "gy", "gx"),
            P("gx", "gy", None, None),
            P("gx", "gy", None, None),
            P(None, "gz", "gy", "gx"),
            P("gz", "gy", "gx"),
            P("gz", "gy", "gx"),
            P("gz", "gy", "gx"),
            P("gz", "gy", "gx", None),
            P(),
            P("gz", "gy", "gx", None),
            P("gz", "gy", "gx", None, None),
            P(),
        ),
        out_specs=(P(None, "gz", "gy", "gx"), P("gz", "gy", "gx"), P("gz", "gy", "gx")),
        check_vma=False,
    )
```

```python
import functools

import jax
import jax.numpy as jnp
from jax import lax
from jax.experimental import pallas as pl
from jax.experimental.pallas import tpu as pltpu
from jax.sharding import PartitionSpec as P

VX, VY, VZ, SXX, SYY, SZZ, SXY, SXZ, SYZ = range(9)
FWD, ADJ, BUOY, LAM, MU, INJ, SRC = 0, 9, 18, 19, 20, 21, 22
FIELDS = 23
HALO = 2

ADJ_Z = {VX: (2, 2), VY: (2, 2), VZ: (2, 2), SXX: (1, 1), SYY: (1, 1), SZZ: (1, 2), SXY: (1, 1), SXZ: (2, 1), SYZ: (2, 1)}
OTHER_Z = {BUOY: (2, 2), LAM: (1, 2), MU: (2, 2), INJ: (0, 1), SRC: (1, 1)}
F32_Z = {**{ADJ + f: c for f, c in ADJ_Z.items()}, **OTHER_Z}

Y_ROWS = {
    FWD + VX: (None, (2, -1, 1), (1, -1, 1), (2, -2, 0)),
    FWD + VY: ((2, -2, 0), (1, -1, 1), (2, -1, 1), None),
    FWD + VZ: (None, (1, -2, 1), (1, -1, 1), (2, -2, 0)),
    FWD + SXX: (None, (2, -1, 1), (1, -1, 1), (2, -2, 1)),
    FWD + SYY: ((2, -2, 0), (1, -1, 1), (1, 0, 1), (2, -1, 1)),
    FWD + SZZ: (None, (1, -1, 1), (1, 0, 1), (2, -1, 0)),
    FWD + SXY: ((2, -1, 1), (1, 0, 1), (1, -1, 1), (2, -2, 0)),
    FWD + SXZ: (None, (1, -1, 1), (0, -1, 1), (1, -2, 1)),
    FWD + SYZ: ((1, -2, 1), (0, -1, 1), (1, -1, 1), (2, -2, 0)),
    ADJ + VX: ((2, -2, 0), (1, -1, 1), (1, -1, 1), (2, -2, 1)),
    ADJ + VY: ((2, -1, 1), (1, 0, 1), (1, -1, 1), (2, -2, 0)),
    ADJ + VZ: ((2, -2, 0), (1, -1, 1), (0, -1, 1), (1, -2, 0)),
    ADJ + SXX: (None, (2, -2, 1), (2, -2, 1), None),
    ADJ + SYY: (None, (2, -1, 1), (1, -1, 1), (2, -2, 0)),
    ADJ + SZZ: (None, (2, -1, 0), (1, -1, 0), None),
    ADJ + SXY: ((2, -2, 0), (1, -1, 1), (2, -2, 1), None),
    ADJ + SXZ: (None, (1, -2, 1), (1, -2, 1), None),
    ADJ + SYZ: ((2, -2, 0), (1, -1, 1), (1, -2, 0), None),
    BUOY: ((2, -2, 0), (1, -1, 1), (1, -1, 1), (2, -2, 0)),
    LAM: (None, (2, -1, 1), (1, -1, 1), (2, -2, 0)),
    MU: ((2, -2, 0), (1, -1, 1), (1, -1, 1), (2, -2, 0)),
    INJ: (None, None, (2, -2, 0), None),
    SRC: (None, (2, -2, 0), (2, -1, 1), None),
}

EXACT_ROWS = {-1: (ADJ + VY, ADJ + SXY, ADJ + SYZ, BUOY, SRC), 0: (ADJ + SYY, LAM, INJ, SRC)}

PAD = 1
VMEM_LIMIT = 48 * 1024 * 1024


def vmem():
    return pl.BlockSpec(memory_space=pltpu.VMEM)


def hbm():
    return pl.BlockSpec(memory_space=pl.ANY)


def faces(cz, up):
    near, far = [], []
    for f in sorted(F32_Z):
        before, after = F32_Z[f]
        depth = before if up else after
        for d in range(depth):
            layer = cz - 1 - d if up else d
            (far if d else near).append((f, layer, HALO - 1 - d if up else HALO + cz + d))
    return near, far


def face_counts(cz):
    sides = [faces(cz, up) for up in (True, False)]
    return max(len(s[0]) for s in sides), max(len(s[1]) for s in sides)


def y_rows(cz, cy, up):
    layers = cz + 2 * HALO
    narrow, wide, strip = [], [], []
    for f in sorted(Y_ROWS):
        for offset in (-1, -2) if up else (0, 1):
            spec = Y_ROWS[f][offset + HALO]
            if spec is None:
                continue
            source = cy + offset if up else offset
            target = cy - HALO + offset if up else HALO + offset
            exact = f in EXACT_ROWS.get(offset, ())
            (wide if exact else narrow).extend((f, z, source, target) for z in range(spec[0], layers + spec[1]))
            if spec[2]:
                strip.append((f, layers, source, target))
    return narrow, wide, strip


def row_counts(cz, cy, up):
    return tuple(-(-len(rows) // 8) for rows in y_rows(cz, cy, up))


def row_tiles(cz, cy):
    sides = [row_counts(cz, cy, up) for up in (True, False)]
    return max(c for _, _, c in sides), max(n + 2 * w for n, w, _ in sides)


def split(value):
    high = value.astype(jnp.bfloat16)
    low = (value - high.astype(jnp.float32)).astype(jnp.bfloat16)
    return high, low


def joined(high, low):
    return high.astype(jnp.float32) + low.astype(jnp.float32)


def even_mask(axes, shape):
    total = sum(lax.axis_index(a) for a in ((axes,) if isinstance(axes, str) else axes))
    return jnp.full(shape, lax.rem(total, 2), jnp.int32) == 0


def has_neighbours(axis):
    index = lax.axis_index(axis)
    return (index > 0).astype(jnp.float32), (index < lax.axis_size(axis) - 1).astype(jnp.float32)


def copies(sems, *pairs):
    out = [pltpu.make_async_copy(source, target, sems.at[i]) for i, (source, target) in enumerate(pairs)]
    for copy in out:
        copy.start()
    return out


def scatter_rows(packed, listed, row_of):
    for r, (f, z, y, _) in enumerate(listed):
        packed[r // 8, r % 8 : r % 8 + 1, :] = row_of(f, z, y)


def pack_tiles(sides, sends, first, count):
    even = even_mask(("gy", "gz"), sends[0].shape[1:])
    for t in range(count):
        up, down = (side[min(t, len(side) - 1)] for side in sides)
        sends[0][first + t] = jnp.where(even, down, up).astype(jnp.bfloat16)
        sends[1][first + t] = jnp.where(even, up, down).astype(jnp.bfloat16)


def layer_rows_kernel(cz, ring_f, ring_w, send_a, send_b, packed):
    cy = ring_f.shape[2]
    strip_tiles, tiles = row_tiles(cz, cy)

    def row_of(f, z, y):
        return ring_f[f, z, y : y + 1, :] if f < ADJ else ring_w[f - ADJ, z, y : y + 1, :]

    sides = []
    for side, up in enumerate((True, False)):
        narrow, wide, _ = y_rows(cz, cy, up)
        n, w, _ = row_counts(cz, cy, up)
        scatter_rows(packed.at[side], narrow, row_of)
        scatter_rows(packed.at[side, pl.ds(n, w)], wide, row_of)
        rest = [split(packed[side, n + t])[1].astype(jnp.float32) for t in range(w)]
        sides.append([packed[side, t] for t in range(n + w)] + rest)
    pack_tiles(sides, (send_a, send_b), strip_tiles, tiles)


def unpack_rows(cz, cy, first, message, packed, edges):
    has_lower, has_upper = has_neighbours("gy")
    strip_tiles, _ = row_tiles(cz, cy)
    parity = lax.rem(lax.axis_index("gy") + lax.axis_index("gz"), 2)

    def side(up, keep):
        narrow, wide, strip = y_rows(cz, cy, up)
        n, w, c = row_counts(cz, cy, up)
        for t in range(n + w):
            value = message[strip_tiles + t].astype(jnp.float32)
            if t >= n:
                value = value + message[strip_tiles + w + t].astype(jnp.float32)
            packed[t] = value * keep
        for t in range(c):
            packed[n + w + t] = message[t].astype(jnp.float32) * keep
        for base, listed in ((0, narrow), (n, wide), (n + w, strip)):
            for r, (f, z, _, y) in enumerate(listed):
                edges[f, z, y : y + 1, :] = packed[base + r // 8, r % 8 : r % 8 + 1, :]

    @pl.when(parity == (0 if first else 1))
    def _():
        side(True, has_lower)

    @pl.when(parity == (1 if first else 0))
    def _():
        side(False, has_upper)


def first_rows_kernel(cz, message, edges_in, edges, packed):
    unpack_rows(cz, edges.shape[2], True, message, packed, edges)


def start_kernel(
    cz, store, adjoint, lam, mu, buoy, source, wavelet, receiver, traces, plan, peer, slot,
    near_out, far_out, own, peer_out, slot_out, cells, samples, spots, wave, steps, sems,
):
    cy, lanes = own.shape[2], own.shape[3]
    rows = cz * cy
    tiles = store.shape[0]
    small = copies(sems, (plan, steps), (wavelet, wave), (source, spots), (receiver, cells), (traces, samples))
    large = copies(
        sems.at[pl.ds(len(small), 7)],
        (adjoint, own.at[pl.ds(0, 9)]),
        (buoy, own.at[BUOY - ADJ]),
        (lam, own.at[LAM - ADJ]),
        (mu, own.at[MU - ADJ]),
        (store, near_out.at[pl.ds(0, tiles)]),
        (peer, peer_out),
        (slot, slot_out),
    )
    for copy in small:
        copy.wait()
    listed = cells[...]
    count = listed.shape[1]
    row_hot = (lax.broadcasted_iota(jnp.int32, (rows, count), 0) == listed // lanes).astype(jnp.float32)
    lane_hit = lax.broadcasted_iota(jnp.int32, (lanes, count), 0) == listed % lanes
    injected = []
    for step in (1, 0):
        sample = samples[pl.ds(steps[step], 1), :]
        field = lax.dot_general(
            row_hot,
            jnp.where(lane_hit, sample, 0.0),
            (((1,), (1,)), ((), ())),
            precision=lax.Precision.HIGHEST,
            preferred_element_type=jnp.float32,
        )
        injected.append(field.reshape(cz, cy, lanes))
    own[INJ - ADJ] = injected[1]
    flat = lax.broadcasted_iota(jnp.int32, (rows, lanes), 0) * lanes + lax.broadcasted_iota(jnp.int32, (rows, lanes), 1)
    for step in range(2):
        value = wave[steps[step]]
        field = jnp.zeros((rows, lanes), jnp.float32)
        for j in range(source.shape[1]):
            field = field + jnp.where(flat == spots[0, j], value, 0.0)
        own[SRC - ADJ + step] = field.reshape(cz, cy, lanes)
    for copy in large:
        copy.wait()
    for f in (SXX, SYY, SZZ):
        own[f] = own[f] + injected[0]

    even = even_mask("gz", (cy, lanes))
    near, far = face_counts(cz)
    up, down = faces(cz, True), faces(cz, False)
    zero = jnp.zeros((cy, lanes), jnp.float32)

    def tile(side, i):
        return own[side[i][0] - ADJ, side[i][1]] if i < len(side) else zero

    for i in range(near):
        above, below = tile(up[0], i), tile(down[0], i)
        for out, base, value in (
            (near_out, tiles, jnp.where(even, above, below)),
            (far_out, 0, jnp.where(even, below, above)),
        ):
            out[base + i], out[base + near + i] = split(value)
    for i in range(far):
        above, below = tile(up[1], i), tile(down[1], i)
        near_out[tiles + 2 * near + i] = jnp.where(even, above, below).astype(jnp.bfloat16)
        far_out[2 * near + i] = jnp.where(even, below, above).astype(jnp.bfloat16)
    for i in range(2 * near + far, far_out.shape[0]):
        far_out[i] = zero.astype(jnp.bfloat16)


def strip_part(tile, main, listed):
    lanes = tile.shape[1]
    lane = lax.broadcasted_iota(jnp.int32, tile.shape, 1)
    for z in listed:
        tile = jnp.where((lane >= 8 * z) & (lane < 8 * z + 4), pltpu.roll(main(z), (8 * z + 2) % lanes, 1), tile)
    return tile


def strip_whole(tile):
    position = lax.broadcasted_iota(jnp.int32, tile.shape, 1) % 8
    return jnp.where(position < 2, tile, jnp.where(position >= 6, pltpu.roll(tile, 4, 1), 0.0))


def pieces(cz, peers, slots):
    me, count = lax.axis_index("gz"), lax.axis_size("gz")
    below, above = jnp.maximum(me - 1, 0), jnp.minimum(me + 1, count - 1)
    has_below, has_above = has_neighbours("gz")
    for z in range(cz + 2 * HALO):
        if z < HALO:
            brick, piece, keep = below, cz - HALO + z, has_below
        elif z < HALO + cz:
            brick, piece, keep = me, z - HALO, None
        else:
            brick, piece, keep = above, z - HALO - cz, has_above
        yield z, peers[brick, piece] ^ me, slots[brick, piece] * 9, keep


def frame_kernel(cz, mine, core, chip, peer, slot, own, ring_f, ring, peers, slots, sems):
    moves = copies(sems, (peer, peers), (slot, slots))
    cy, lanes = own.shape[2], own.shape[3]
    layers = cz + 2 * HALO
    zero = jnp.zeros((cy, lanes), jnp.float32)
    filled = {(f - ADJ, z) for up in (True, False) for listed in faces(cz, up) for f, _, z in listed}
    for f in range(ring.shape[0]):
        for z in range(cz):
            ring[f, HALO + z] = own[f, z]
        for z in (0, 1, layers - 2, layers - 1):
            if (f, z) not in filled:
                ring[f, z] = zero
        ring[f, layers] = strip_part(zero, lambda z: own[f, z - HALO], range(HALO, HALO + cz))
    for move in moves:
        move.wait()
    for z, hops, row, keep in pieces(cz, peers, slots):
        hops = jnp.full((cy, lanes), hops, jnp.int32)
        for f in range(9):
            a, b, c = (ref[row + f].astype(jnp.float32) for ref in (mine, core, chip))
            value = jnp.where(hops == 0, a, jnp.where(hops == 1, b, c))
            ring_f[f, z] = value if keep is None else value * keep


def column_kernel(
    cz, core, both_a, both_b, far, peer, slot, ring_f_in, ring_w_in,
    ring_f, ring, x_a, x_b, peers, slots, sems,
):
    cy, lanes = core.shape[1], core.shape[2]
    layers = cz + 2 * HALO
    half = both_a.shape[0]
    tiles = half + both_b.shape[0]
    moves = copies(sems, (peer, peers), (slot, slots))
    near, _ = face_counts(cz)
    even = even_mask("gz", (cy, lanes))
    has_below, has_above = has_neighbours("gz")
    zero = jnp.zeros((cy, lanes), jnp.float32)
    filled = {}
    for up in (True, False):
        for depth, listed in enumerate(faces(cz, up)):
            for i, (f, _, z) in enumerate(listed):
                values = []
                for ref, base in ((core, tiles), (far, 0)):
                    if depth == 0:
                        values.append(joined(ref[base + i], ref[base + near + i]))
                    else:
                        values.append(ref[base + 2 * near + i].astype(jnp.float32))
                value = jnp.where(even, values[1], values[0]) if up else jnp.where(even, values[0], values[1])
                value = value * (has_below if up else has_above)
                ring[f - ADJ, z] = value
                filled.setdefault(f - ADJ, {})[z] = value
    strip = []
    for f in range(ring.shape[0]):
        there = filled.get(f, {})
        tile = strip_whole(strip_part(ring[f, layers], lambda z: there[z], sorted(there)))
        ring[f, layers] = tile
        strip.append(tile)
    for move in moves:
        move.wait()
    for z, hops, row, keep in pieces(cz, peers, slots):
        last = jnp.full((cy, lanes), hops, jnp.int32) == 3
        late = jnp.full((cy, lanes), row, jnp.int32) >= half
        row_a, row_b = jnp.minimum(row, half - 9), jnp.maximum(row - half, 0)
        for f in range(9):
            a, b = both_a[row_a + f].astype(jnp.float32), both_b[row_b + f].astype(jnp.float32)
            value = jnp.where(late, b, a)
            ring_f[f, z] = jnp.where(last, value if keep is None else value * keep, ring_f[f, z])
    for f in range(9):
        ring_f[f, layers] = strip_whole(strip_part(zero, lambda z: ring_f[f, z], range(layers)))
    strip = [ring_f[f, layers] for f in range(9)] + strip
    position = lax.broadcasted_iota(jnp.int32, (cy, lanes), 1) % 8
    even_x = even_mask("gx", (cy, lanes))
    for out, tail_from_even in ((x_a, True), (x_b, False)):
        if out is None:
            continue
        place = 0
        for fields, narrow in ((range(ADJ), True), (range(ADJ, FIELDS), False)):
            quads = [fields[i : i + 4] for i in range(0, len(fields), 4)]
            for i, quad in enumerate(quads):
                tile = zero
                for g, f in enumerate(quad):
                    tail, head = strip[f], pltpu.roll(strip[f], lanes - 6, 1)
                    value = jnp.where(even_x, tail, head) if tail_from_even else jnp.where(even_x, head, tail)
                    value = value if g == 0 else pltpu.roll(value, 2 * g, 1)
                    tile = jnp.where(position // 2 == g, value, tile)
                high, low = split(tile)
                out[place + i] = high
                if not narrow:
                    out[place + len(quads) + i] = low
            place += len(quads) if narrow else 2 * len(quads)


def x_tiles():
    return -(-ADJ // 4) + 2 * -(-(FIELDS - ADJ) // 4)


def strip_rows_kernel(cz, ring_f, ring_w, x_a, x_b, y_a_in, y_b_in, strips, y_a, y_b, packed):
    cy, lanes = strips.shape[1], strips.shape[2]
    layers = cz + 2 * HALO
    pair = lax.broadcasted_iota(jnp.int32, (cy, lanes), 1) % 8 // 2
    even_x = even_mask("gx", (cy, lanes))
    has_left, has_right = has_neighbours("gx")
    zero = jnp.zeros((cy, lanes), jnp.float32)
    place = 0
    for fields, narrow in ((range(ADJ), True), (range(ADJ, FIELDS), False)):
        quads = [fields[i : i + 4] for i in range(0, len(fields), 4)]
        for i, quad in enumerate(quads):
            got = []
            for ref in (x_a, x_b):
                if ref is None:
                    got.append(zero)
                elif narrow:
                    got.append(ref[place + i].astype(jnp.float32))
                else:
                    got.append(joined(ref[place + i], ref[place + len(quads) + i]))
            right = jnp.where(even_x, got[0], got[1]) * has_right
            left = jnp.where(even_x, got[1], got[0]) * has_left
            for g, f in enumerate(quad):
                strip = ring_f[f, layers] if f < ADJ else ring_w[f - ADJ, layers]
                tile = jnp.where(pair == 1, pltpu.roll(right, (2 - 2 * g) % lanes, 1), strip)
                strips[f] = jnp.where(pair == 2, pltpu.roll(left, (4 - 2 * g) % lanes, 1), tile)
        place += len(quads) if narrow else 2 * len(quads)
    sides = []
    for side, up in enumerate((True, False)):
        scatter_rows(packed.at[side], y_rows(cz, cy, up)[2], lambda f, z, y: strips[f, y : y + 1, :])
        sides.append([packed[side, t] for t in range(row_counts(cz, cy, up)[2])])
    pack_tiles(sides, (y_a, y_b), 0, packed.shape[1])


STAGE = {"fv": 0, "fs": 3, "fw": 9, "as": 12, "av": 18, "at": 21}
STAGES = 27
NORMAL = (SXX, SYY, SZZ)
STRESS = range(SXX, SYZ + 1)


def window(cz, base, stage, after, before, put):
    layers = cz + 2 * HALO
    edge = layers
    cy, lanes = stage.shape[2], stage.shape[3]
    lane = lax.broadcasted_iota(jnp.int32, (cy, lanes), 1)
    first_lane, last_lane = lane == 0, lane == lanes - 1
    inner = range(HALO, HALO + cz)

    def start(field):
        return lambda z: base(field, z)

    def kept(name, field):
        index = STAGE[name] + field
        return lambda z: stage[index, z]

    def x_next(of, z):
        value = pltpu.roll(of(z), lanes - 1, 1)
        if z == edge:
            return value
        return jnp.where(last_lane, pltpu.roll(of(edge), (lanes - 1 - (8 * z + 2)) % lanes, 1), value)

    def x_prev(of, z):
        value = pltpu.roll(of(z), 1, 1)
        if z == edge:
            return value
        return jnp.where(first_lane, pltpu.roll(of(edge), (lanes - (8 * z + 5)) % lanes, 1), value)

    def z_next(of, z):
        return pltpu.roll(of(edge), lanes - 8, 1) if z == edge else of(z + 1)

    def z_prev(of, z):
        return pltpu.roll(of(edge), 8, 1) if z == edge else of(z - 1)

    def velocity_rates(k, s, z, want):
        buoy = base(BUOY, z)
        sxx, syy, szz, sxy, sxz, syz = s
        out = {}
        if VX in want:
            xy = sxy(z)
            out[VX] = buoy * (
                (x_next(sxx, z) - sxx(z)) + (xy - before(k, 0, z, xy)) + (sxz(z) - z_prev(sxz, z))
            )
        if VY in want:
            yy = syy(z)
            out[VY] = buoy * (
                (sxy(z) - x_prev(sxy, z)) + (after(k, 1, z, yy) - yy) + (syz(z) - z_prev(syz, z))
            )
        if VZ in want:
            yz = syz(z)
            out[VZ] = buoy * (
                (sxz(z) - x_prev(sxz, z)) + (yz - before(k, 2, z, yz)) + (z_next(szz, z) - szz(z))
            )
        return out

    def stress_rates(k, v, z, want):
        lam, mu = base(LAM, z), base(MU, z)
        of_x, of_y, of_z = v
        vx, vy, vz = of_x(z), of_y(z), of_z(z)
        out = {}
        if SXX in want:
            exx = vx - x_prev(of_x, z)
            eyy = vy - before(k, 0, z, vy)
            ezz = vz - z_prev(of_z, z)
            common = lam * (exx + eyy + ezz)
            twice = 2.0 * mu
            out[SXX] = common + twice * exx
            out[SYY] = common + twice * eyy
            out[SZZ] = common + twice * ezz
        if SXY in want:
            out[SXY] = mu * ((after(k, 1, z, vx) - vx) + (x_next(of_y, z) - vy))
        if SXZ in want:
            out[SXZ] = mu * ((z_next(of_x, z) - vx) + (x_next(of_z, z) - vz))
            out[SYZ] = mu * ((z_next(of_y, z) - vy) + (after(k, 2, z, vz) - vz))
        return out

    def spread(ranges):
        for z in range(layers + 1):
            want = {f for f, (a, b) in ranges.items() if z == edge or a <= z < b}
            if want:
                yield z, want

    def velocity_step(k, name, v, s, sign, ranges):
        for z, want in spread(ranges):
            for f, rate in velocity_rates(k, s, z, want).items():
                stage[STAGE[name] + f, z] = v[f](z) + rate if sign > 0 else v[f](z) - rate
        return [kept(name, f) for f in (VX, VY, VZ)]

    def stress_step(k, name, v, s, sign, ranges, ahead=None, behind=None):
        for z, want in spread(ranges):
            for f, rate in stress_rates(k, v, z, want).items():
                value = s[f - SXX](z)
                if ahead is not None and f in NORMAL:
                    value = value + base(ahead, z)
                value = value + rate if sign > 0 else value - rate
                if behind is not None and f in NORMAL:
                    value = value + base(behind, z)
                stage[STAGE[name] + f - SXX, z] = value
        return [kept(name, f - SXX) for f in STRESS]

    def terms(f, a):
        term_lam = (f[0] + f[1] + f[2]) * (a[0] + a[1] + a[2])
        term_mu = f[0] * a[0] + f[1] * a[1] + f[2] * a[2] + 2.0 * (f[3] * a[3] + f[4] * a[4] + f[5] * a[5])
        return term_lam, term_mu

    n = layers
    fv, fs = [start(FWD + f) for f in (VX, VY, VZ)], [start(FWD + f) for f in STRESS]
    av, first = [start(ADJ + f) for f in (VX, VY, VZ)], [start(ADJ + f) for f in STRESS]
    a_s = stress_step(0, "as", av, first, -1, {SXX: (1, n), SXY: (0, n), SXZ: (0, n - 1)})
    fv = velocity_step(1, "fv", fv, fs, 1, {VX: (1, n), VY: (1, n), VZ: (0, n - 1)})
    fs = stress_step(2, "fs", fv, fs, 1, {SXX: (1, n - 1), SXY: (1, n - 1), SXZ: (1, n - 1)}, behind=SRC)
    fv = velocity_step(3, "fw", fv, fs, 1, {VX: (2, n - 1), VY: (2, n - 1), VZ: (1, n - 2)})
    for z in inner:
        rates = stress_rates(4, fv, z, set(STRESS))
        now = [of(z) for of in fs]
        later = [now[s - SXX] + rates[s] + (base(FIELDS, z) if s in NORMAL else 0.0) for s in STRESS]
        lam_late, mu_late = terms(later, [of(z) for of in first])
        with_traces = [of(z) + (base(INJ, z) if s in NORMAL else 0.0) for s, of in zip(STRESS, a_s)]
        lam_early, mu_early = terms(now, with_traces)
        put(9, z - HALO, lam_late + lam_early)
        put(10, z - HALO, mu_late + mu_early)
    av = velocity_step(5, "av", av, a_s, -1, {VX: (1, n - 1), VY: (1, n - 1), VZ: (1, n - 1)})
    a_s = stress_step(6, "at", av, a_s, -1, {SXX: (2, n - 1), SXY: (1, n - 1), SXZ: (1, n - 2)}, ahead=INJ)
    for s, of in zip(STRESS, a_s):
        for z in inner:
            put(s, z - HALO, of(z))
    for z in inner:
        rates = velocity_rates(7, a_s, z, {VX, VY, VZ})
        for f in (VX, VY, VZ):
            put(f, z - HALO, av[f](z) - rates[f])


def middle_kernel(cz, ring_f, ring_w, strips, own, edges, sides, middle, stage):
    cy, lanes = own.shape[2], own.shape[3]
    layers = cz + 2 * HALO

    def base(f, z):
        if f == FIELDS:
            return own[f - ADJ, z - HALO]
        if z == layers:
            return strips[f]
        return ring_f[f, z] if f < ADJ else ring_w[f - ADJ, z]

    row = lax.broadcasted_iota(jnp.int32, (cy, lanes), 0)
    for f in range(FIELDS + 1):
        for z in range(HALO, HALO + cz) if f == FIELDS else range(layers + 1):
            tile = base(f, z)
            tail, head = pltpu.roll(tile, HALO, 0), pltpu.roll(tile, cy - HALO, 0)
            edges[f, z] = jnp.where(row < HALO, tail, jnp.where(row >= cy - HALO, head, 0.0))

    def after(k, j, z, tile):
        sides[k, j, z] = pltpu.roll(tile, cy - 1 - HALO, 0)
        return pltpu.roll(tile, cy - 1, 0)

    def before(k, j, z, tile):
        sides[k, j, z] = pltpu.roll(tile, HALO + 1, 0)
        return pltpu.roll(tile, 1, 0)

    def put(i, z, value):
        middle[i, z] = value

    window(cz, base, stage, after, before, put)


def edge_kernel(
    cz, edges_in, sides, middle, message, final, image_lam, image_mu, edges, packed, stage, result, sems
):
    cy, lanes = middle.shape[2], middle.shape[3]

    unpack_rows(cz, cy, False, message, packed, edges)
    row = lax.broadcasted_iota(jnp.int32, (cy, lanes), 0)

    def after(k, j, z, tile):
        return jnp.where(row == cy - 1, sides[k, j, z], pltpu.roll(tile, cy - 1, 0))

    def before(k, j, z, tile):
        return jnp.where(row == 0, sides[k, j, z], pltpu.roll(tile, 1, 0))

    moves = []

    def put(i, z, value):
        tail, head = pltpu.roll(value, HALO, 0), pltpu.roll(value, cy - HALO, 0)
        result[i, z] = jnp.where(row < HALO, tail, jnp.where(row >= cy - HALO, head, middle[i, z]))
        if z == cz - 1:
            if i == 10:
                moves.extend(copies(sems, (result.at[9], image_lam), (result.at[10], image_mu)))
            if i == SYZ:
                part = pl.ds(SXX, SYZ + 1 - SXX)
                moves.extend(copies(sems.at[pl.ds(2, 1)], (result.at[part], final.at[part])))
            if i == VZ:
                part = pl.ds(VX, VZ + 1 - VX)
                moves.extend(copies(sems.at[pl.ds(3, 1)], (result.at[part], final.at[part])))

    window(cz, lambda f, z: edges[f, z], stage, after, before, put)
    for move in moves:
        move.wait()


def swap_pairs(count, first):
    pairs = [(i + d, i + 1 - d) for i in range(first, count - 1, 2) for d in (0, 1)]
    return pairs + [(i, i) for i in range(count) if i not in dict(pairs)]


def swapped(value_a, value_b, axis):
    count = lax.axis_size(axis)
    got_a = lax.ppermute(value_a, axis, swap_pairs(count, 0))
    return got_a, None if value_b is None else lax.ppermute(value_b, axis, swap_pairs(count, 1))


def stay(value, spec):
    return pltpu.with_memory_space_constraint(value, pltpu.HBM) if spec.memory_space == pl.ANY else value


def kernel_call(body, args, in_specs, out_shape, scratch_shapes=(), aliases=None, out_specs=None):
    here = [a is not None for a in args]
    there = [o is not None for o in out_shape]

    def run(*refs):
        refs = iter(refs)
        full = [next(refs) if h else None for h in here + there]
        body(*full, *refs)

    out = iter(
        pl.pallas_call(
            run,
            out_shape=tuple(o for o in out_shape if o is not None),
            in_specs=[s for s, h in zip(in_specs, here) if h],
            out_specs=out_specs or tuple(vmem() for h in there if h),
            scratch_shapes=list(scratch_shapes),
            input_output_aliases=aliases or {},
            compiler_params=pltpu.CompilerParams(vmem_limit_bytes=VMEM_LIMIT),
        )(*[stay(a, s) for a, s in zip(args, in_specs) if a is not None])
    )
    return tuple(next(out) if h else None for h in there)


def on_device(
    checkpoint_store,
    holder_peer,
    holder_slot,
    adjoint_state,
    lame_lambda,
    lame_mu,
    buoyancy,
    source_cell,
    wavelet,
    receiver_cell,
    traces,
    plan,
):
    cz, cy, cx = lame_mu.shape
    layers = cz + 2 * HALO
    bf16, f32 = jnp.bfloat16, jnp.float32
    store = checkpoint_store.reshape(-1, cy, cx)
    tiles = store.shape[0]
    peer, slot = holder_peer[0, 0], holder_slot[0, 0]
    source, receiver = source_cell.reshape(1, -1), receiver_cell.reshape(1, -1)
    traces = traces.reshape(traces.shape[-2:])
    holders = lax.axis_size("gz")
    assert holders == 4
    near, far = face_counts(cz)
    face = 2 * near + far
    half = tiles // 2

    def shape(*dims, dtype=f32):
        return jax.ShapeDtypeStruct(dims, dtype)

    wide_x = lax.axis_size("gx") > 2
    chip = lax.ppermute(store, "gz", [(i, i ^ 2) for i in range(holders)])
    to_core, to_far, own, peer, slot = kernel_call(
        functools.partial(start_kernel, cz),
        (store, adjoint_state, lame_lambda, lame_mu, buoyancy, source, wavelet, receiver, traces, plan, peer, slot),
        [hbm()] * 12,
        (shape(tiles + face, cy, cx, dtype=bf16), shape(max(face, half) + PAD, cy, cx, dtype=bf16), shape(15, cz, cy, cx),
         shape(*peer.shape, dtype=jnp.int32), shape(*slot.shape, dtype=jnp.int32)),
        [
            pltpu.VMEM(receiver.shape, jnp.int32),
            pltpu.VMEM(traces.shape, f32),
            pltpu.SMEM(source.shape, jnp.int32),
            pltpu.SMEM(wavelet.shape, f32),
            pltpu.SMEM(plan.shape, jnp.int32),
            pltpu.SemaphoreType.DMA((12,)),
        ],
    )
    core = lax.ppermute(to_core, "gz", [(i, i ^ 1) for i in range(holders)])
    gy = lax.axis_size("gy")
    across = {
        (i, c): (i, 3 - c) if c in (1, 2) else (i ^ 1, c)
        for i in range(gy) for c in range(holders)
    }
    far_face = lax.ppermute(
        to_far, ("gy", "gz"), [(a[0] * holders + a[1], b[0] * holders + b[1]) for a, b in across.items()]
    )
    both = [lax.ppermute(part, "gz", [(i, i ^ 1) for i in range(holders)]) for part in (chip[:half], chip[half:])]

    table_scratch = [
        pltpu.SMEM(peer.shape, jnp.int32),
        pltpu.SMEM(slot.shape, jnp.int32),
        pltpu.SemaphoreType.DMA((2,)),
    ]
    ring_f, ring_w = kernel_call(
        functools.partial(frame_kernel, cz),
        (to_core, core, chip, peer, slot, own),
        [vmem()] * 6,
        (shape(ADJ, layers + 1, cy, cx), shape(FIELDS - ADJ, layers + 1, cy, cx)),
        table_scratch,
    )
    x_send = shape(x_tiles(), cy, cx, dtype=bf16)
    ring_f, ring_w, x_a, x_b = kernel_call(
        functools.partial(column_kernel, cz),
        (core, *both, far_face, peer, slot, ring_f, ring_w),
        [vmem()] * 8,
        (shape(*ring_f.shape), shape(*ring_w.shape), x_send, x_send if wide_x else None),
        table_scratch,
        {6: 0, 7: 1},
    )
    axes = ("gx", "gy", "gz")
    gx = lax.axis_size("gx")

    def partner(i, j, c, x_turn, y_turn):
        if x_turn is not None:
            i = dict(swap_pairs(gx, x_turn))[i]
        if y_turn is not None:
            other = dict(swap_pairs(gy, (c + y_turn + 1) % 2))[j]
            i, j = (i ^ 1, j) if other == j else (i, other)
        return (i * gy + j) * holders + c

    def swap(value, x_turn, y_turn):
        if value is None:
            return None
        pairs = [
            ((i * gy + j) * holders + c, partner(i, j, c, x_turn, y_turn))
            for i in range(gx) for j in range(gy) for c in range(holders)
        ]
        return lax.ppermute(value, axes, pairs)

    strip_tiles, tiles = row_tiles(cz, cy)
    y_send = shape(strip_tiles + tiles, cy, cx, dtype=bf16)
    scratch_tiles = max(sum(row_counts(cz, cy, up)) for up in (True, False))
    y_a, y_b = kernel_call(
        functools.partial(layer_rows_kernel, cz),
        (ring_f, ring_w),
        [vmem()] * 2,
        (y_send, y_send),
        [pltpu.VMEM((2, scratch_tiles, 8, cx), f32)],
    )
    strips, y_a, y_b = kernel_call(
        functools.partial(strip_rows_kernel, cz),
        (ring_f, ring_w, swap(x_a, 0, None), swap(x_b, 1, None), y_a, y_b),
        [vmem()] * 6,
        (shape(FIELDS, cy, cx), y_send, y_send),
        [pltpu.VMEM((2, strip_tiles, 8, cx), f32)],
        {4 if wide_x else 3: 1, 5 if wide_x else 4: 2},
    )
    edges, sides, middle = kernel_call(
        functools.partial(middle_kernel, cz),
        (ring_f, ring_w, strips, own),
        [vmem()] * 4,
        (
            shape(FIELDS + 1, layers + 1, cy, cx),
            shape(8, 3, layers + 1, cy, cx),
            shape(11, cz, cy, cx),
        ),
        [pltpu.VMEM((STAGES, layers + 1, cy, cx), f32)],
    )
    row_scratch = pltpu.VMEM((scratch_tiles, 8, cx), f32)
    (edges,) = kernel_call(
        functools.partial(first_rows_kernel, cz),
        (swap(y_a, None, 0), edges),
        [vmem()] * 2,
        (shape(*edges.shape),),
        [row_scratch],
        {1: 0},
    )
    result = kernel_call(
        functools.partial(edge_kernel, cz),
        (edges, sides, middle, swap(y_b, None, 1)),
        [vmem()] * 4,
        (shape(9, cz, cy, cx), shape(cz, cy, cx), shape(cz, cy, cx), shape(*edges.shape)),
        [
            row_scratch,
            pltpu.VMEM((STAGES, layers + 1, cy, cx), f32),
            pltpu.VMEM((11, cz, cy, cx), f32),
            pltpu.SemaphoreType.DMA((4,)),
        ],
        {0: 3},
        (hbm(),) * 3 + (vmem(),),
    )
    return result[:3]


def solution(mesh):
    return jax.shard_map(
        on_device,
        mesh=mesh,
        in_specs=(
            P("gz", None, None, "gy", "gx"),
            P("gx", "gy", None, None),
            P("gx", "gy", None, None),
            P(None, "gz", "gy", "gx"),
            P("gz", "gy", "gx"),
            P("gz", "gy", "gx"),
            P("gz", "gy", "gx"),
            P("gz", "gy", "gx", None),
            P(),
            P("gz", "gy", "gx", None),
            P("gz", "gy", "gx", None, None),
            P(),
        ),
        out_specs=(P(None, "gz", "gy", "gx"), P("gz", "gy", "gx"), P("gz", "gy", "gx")),
        check_vma=False,
    )
```

```python
import functools

import jax
import jax.numpy as jnp
from jax import lax
from jax.experimental import pallas as pl
from jax.experimental.pallas import tpu as pltpu
from jax.sharding import PartitionSpec as P

VX, VY, VZ, SXX, SYY, SZZ, SXY, SXZ, SYZ = range(9)
FWD, ADJ, BUOY, LAM, MU, INJ, SRC = 0, 9, 18, 19, 20, 21, 22
FIELDS = 23
HALO = 2

ADJ_Z = {VX: (2, 2), VY: (2, 2), VZ: (2, 2), SXX: (1, 1), SYY: (1, 1), SZZ: (1, 2), SXY: (1, 1), SXZ: (2, 1), SYZ: (2, 1)}
OTHER_Z = {BUOY: (2, 2), LAM: (1, 2), MU: (2, 2), INJ: (0, 1), SRC: (1, 1)}
F32_Z = {**{ADJ + f: c for f, c in ADJ_Z.items()}, **OTHER_Z}

Y_ROWS = {
    FWD + VX: (None, (2, -1, 1), (1, -1, 1), (2, -2, 0)),
    FWD + VY: ((2, -2, 0), (1, -1, 1), (2, -1, 1), None),
    FWD + VZ: (None, (1, -2, 1), (1, -1, 1), (2, -2, 0)),
    FWD + SXX: (None, (2, -1, 1), (1, -1, 1), (2, -2, 1)),
    FWD + SYY: ((2, -2, 0), (1, -1, 1), (1, 0, 1), (2, -1, 1)),
    FWD + SZZ: (None, (1, -1, 1), (1, 0, 1), (2, -1, 0)),
    FWD + SXY: ((2, -1, 1), (1, 0, 1), (1, -1, 1), (2, -2, 0)),
    FWD + SXZ: (None, (1, -1, 1), (0, -1, 1), (1, -2, 1)),
    FWD + SYZ: ((1, -2, 1), (0, -1, 1), (1, -1, 1), (2, -2, 0)),
    ADJ + VX: ((2, -2, 0), (1, -1, 1), (1, -1, 1), (2, -2, 1)),
    ADJ + VY: ((2, -1, 1), (1, 0, 1), (1, -1, 1), (2, -2, 0)),
    ADJ + VZ: ((2, -2, 0), (1, -1, 1), (0, -1, 1), (1, -2, 0)),
    ADJ + SXX: (None, (2, -2, 1), (2, -2, 1), None),
    ADJ + SYY: (None, (2, -1, 1), (1, -1, 1), (2, -2, 0)),
    ADJ + SZZ: (None, (2, -1, 0), (1, -1, 0), None),
    ADJ + SXY: ((2, -2, 0), (1, -1, 1), (2, -2, 1), None),
    ADJ + SXZ: (None, (1, -2, 1), (1, -2, 1), None),
    ADJ + SYZ: ((2, -2, 0), (1, -1, 1), (1, -2, 0), None),
    BUOY: ((2, -2, 0), (1, -1, 1), (1, -1, 1), (2, -2, 0)),
    LAM: (None, (2, -1, 1), (1, -1, 1), (2, -2, 0)),
    MU: ((2, -2, 0), (1, -1, 1), (1, -1, 1), (2, -2, 0)),
    INJ: (None, None, (2, -2, 0), None),
    SRC: (None, (2, -2, 0), (2, -1, 1), None),
}

EXACT_ROWS = {-1: (ADJ + VY, ADJ + SXY, ADJ + SYZ, BUOY, SRC), 0: (ADJ + SYY, LAM, INJ, SRC)}

PAD = 1
VMEM_LIMIT = 48 * 1024 * 1024


def vmem():
    return pl.BlockSpec(memory_space=pltpu.VMEM)


def hbm():
    return pl.BlockSpec(memory_space=pl.ANY)


def faces(cz, up):
    near, far = [], []
    for f in sorted(F32_Z):
        before, after = F32_Z[f]
        depth = before if up else after
        for d in range(depth):
            layer = cz - 1 - d if up else d
            (far if d else near).append((f, layer, HALO - 1 - d if up else HALO + cz + d))
    return near, far


def face_counts(cz):
    sides = [faces(cz, up) for up in (True, False)]
    return max(len(s[0]) for s in sides), max(len(s[1]) for s in sides)


def y_rows(cz, cy, up):
    layers = cz + 2 * HALO
    narrow, wide, strip = [], [], []
    for f in sorted(Y_ROWS):
        for offset in (-1, -2) if up else (0, 1):
            spec = Y_ROWS[f][offset + HALO]
            if spec is None:
                continue
            source = cy + offset if up else offset
            target = cy - HALO + offset if up else HALO + offset
            exact = f in EXACT_ROWS.get(offset, ())
            (wide if exact else narrow).extend((f, z, source, target) for z in range(spec[0], layers + spec[1]))
            if spec[2]:
                strip.append((f, layers, source, target))
    return narrow, wide, strip


def row_counts(cz, cy, up):
    return tuple(-(-len(rows) // 8) for rows in y_rows(cz, cy, up))


def row_tiles(cz, cy):
    sides = [row_counts(cz, cy, up) for up in (True, False)]
    return max(c for _, _, c in sides), max(n + 2 * w for n, w, _ in sides)


def split(value):
    high = value.astype(jnp.bfloat16)
    low = (value - high.astype(jnp.float32)).astype(jnp.bfloat16)
    return high, low


def joined(high, low):
    return high.astype(jnp.float32) + low.astype(jnp.float32)


def even_mask(axes, shape):
    total = sum(lax.axis_index(a) for a in ((axes,) if isinstance(axes, str) else axes))
    return jnp.full(shape, lax.rem(total, 2), jnp.int32) == 0


def has_neighbours(axis):
    index = lax.axis_index(axis)
    return (index > 0).astype(jnp.float32), (index < lax.axis_size(axis) - 1).astype(jnp.float32)


def copies(sems, *pairs):
    out = [pltpu.make_async_copy(source, target, sems.at[i]) for i, (source, target) in enumerate(pairs)]
    for copy in out:
        copy.start()
    return out


def scatter_rows(packed, listed, row_of):
    for r, (f, z, y, _) in enumerate(listed):
        packed[r // 8, r % 8 : r % 8 + 1, :] = row_of(f, z, y)


def pack_tiles(sides, sends, first, count):
    even = even_mask(("gy", "gz"), sends[0].shape[1:])
    for t in range(count):
        up, down = (side[min(t, len(side) - 1)] for side in sides)
        sends[0][first + t] = jnp.where(even, down, up).astype(jnp.bfloat16)
        sends[1][first + t] = jnp.where(even, up, down).astype(jnp.bfloat16)


def layer_rows_kernel(cz, ring_f, ring_w, send_a, send_b, packed):
    cy = ring_f.shape[2]
    strip_tiles, tiles = row_tiles(cz, cy)

    def row_of(f, z, y):
        return ring_f[f, z, y : y + 1, :] if f < ADJ else ring_w[f - ADJ, z, y : y + 1, :]

    sides = []
    for side, up in enumerate((True, False)):
        narrow, wide, _ = y_rows(cz, cy, up)
        n, w, _ = row_counts(cz, cy, up)
        scatter_rows(packed.at[side], narrow, row_of)
        scatter_rows(packed.at[side, pl.ds(n, w)], wide, row_of)
        rest = [split(packed[side, n + t])[1].astype(jnp.float32) for t in range(w)]
        sides.append([packed[side, t] for t in range(n + w)] + rest)
    pack_tiles(sides, (send_a, send_b), strip_tiles, tiles)


def unpack_rows(cz, cy, first, message, packed, edges):
    has_lower, has_upper = has_neighbours("gy")
    strip_tiles, _ = row_tiles(cz, cy)
    parity = lax.rem(lax.axis_index("gy") + lax.axis_index("gz"), 2)

    def side(up, keep):
        narrow, wide, strip = y_rows(cz, cy, up)
        n, w, c = row_counts(cz, cy, up)
        for t in range(n + w):
            value = message[strip_tiles + t].astype(jnp.float32)
            if t >= n:
                value = value + message[strip_tiles + w + t].astype(jnp.float32)
            packed[t] = value * keep
        for t in range(c):
            packed[n + w + t] = message[t].astype(jnp.float32) * keep
        for base, listed in ((0, narrow), (n, wide), (n + w, strip)):
            for r, (f, z, _, y) in enumerate(listed):
                edges[f, z, y : y + 1, :] = packed[base + r // 8, r % 8 : r % 8 + 1, :]

    @pl.when(parity == (0 if first else 1))
    def _():
        side(True, has_lower)

    @pl.when(parity == (1 if first else 0))
    def _():
        side(False, has_upper)


def first_rows_kernel(cz, message, edges_in, edges, packed):
    unpack_rows(cz, edges.shape[2], True, message, packed, edges)


def start_kernel(
    cz, store, adjoint, lam, mu, buoy, source, wavelet, receiver, traces, plan, peer, slot,
    near_out, far_out, own, codes, cells, samples, spots, wave, steps, peers, slots, sems,
):
    cy, lanes = own.shape[2], own.shape[3]
    rows = cz * cy
    tiles = store.shape[0]
    small = copies(
        sems, (plan, steps), (wavelet, wave), (source, spots), (receiver, cells), (traces, samples),
        (peer, peers), (slot, slots),
    )
    large = copies(
        sems.at[pl.ds(len(small), 5)],
        (adjoint, own.at[pl.ds(0, 9)]),
        (buoy, own.at[BUOY - ADJ]),
        (lam, own.at[LAM - ADJ]),
        (mu, own.at[MU - ADJ]),
        (store, near_out.at[pl.ds(0, tiles)]),
    )
    for copy in small:
        copy.wait()
    lane = lax.broadcasted_iota(jnp.int32, (cy, lanes), 1)
    code = jnp.zeros((cy, lanes), jnp.int32)
    for z, hops, row in pieces(cz, peers, slots):
        code = jnp.where(lane == z, row * 4 + hops, code)
    codes[...] = code
    listed = cells[...]
    count = listed.shape[1]
    row_hot = (lax.broadcasted_iota(jnp.int32, (rows, count), 0) == listed // lanes).astype(jnp.float32)
    lane_hit = lax.broadcasted_iota(jnp.int32, (lanes, count), 0) == listed % lanes
    injected = []
    for step in (1, 0):
        sample = samples[pl.ds(steps[step], 1), :]
        field = lax.dot_general(
            row_hot,
            jnp.where(lane_hit, sample, 0.0),
            (((1,), (1,)), ((), ())),
            precision=lax.Precision.HIGHEST,
            preferred_element_type=jnp.float32,
        )
        injected.append(field.reshape(cz, cy, lanes))
    own[INJ - ADJ] = injected[1]
    flat = lax.broadcasted_iota(jnp.int32, (rows, lanes), 0) * lanes + lax.broadcasted_iota(jnp.int32, (rows, lanes), 1)
    for step in range(2):
        value = wave[steps[step]]
        field = jnp.zeros((rows, lanes), jnp.float32)
        for j in range(source.shape[1]):
            field = field + jnp.where(flat == spots[0, j], value, 0.0)
        own[SRC - ADJ + step] = field.reshape(cz, cy, lanes)
    for copy in large:
        copy.wait()
    for f in (SXX, SYY, SZZ):
        own[f] = own[f] + injected[0]

    even = even_mask("gz", (cy, lanes))
    near, far = face_counts(cz)
    up, down = faces(cz, True), faces(cz, False)
    zero = jnp.zeros((cy, lanes), jnp.float32)

    def tile(side, i):
        return own[side[i][0] - ADJ, side[i][1]] if i < len(side) else zero

    for i in range(near):
        above, below = tile(up[0], i), tile(down[0], i)
        for out, base, value in (
            (near_out, tiles, jnp.where(even, above, below)),
            (far_out, 0, jnp.where(even, below, above)),
        ):
            out[base + i], out[base + near + i] = split(value)
    for i in range(far):
        above, below = tile(up[1], i), tile(down[1], i)
        near_out[tiles + 2 * near + i] = jnp.where(even, above, below).astype(jnp.bfloat16)
        far_out[2 * near + i] = jnp.where(even, below, above).astype(jnp.bfloat16)
    for i in range(2 * near + far, far_out.shape[0]):
        far_out[i] = zero.astype(jnp.bfloat16)


def strip_part(tile, main, listed):
    lanes = tile.shape[1]
    lane = lax.broadcasted_iota(jnp.int32, tile.shape, 1)
    for z in listed:
        tile = jnp.where((lane >= 8 * z) & (lane < 8 * z + 4), pltpu.roll(main(z), (8 * z + 2) % lanes, 1), tile)
    return tile


def strip_whole(tile):
    position = lax.broadcasted_iota(jnp.int32, tile.shape, 1) % 8
    return jnp.where(position < 2, tile, jnp.where(position >= 6, pltpu.roll(tile, 4, 1), 0.0))


def pieces(cz, peers, slots):
    me, count = lax.axis_index("gz"), lax.axis_size("gz")
    below, above = jnp.maximum(me - 1, 0), jnp.minimum(me + 1, count - 1)
    for z in range(cz + 2 * HALO):
        if z < HALO:
            brick, piece = below, cz - HALO + z
        elif z < HALO + cz:
            brick, piece = me, z - HALO
        else:
            brick, piece = above, z - HALO - cz
        yield z, peers[brick, piece] ^ me, slots[brick, piece] * 9


def coded(cz, codes):
    has_below, has_above = has_neighbours("gz")
    listed = codes[0:1, :]
    for z in range(cz + 2 * HALO):
        code = listed[0, z]
        keep = has_below if z < HALO else None if z < HALO + cz else has_above
        yield z, code & 3, code >> 2, keep


def frame_kernel(cz, mine, core, chip, codes, own, ring_f, ring):
    cy, lanes = own.shape[2], own.shape[3]
    layers = cz + 2 * HALO
    zero = jnp.zeros((cy, lanes), jnp.float32)
    filled = {(f - ADJ, z) for up in (True, False) for listed in faces(cz, up) for f, _, z in listed}
    for f in range(ring.shape[0]):
        for z in range(cz):
            ring[f, HALO + z] = own[f, z]
        for z in (0, 1, layers - 2, layers - 1):
            if (f, z) not in filled:
                ring[f, z] = zero
        ring[f, layers] = strip_part(zero, lambda z: own[f, z - HALO], range(HALO, HALO + cz))
    for z, hops, row, keep in coded(cz, codes):
        hops = jnp.full((cy, lanes), hops, jnp.int32)
        for f in range(9):
            a, b, c = (ref[row + f].astype(jnp.float32) for ref in (mine, core, chip))
            value = jnp.where(hops == 0, a, jnp.where(hops == 1, b, c))
            ring_f[f, z] = value if keep is None else value * keep


def column_kernel(
    cz, core, both_a, both_b, far, codes, ring_f_in, ring_w_in, ring_f, ring, x_a, x_b
):
    cy, lanes = core.shape[1], core.shape[2]
    layers = cz + 2 * HALO
    half = both_a.shape[0]
    tiles = half + both_b.shape[0]
    near, _ = face_counts(cz)
    even = even_mask("gz", (cy, lanes))
    has_below, has_above = has_neighbours("gz")
    zero = jnp.zeros((cy, lanes), jnp.float32)
    filled = {}
    for up in (True, False):
        for depth, listed in enumerate(faces(cz, up)):
            for i, (f, _, z) in enumerate(listed):
                values = []
                for ref, base in ((core, tiles), (far, 0)):
                    if depth == 0:
                        values.append(joined(ref[base + i], ref[base + near + i]))
                    else:
                        values.append(ref[base + 2 * near + i].astype(jnp.float32))
                value = jnp.where(even, values[1], values[0]) if up else jnp.where(even, values[0], values[1])
                value = value * (has_below if up else has_above)
                ring[f - ADJ, z] = value
                filled.setdefault(f - ADJ, {})[z] = value
    strip = []
    for f in range(ring.shape[0]):
        there = filled.get(f, {})
        tile = strip_whole(strip_part(ring[f, layers], lambda z: there[z], sorted(there)))
        ring[f, layers] = tile
        strip.append(tile)
    for z, hops, row, keep in coded(cz, codes):
        last = jnp.full((cy, lanes), hops, jnp.int32) == 3
        late = jnp.full((cy, lanes), row, jnp.int32) >= half
        row_a, row_b = jnp.minimum(row, half - 9), jnp.maximum(row - half, 0)
        for f in range(9):
            a, b = both_a[row_a + f].astype(jnp.float32), both_b[row_b + f].astype(jnp.float32)
            value = jnp.where(late, b, a)
            ring_f[f, z] = jnp.where(last, value if keep is None else value * keep, ring_f[f, z])
    for f in range(9):
        ring_f[f, layers] = strip_whole(strip_part(zero, lambda z: ring_f[f, z], range(layers)))
    strip = [ring_f[f, layers] for f in range(9)] + strip
    position = lax.broadcasted_iota(jnp.int32, (cy, lanes), 1) % 8
    even_x = even_mask("gx", (cy, lanes))
    for out, tail_from_even in ((x_a, True), (x_b, False)):
        if out is None:
            continue
        place = 0
        for fields, narrow in ((range(ADJ), True), (range(ADJ, FIELDS), False)):
            quads = [fields[i : i + 4] for i in range(0, len(fields), 4)]
            for i, quad in enumerate(quads):
                tile = zero
                for g, f in enumerate(quad):
                    tail, head = strip[f], pltpu.roll(strip[f], lanes - 6, 1)
                    value = jnp.where(even_x, tail, head) if tail_from_even else jnp.where(even_x, head, tail)
                    value = value if g == 0 else pltpu.roll(value, 2 * g, 1)
                    tile = jnp.where(position // 2 == g, value, tile)
                high, low = split(tile)
                out[place + i] = high
                if not narrow:
                    out[place + len(quads) + i] = low
            place += len(quads) if narrow else 2 * len(quads)


def x_tiles():
    return -(-ADJ // 4) + 2 * -(-(FIELDS - ADJ) // 4)


def strip_rows_kernel(cz, ring_f, ring_w, x_a, x_b, y_a_in, y_b_in, strips, y_a, y_b, packed):
    cy, lanes = strips.shape[1], strips.shape[2]
    layers = cz + 2 * HALO
    pair = lax.broadcasted_iota(jnp.int32, (cy, lanes), 1) % 8 // 2
    even_x = even_mask("gx", (cy, lanes))
    has_left, has_right = has_neighbours("gx")
    zero = jnp.zeros((cy, lanes), jnp.float32)
    place = 0
    for fields, narrow in ((range(ADJ), True), (range(ADJ, FIELDS), False)):
        quads = [fields[i : i + 4] for i in range(0, len(fields), 4)]
        for i, quad in enumerate(quads):
            got = []
            for ref in (x_a, x_b):
                if ref is None:
                    got.append(zero)
                elif narrow:
                    got.append(ref[place + i].astype(jnp.float32))
                else:
                    got.append(joined(ref[place + i], ref[place + len(quads) + i]))
            right = jnp.where(even_x, got[0], got[1]) * has_right
            left = jnp.where(even_x, got[1], got[0]) * has_left
            for g, f in enumerate(quad):
                strip = ring_f[f, layers] if f < ADJ else ring_w[f - ADJ, layers]
                tile = jnp.where(pair == 1, pltpu.roll(right, (2 - 2 * g) % lanes, 1), strip)
                strips[f] = jnp.where(pair == 2, pltpu.roll(left, (4 - 2 * g) % lanes, 1), tile)
        place += len(quads) if narrow else 2 * len(quads)
    sides = []
    for side, up in enumerate((True, False)):
        scatter_rows(packed.at[side], y_rows(cz, cy, up)[2], lambda f, z, y: strips[f, y : y + 1, :])
        sides.append([packed[side, t] for t in range(row_counts(cz, cy, up)[2])])
    pack_tiles(sides, (y_a, y_b), 0, packed.shape[1])


STAGE = {"fv": 0, "fs": 3, "fw": 9, "as": 12, "av": 18, "at": 21}
STAGES = 27
NORMAL = (SXX, SYY, SZZ)
STRESS = range(SXX, SYZ + 1)


def window(cz, base, stage, after, before, put):
    layers = cz + 2 * HALO
    edge = layers
    cy, lanes = stage.shape[2], stage.shape[3]
    lane = lax.broadcasted_iota(jnp.int32, (cy, lanes), 1)
    first_lane, last_lane = lane == 0, lane == lanes - 1
    inner = range(HALO, HALO + cz)

    def start(field):
        return lambda z: base(field, z)

    def kept(name, field):
        index = STAGE[name] + field
        return lambda z: stage[index, z]

    def x_next(of, z):
        value = pltpu.roll(of(z), lanes - 1, 1)
        if z == edge:
            return value
        return jnp.where(last_lane, pltpu.roll(of(edge), (lanes - 1 - (8 * z + 2)) % lanes, 1), value)

    def x_prev(of, z):
        value = pltpu.roll(of(z), 1, 1)
        if z == edge:
            return value
        return jnp.where(first_lane, pltpu.roll(of(edge), (lanes - (8 * z + 5)) % lanes, 1), value)

    def z_next(of, z):
        return pltpu.roll(of(edge), lanes - 8, 1) if z == edge else of(z + 1)

    def z_prev(of, z):
        return pltpu.roll(of(edge), 8, 1) if z == edge else of(z - 1)

    def velocity_rates(k, s, z, want):
        buoy = base(BUOY, z)
        sxx, syy, szz, sxy, sxz, syz = s
        out = {}
        if VX in want:
            xy = sxy(z)
            out[VX] = buoy * (
                (x_next(sxx, z) - sxx(z)) + (xy - before(k, 0, z, xy)) + (sxz(z) - z_prev(sxz, z))
            )
        if VY in want:
            yy = syy(z)
            out[VY] = buoy * (
                (sxy(z) - x_prev(sxy, z)) + (after(k, 1, z, yy) - yy) + (syz(z) - z_prev(syz, z))
            )
        if VZ in want:
            yz = syz(z)
            out[VZ] = buoy * (
                (sxz(z) - x_prev(sxz, z)) + (yz - before(k, 2, z, yz)) + (z_next(szz, z) - szz(z))
            )
        return out

    def stress_rates(k, v, z, want):
        lam, mu = base(LAM, z), base(MU, z)
        of_x, of_y, of_z = v
        vx, vy, vz = of_x(z), of_y(z), of_z(z)
        out = {}
        if SXX in want:
            exx = vx - x_prev(of_x, z)
            eyy = vy - before(k, 0, z, vy)
            ezz = vz - z_prev(of_z, z)
            common = lam * (exx + eyy + ezz)
            twice = 2.0 * mu
            out[SXX] = common + twice * exx
            out[SYY] = common + twice * eyy
            out[SZZ] = common + twice * ezz
        if SXY in want:
            out[SXY] = mu * ((after(k, 1, z, vx) - vx) + (x_next(of_y, z) - vy))
        if SXZ in want:
            out[SXZ] = mu * ((z_next(of_x, z) - vx) + (x_next(of_z, z) - vz))
            out[SYZ] = mu * ((z_next(of_y, z) - vy) + (after(k, 2, z, vz) - vz))
        return out

    def spread(ranges):
        for z in range(layers + 1):
            want = {f for f, (a, b) in ranges.items() if z == edge or a <= z < b}
            if want:
                yield z, want

    def velocity_step(k, name, v, s, sign, ranges):
        for z, want in spread(ranges):
            for f, rate in velocity_rates(k, s, z, want).items():
                stage[STAGE[name] + f, z] = v[f](z) + rate if sign > 0 else v[f](z) - rate
        return [kept(name, f) for f in (VX, VY, VZ)]

    def stress_step(k, name, v, s, sign, ranges, ahead=None, behind=None):
        for z, want in spread(ranges):
            for f, rate in stress_rates(k, v, z, want).items():
                value = s[f - SXX](z)
                if ahead is not None and f in NORMAL:
                    value = value + base(ahead, z)
                value = value + rate if sign > 0 else value - rate
                if behind is not None and f in NORMAL:
                    value = value + base(behind, z)
                stage[STAGE[name] + f - SXX, z] = value
        return [kept(name, f - SXX) for f in STRESS]

    def terms(f, a):
        term_lam = (f[0] + f[1] + f[2]) * (a[0] + a[1] + a[2])
        term_mu = f[0] * a[0] + f[1] * a[1] + f[2] * a[2] + 2.0 * (f[3] * a[3] + f[4] * a[4] + f[5] * a[5])
        return term_lam, term_mu

    n = layers
    fv, fs = [start(FWD + f) for f in (VX, VY, VZ)], [start(FWD + f) for f in STRESS]
    av, first = [start(ADJ + f) for f in (VX, VY, VZ)], [start(ADJ + f) for f in STRESS]
    a_s = stress_step(0, "as", av, first, -1, {SXX: (1, n), SXY: (0, n), SXZ: (0, n - 1)})
    fv = velocity_step(1, "fv", fv, fs, 1, {VX: (1, n), VY: (1, n), VZ: (0, n - 1)})
    fs = stress_step(2, "fs", fv, fs, 1, {SXX: (1, n - 1), SXY: (1, n - 1), SXZ: (1, n - 1)}, behind=SRC)
    fv = velocity_step(3, "fw", fv, fs, 1, {VX: (2, n - 1), VY: (2, n - 1), VZ: (1, n - 2)})
    for z in inner:
        rates = stress_rates(4, fv, z, set(STRESS))
        now = [of(z) for of in fs]
        later = [now[s - SXX] + rates[s] + (base(FIELDS, z) if s in NORMAL else 0.0) for s in STRESS]
        lam_late, mu_late = terms(later, [of(z) for of in first])
        with_traces = [of(z) + (base(INJ, z) if s in NORMAL else 0.0) for s, of in zip(STRESS, a_s)]
        lam_early, mu_early = terms(now, with_traces)
        put(9, z - HALO, lam_late + lam_early)
        put(10, z - HALO, mu_late + mu_early)
    av = velocity_step(5, "av", av, a_s, -1, {VX: (1, n - 1), VY: (1, n - 1), VZ: (1, n - 1)})
    a_s = stress_step(6, "at", av, a_s, -1, {SXX: (2, n - 1), SXY: (1, n - 1), SXZ: (1, n - 2)}, ahead=INJ)
    for s, of in zip(STRESS, a_s):
        for z in inner:
            put(s, z - HALO, of(z))
    for z in inner:
        rates = velocity_rates(7, a_s, z, {VX, VY, VZ})
        for f in (VX, VY, VZ):
            put(f, z - HALO, av[f](z) - rates[f])


def middle_kernel(cz, ring_f, ring_w, strips, own, edges, sides, middle, stage):
    cy, lanes = own.shape[2], own.shape[3]
    layers = cz + 2 * HALO

    def base(f, z):
        if f == FIELDS:
            return own[f - ADJ, z - HALO]
        if z == layers:
            return strips[f]
        return ring_f[f, z] if f < ADJ else ring_w[f - ADJ, z]

    row = lax.broadcasted_iota(jnp.int32, (cy, lanes), 0)
    for f in range(FIELDS + 1):
        for z in range(HALO, HALO + cz) if f == FIELDS else range(layers + 1):
            tile = base(f, z)
            tail, head = pltpu.roll(tile, HALO, 0), pltpu.roll(tile, cy - HALO, 0)
            edges[f, z] = jnp.where(row < HALO, tail, jnp.where(row >= cy - HALO, head, 0.0))

    def after(k, j, z, tile):
        sides[k, j, z] = pltpu.roll(tile, cy - 1 - HALO, 0)
        return pltpu.roll(tile, cy - 1, 0)

    def before(k, j, z, tile):
        sides[k, j, z] = pltpu.roll(tile, HALO + 1, 0)
        return pltpu.roll(tile, 1, 0)

    def put(i, z, value):
        middle[i, z] = value

    window(cz, base, stage, after, before, put)


def edge_kernel(
    cz, edges_in, sides, middle, message, final, image_lam, image_mu, edges, packed, stage, result, sems
):
    cy, lanes = middle.shape[2], middle.shape[3]

    unpack_rows(cz, cy, False, message, packed, edges)
    row = lax.broadcasted_iota(jnp.int32, (cy, lanes), 0)

    def after(k, j, z, tile):
        return jnp.where(row == cy - 1, sides[k, j, z], pltpu.roll(tile, cy - 1, 0))

    def before(k, j, z, tile):
        return jnp.where(row == 0, sides[k, j, z], pltpu.roll(tile, 1, 0))

    moves = []

    def put(i, z, value):
        tail, head = pltpu.roll(value, HALO, 0), pltpu.roll(value, cy - HALO, 0)
        result[i, z] = jnp.where(row < HALO, tail, jnp.where(row >= cy - HALO, head, middle[i, z]))
        if z == cz - 1:
            if i == 10:
                moves.extend(copies(sems, (result.at[9], image_lam), (result.at[10], image_mu)))
            if i == SYZ:
                part = pl.ds(SXX, SYZ + 1 - SXX)
                moves.extend(copies(sems.at[pl.ds(2, 1)], (result.at[part], final.at[part])))
            if i == VZ:
                part = pl.ds(VX, VZ + 1 - VX)
                moves.extend(copies(sems.at[pl.ds(3, 1)], (result.at[part], final.at[part])))

    window(cz, lambda f, z: edges[f, z], stage, after, before, put)
    for move in moves:
        move.wait()


def swap_pairs(count, first):
    pairs = [(i + d, i + 1 - d) for i in range(first, count - 1, 2) for d in (0, 1)]
    return pairs + [(i, i) for i in range(count) if i not in dict(pairs)]


def swapped(value_a, value_b, axis):
    count = lax.axis_size(axis)
    got_a = lax.ppermute(value_a, axis, swap_pairs(count, 0))
    return got_a, None if value_b is None else lax.ppermute(value_b, axis, swap_pairs(count, 1))


def stay(value, spec):
    return pltpu.with_memory_space_constraint(value, pltpu.HBM) if spec.memory_space == pl.ANY else value


def kernel_call(body, args, in_specs, out_shape, scratch_shapes=(), aliases=None, out_specs=None):
    here = [a is not None for a in args]
    there = [o is not None for o in out_shape]

    def run(*refs):
        refs = iter(refs)
        full = [next(refs) if h else None for h in here + there]
        body(*full, *refs)

    out = iter(
        pl.pallas_call(
            run,
            out_shape=tuple(o for o in out_shape if o is not None),
            in_specs=[s for s, h in zip(in_specs, here) if h],
            out_specs=out_specs or tuple(vmem() for h in there if h),
            scratch_shapes=list(scratch_shapes),
            input_output_aliases=aliases or {},
            compiler_params=pltpu.CompilerParams(vmem_limit_bytes=VMEM_LIMIT),
        )(*[stay(a, s) for a, s in zip(args, in_specs) if a is not None])
    )
    return tuple(next(out) if h else None for h in there)


def on_device(
    checkpoint_store,
    holder_peer,
    holder_slot,
    adjoint_state,
    lame_lambda,
    lame_mu,
    buoyancy,
    source_cell,
    wavelet,
    receiver_cell,
    traces,
    plan,
):
    cz, cy, cx = lame_mu.shape
    layers = cz + 2 * HALO
    bf16, f32 = jnp.bfloat16, jnp.float32
    store = checkpoint_store.reshape(-1, cy, cx)
    tiles = store.shape[0]
    peer, slot = holder_peer[0, 0], holder_slot[0, 0]
    source, receiver = source_cell.reshape(1, -1), receiver_cell.reshape(1, -1)
    traces = traces.reshape(traces.shape[-2:])
    holders = lax.axis_size("gz")
    assert holders == 4
    near, far = face_counts(cz)
    face = 2 * near + far
    half = tiles // 2

    def shape(*dims, dtype=f32):
        return jax.ShapeDtypeStruct(dims, dtype)

    wide_x = lax.axis_size("gx") > 2
    chip = lax.ppermute(store, "gz", [(i, i ^ 2) for i in range(holders)])
    to_core, to_far, own, codes = kernel_call(
        functools.partial(start_kernel, cz),
        (store, adjoint_state, lame_lambda, lame_mu, buoyancy, source, wavelet, receiver, traces, plan, peer, slot),
        [hbm()] * 12,
        (shape(tiles + face, cy, cx, dtype=bf16), shape(max(face, half) + PAD, cy, cx, dtype=bf16), shape(15, cz, cy, cx),
         shape(cy, cx, dtype=jnp.int32)),
        [
            pltpu.VMEM(receiver.shape, jnp.int32),
            pltpu.VMEM(traces.shape, f32),
            pltpu.SMEM(source.shape, jnp.int32),
            pltpu.SMEM(wavelet.shape, f32),
            pltpu.SMEM(plan.shape, jnp.int32),
            pltpu.SMEM(peer.shape, jnp.int32),
            pltpu.SMEM(slot.shape, jnp.int32),
            pltpu.SemaphoreType.DMA((12,)),
        ],
    )
    core = lax.ppermute(to_core, "gz", [(i, i ^ 1) for i in range(holders)])
    gy = lax.axis_size("gy")
    across = {
        (i, c): (i, 3 - c) if c in (1, 2) else (i ^ 1, c)
        for i in range(gy) for c in range(holders)
    }
    far_face = lax.ppermute(
        to_far, ("gy", "gz"), [(a[0] * holders + a[1], b[0] * holders + b[1]) for a, b in across.items()]
    )
    both = [lax.ppermute(part, "gz", [(i, i ^ 1) for i in range(holders)]) for part in (chip[:half], chip[half:])]

    ring_f, ring_w = kernel_call(
        functools.partial(frame_kernel, cz),
        (to_core, core, chip, codes, own),
        [vmem()] * 5,
        (shape(ADJ, layers + 1, cy, cx), shape(FIELDS - ADJ, layers + 1, cy, cx)),
    )
    x_send = shape(x_tiles(), cy, cx, dtype=bf16)
    ring_f, ring_w, x_a, x_b = kernel_call(
        functools.partial(column_kernel, cz),
        (core, *both, far_face, codes, ring_f, ring_w),
        [vmem()] * 7,
        (shape(*ring_f.shape), shape(*ring_w.shape), x_send, x_send if wide_x else None),
        (),
        {5: 0, 6: 1},
    )
    axes = ("gx", "gy", "gz")
    gx = lax.axis_size("gx")

    def partner(i, j, c, x_turn, y_turn):
        if x_turn is not None:
            i = dict(swap_pairs(gx, x_turn))[i]
        if y_turn is not None:
            other = dict(swap_pairs(gy, (c + y_turn + 1) % 2))[j]
            i, j = (i ^ 1, j) if other == j else (i, other)
        return (i * gy + j) * holders + c

    def swap(value, x_turn, y_turn):
        if value is None:
            return None
        pairs = [
            ((i * gy + j) * holders + c, partner(i, j, c, x_turn, y_turn))
            for i in range(gx) for j in range(gy) for c in range(holders)
        ]
        return lax.ppermute(value, axes, pairs)

    strip_tiles, tiles = row_tiles(cz, cy)
    y_send = shape(strip_tiles + tiles, cy, cx, dtype=bf16)
    scratch_tiles = max(sum(row_counts(cz, cy, up)) for up in (True, False))
    y_a, y_b = kernel_call(
        functools.partial(layer_rows_kernel, cz),
        (ring_f, ring_w),
        [vmem()] * 2,
        (y_send, y_send),
        [pltpu.VMEM((2, scratch_tiles, 8, cx), f32)],
    )
    strips, y_a, y_b = kernel_call(
        functools.partial(strip_rows_kernel, cz),
        (ring_f, ring_w, swap(x_a, 0, None), swap(x_b, 1, None), y_a, y_b),
        [vmem()] * 6,
        (shape(FIELDS, cy, cx), y_send, y_send),
        [pltpu.VMEM((2, strip_tiles, 8, cx), f32)],
        {4 if wide_x else 3: 1, 5 if wide_x else 4: 2},
    )
    edges, sides, middle = kernel_call(
        functools.partial(middle_kernel, cz),
        (ring_f, ring_w, strips, own),
        [vmem()] * 4,
        (
            shape(FIELDS + 1, layers + 1, cy, cx),
            shape(8, 3, layers + 1, cy, cx),
            shape(11, cz, cy, cx),
        ),
        [pltpu.VMEM((STAGES, layers + 1, cy, cx), f32)],
    )
    row_scratch = pltpu.VMEM((scratch_tiles, 8, cx), f32)
    (edges,) = kernel_call(
        functools.partial(first_rows_kernel, cz),
        (swap(y_a, None, 0), edges),
        [vmem()] * 2,
        (shape(*edges.shape),),
        [row_scratch],
        {1: 0},
    )
    result = kernel_call(
        functools.partial(edge_kernel, cz),
        (edges, sides, middle, swap(y_b, None, 1)),
        [vmem()] * 4,
        (shape(9, cz, cy, cx), shape(cz, cy, cx), shape(cz, cy, cx), shape(*edges.shape)),
        [
            row_scratch,
            pltpu.VMEM((STAGES, layers + 1, cy, cx), f32),
            pltpu.VMEM((11, cz, cy, cx), f32),
            pltpu.SemaphoreType.DMA((4,)),
        ],
        {0: 3},
        (hbm(),) * 3 + (vmem(),),
    )
    return result[:3]


def solution(mesh):
    return jax.shard_map(
        on_device,
        mesh=mesh,
        in_specs=(
            P("gz", None, None, "gy", "gx"),
            P("gx", "gy", None, None),
            P("gx", "gy", None, None),
            P(None, "gz", "gy", "gx"),
            P("gz", "gy", "gx"),
            P("gz", "gy", "gx"),
            P("gz", "gy", "gx"),
            P("gz", "gy", "gx", None),
            P(),
            P("gz", "gy", "gx", None),
            P("gz", "gy", "gx", None, None),
            P(),
        ),
        out_specs=(P(None, "gz", "gy", "gx"), P("gz", "gy", "gx"), P("gz", "gy", "gx")),
        check_vma=False,
    )
```

```python
import functools

import jax
import jax.numpy as jnp
from jax import lax
from jax.experimental import pallas as pl
from jax.experimental.pallas import tpu as pltpu
from jax.sharding import PartitionSpec as P

VX, VY, VZ, SXX, SYY, SZZ, SXY, SXZ, SYZ = range(9)
FWD, ADJ, BUOY, LAM, MU, INJ, SRC = 0, 9, 18, 19, 20, 21, 22
FIELDS = 23
HALO = 2

ADJ_Z = {VX: (2, 2), VY: (2, 2), VZ: (2, 2), SXX: (1, 1), SYY: (1, 1), SZZ: (1, 2), SXY: (1, 1), SXZ: (2, 1), SYZ: (2, 1)}
OTHER_Z = {BUOY: (2, 2), LAM: (1, 2), MU: (2, 2), INJ: (0, 1), SRC: (1, 1)}
F32_Z = {**{ADJ + f: c for f, c in ADJ_Z.items()}, **OTHER_Z}

Y_ROWS = {
    FWD + VX: (None, (2, -1, 1), (1, -1, 1), (2, -2, 0)),
    FWD + VY: ((2, -2, 0), (1, -1, 1), (2, -1, 1), None),
    FWD + VZ: (None, (1, -2, 1), (1, -1, 1), (2, -2, 0)),
    FWD + SXX: (None, (2, -1, 1), (1, -1, 1), (2, -2, 1)),
    FWD + SYY: ((2, -2, 0), (1, -1, 1), (1, 0, 1), (2, -1, 1)),
    FWD + SZZ: (None, (1, -1, 1), (1, 0, 1), (2, -1, 0)),
    FWD + SXY: ((2, -1, 1), (1, 0, 1), (1, -1, 1), (2, -2, 0)),
    FWD + SXZ: (None, (1, -1, 1), (0, -1, 1), (1, -2, 1)),
    FWD + SYZ: ((1, -2, 1), (0, -1, 1), (1, -1, 1), (2, -2, 0)),
    ADJ + VX: ((2, -2, 0), (1, -1, 1), (1, -1, 1), (2, -2, 1)),
    ADJ + VY: ((2, -1, 1), (1, 0, 1), (1, -1, 1), (2, -2, 0)),
    ADJ + VZ: ((2, -2, 0), (1, -1, 1), (0, -1, 1), (1, -2, 0)),
    ADJ + SXX: (None, (2, -2, 1), (2, -2, 1), None),
    ADJ + SYY: (None, (2, -1, 1), (1, -1, 1), (2, -2, 0)),
    ADJ + SZZ: (None, (2, -1, 0), (1, -1, 0), None),
    ADJ + SXY: ((2, -2, 0), (1, -1, 1), (2, -2, 1), None),
    ADJ + SXZ: (None, (1, -2, 1), (1, -2, 1), None),
    ADJ + SYZ: ((2, -2, 0), (1, -1, 1), (1, -2, 0), None),
    BUOY: ((2, -2, 0), (1, -1, 1), (1, -1, 1), (2, -2, 0)),
    LAM: (None, (2, -1, 1), (1, -1, 1), (2, -2, 0)),
    MU: ((2, -2, 0), (1, -1, 1), (1, -1, 1), (2, -2, 0)),
    INJ: (None, None, (2, -2, 0), None),
    SRC: (None, (2, -2, 0), (2, -1, 1), None),
}

EXACT_ROWS = {-1: (ADJ + VY, ADJ + SXY, ADJ + SYZ, BUOY, SRC), 0: (ADJ + SYY, LAM, INJ, SRC)}

PAD = 1
VMEM_LIMIT = 48 * 1024 * 1024


def vmem():
    return pl.BlockSpec(memory_space=pltpu.VMEM)


def hbm():
    return pl.BlockSpec(memory_space=pl.ANY)


def faces(cz, up):
    near, far = [], []
    for f in sorted(F32_Z):
        before, after = F32_Z[f]
        depth = before if up else after
        for d in range(depth):
            layer = cz - 1 - d if up else d
            (far if d else near).append((f, layer, HALO - 1 - d if up else HALO + cz + d))
    return near, far


def face_counts(cz):
    sides = [faces(cz, up) for up in (True, False)]
    return max(len(s[0]) for s in sides), max(len(s[1]) for s in sides)


def y_rows(cz, cy, up):
    layers = cz + 2 * HALO
    narrow, wide, strip = [], [], []
    for f in sorted(Y_ROWS):
        for offset in (-1, -2) if up else (0, 1):
            spec = Y_ROWS[f][offset + HALO]
            if spec is None:
                continue
            source = cy + offset if up else offset
            target = cy - HALO + offset if up else HALO + offset
            exact = f in EXACT_ROWS.get(offset, ())
            (wide if exact else narrow).extend((f, z, source, target) for z in range(spec[0], layers + spec[1]))
            if spec[2]:
                strip.append((f, layers, source, target))
    return narrow, wide, strip


def row_counts(cz, cy, up):
    return tuple(-(-len(rows) // 8) for rows in y_rows(cz, cy, up))


def row_tiles(cz, cy):
    sides = [row_counts(cz, cy, up) for up in (True, False)]
    return max(c for _, _, c in sides), max(n + 2 * w for n, w, _ in sides)


def split(value):
    high = value.astype(jnp.bfloat16)
    low = (value - high.astype(jnp.float32)).astype(jnp.bfloat16)
    return high, low


def joined(high, low):
    return high.astype(jnp.float32) + low.astype(jnp.float32)


def even_mask(axes, shape):
    total = sum(lax.axis_index(a) for a in ((axes,) if isinstance(axes, str) else axes))
    return jnp.full(shape, lax.rem(total, 2), jnp.int32) == 0


def has_neighbours(axis):
    index = lax.axis_index(axis)
    return (index > 0).astype(jnp.float32), (index < lax.axis_size(axis) - 1).astype(jnp.float32)


def copies(sems, *pairs):
    out = [pltpu.make_async_copy(source, target, sems.at[i]) for i, (source, target) in enumerate(pairs)]
    for copy in out:
        copy.start()
    return out


def scatter_rows(packed, listed, row_of):
    for r, (f, z, y, _) in enumerate(listed):
        packed[r // 8, r % 8 : r % 8 + 1, :] = row_of(f, z, y)


def pack_tiles(sides, sends, first, count):
    even = even_mask(("gy", "gz"), sends[0].shape[1:])
    for t in range(count):
        up, down = (side[min(t, len(side) - 1)] for side in sides)
        sends[0][first + t] = jnp.where(even, down, up).astype(jnp.bfloat16)
        sends[1][first + t] = jnp.where(even, up, down).astype(jnp.bfloat16)


def layer_rows_kernel(cz, ring_f, ring_w, send_a, send_b, packed):
    cy = ring_f.shape[2]
    strip_tiles, tiles = row_tiles(cz, cy)

    def row_of(f, z, y):
        return ring_f[f, z, y : y + 1, :] if f < ADJ else ring_w[f - ADJ, z, y : y + 1, :]

    sides = []
    for side, up in enumerate((True, False)):
        narrow, wide, _ = y_rows(cz, cy, up)
        n, w, _ = row_counts(cz, cy, up)
        scatter_rows(packed.at[side], narrow, row_of)
        scatter_rows(packed.at[side, pl.ds(n, w)], wide, row_of)
        rest = [split(packed[side, n + t])[1].astype(jnp.float32) for t in range(w)]
        sides.append([packed[side, t] for t in range(n + w)] + rest)
    pack_tiles(sides, (send_a, send_b), strip_tiles, tiles)


def unpack_rows(cz, cy, first, message, packed, edges):
    has_lower, has_upper = has_neighbours("gy")
    strip_tiles, _ = row_tiles(cz, cy)
    parity = lax.rem(lax.axis_index("gy") + lax.axis_index("gz"), 2)

    def side(up, keep):
        narrow, wide, strip = y_rows(cz, cy, up)
        n, w, c = row_counts(cz, cy, up)
        for t in range(n + w):
            value = message[strip_tiles + t].astype(jnp.float32)
            if t >= n:
                value = value + message[strip_tiles + w + t].astype(jnp.float32)
            packed[t] = value * keep
        for t in range(c):
            packed[n + w + t] = message[t].astype(jnp.float32) * keep
        for base, listed in ((0, narrow), (n, wide), (n + w, strip)):
            for r, (f, z, _, y) in enumerate(listed):
                edges[f, z, y : y + 1, :] = packed[base + r // 8, r % 8 : r % 8 + 1, :]

    @pl.when(parity == (0 if first else 1))
    def _():
        side(True, has_lower)

    @pl.when(parity == (1 if first else 0))
    def _():
        side(False, has_upper)


def first_rows_kernel(cz, message, edges_in, edges, packed):
    unpack_rows(cz, edges.shape[2], True, message, packed, edges)


def start_kernel(
    cz, store, adjoint, lam, mu, buoy, source, wavelet, receiver, traces, plan, peer, slot,
    near_out, far_out, own, codes, cells, samples, spots, wave, steps, peers, slots, sems,
):
    cy, lanes = own.shape[2], own.shape[3]
    rows = cz * cy
    tiles = store.shape[0]
    small = copies(
        sems, (plan, steps), (wavelet, wave), (source, spots), (receiver, cells), (traces, samples),
        (peer, peers), (slot, slots),
    )
    large = copies(
        sems.at[pl.ds(len(small), 5)],
        (adjoint, own.at[pl.ds(0, 9)]),
        (buoy, own.at[BUOY - ADJ]),
        (lam, own.at[LAM - ADJ]),
        (mu, own.at[MU - ADJ]),
        (store, near_out.at[pl.ds(0, tiles)]),
    )
    for copy in small:
        copy.wait()
    lane = lax.broadcasted_iota(jnp.int32, (cy, lanes), 1)
    code = jnp.zeros((cy, lanes), jnp.int32)
    for z, hops, row in pieces(cz, peers, slots):
        code = jnp.where(lane == z, row * 4 + hops, code)
    codes[...] = code
    listed = cells[...]
    count = listed.shape[1]
    row_hot = (lax.broadcasted_iota(jnp.int32, (rows, count), 0) == listed // lanes).astype(jnp.float32)
    lane_hit = lax.broadcasted_iota(jnp.int32, (lanes, count), 0) == listed % lanes
    injected = []
    for step in (1, 0):
        sample = samples[pl.ds(steps[step], 1), :]
        field = lax.dot_general(
            row_hot,
            jnp.where(lane_hit, sample, 0.0),
            (((1,), (1,)), ((), ())),
            precision=lax.Precision.HIGHEST,
            preferred_element_type=jnp.float32,
        )
        injected.append(field.reshape(cz, cy, lanes))
    own[INJ - ADJ] = injected[1]
    flat = lax.broadcasted_iota(jnp.int32, (rows, lanes), 0) * lanes + lax.broadcasted_iota(jnp.int32, (rows, lanes), 1)
    for step in range(2):
        value = wave[steps[step]]
        field = jnp.zeros((rows, lanes), jnp.float32)
        for j in range(source.shape[1]):
            field = field + jnp.where(flat == spots[0, j], value, 0.0)
        own[SRC - ADJ + step] = field.reshape(cz, cy, lanes)
    for copy in large:
        copy.wait()
    for f in (SXX, SYY, SZZ):
        own[f] = own[f] + injected[0]

    even = even_mask("gz", (cy, lanes))
    near, far = face_counts(cz)
    up, down = faces(cz, True), faces(cz, False)
    zero = jnp.zeros((cy, lanes), jnp.float32)

    def tile(side, i):
        return own[side[i][0] - ADJ, side[i][1]] if i < len(side) else zero

    for i in range(near):
        above, below = tile(up[0], i), tile(down[0], i)
        for out, base, value in (
            (near_out, tiles, jnp.where(even, above, below)),
            (far_out, 0, jnp.where(even, below, above)),
        ):
            out[base + i], out[base + near + i] = split(value)
    for i in range(far):
        above, below = tile(up[1], i), tile(down[1], i)
        near_out[tiles + 2 * near + i] = jnp.where(even, above, below).astype(jnp.bfloat16)
        far_out[2 * near + i] = jnp.where(even, below, above).astype(jnp.bfloat16)
    for i in range(2 * near + far, far_out.shape[0]):
        far_out[i] = zero.astype(jnp.bfloat16)


def strip_part(tile, main, listed):
    lanes = tile.shape[1]
    lane = lax.broadcasted_iota(jnp.int32, tile.shape, 1)
    for z in listed:
        tile = jnp.where((lane >= 8 * z) & (lane < 8 * z + 4), pltpu.roll(main(z), (8 * z + 2) % lanes, 1), tile)
    return tile


def strip_whole(tile):
    position = lax.broadcasted_iota(jnp.int32, tile.shape, 1) % 8
    return jnp.where(position < 2, tile, jnp.where(position >= 6, pltpu.roll(tile, 4, 1), 0.0))


def pieces(cz, peers, slots):
    me, count = lax.axis_index("gz"), lax.axis_size("gz")
    below, above = jnp.maximum(me - 1, 0), jnp.minimum(me + 1, count - 1)
    for z in range(cz + 2 * HALO):
        if z < HALO:
            brick, piece = below, cz - HALO + z
        elif z < HALO + cz:
            brick, piece = me, z - HALO
        else:
            brick, piece = above, z - HALO - cz
        yield z, peers[brick, piece] ^ me, slots[brick, piece] * 9


def coded(cz, codes):
    has_below, has_above = has_neighbours("gz")
    listed = codes[0:1, :]
    for z in range(cz + 2 * HALO):
        code = listed[0, z]
        keep = has_below if z < HALO else None if z < HALO + cz else has_above
        yield z, code & 3, code >> 2, keep


def frame_kernel(cz, mine, core, chip, codes, own, ring_f, ring):
    cy, lanes = own.shape[2], own.shape[3]
    layers = cz + 2 * HALO
    zero = jnp.zeros((cy, lanes), jnp.float32)
    filled = {(f - ADJ, z) for up in (True, False) for listed in faces(cz, up) for f, _, z in listed}
    for f in range(ring.shape[0]):
        for z in range(cz):
            ring[f, HALO + z] = own[f, z]
        for z in (0, 1, layers - 2, layers - 1):
            if (f, z) not in filled:
                ring[f, z] = zero
        ring[f, layers] = strip_part(zero, lambda z: own[f, z - HALO], range(HALO, HALO + cz))
    for z, hops, row, keep in coded(cz, codes):
        hops = jnp.full((cy, lanes), hops, jnp.int32)
        for f in range(9):
            a, b, c = (ref[row + f].astype(jnp.float32) for ref in (mine, core, chip))
            value = jnp.where(hops == 0, a, jnp.where(hops == 1, b, c))
            ring_f[f, z] = value if keep is None else value * keep


def column_kernel(
    cz, core, both_a, both_b, far, codes, ring_f_in, ring_w_in, ring_f, ring, x_a, x_b
):
    cy, lanes = core.shape[1], core.shape[2]
    layers = cz + 2 * HALO
    half = both_a.shape[0]
    tiles = half + both_b.shape[0]
    near, _ = face_counts(cz)
    even = even_mask("gz", (cy, lanes))
    has_below, has_above = has_neighbours("gz")
    zero = jnp.zeros((cy, lanes), jnp.float32)
    filled = {}
    for up in (True, False):
        for depth, listed in enumerate(faces(cz, up)):
            for i, (f, _, z) in enumerate(listed):
                values = []
                for ref, base in ((core, tiles), (far, 0)):
                    if depth == 0:
                        values.append(joined(ref[base + i], ref[base + near + i]))
                    else:
                        values.append(ref[base + 2 * near + i].astype(jnp.float32))
                value = jnp.where(even, values[1], values[0]) if up else jnp.where(even, values[0], values[1])
                value = value * (has_below if up else has_above)
                ring[f - ADJ, z] = value
                filled.setdefault(f - ADJ, {})[z] = value
    strip = []
    for f in range(ring.shape[0]):
        there = filled.get(f, {})
        tile = strip_whole(strip_part(ring[f, layers], lambda z: there[z], sorted(there)))
        ring[f, layers] = tile
        strip.append(tile)
    for z, hops, row, keep in coded(cz, codes):
        last = jnp.full((cy, lanes), hops, jnp.int32) == 3
        late = jnp.full((cy, lanes), row, jnp.int32) >= half
        row_a, row_b = jnp.minimum(row, half - 9), jnp.maximum(row - half, 0)
        for f in range(9):
            a, b = both_a[row_a + f].astype(jnp.float32), both_b[row_b + f].astype(jnp.float32)
            value = jnp.where(late, b, a)
            ring_f[f, z] = jnp.where(last, value if keep is None else value * keep, ring_f[f, z])
    for f in range(9):
        ring_f[f, layers] = strip_whole(strip_part(zero, lambda z: ring_f[f, z], range(layers)))
    strip = [ring_f[f, layers] for f in range(9)] + strip
    position = lax.broadcasted_iota(jnp.int32, (cy, lanes), 1) % 8
    even_x = even_mask("gx", (cy, lanes))
    for out, tail_from_even in ((x_a, True), (x_b, False)):
        if out is None:
            continue
        place = 0
        for fields in (range(ADJ), range(ADJ, FIELDS)):
            quads = [fields[i : i + 4] for i in range(0, len(fields), 4)]
            for i, quad in enumerate(quads):
                tile = zero
                for g, f in enumerate(quad):
                    tail, head = strip[f], pltpu.roll(strip[f], lanes - 6, 1)
                    value = jnp.where(even_x, tail, head) if tail_from_even else jnp.where(even_x, head, tail)
                    value = value if g == 0 else pltpu.roll(value, 2 * g, 1)
                    tile = jnp.where(position // 2 == g, value, tile)
                high, low = split(tile)
                out[place + i] = high
                if quad[-1] >= INJ:
                    out[x_tiles() - 1] = low
            place += len(quads)


def x_tiles():
    return -(-ADJ // 4) + -(-(FIELDS - ADJ) // 4) + 1


def strip_rows_kernel(cz, ring_f, ring_w, x_a, x_b, y_a_in, y_b_in, strips, y_a, y_b, packed):
    cy, lanes = strips.shape[1], strips.shape[2]
    layers = cz + 2 * HALO
    pair = lax.broadcasted_iota(jnp.int32, (cy, lanes), 1) % 8 // 2
    even_x = even_mask("gx", (cy, lanes))
    has_left, has_right = has_neighbours("gx")
    zero = jnp.zeros((cy, lanes), jnp.float32)
    place = 0
    for fields in (range(ADJ), range(ADJ, FIELDS)):
        quads = [fields[i : i + 4] for i in range(0, len(fields), 4)]
        for i, quad in enumerate(quads):
            got = []
            for ref in (x_a, x_b):
                if ref is None:
                    got.append(zero)
                elif quad[-1] < INJ:
                    got.append(ref[place + i].astype(jnp.float32))
                else:
                    got.append(joined(ref[place + i], ref[x_tiles() - 1]))
            right = jnp.where(even_x, got[0], got[1]) * has_right
            left = jnp.where(even_x, got[1], got[0]) * has_left
            for g, f in enumerate(quad):
                strip = ring_f[f, layers] if f < ADJ else ring_w[f - ADJ, layers]
                tile = jnp.where(pair == 1, pltpu.roll(right, (2 - 2 * g) % lanes, 1), strip)
                strips[f] = jnp.where(pair == 2, pltpu.roll(left, (4 - 2 * g) % lanes, 1), tile)
        place += len(quads)
    sides = []
    for side, up in enumerate((True, False)):
        scatter_rows(packed.at[side], y_rows(cz, cy, up)[2], lambda f, z, y: strips[f, y : y + 1, :])
        sides.append([packed[side, t] for t in range(row_counts(cz, cy, up)[2])])
    pack_tiles(sides, (y_a, y_b), 0, packed.shape[1])


STAGE = {"fv": 0, "fs": 3, "fw": 9, "as": 12, "av": 18, "at": 21}
STAGES = 27
NORMAL = (SXX, SYY, SZZ)
STRESS = range(SXX, SYZ + 1)


def window(cz, base, stage, after, before, put):
    layers = cz + 2 * HALO
    edge = layers
    cy, lanes = stage.shape[2], stage.shape[3]
    lane = lax.broadcasted_iota(jnp.int32, (cy, lanes), 1)
    first_lane, last_lane = lane == 0, lane == lanes - 1
    inner = range(HALO, HALO + cz)

    def start(field):
        return lambda z: base(field, z)

    def kept(name, field):
        index = STAGE[name] + field
        return lambda z: stage[index, z]

    def x_next(of, z):
        value = pltpu.roll(of(z), lanes - 1, 1)
        if z == edge:
            return value
        return jnp.where(last_lane, pltpu.roll(of(edge), (lanes - 1 - (8 * z + 2)) % lanes, 1), value)

    def x_prev(of, z):
        value = pltpu.roll(of(z), 1, 1)
        if z == edge:
            return value
        return jnp.where(first_lane, pltpu.roll(of(edge), (lanes - (8 * z + 5)) % lanes, 1), value)

    def z_next(of, z):
        return pltpu.roll(of(edge), lanes - 8, 1) if z == edge else of(z + 1)

    def z_prev(of, z):
        return pltpu.roll(of(edge), 8, 1) if z == edge else of(z - 1)

    def velocity_rates(k, s, z, want):
        buoy = base(BUOY, z)
        sxx, syy, szz, sxy, sxz, syz = s
        out = {}
        if VX in want:
            xy = sxy(z)
            out[VX] = buoy * (
                (x_next(sxx, z) - sxx(z)) + (xy - before(k, 0, z, xy)) + (sxz(z) - z_prev(sxz, z))
            )
        if VY in want:
            yy = syy(z)
            out[VY] = buoy * (
                (sxy(z) - x_prev(sxy, z)) + (after(k, 1, z, yy) - yy) + (syz(z) - z_prev(syz, z))
            )
        if VZ in want:
            yz = syz(z)
            out[VZ] = buoy * (
                (sxz(z) - x_prev(sxz, z)) + (yz - before(k, 2, z, yz)) + (z_next(szz, z) - szz(z))
            )
        return out

    def stress_rates(k, v, z, want):
        lam, mu = base(LAM, z), base(MU, z)
        of_x, of_y, of_z = v
        vx, vy, vz = of_x(z), of_y(z), of_z(z)
        out = {}
        if SXX in want:
            exx = vx - x_prev(of_x, z)
            eyy = vy - before(k, 0, z, vy)
            ezz = vz - z_prev(of_z, z)
            common = lam * (exx + eyy + ezz)
            twice = 2.0 * mu
            out[SXX] = common + twice * exx
            out[SYY] = common + twice * eyy
            out[SZZ] = common + twice * ezz
        if SXY in want:
            out[SXY] = mu * ((after(k, 1, z, vx) - vx) + (x_next(of_y, z) - vy))
        if SXZ in want:
            out[SXZ] = mu * ((z_next(of_x, z) - vx) + (x_next(of_z, z) - vz))
            out[SYZ] = mu * ((z_next(of_y, z) - vy) + (after(k, 2, z, vz) - vz))
        return out

    def spread(ranges):
        for z in range(layers + 1):
            want = {f for f, (a, b) in ranges.items() if z == edge or a <= z < b}
            if want:
                yield z, want

    def velocity_step(k, name, v, s, sign, ranges):
        for z, want in spread(ranges):
            for f, rate in velocity_rates(k, s, z, want).items():
                stage[STAGE[name] + f, z] = v[f](z) + rate if sign > 0 else v[f](z) - rate
        return [kept(name, f) for f in (VX, VY, VZ)]

    def stress_step(k, name, v, s, sign, ranges, ahead=None, behind=None):
        for z, want in spread(ranges):
            for f, rate in stress_rates(k, v, z, want).items():
                value = s[f - SXX](z)
                if ahead is not None and f in NORMAL:
                    value = value + base(ahead, z)
                value = value + rate if sign > 0 else value - rate
                if behind is not None and f in NORMAL:
                    value = value + base(behind, z)
                stage[STAGE[name] + f - SXX, z] = value
        return [kept(name, f - SXX) for f in STRESS]

    def terms(f, a):
        term_lam = (f[0] + f[1] + f[2]) * (a[0] + a[1] + a[2])
        term_mu = f[0] * a[0] + f[1] * a[1] + f[2] * a[2] + 2.0 * (f[3] * a[3] + f[4] * a[4] + f[5] * a[5])
        return term_lam, term_mu

    n = layers
    fv, fs = [start(FWD + f) for f in (VX, VY, VZ)], [start(FWD + f) for f in STRESS]
    av, first = [start(ADJ + f) for f in (VX, VY, VZ)], [start(ADJ + f) for f in STRESS]
    a_s = stress_step(0, "as", av, first, -1, {SXX: (1, n), SXY: (0, n), SXZ: (0, n - 1)})
    fv = velocity_step(1, "fv", fv, fs, 1, {VX: (1, n), VY: (1, n), VZ: (0, n - 1)})
    fs = stress_step(2, "fs", fv, fs, 1, {SXX: (1, n - 1), SXY: (1, n - 1), SXZ: (1, n - 1)}, behind=SRC)
    fv = velocity_step(3, "fw", fv, fs, 1, {VX: (2, n - 1), VY: (2, n - 1), VZ: (1, n - 2)})
    for z in inner:
        rates = stress_rates(4, fv, z, set(STRESS))
        now = [of(z) for of in fs]
        later = [now[s - SXX] + rates[s] + (base(FIELDS, z) if s in NORMAL else 0.0) for s in STRESS]
        lam_late, mu_late = terms(later, [of(z) for of in first])
        with_traces = [of(z) + (base(INJ, z) if s in NORMAL else 0.0) for s, of in zip(STRESS, a_s)]
        lam_early, mu_early = terms(now, with_traces)
        put(9, z - HALO, lam_late + lam_early)
        put(10, z - HALO, mu_late + mu_early)
    av = velocity_step(5, "av", av, a_s, -1, {VX: (1, n - 1), VY: (1, n - 1), VZ: (1, n - 1)})
    a_s = stress_step(6, "at", av, a_s, -1, {SXX: (2, n - 1), SXY: (1, n - 1), SXZ: (1, n - 2)}, ahead=INJ)
    for s, of in zip(STRESS, a_s):
        for z in inner:
            put(s, z - HALO, of(z))
    for z in inner:
        rates = velocity_rates(7, a_s, z, {VX, VY, VZ})
        for f in (VX, VY, VZ):
            put(f, z - HALO, av[f](z) - rates[f])


def middle_kernel(cz, ring_f, ring_w, strips, own, edges, sides, middle, stage):
    cy, lanes = own.shape[2], own.shape[3]
    layers = cz + 2 * HALO

    def base(f, z):
        if f == FIELDS:
            return own[f - ADJ, z - HALO]
        if z == layers:
            return strips[f]
        return ring_f[f, z] if f < ADJ else ring_w[f - ADJ, z]

    row = lax.broadcasted_iota(jnp.int32, (cy, lanes), 0)
    for f in range(FIELDS + 1):
        for z in range(HALO, HALO + cz) if f == FIELDS else range(layers + 1):
            tile = base(f, z)
            tail, head = pltpu.roll(tile, HALO, 0), pltpu.roll(tile, cy - HALO, 0)
            edges[f, z] = jnp.where(row < HALO, tail, jnp.where(row >= cy - HALO, head, 0.0))

    def after(k, j, z, tile):
        sides[k, j, z] = pltpu.roll(tile, cy - 1 - HALO, 0)
        return pltpu.roll(tile, cy - 1, 0)

    def before(k, j, z, tile):
        sides[k, j, z] = pltpu.roll(tile, HALO + 1, 0)
        return pltpu.roll(tile, 1, 0)

    def put(i, z, value):
        middle[i, z] = value

    window(cz, base, stage, after, before, put)


def edge_kernel(
    cz, edges_in, sides, middle, message, final, image_lam, image_mu, edges, packed, stage, result, sems
):
    cy, lanes = middle.shape[2], middle.shape[3]

    unpack_rows(cz, cy, False, message, packed, edges)
    row = lax.broadcasted_iota(jnp.int32, (cy, lanes), 0)

    def after(k, j, z, tile):
        return jnp.where(row == cy - 1, sides[k, j, z], pltpu.roll(tile, cy - 1, 0))

    def before(k, j, z, tile):
        return jnp.where(row == 0, sides[k, j, z], pltpu.roll(tile, 1, 0))

    moves = []

    def put(i, z, value):
        tail, head = pltpu.roll(value, HALO, 0), pltpu.roll(value, cy - HALO, 0)
        result[i, z] = jnp.where(row < HALO, tail, jnp.where(row >= cy - HALO, head, middle[i, z]))
        if z == cz - 1:
            if i == 10:
                moves.extend(copies(sems, (result.at[9], image_lam), (result.at[10], image_mu)))
            if i == SYZ:
                part = pl.ds(SXX, SYZ + 1 - SXX)
                moves.extend(copies(sems.at[pl.ds(2, 1)], (result.at[part], final.at[part])))
            if i == VZ:
                part = pl.ds(VX, VZ + 1 - VX)
                moves.extend(copies(sems.at[pl.ds(3, 1)], (result.at[part], final.at[part])))

    window(cz, lambda f, z: edges[f, z], stage, after, before, put)
    for move in moves:
        move.wait()


def swap_pairs(count, first):
    pairs = [(i + d, i + 1 - d) for i in range(first, count - 1, 2) for d in (0, 1)]
    return pairs + [(i, i) for i in range(count) if i not in dict(pairs)]


def swapped(value_a, value_b, axis):
    count = lax.axis_size(axis)
    got_a = lax.ppermute(value_a, axis, swap_pairs(count, 0))
    return got_a, None if value_b is None else lax.ppermute(value_b, axis, swap_pairs(count, 1))


def stay(value, spec):
    return pltpu.with_memory_space_constraint(value, pltpu.HBM) if spec.memory_space == pl.ANY else value


def kernel_call(body, args, in_specs, out_shape, scratch_shapes=(), aliases=None, out_specs=None):
    here = [a is not None for a in args]
    there = [o is not None for o in out_shape]

    def run(*refs):
        refs = iter(refs)
        full = [next(refs) if h else None for h in here + there]
        body(*full, *refs)

    out = iter(
        pl.pallas_call(
            run,
            out_shape=tuple(o for o in out_shape if o is not None),
            in_specs=[s for s, h in zip(in_specs, here) if h],
            out_specs=out_specs or tuple(vmem() for h in there if h),
            scratch_shapes=list(scratch_shapes),
            input_output_aliases=aliases or {},
            compiler_params=pltpu.CompilerParams(vmem_limit_bytes=VMEM_LIMIT),
        )(*[stay(a, s) for a, s in zip(args, in_specs) if a is not None])
    )
    return tuple(next(out) if h else None for h in there)


def on_device(
    checkpoint_store,
    holder_peer,
    holder_slot,
    adjoint_state,
    lame_lambda,
    lame_mu,
    buoyancy,
    source_cell,
    wavelet,
    receiver_cell,
    traces,
    plan,
):
    cz, cy, cx = lame_mu.shape
    layers = cz + 2 * HALO
    bf16, f32 = jnp.bfloat16, jnp.float32
    store = checkpoint_store.reshape(-1, cy, cx)
    tiles = store.shape[0]
    peer, slot = holder_peer[0, 0], holder_slot[0, 0]
    source, receiver = source_cell.reshape(1, -1), receiver_cell.reshape(1, -1)
    traces = traces.reshape(traces.shape[-2:])
    holders = lax.axis_size("gz")
    assert holders == 4
    near, far = face_counts(cz)
    face = 2 * near + far
    half = tiles // 2

    def shape(*dims, dtype=f32):
        return jax.ShapeDtypeStruct(dims, dtype)

    wide_x = lax.axis_size("gx") > 2
    chip = lax.ppermute(store, "gz", [(i, i ^ 2) for i in range(holders)])
    to_core, to_far, own, codes = kernel_call(
        functools.partial(start_kernel, cz),
        (store, adjoint_state, lame_lambda, lame_mu, buoyancy, source, wavelet, receiver, traces, plan, peer, slot),
        [hbm()] * 12,
        (shape(tiles + face, cy, cx, dtype=bf16), shape(max(face, half) + PAD, cy, cx, dtype=bf16), shape(15, cz, cy, cx),
         shape(cy, cx, dtype=jnp.int32)),
        [
            pltpu.VMEM(receiver.shape, jnp.int32),
            pltpu.VMEM(traces.shape, f32),
            pltpu.SMEM(source.shape, jnp.int32),
            pltpu.SMEM(wavelet.shape, f32),
            pltpu.SMEM(plan.shape, jnp.int32),
            pltpu.SMEM(peer.shape, jnp.int32),
            pltpu.SMEM(slot.shape, jnp.int32),
            pltpu.SemaphoreType.DMA((12,)),
        ],
    )
    core = lax.ppermute(to_core, "gz", [(i, i ^ 1) for i in range(holders)])
    gy = lax.axis_size("gy")
    axes = ("gx", "gy", "gz")
    gx = lax.axis_size("gx")
    across = [
        ((i * gy + j) * holders + c, (i * gy + j) * holders + 3 - c if c in (1, 2) else ((i ^ 1) * gy + j) * holders + c)
        for i in range(gx) for j in range(gy) for c in range(holders)
    ]
    far_face = lax.ppermute(to_far, axes, across)
    both = [lax.ppermute(part, "gz", [(i, i ^ 1) for i in range(holders)]) for part in (chip[:half], chip[half:])]

    ring_f, ring_w = kernel_call(
        functools.partial(frame_kernel, cz),
        (to_core, core, chip, codes, own),
        [vmem()] * 5,
        (shape(ADJ, layers + 1, cy, cx), shape(FIELDS - ADJ, layers + 1, cy, cx)),
    )
    x_send = shape(x_tiles(), cy, cx, dtype=bf16)
    ring_f, ring_w, x_a, x_b = kernel_call(
        functools.partial(column_kernel, cz),
        (core, *both, far_face, codes, ring_f, ring_w),
        [vmem()] * 7,
        (shape(*ring_f.shape), shape(*ring_w.shape), x_send, x_send if wide_x else None),
        (),
        {5: 0, 6: 1},
    )
    def partner(i, j, c, x_turn, y_turn):
        if x_turn is not None:
            i = dict(swap_pairs(gx, x_turn))[i]
        if y_turn is not None:
            other = dict(swap_pairs(gy, (c + y_turn + 1) % 2))[j]
            i, j = (i ^ 1, j) if other == j else (i, other)
        return (i * gy + j) * holders + c

    def swap(value, x_turn, y_turn):
        if value is None:
            return None
        pairs = [
            ((i * gy + j) * holders + c, partner(i, j, c, x_turn, y_turn))
            for i in range(gx) for j in range(gy) for c in range(holders)
        ]
        return lax.ppermute(value, axes, pairs)

    strip_tiles, tiles = row_tiles(cz, cy)
    y_send = shape(strip_tiles + tiles, cy, cx, dtype=bf16)
    scratch_tiles = max(sum(row_counts(cz, cy, up)) for up in (True, False))
    y_a, y_b = kernel_call(
        functools.partial(layer_rows_kernel, cz),
        (ring_f, ring_w),
        [vmem()] * 2,
        (y_send, y_send),
        [pltpu.VMEM((2, scratch_tiles, 8, cx), f32)],
    )
    strips, y_a, y_b = kernel_call(
        functools.partial(strip_rows_kernel, cz),
        (ring_f, ring_w, swap(x_a, 0, None), swap(x_b, 1, None), y_a, y_b),
        [vmem()] * 6,
        (shape(FIELDS, cy, cx), y_send, y_send),
        [pltpu.VMEM((2, strip_tiles, 8, cx), f32)],
        {4 if wide_x else 3: 1, 5 if wide_x else 4: 2},
    )
    edges, sides, middle = kernel_call(
        functools.partial(middle_kernel, cz),
        (ring_f, ring_w, strips, own),
        [vmem()] * 4,
        (
            shape(FIELDS + 1, layers + 1, cy, cx),
            shape(8, 3, layers + 1, cy, cx),
            shape(11, cz, cy, cx),
        ),
        [pltpu.VMEM((STAGES, layers + 1, cy, cx), f32)],
    )
    row_scratch = pltpu.VMEM((scratch_tiles, 8, cx), f32)
    (edges,) = kernel_call(
        functools.partial(first_rows_kernel, cz),
        (swap(y_a, None, 0), edges),
        [vmem()] * 2,
        (shape(*edges.shape),),
        [row_scratch],
        {1: 0},
    )
    result = kernel_call(
        functools.partial(edge_kernel, cz),
        (edges, sides, middle, swap(y_b, None, 1)),
        [vmem()] * 4,
        (shape(9, cz, cy, cx), shape(cz, cy, cx), shape(cz, cy, cx), shape(*edges.shape)),
        [
            row_scratch,
            pltpu.VMEM((STAGES, layers + 1, cy, cx), f32),
            pltpu.VMEM((11, cz, cy, cx), f32),
            pltpu.SemaphoreType.DMA((4,)),
        ],
        {0: 3},
        (hbm(),) * 3 + (vmem(),),
    )
    return result[:3]


def solution(mesh):
    return jax.shard_map(
        on_device,
        mesh=mesh,
        in_specs=(
            P("gz", None, None, "gy", "gx"),
            P("gx", "gy", None, None),
            P("gx", "gy", None, None),
            P(None, "gz", "gy", "gx"),
            P("gz", "gy", "gx"),
            P("gz", "gy", "gx"),
            P("gz", "gy", "gx"),
            P("gz", "gy", "gx", None),
            P(),
            P("gz", "gy", "gx", None),
            P("gz", "gy", "gx", None, None),
            P(),
        ),
        out_specs=(P(None, "gz", "gy", "gx"), P("gz", "gy", "gx"), P("gz", "gy", "gx")),
        check_vma=False,
    )
```

```python
import functools

import jax
import jax.numpy as jnp
from jax import lax
from jax.experimental import pallas as pl
from jax.experimental.pallas import tpu as pltpu
from jax.sharding import PartitionSpec as P

VX, VY, VZ, SXX, SYY, SZZ, SXY, SXZ, SYZ = range(9)
FWD, ADJ, BUOY, LAM, MU, INJ, SRC = 0, 9, 18, 19, 20, 21, 22
FIELDS = 23
HALO = 2

ADJ_Z = {VX: (2, 2), VY: (2, 2), VZ: (2, 2), SXX: (1, 1), SYY: (1, 1), SZZ: (1, 2), SXY: (1, 1), SXZ: (2, 1), SYZ: (2, 1)}
OTHER_Z = {BUOY: (2, 2), LAM: (1, 2), MU: (2, 2), INJ: (0, 1), SRC: (1, 1)}
F32_Z = {**{ADJ + f: c for f, c in ADJ_Z.items()}, **OTHER_Z}

Y_ROWS = {
    FWD + VX: (None, (2, -1, 1), (1, -1, 1), (2, -2, 0)),
    FWD + VY: ((2, -2, 0), (1, -1, 1), (2, -1, 1), None),
    FWD + VZ: (None, (1, -2, 1), (1, -1, 1), (2, -2, 0)),
    FWD + SXX: (None, (2, -1, 1), (1, -1, 1), (2, -2, 1)),
    FWD + SYY: ((2, -2, 0), (1, -1, 1), (1, 0, 1), (2, -1, 1)),
    FWD + SZZ: (None, (1, -1, 1), (1, 0, 1), (2, -1, 0)),
    FWD + SXY: ((2, -1, 1), (1, 0, 1), (1, -1, 1), (2, -2, 0)),
    FWD + SXZ: (None, (1, -1, 1), (0, -1, 1), (1, -2, 1)),
    FWD + SYZ: ((1, -2, 1), (0, -1, 1), (1, -1, 1), (2, -2, 0)),
    ADJ + VX: ((2, -2, 0), (1, -1, 1), (1, -1, 1), (2, -2, 1)),
    ADJ + VY: ((2, -1, 1), (1, 0, 1), (1, -1, 1), (2, -2, 0)),
    ADJ + VZ: ((2, -2, 0), (1, -1, 1), (0, -1, 1), (1, -2, 0)),
    ADJ + SXX: (None, (2, -2, 1), (2, -2, 1), None),
    ADJ + SYY: (None, (2, -1, 1), (1, -1, 1), (2, -2, 0)),
    ADJ + SZZ: (None, (2, -1, 0), (1, -1, 0), None),
    ADJ + SXY: ((2, -2, 0), (1, -1, 1), (2, -2, 1), None),
    ADJ + SXZ: (None, (1, -2, 1), (1, -2, 1), None),
    ADJ + SYZ: ((2, -2, 0), (1, -1, 1), (1, -2, 0), None),
    BUOY: ((2, -2, 0), (1, -1, 1), (1, -1, 1), (2, -2, 0)),
    LAM: (None, (2, -1, 1), (1, -1, 1), (2, -2, 0)),
    MU: ((2, -2, 0), (1, -1, 1), (1, -1, 1), (2, -2, 0)),
    INJ: (None, None, (2, -2, 0), None),
    SRC: (None, (2, -2, 0), (2, -1, 1), None),
}

EXACT_ROWS = {-1: (ADJ + VY, ADJ + SXY, ADJ + SYZ, BUOY, SRC), 0: (ADJ + SYY, LAM, INJ, SRC)}

PAD = 1
VMEM_LIMIT = 48 * 1024 * 1024


def vmem():
    return pl.BlockSpec(memory_space=pltpu.VMEM)


def hbm():
    return pl.BlockSpec(memory_space=pl.ANY)


def faces(cz, up):
    near, far = [], []
    for f in sorted(F32_Z):
        before, after = F32_Z[f]
        depth = before if up else after
        for d in range(depth):
            layer = cz - 1 - d if up else d
            (far if d else near).append((f, layer, HALO - 1 - d if up else HALO + cz + d))
    return near, far


def face_counts(cz):
    sides = [faces(cz, up) for up in (True, False)]
    return max(len(s[0]) for s in sides), max(len(s[1]) for s in sides)


def y_rows(cz, cy, up):
    layers = cz + 2 * HALO
    narrow, wide, strip = [], [], []
    for f in sorted(Y_ROWS):
        for offset in (-1, -2) if up else (0, 1):
            spec = Y_ROWS[f][offset + HALO]
            if spec is None:
                continue
            source = cy + offset if up else offset
            target = cy - HALO + offset if up else HALO + offset
            exact = f in EXACT_ROWS.get(offset, ())
            (wide if exact else narrow).extend((f, z, source, target) for z in range(spec[0], layers + spec[1]))
            if spec[2]:
                strip.append((f, layers, source, target))
    return narrow, wide, strip


def row_counts(cz, cy, up):
    return tuple(-(-len(rows) // 8) for rows in y_rows(cz, cy, up))


def row_tiles(cz, cy):
    sides = [row_counts(cz, cy, up) for up in (True, False)]
    return max(c for _, _, c in sides), max(n + 2 * w for n, w, _ in sides)


def split(value):
    high = value.astype(jnp.bfloat16)
    low = (value - high.astype(jnp.float32)).astype(jnp.bfloat16)
    return high, low


def joined(high, low):
    return high.astype(jnp.float32) + low.astype(jnp.float32)


def even_mask(axes, shape):
    total = sum(lax.axis_index(a) for a in ((axes,) if isinstance(axes, str) else axes))
    return jnp.full(shape, lax.rem(total, 2), jnp.int32) == 0


def has_neighbours(axis):
    index = lax.axis_index(axis)
    return (index > 0).astype(jnp.float32), (index < lax.axis_size(axis) - 1).astype(jnp.float32)


def copies(sems, *pairs):
    out = [pltpu.make_async_copy(source, target, sems.at[i]) for i, (source, target) in enumerate(pairs)]
    for copy in out:
        copy.start()
    return out


def scatter_rows(packed, listed, row_of):
    for r, (f, z, y, _) in enumerate(listed):
        packed[r // 8, r % 8 : r % 8 + 1, :] = row_of(f, z, y)


def pack_tiles(sides, sends, first, count):
    even = even_mask(("gy", "gz"), sends[0].shape[1:])
    for t in range(count):
        up, down = (side[min(t, len(side) - 1)] for side in sides)
        sends[0][first + t] = jnp.where(even, down, up).astype(jnp.bfloat16)
        sends[1][first + t] = jnp.where(even, up, down).astype(jnp.bfloat16)


def layer_rows_kernel(cz, ring_f, ring_w, send_a, send_b, packed):
    cy = ring_f.shape[2]
    strip_tiles, tiles = row_tiles(cz, cy)

    def row_of(f, z, y):
        return ring_f[f, z, y : y + 1, :] if f < ADJ else ring_w[f - ADJ, z, y : y + 1, :]

    sides = []
    for side, up in enumerate((True, False)):
        narrow, wide, _ = y_rows(cz, cy, up)
        n, w, _ = row_counts(cz, cy, up)
        scatter_rows(packed.at[side], narrow, row_of)
        scatter_rows(packed.at[side, pl.ds(n, w)], wide, row_of)
        rest = [split(packed[side, n + t])[1].astype(jnp.float32) for t in range(w)]
        sides.append([packed[side, t] for t in range(n + w)] + rest)
    pack_tiles(sides, (send_a, send_b), strip_tiles, tiles)


def unpack_rows(cz, cy, first, message, packed, edges):
    has_lower, has_upper = has_neighbours("gy")
    strip_tiles, _ = row_tiles(cz, cy)
    parity = lax.rem(lax.axis_index("gy") + lax.axis_index("gz"), 2)

    def side(up, keep):
        narrow, wide, strip = y_rows(cz, cy, up)
        n, w, c = row_counts(cz, cy, up)
        for t in range(n + w):
            value = message[strip_tiles + t].astype(jnp.float32)
            if t >= n:
                value = value + message[strip_tiles + w + t].astype(jnp.float32)
            packed[t] = value * keep
        for t in range(c):
            packed[n + w + t] = message[t].astype(jnp.float32) * keep
        for base, listed in ((0, narrow), (n, wide), (n + w, strip)):
            for r, (f, z, _, y) in enumerate(listed):
                edges[f, z, y : y + 1, :] = packed[base + r // 8, r % 8 : r % 8 + 1, :]

    @pl.when(parity == (0 if first else 1))
    def _():
        side(True, has_lower)

    @pl.when(parity == (1 if first else 0))
    def _():
        side(False, has_upper)


def first_rows_kernel(cz, message, edges_in, edges, packed):
    unpack_rows(cz, edges.shape[2], True, message, packed, edges)


def start_kernel(
    cz, store, adjoint, lam, mu, buoy, source, wavelet, receiver, traces, plan, peer, slot,
    near_out, far_out, own, codes, cells, samples, spots, wave, steps, peers, slots, sems,
):
    cy, lanes = own.shape[2], own.shape[3]
    rows = cz * cy
    tiles = store.shape[0]
    small = copies(
        sems, (plan, steps), (wavelet, wave), (source, spots), (receiver, cells), (traces, samples),
        (peer, peers), (slot, slots),
    )
    large = copies(
        sems.at[pl.ds(len(small), 5)],
        (adjoint, own.at[pl.ds(0, 9)]),
        (buoy, own.at[BUOY - ADJ]),
        (lam, own.at[LAM - ADJ]),
        (mu, own.at[MU - ADJ]),
        (store, near_out.at[pl.ds(0, tiles)]),
    )
    for copy in small:
        copy.wait()
    lane = lax.broadcasted_iota(jnp.int32, (cy, lanes), 1)
    code = jnp.zeros((cy, lanes), jnp.int32)
    for z, hops, row in pieces(cz, peers, slots):
        code = jnp.where(lane == z, row * 4 + hops, code)
    codes[...] = code
    listed = cells[...]
    count = listed.shape[1]
    row_hot = (lax.broadcasted_iota(jnp.int32, (rows, count), 0) == listed // lanes).astype(jnp.bfloat16)
    lane_hit = lax.broadcasted_iota(jnp.int32, (lanes, count), 0) == listed % lanes
    rest = jnp.concatenate([jnp.where(lane_hit, samples[pl.ds(steps[step], 1), :], 0.0) for step in (1, 0)], axis=0)
    both = jnp.zeros((rows, 2 * lanes), jnp.float32)
    for _ in range(3):
        part = rest.astype(jnp.bfloat16)
        rest = rest - part.astype(jnp.float32)
        both = both + lax.dot_general(
            row_hot, part, (((1,), (1,)), ((), ())), preferred_element_type=jnp.float32
        )
    injected = [both[:, :lanes].reshape(cz, cy, lanes), both[:, lanes:].reshape(cz, cy, lanes)]
    own[INJ - ADJ] = injected[1]
    flat = lax.broadcasted_iota(jnp.int32, (rows, lanes), 0) * lanes + lax.broadcasted_iota(jnp.int32, (rows, lanes), 1)
    for step in range(2):
        value = wave[steps[step]]
        field = jnp.zeros((rows, lanes), jnp.float32)
        for j in range(source.shape[1]):
            field = field + jnp.where(flat == spots[0, j], value, 0.0)
        own[SRC - ADJ + step] = field.reshape(cz, cy, lanes)
    for copy in large:
        copy.wait()
    for f in (SXX, SYY, SZZ):
        own[f] = own[f] + injected[0]

    even = even_mask("gz", (cy, lanes))
    near, far = face_counts(cz)
    up, down = faces(cz, True), faces(cz, False)
    zero = jnp.zeros((cy, lanes), jnp.float32)

    def tile(side, i):
        return own[side[i][0] - ADJ, side[i][1]] if i < len(side) else zero

    for i in range(near):
        above, below = tile(up[0], i), tile(down[0], i)
        for out, base, value in (
            (near_out, tiles, jnp.where(even, above, below)),
            (far_out, 0, jnp.where(even, below, above)),
        ):
            out[base + i], out[base + near + i] = split(value)
    for i in range(far):
        above, below = tile(up[1], i), tile(down[1], i)
        near_out[tiles + 2 * near + i] = jnp.where(even, above, below).astype(jnp.bfloat16)
        far_out[2 * near + i] = jnp.where(even, below, above).astype(jnp.bfloat16)
    for i in range(2 * near + far, far_out.shape[0]):
        far_out[i] = zero.astype(jnp.bfloat16)


def strip_part(tile, main, listed):
    lanes = tile.shape[1]
    lane = lax.broadcasted_iota(jnp.int32, tile.shape, 1)
    for z in listed:
        tile = jnp.where((lane >= 8 * z) & (lane < 8 * z + 4), pltpu.roll(main(z), (8 * z + 2) % lanes, 1), tile)
    return tile


def strip_whole(tile):
    position = lax.broadcasted_iota(jnp.int32, tile.shape, 1) % 8
    return jnp.where(position < 2, tile, jnp.where(position >= 6, pltpu.roll(tile, 4, 1), 0.0))


def pieces(cz, peers, slots):
    me, count = lax.axis_index("gz"), lax.axis_size("gz")
    below, above = jnp.maximum(me - 1, 0), jnp.minimum(me + 1, count - 1)
    for z in range(cz + 2 * HALO):
        if z < HALO:
            brick, piece = below, cz - HALO + z
        elif z < HALO + cz:
            brick, piece = me, z - HALO
        else:
            brick, piece = above, z - HALO - cz
        yield z, peers[brick, piece] ^ me, slots[brick, piece] * 9


def coded(cz, codes):
    has_below, has_above = has_neighbours("gz")
    listed = codes[0:1, :]
    for z in range(cz + 2 * HALO):
        code = listed[0, z]
        keep = has_below if z < HALO else None if z < HALO + cz else has_above
        yield z, code & 3, code >> 2, keep


def frame_kernel(cz, mine, core, chip, codes, own, ring_f, ring):
    cy, lanes = own.shape[2], own.shape[3]
    layers = cz + 2 * HALO
    zero = jnp.zeros((cy, lanes), jnp.float32)
    filled = {(f - ADJ, z) for up in (True, False) for listed in faces(cz, up) for f, _, z in listed}
    for f in range(ring.shape[0]):
        for z in range(cz):
            ring[f, HALO + z] = own[f, z]
        for z in (0, 1, layers - 2, layers - 1):
            if (f, z) not in filled:
                ring[f, z] = zero
        ring[f, layers] = strip_part(zero, lambda z: own[f, z - HALO], range(HALO, HALO + cz))
    for z, hops, row, keep in coded(cz, codes):
        hops = jnp.full((cy, lanes), hops, jnp.int32)
        for f in range(9):
            a, b, c = (ref[row + f].astype(jnp.float32) for ref in (mine, core, chip))
            value = jnp.where(hops == 0, a, jnp.where(hops == 1, b, c))
            ring_f[f, z] = value if keep is None else value * keep


def column_kernel(
    cz, core, both_a, both_b, far, codes, ring_f_in, ring_w_in, ring_f, ring, x_a, x_b
):
    cy, lanes = core.shape[1], core.shape[2]
    layers = cz + 2 * HALO
    half = both_a.shape[0]
    tiles = half + both_b.shape[0]
    near, _ = face_counts(cz)
    even = even_mask("gz", (cy, lanes))
    has_below, has_above = has_neighbours("gz")
    zero = jnp.zeros((cy, lanes), jnp.float32)
    filled = {}
    for up in (True, False):
        for depth, listed in enumerate(faces(cz, up)):
            for i, (f, _, z) in enumerate(listed):
                values = []
                for ref, base in ((core, tiles), (far, 0)):
                    if depth == 0:
                        values.append(joined(ref[base + i], ref[base + near + i]))
                    else:
                        values.append(ref[base + 2 * near + i].astype(jnp.float32))
                value = jnp.where(even, values[1], values[0]) if up else jnp.where(even, values[0], values[1])
                value = value * (has_below if up else has_above)
                ring[f - ADJ, z] = value
                filled.setdefault(f - ADJ, {})[z] = value
    strip = []
    for f in range(ring.shape[0]):
        there = filled.get(f, {})
        tile = strip_whole(strip_part(ring[f, layers], lambda z: there[z], sorted(there)))
        ring[f, layers] = tile
        strip.append(tile)
    for z, hops, row, keep in coded(cz, codes):
        last = jnp.full((cy, lanes), hops, jnp.int32) == 3
        late = jnp.full((cy, lanes), row, jnp.int32) >= half
        row_a, row_b = jnp.minimum(row, half - 9), jnp.maximum(row - half, 0)
        for f in range(9):
            a, b = both_a[row_a + f].astype(jnp.float32), both_b[row_b + f].astype(jnp.float32)
            value = jnp.where(late, b, a)
            ring_f[f, z] = jnp.where(last, value if keep is None else value * keep, ring_f[f, z])
    for f in range(9):
        ring_f[f, layers] = strip_whole(strip_part(zero, lambda z: ring_f[f, z], range(layers)))
    strip = [ring_f[f, layers] for f in range(9)] + strip
    position = lax.broadcasted_iota(jnp.int32, (cy, lanes), 1) % 8
    even_x = even_mask("gx", (cy, lanes))
    for out, tail_from_even in ((x_a, True), (x_b, False)):
        if out is None:
            continue
        place = 0
        for fields, narrow in ((range(ADJ), True), (range(ADJ, FIELDS), False)):
            quads = [fields[i : i + 4] for i in range(0, len(fields), 4)]
            for i, quad in enumerate(quads):
                tile = zero
                for g, f in enumerate(quad):
                    tail, head = strip[f], pltpu.roll(strip[f], lanes - 6, 1)
                    value = jnp.where(even_x, tail, head) if tail_from_even else jnp.where(even_x, head, tail)
                    value = value if g == 0 else pltpu.roll(value, 2 * g, 1)
                    tile = jnp.where(position // 2 == g, value, tile)
                high, low = split(tile)
                out[place + i] = high
                if not narrow:
                    out[place + len(quads) + i] = low
            place += len(quads) if narrow else 2 * len(quads)


def x_tiles():
    return -(-ADJ // 4) + 2 * -(-(FIELDS - ADJ) // 4)


def strip_rows_kernel(cz, ring_f, ring_w, x_a, x_b, y_a_in, y_b_in, strips, y_a, y_b, packed):
    cy, lanes = strips.shape[1], strips.shape[2]
    layers = cz + 2 * HALO
    pair = lax.broadcasted_iota(jnp.int32, (cy, lanes), 1) % 8 // 2
    even_x = even_mask("gx", (cy, lanes))
    has_left, has_right = has_neighbours("gx")
    zero = jnp.zeros((cy, lanes), jnp.float32)
    place = 0
    for fields, narrow in ((range(ADJ), True), (range(ADJ, FIELDS), False)):
        quads = [fields[i : i + 4] for i in range(0, len(fields), 4)]
        for i, quad in enumerate(quads):
            got = []
            for ref in (x_a, x_b):
                if ref is None:
                    got.append(zero)
                elif narrow:
                    got.append(ref[place + i].astype(jnp.float32))
                else:
                    got.append(joined(ref[place + i], ref[place + len(quads) + i]))
            right = jnp.where(even_x, got[0], got[1]) * has_right
            left = jnp.where(even_x, got[1], got[0]) * has_left
            for g, f in enumerate(quad):
                strip = ring_f[f, layers] if f < ADJ else ring_w[f - ADJ, layers]
                tile = jnp.where(pair == 1, pltpu.roll(right, (2 - 2 * g) % lanes, 1), strip)
                strips[f] = jnp.where(pair == 2, pltpu.roll(left, (4 - 2 * g) % lanes, 1), tile)
        place += len(quads) if narrow else 2 * len(quads)
    sides = []
    for side, up in enumerate((True, False)):
        scatter_rows(packed.at[side], y_rows(cz, cy, up)[2], lambda f, z, y: strips[f, y : y + 1, :])
        sides.append([packed[side, t] for t in range(row_counts(cz, cy, up)[2])])
    pack_tiles(sides, (y_a, y_b), 0, packed.shape[1])


STAGE = {"fv": 0, "fs": 3, "fw": 9, "as": 12, "av": 18, "at": 21}
STAGES = 27
NORMAL = (SXX, SYY, SZZ)
STRESS = range(SXX, SYZ + 1)


def window(cz, base, stage, after, before, put):
    layers = cz + 2 * HALO
    edge = layers
    cy, lanes = stage.shape[2], stage.shape[3]
    lane = lax.broadcasted_iota(jnp.int32, (cy, lanes), 1)
    first_lane, last_lane = lane == 0, lane == lanes - 1
    inner = range(HALO, HALO + cz)

    seen = {}

    def once(key, z, load):
        if (key, z) not in seen:
            seen[key, z] = load()
        return seen[key, z]

    def forget(step):
        for key in [key for key in seen if step or key[1] != edge]:
            del seen[key]

    def start(field):
        return lambda z: once(field, z, lambda: base(field, z))

    def kept(name, field):
        index = STAGE[name] + field
        return lambda z: once(("stage", index), z, lambda: stage[index, z])

    def x_next(of, z):
        value = pltpu.roll(of(z), lanes - 1, 1)
        if z == edge:
            return value
        return jnp.where(last_lane, pltpu.roll(of(edge), (lanes - 1 - (8 * z + 2)) % lanes, 1), value)

    def x_prev(of, z):
        value = pltpu.roll(of(z), 1, 1)
        if z == edge:
            return value
        return jnp.where(first_lane, pltpu.roll(of(edge), (lanes - (8 * z + 5)) % lanes, 1), value)

    def z_next(of, z):
        return pltpu.roll(of(edge), lanes - 8, 1) if z == edge else of(z + 1)

    def z_prev(of, z):
        return pltpu.roll(of(edge), 8, 1) if z == edge else of(z - 1)

    def velocity_rates(k, s, z, want):
        buoy = base(BUOY, z)
        sxx, syy, szz, sxy, sxz, syz = s
        out = {}
        if VX in want:
            xy = sxy(z)
            out[VX] = buoy * (
                (x_next(sxx, z) - sxx(z)) + (xy - before(k, 0, z, xy)) + (sxz(z) - z_prev(sxz, z))
            )
        if VY in want:
            yy = syy(z)
            out[VY] = buoy * (
                (sxy(z) - x_prev(sxy, z)) + (after(k, 1, z, yy) - yy) + (syz(z) - z_prev(syz, z))
            )
        if VZ in want:
            yz = syz(z)
            out[VZ] = buoy * (
                (sxz(z) - x_prev(sxz, z)) + (yz - before(k, 2, z, yz)) + (z_next(szz, z) - szz(z))
            )
        return out

    def stress_rates(k, v, z, want):
        lam, mu = base(LAM, z), base(MU, z)
        of_x, of_y, of_z = v
        vx, vy, vz = of_x(z), of_y(z), of_z(z)
        out = {}
        if SXX in want:
            exx = vx - x_prev(of_x, z)
            eyy = vy - before(k, 0, z, vy)
            ezz = vz - z_prev(of_z, z)
            common = lam * (exx + eyy + ezz)
            twice = 2.0 * mu
            out[SXX] = common + twice * exx
            out[SYY] = common + twice * eyy
            out[SZZ] = common + twice * ezz
        if SXY in want:
            out[SXY] = mu * ((after(k, 1, z, vx) - vx) + (x_next(of_y, z) - vy))
        if SXZ in want:
            out[SXZ] = mu * ((z_next(of_x, z) - vx) + (x_next(of_z, z) - vz))
            out[SYZ] = mu * ((z_next(of_y, z) - vy) + (after(k, 2, z, vz) - vz))
        return out

    def spread(ranges):
        forget(True)
        for z in range(layers + 1):
            want = {f for f, (a, b) in ranges.items() if z == edge or a <= z < b}
            if want:
                forget(False)
                yield z, want

    def velocity_step(k, name, v, s, sign, ranges):
        for z, want in spread(ranges):
            for f, rate in velocity_rates(k, s, z, want).items():
                stage[STAGE[name] + f, z] = v[f](z) + rate if sign > 0 else v[f](z) - rate
        return [kept(name, f) for f in (VX, VY, VZ)]

    def stress_step(k, name, v, s, sign, ranges, ahead=None, behind=None):
        for z, want in spread(ranges):
            for f, rate in stress_rates(k, v, z, want).items():
                value = s[f - SXX](z)
                if ahead is not None and f in NORMAL:
                    value = value + base(ahead, z)
                value = value + rate if sign > 0 else value - rate
                if behind is not None and f in NORMAL:
                    value = value + base(behind, z)
                stage[STAGE[name] + f - SXX, z] = value
        return [kept(name, f - SXX) for f in STRESS]

    def terms(f, a):
        term_lam = (f[0] + f[1] + f[2]) * (a[0] + a[1] + a[2])
        term_mu = f[0] * a[0] + f[1] * a[1] + f[2] * a[2] + 2.0 * (f[3] * a[3] + f[4] * a[4] + f[5] * a[5])
        return term_lam, term_mu

    n = layers
    fv, fs = [start(FWD + f) for f in (VX, VY, VZ)], [start(FWD + f) for f in STRESS]
    av, first = [start(ADJ + f) for f in (VX, VY, VZ)], [start(ADJ + f) for f in STRESS]
    a_s = stress_step(0, "as", av, first, -1, {SXX: (1, n), SXY: (0, n), SXZ: (0, n - 1)})
    fv = velocity_step(1, "fv", fv, fs, 1, {VX: (1, n), VY: (1, n), VZ: (0, n - 1)})
    fs = stress_step(2, "fs", fv, fs, 1, {SXX: (1, n - 1), SXY: (1, n - 1), SXZ: (1, n - 1)}, behind=SRC)
    fv = velocity_step(3, "fw", fv, fs, 1, {VX: (2, n - 1), VY: (2, n - 1), VZ: (1, n - 2)})
    forget(True)
    for z in inner:
        forget(False)
        rates = stress_rates(4, fv, z, set(STRESS))
        now = [of(z) for of in fs]
        later = [now[s - SXX] + rates[s] + (base(FIELDS, z) if s in NORMAL else 0.0) for s in STRESS]
        lam_late, mu_late = terms(later, [of(z) for of in first])
        with_traces = [of(z) + (base(INJ, z) if s in NORMAL else 0.0) for s, of in zip(STRESS, a_s)]
        lam_early, mu_early = terms(now, with_traces)
        put(9, z - HALO, lam_late + lam_early)
        put(10, z - HALO, mu_late + mu_early)
    av = velocity_step(5, "av", av, a_s, -1, {VX: (1, n - 1), VY: (1, n - 1), VZ: (1, n - 1)})
    a_s = stress_step(6, "at", av, a_s, -1, {SXX: (2, n - 1), SXY: (1, n - 1), SXZ: (1, n - 2)}, ahead=INJ)
    forget(True)
    for s, of in zip(STRESS, a_s):
        for z in inner:
            put(s, z - HALO, of(z))
    forget(True)
    for z in inner:
        forget(False)
        rates = velocity_rates(7, a_s, z, {VX, VY, VZ})
        for f in (VX, VY, VZ):
            put(f, z - HALO, av[f](z) - rates[f])


def middle_kernel(cz, ring_f, ring_w, strips, own, edges, sides, middle, stage):
    cy, lanes = own.shape[2], own.shape[3]
    layers = cz + 2 * HALO

    def base(f, z):
        if f == FIELDS:
            return own[f - ADJ, z - HALO]
        if z == layers:
            return strips[f]
        return ring_f[f, z] if f < ADJ else ring_w[f - ADJ, z]

    row = lax.broadcasted_iota(jnp.int32, (cy, lanes), 0)
    for f in range(FIELDS + 1):
        for z in range(HALO, HALO + cz) if f == FIELDS else range(layers + 1):
            tile = base(f, z)
            tail, head = pltpu.roll(tile, HALO, 0), pltpu.roll(tile, cy - HALO, 0)
            edges[f, z] = jnp.where(row < HALO, tail, jnp.where(row >= cy - HALO, head, 0.0))

    def after(k, j, z, tile):
        sides[k, j, z] = pltpu.roll(tile, cy - 1 - HALO, 0)
        return pltpu.roll(tile, cy - 1, 0)

    def before(k, j, z, tile):
        sides[k, j, z] = pltpu.roll(tile, HALO + 1, 0)
        return pltpu.roll(tile, 1, 0)

    def put(i, z, value):
        middle[i, z] = value

    window(cz, base, stage, after, before, put)


def edge_kernel(
    cz, edges_in, sides, middle, message, final, image_lam, image_mu, edges, packed, stage, result, sems
):
    cy, lanes = middle.shape[2], middle.shape[3]

    unpack_rows(cz, cy, False, message, packed, edges)
    row = lax.broadcasted_iota(jnp.int32, (cy, lanes), 0)

    def after(k, j, z, tile):
        return jnp.where(row == cy - 1, sides[k, j, z], pltpu.roll(tile, cy - 1, 0))

    def before(k, j, z, tile):
        return jnp.where(row == 0, sides[k, j, z], pltpu.roll(tile, 1, 0))

    moves = []

    def put(i, z, value):
        tail, head = pltpu.roll(value, HALO, 0), pltpu.roll(value, cy - HALO, 0)
        result[i, z] = jnp.where(row < HALO, tail, jnp.where(row >= cy - HALO, head, middle[i, z]))
        if z == cz - 1:
            if i == 10:
                moves.extend(copies(sems, (result.at[9], image_lam), (result.at[10], image_mu)))
            if i == SYZ:
                part = pl.ds(SXX, SYZ + 1 - SXX)
                moves.extend(copies(sems.at[pl.ds(2, 1)], (result.at[part], final.at[part])))
            if i == VZ:
                part = pl.ds(VX, VZ + 1 - VX)
                moves.extend(copies(sems.at[pl.ds(3, 1)], (result.at[part], final.at[part])))

    window(cz, lambda f, z: edges[f, z], stage, after, before, put)
    for move in moves:
        move.wait()


def swap_pairs(count, first):
    pairs = [(i + d, i + 1 - d) for i in range(first, count - 1, 2) for d in (0, 1)]
    return pairs + [(i, i) for i in range(count) if i not in dict(pairs)]


def swapped(value_a, value_b, axis):
    count = lax.axis_size(axis)
    got_a = lax.ppermute(value_a, axis, swap_pairs(count, 0))
    return got_a, None if value_b is None else lax.ppermute(value_b, axis, swap_pairs(count, 1))


def stay(value, spec):
    return pltpu.with_memory_space_constraint(value, pltpu.HBM) if spec.memory_space == pl.ANY else value


def kernel_call(body, args, in_specs, out_shape, scratch_shapes=(), aliases=None, out_specs=None):
    here = [a is not None for a in args]
    there = [o is not None for o in out_shape]

    def run(*refs):
        refs = iter(refs)
        full = [next(refs) if h else None for h in here + there]
        body(*full, *refs)

    out = iter(
        pl.pallas_call(
            run,
            out_shape=tuple(o for o in out_shape if o is not None),
            in_specs=[s for s, h in zip(in_specs, here) if h],
            out_specs=out_specs or tuple(vmem() for h in there if h),
            scratch_shapes=list(scratch_shapes),
            input_output_aliases=aliases or {},
            compiler_params=pltpu.CompilerParams(vmem_limit_bytes=VMEM_LIMIT),
        )(*[stay(a, s) for a, s in zip(args, in_specs) if a is not None])
    )
    return tuple(next(out) if h else None for h in there)


def on_device(
    checkpoint_store,
    holder_peer,
    holder_slot,
    adjoint_state,
    lame_lambda,
    lame_mu,
    buoyancy,
    source_cell,
    wavelet,
    receiver_cell,
    traces,
    plan,
):
    cz, cy, cx = lame_mu.shape
    layers = cz + 2 * HALO
    bf16, f32 = jnp.bfloat16, jnp.float32
    store = checkpoint_store.reshape(-1, cy, cx)
    tiles = store.shape[0]
    peer, slot = holder_peer[0, 0], holder_slot[0, 0]
    source, receiver = source_cell.reshape(1, -1), receiver_cell.reshape(1, -1)
    traces = traces.reshape(traces.shape[-2:])
    holders = lax.axis_size("gz")
    assert holders == 4
    near, far = face_counts(cz)
    face = 2 * near + far
    half = tiles // 2

    def shape(*dims, dtype=f32):
        return jax.ShapeDtypeStruct(dims, dtype)

    wide_x = lax.axis_size("gx") > 2
    chip = lax.ppermute(store, "gz", [(i, i ^ 2) for i in range(holders)])
    to_core, to_far, own, codes = kernel_call(
        functools.partial(start_kernel, cz),
        (store, adjoint_state, lame_lambda, lame_mu, buoyancy, source, wavelet, receiver, traces, plan, peer, slot),
        [hbm()] * 12,
        (shape(tiles + face, cy, cx, dtype=bf16), shape(max(face, half) + PAD, cy, cx, dtype=bf16), shape(15, cz, cy, cx),
         shape(cy, cx, dtype=jnp.int32)),
        [
            pltpu.VMEM(receiver.shape, jnp.int32),
            pltpu.VMEM(traces.shape, f32),
            pltpu.SMEM(source.shape, jnp.int32),
            pltpu.SMEM(wavelet.shape, f32),
            pltpu.SMEM(plan.shape, jnp.int32),
            pltpu.SMEM(peer.shape, jnp.int32),
            pltpu.SMEM(slot.shape, jnp.int32),
            pltpu.SemaphoreType.DMA((12,)),
        ],
    )
    core = lax.ppermute(to_core, "gz", [(i, i ^ 1) for i in range(holders)])
    gy = lax.axis_size("gy")
    across = {
        (i, c): (i, 3 - c) if c in (1, 2) else (i ^ 1, c)
        for i in range(gy) for c in range(holders)
    }
    far_face = lax.ppermute(
        to_far, ("gy", "gz"), [(a[0] * holders + a[1], b[0] * holders + b[1]) for a, b in across.items()]
    )
    both = [lax.ppermute(part, "gz", [(i, i ^ 1) for i in range(holders)]) for part in (chip[:half], chip[half:])]

    ring_f, ring_w = kernel_call(
        functools.partial(frame_kernel, cz),
        (to_core, core, chip, codes, own),
        [vmem()] * 5,
        (shape(ADJ, layers + 1, cy, cx), shape(FIELDS - ADJ, layers + 1, cy, cx)),
    )
    x_send = shape(x_tiles(), cy, cx, dtype=bf16)
    ring_f, ring_w, x_a, x_b = kernel_call(
        functools.partial(column_kernel, cz),
        (core, *both, far_face, codes, ring_f, ring_w),
        [vmem()] * 7,
        (shape(*ring_f.shape), shape(*ring_w.shape), x_send, x_send if wide_x else None),
        (),
        {5: 0, 6: 1},
    )
    axes = ("gx", "gy", "gz")
    gx = lax.axis_size("gx")

    def partner(i, j, c, x_turn, y_turn):
        if x_turn is not None:
            i = dict(swap_pairs(gx, x_turn))[i]
        if y_turn is not None:
            other = dict(swap_pairs(gy, (c + y_turn + 1) % 2))[j]
            i, j = (i ^ 1, j) if other == j else (i, other)
        return (i * gy + j) * holders + c

    def swap(value, x_turn, y_turn):
        if value is None:
            return None
        pairs = [
            ((i * gy + j) * holders + c, partner(i, j, c, x_turn, y_turn))
            for i in range(gx) for j in range(gy) for c in range(holders)
        ]
        return lax.ppermute(value, axes, pairs)

    strip_tiles, tiles = row_tiles(cz, cy)
    y_send = shape(strip_tiles + tiles, cy, cx, dtype=bf16)
    scratch_tiles = max(sum(row_counts(cz, cy, up)) for up in (True, False))
    y_a, y_b = kernel_call(
        functools.partial(layer_rows_kernel, cz),
        (ring_f, ring_w),
        [vmem()] * 2,
        (y_send, y_send),
        [pltpu.VMEM((2, scratch_tiles, 8, cx), f32)],
    )
    strips, y_a, y_b = kernel_call(
        functools.partial(strip_rows_kernel, cz),
        (ring_f, ring_w, swap(x_a, 0, None), swap(x_b, 1, None), y_a, y_b),
        [vmem()] * 6,
        (shape(FIELDS, cy, cx), y_send, y_send),
        [pltpu.VMEM((2, strip_tiles, 8, cx), f32)],
        {4 if wide_x else 3: 1, 5 if wide_x else 4: 2},
    )
    edges, sides, middle = kernel_call(
        functools.partial(middle_kernel, cz),
        (ring_f, ring_w, strips, own),
        [vmem()] * 4,
        (
            shape(FIELDS + 1, layers + 1, cy, cx),
            shape(8, 3, layers + 1, cy, cx),
            shape(11, cz, cy, cx),
        ),
        [pltpu.VMEM((STAGES, layers + 1, cy, cx), f32)],
    )
    row_scratch = pltpu.VMEM((scratch_tiles, 8, cx), f32)
    (edges,) = kernel_call(
        functools.partial(first_rows_kernel, cz),
        (swap(y_a, None, 0), edges),
        [vmem()] * 2,
        (shape(*edges.shape),),
        [row_scratch],
        {1: 0},
    )
    result = kernel_call(
        functools.partial(edge_kernel, cz),
        (edges, sides, middle, swap(y_b, None, 1)),
        [vmem()] * 4,
        (shape(9, cz, cy, cx), shape(cz, cy, cx), shape(cz, cy, cx), shape(*edges.shape)),
        [
            row_scratch,
            pltpu.VMEM((STAGES, layers + 1, cy, cx), f32),
            pltpu.VMEM((11, cz, cy, cx), f32),
            pltpu.SemaphoreType.DMA((4,)),
        ],
        {0: 3},
        (hbm(),) * 3 + (vmem(),),
    )
    return result[:3]


def solution(mesh):
    return jax.shard_map(
        on_device,
        mesh=mesh,
        in_specs=(
            P("gz", None, None, "gy", "gx"),
            P("gx", "gy", None, None),
            P("gx", "gy", None, None),
            P(None, "gz", "gy", "gx"),
            P("gz", "gy", "gx"),
            P("gz", "gy", "gx"),
            P("gz", "gy", "gx"),
            P("gz", "gy", "gx", None),
            P(),
            P("gz", "gy", "gx", None),
            P("gz", "gy", "gx", None, None),
            P(),
        ),
        out_specs=(P(None, "gz", "gy", "gx"), P("gz", "gy", "gx"), P("gz", "gy", "gx")),
        check_vma=False,
    )
```

```python
import functools

import jax
import jax.numpy as jnp
from jax import lax
from jax.experimental import pallas as pl
from jax.experimental.pallas import tpu as pltpu
from jax.sharding import PartitionSpec as P

VX, VY, VZ, SXX, SYY, SZZ, SXY, SXZ, SYZ = range(9)
FWD, ADJ, BUOY, LAM, MU, INJ, SRC = 0, 9, 18, 19, 20, 21, 22
FIELDS = 23
HALO = 2

ADJ_Z = {VX: (2, 2), VY: (2, 2), VZ: (2, 2), SXX: (1, 1), SYY: (1, 1), SZZ: (1, 2), SXY: (1, 1), SXZ: (2, 1), SYZ: (2, 1)}
OTHER_Z = {BUOY: (2, 2), LAM: (1, 2), MU: (2, 2), INJ: (0, 1), SRC: (1, 1)}
F32_Z = {**{ADJ + f: c for f, c in ADJ_Z.items()}, **OTHER_Z}

Y_ROWS = {
    FWD + VX: (None, (2, -1, 1), (1, -1, 1), (2, -2, 0)),
    FWD + VY: ((2, -2, 0), (1, -1, 1), (2, -1, 1), None),
    FWD + VZ: (None, (1, -2, 1), (1, -1, 1), (2, -2, 0)),
    FWD + SXX: (None, (2, -1, 1), (1, -1, 1), (2, -2, 1)),
    FWD + SYY: ((2, -2, 0), (1, -1, 1), (1, 0, 1), (2, -1, 1)),
    FWD + SZZ: (None, (1, -1, 1), (1, 0, 1), (2, -1, 0)),
    FWD + SXY: ((2, -1, 1), (1, 0, 1), (1, -1, 1), (2, -2, 0)),
    FWD + SXZ: (None, (1, -1, 1), (0, -1, 1), (1, -2, 1)),
    FWD + SYZ: ((1, -2, 1), (0, -1, 1), (1, -1, 1), (2, -2, 0)),
    ADJ + VX: ((2, -2, 0), (1, -1, 1), (1, -1, 1), (2, -2, 1)),
    ADJ + VY: ((2, -1, 1), (1, 0, 1), (1, -1, 1), (2, -2, 0)),
    ADJ + VZ: ((2, -2, 0), (1, -1, 1), (0, -1, 1), (1, -2, 0)),
    ADJ + SXX: (None, (2, -2, 1), (2, -2, 1), None),
    ADJ + SYY: (None, (2, -1, 1), (1, -1, 1), (2, -2, 0)),
    ADJ + SZZ: (None, (2, -1, 0), (1, -1, 0), None),
    ADJ + SXY: ((2, -2, 0), (1, -1, 1), (2, -2, 1), None),
    ADJ + SXZ: (None, (1, -2, 1), (1, -2, 1), None),
    ADJ + SYZ: ((2, -2, 0), (1, -1, 1), (1, -2, 0), None),
    BUOY: ((2, -2, 0), (1, -1, 1), (1, -1, 1), (2, -2, 0)),
    LAM: (None, (2, -1, 1), (1, -1, 1), (2, -2, 0)),
    MU: ((2, -2, 0), (1, -1, 1), (1, -1, 1), (2, -2, 0)),
    INJ: (None, None, (2, -2, 0), None),
    SRC: (None, (2, -2, 0), (2, -1, 1), None),
}

EXACT_ROWS = {-1: (ADJ + VY, ADJ + SXY, ADJ + SYZ, BUOY, SRC), 0: (ADJ + SYY, LAM, INJ, SRC)}

PAD = 1
VMEM_LIMIT = 48 * 1024 * 1024


def vmem():
    return pl.BlockSpec(memory_space=pltpu.VMEM)


def hbm():
    return pl.BlockSpec(memory_space=pl.ANY)


def faces(cz, up):
    near, far = [], []
    for f in sorted(F32_Z):
        before, after = F32_Z[f]
        depth = before if up else after
        for d in range(depth):
            layer = cz - 1 - d if up else d
            (far if d else near).append((f, layer, HALO - 1 - d if up else HALO + cz + d))
    return near, far


def face_counts(cz):
    sides = [faces(cz, up) for up in (True, False)]
    return max(len(s[0]) for s in sides), max(len(s[1]) for s in sides)


def y_rows(cz, cy, up):
    layers = cz + 2 * HALO
    narrow, wide, strip = [], [], []
    for f in sorted(Y_ROWS):
        for offset in (-1, -2) if up else (0, 1):
            spec = Y_ROWS[f][offset + HALO]
            if spec is None:
                continue
            source = cy + offset if up else offset
            target = cy - HALO + offset if up else HALO + offset
            exact = f in EXACT_ROWS.get(offset, ())
            (wide if exact else narrow).extend((f, z, source, target) for z in range(spec[0], layers + spec[1]))
            if spec[2]:
                strip.append((f, layers, source, target))
    return narrow, wide, strip


def row_counts(cz, cy, up):
    return tuple(-(-len(rows) // 8) for rows in y_rows(cz, cy, up))


def row_tiles(cz, cy):
    sides = [row_counts(cz, cy, up) for up in (True, False)]
    return max(c for _, _, c in sides), max(n + 2 * w for n, w, _ in sides)


def split(value):
    high = value.astype(jnp.bfloat16)
    low = (value - high.astype(jnp.float32)).astype(jnp.bfloat16)
    return high, low


def joined(high, low):
    return high.astype(jnp.float32) + low.astype(jnp.float32)


def even_mask(axes, shape):
    total = sum(lax.axis_index(a) for a in ((axes,) if isinstance(axes, str) else axes))
    return jnp.full(shape, lax.rem(total, 2), jnp.int32) == 0


def has_neighbours(axis):
    index = lax.axis_index(axis)
    return (index > 0).astype(jnp.float32), (index < lax.axis_size(axis) - 1).astype(jnp.float32)


def copies(sems, *pairs):
    out = [pltpu.make_async_copy(source, target, sems.at[i]) for i, (source, target) in enumerate(pairs)]
    for copy in out:
        copy.start()
    return out


def scatter_rows(packed, listed, row_of):
    for r, (f, z, y, _) in enumerate(listed):
        packed[r // 8, r % 8 : r % 8 + 1, :] = row_of(f, z, y)


def pack_tiles(sides, sends, first, count):
    even = even_mask(("gy", "gz"), sends[0].shape[1:])
    for t in range(count):
        up, down = (side[min(t, len(side) - 1)] for side in sides)
        sends[0][first + t] = jnp.where(even, down, up).astype(jnp.bfloat16)
        sends[1][first + t] = jnp.where(even, up, down).astype(jnp.bfloat16)


def layer_rows_kernel(cz, ring_f, ring_w, send_a, send_b, packed):
    cy = ring_f.shape[2]
    strip_tiles, tiles = row_tiles(cz, cy)

    def row_of(f, z, y):
        return ring_f[f, z, y : y + 1, :] if f < ADJ else ring_w[f - ADJ, z, y : y + 1, :]

    sides = []
    for side, up in enumerate((True, False)):
        narrow, wide, _ = y_rows(cz, cy, up)
        n, w, _ = row_counts(cz, cy, up)
        scatter_rows(packed.at[side], narrow, row_of)
        scatter_rows(packed.at[side, pl.ds(n, w)], wide, row_of)
        rest = [split(packed[side, n + t])[1].astype(jnp.float32) for t in range(w)]
        sides.append([packed[side, t] for t in range(n + w)] + rest)
    pack_tiles(sides, (send_a, send_b), strip_tiles, tiles)


def unpack_rows(cz, cy, first, message, packed, edges):
    has_lower, has_upper = has_neighbours("gy")
    strip_tiles, _ = row_tiles(cz, cy)
    parity = lax.rem(lax.axis_index("gy") + lax.axis_index("gz"), 2)

    def side(up, keep):
        narrow, wide, strip = y_rows(cz, cy, up)
        n, w, c = row_counts(cz, cy, up)
        for t in range(n + w):
            value = message[strip_tiles + t].astype(jnp.float32)
            if t >= n:
                value = value + message[strip_tiles + w + t].astype(jnp.float32)
            packed[t] = value * keep
        for t in range(c):
            packed[n + w + t] = message[t].astype(jnp.float32) * keep
        for base, listed in ((0, narrow), (n, wide), (n + w, strip)):
            for r, (f, z, _, y) in enumerate(listed):
                edges[f, z, y : y + 1, :] = packed[base + r // 8, r % 8 : r % 8 + 1, :]

    @pl.when(parity == (0 if first else 1))
    def _():
        side(True, has_lower)

    @pl.when(parity == (1 if first else 0))
    def _():
        side(False, has_upper)


def first_rows_kernel(cz, message, edges_in, edges, packed):
    unpack_rows(cz, edges.shape[2], True, message, packed, edges)


def start_kernel(
    cz, store, adjoint, lam, mu, buoy, source, wavelet, receiver, traces, plan, peer, slot,
    near_out, far_out, own, codes, cells, samples, spots, wave, steps, peers, slots, sems,
):
    cy, lanes = own.shape[2], own.shape[3]
    rows = cz * cy
    tiles = store.shape[0]
    small = copies(
        sems, (plan, steps), (wavelet, wave), (source, spots), (receiver, cells), (traces, samples),
        (peer, peers), (slot, slots),
    )
    large = copies(
        sems.at[pl.ds(len(small), 5)],
        (adjoint, own.at[pl.ds(0, 9)]),
        (buoy, own.at[BUOY - ADJ]),
        (lam, own.at[LAM - ADJ]),
        (mu, own.at[MU - ADJ]),
        (store, near_out.at[pl.ds(0, tiles)]),
    )
    for copy in small:
        copy.wait()
    lane = lax.broadcasted_iota(jnp.int32, (cy, lanes), 1)
    code = jnp.zeros((cy, lanes), jnp.int32)
    for z, hops, row in pieces(cz, peers, slots):
        code = jnp.where(lane == z, row * 4 + hops, code)
    codes[...] = code
    listed = cells[...]
    count = listed.shape[1]
    row_hot = (lax.broadcasted_iota(jnp.int32, (rows, count), 0) == listed // lanes).astype(jnp.bfloat16)
    lane_hit = lax.broadcasted_iota(jnp.int32, (lanes, count), 0) == listed % lanes
    rest = jnp.concatenate([jnp.where(lane_hit, samples[pl.ds(steps[step], 1), :], 0.0) for step in (1, 0)], axis=0)
    both = jnp.zeros((rows, 2 * lanes), jnp.float32)
    for _ in range(3):
        part = rest.astype(jnp.bfloat16)
        rest = rest - part.astype(jnp.float32)
        both = both + lax.dot_general(
            row_hot, part, (((1,), (1,)), ((), ())), preferred_element_type=jnp.float32
        )
    injected = [both[:, :lanes].reshape(cz, cy, lanes), both[:, lanes:].reshape(cz, cy, lanes)]
    own[INJ - ADJ] = injected[1]
    flat = lax.broadcasted_iota(jnp.int32, (rows, lanes), 0) * lanes + lax.broadcasted_iota(jnp.int32, (rows, lanes), 1)
    for step in range(2):
        value = wave[steps[step]]
        field = jnp.zeros((rows, lanes), jnp.float32)
        for j in range(source.shape[1]):
            field = field + jnp.where(flat == spots[0, j], value, 0.0)
        own[SRC - ADJ + step] = field.reshape(cz, cy, lanes)
    for copy in large:
        copy.wait()
    for f in (SXX, SYY, SZZ):
        own[f] = own[f] + injected[0]

    even = even_mask("gz", (cy, lanes))
    near, far = face_counts(cz)
    up, down = faces(cz, True), faces(cz, False)
    zero = jnp.zeros((cy, lanes), jnp.float32)

    def tile(side, i):
        return own[side[i][0] - ADJ, side[i][1]] if i < len(side) else zero

    for i in range(near):
        above, below = tile(up[0], i), tile(down[0], i)
        for out, base, value in (
            (near_out, tiles, jnp.where(even, above, below)),
            (far_out, 0, jnp.where(even, below, above)),
        ):
            out[base + i], out[base + near + i] = split(value)
    for i in range(far):
        above, below = tile(up[1], i), tile(down[1], i)
        near_out[tiles + 2 * near + i] = jnp.where(even, above, below).astype(jnp.bfloat16)
        far_out[2 * near + i] = jnp.where(even, below, above).astype(jnp.bfloat16)
    for i in range(2 * near + far, far_out.shape[0]):
        far_out[i] = zero.astype(jnp.bfloat16)


def strip_part(tile, main, listed):
    lanes = tile.shape[1]
    lane = lax.broadcasted_iota(jnp.int32, tile.shape, 1)
    for z in listed:
        tile = jnp.where((lane >= 8 * z) & (lane < 8 * z + 4), pltpu.roll(main(z), (8 * z + 2) % lanes, 1), tile)
    return tile


def strip_whole(tile):
    position = lax.broadcasted_iota(jnp.int32, tile.shape, 1) % 8
    return jnp.where(position < 2, tile, jnp.where(position >= 6, pltpu.roll(tile, 4, 1), 0.0))


def pieces(cz, peers, slots):
    me, count = lax.axis_index("gz"), lax.axis_size("gz")
    below, above = jnp.maximum(me - 1, 0), jnp.minimum(me + 1, count - 1)
    for z in range(cz + 2 * HALO):
        if z < HALO:
            brick, piece = below, cz - HALO + z
        elif z < HALO + cz:
            brick, piece = me, z - HALO
        else:
            brick, piece = above, z - HALO - cz
        yield z, peers[brick, piece] ^ me, slots[brick, piece] * 9


def coded(cz, codes):
    has_below, has_above = has_neighbours("gz")
    listed = codes[0:1, :]
    for z in range(cz + 2 * HALO):
        code = listed[0, z]
        keep = has_below if z < HALO else None if z < HALO + cz else has_above
        yield z, code & 3, code >> 2, keep


def frame_kernel(cz, mine, core, chip, codes, own, ring_f, ring):
    cy, lanes = own.shape[2], own.shape[3]
    layers = cz + 2 * HALO
    zero = jnp.zeros((cy, lanes), jnp.float32)
    filled = {(f - ADJ, z) for up in (True, False) for listed in faces(cz, up) for f, _, z in listed}
    for f in range(ring.shape[0]):
        for z in range(cz):
            ring[f, HALO + z] = own[f, z]
        for z in (0, 1, layers - 2, layers - 1):
            if (f, z) not in filled:
                ring[f, z] = zero
        ring[f, layers] = strip_part(zero, lambda z: own[f, z - HALO], range(HALO, HALO + cz))
    for z, hops, row, keep in coded(cz, codes):
        hops = jnp.full((cy, lanes), hops, jnp.int32)
        for f in range(9):
            a, b, c = (ref[row + f].astype(jnp.float32) for ref in (mine, core, chip))
            value = jnp.where(hops == 0, a, jnp.where(hops == 1, b, c))
            ring_f[f, z] = value if keep is None else value * keep


def column_kernel(
    cz, core, both_a, both_b, far, codes, ring_f_in, ring_w_in, ring_f, ring, x_a, x_b
):
    cy, lanes = core.shape[1], core.shape[2]
    layers = cz + 2 * HALO
    half = both_a.shape[0]
    tiles = half + both_b.shape[0]
    near, _ = face_counts(cz)
    even = even_mask("gz", (cy, lanes))
    has_below, has_above = has_neighbours("gz")
    zero = jnp.zeros((cy, lanes), jnp.float32)
    filled = {}
    for up in (True, False):
        for depth, listed in enumerate(faces(cz, up)):
            for i, (f, _, z) in enumerate(listed):
                values = []
                for ref, base in ((core, tiles), (far, 0)):
                    if depth == 0:
                        values.append(joined(ref[base + i], ref[base + near + i]))
                    else:
                        values.append(ref[base + 2 * near + i].astype(jnp.float32))
                value = jnp.where(even, values[1], values[0]) if up else jnp.where(even, values[0], values[1])
                value = value * (has_below if up else has_above)
                ring[f - ADJ, z] = value
                filled.setdefault(f - ADJ, {})[z] = value
    strip = []
    for f in range(ring.shape[0]):
        there = filled.get(f, {})
        tile = strip_whole(strip_part(ring[f, layers], lambda z: there[z], sorted(there)))
        ring[f, layers] = tile
        strip.append(tile)
    for z, hops, row, keep in coded(cz, codes):
        last = jnp.full((cy, lanes), hops, jnp.int32) == 3
        late = jnp.full((cy, lanes), row, jnp.int32) >= half
        row_a, row_b = jnp.minimum(row, half - 9), jnp.maximum(row - half, 0)
        for f in range(9):
            a, b = both_a[row_a + f].astype(jnp.float32), both_b[row_b + f].astype(jnp.float32)
            value = jnp.where(late, b, a)
            ring_f[f, z] = jnp.where(last, value if keep is None else value * keep, ring_f[f, z])
    for f in range(9):
        ring_f[f, layers] = strip_whole(strip_part(zero, lambda z: ring_f[f, z], range(layers)))
    strip = [ring_f[f, layers] for f in range(9)] + strip
    position = lax.broadcasted_iota(jnp.int32, (cy, lanes), 1) % 8
    even_x = even_mask("gx", (cy, lanes))
    for out, tail_from_even in ((x_a, True), (x_b, False)):
        if out is None:
            continue
        place = 0
        for fields in (range(ADJ), range(ADJ, FIELDS)):
            quads = [fields[i : i + 4] for i in range(0, len(fields), 4)]
            for i, quad in enumerate(quads):
                tile = zero
                for g, f in enumerate(quad):
                    tail, head = strip[f], pltpu.roll(strip[f], lanes - 6, 1)
                    value = jnp.where(even_x, tail, head) if tail_from_even else jnp.where(even_x, head, tail)
                    value = value if g == 0 else pltpu.roll(value, 2 * g, 1)
                    tile = jnp.where(position // 2 == g, value, tile)
                high, low = split(tile)
                out[place + i] = high
                if quad[-1] >= INJ:
                    out[x_tiles() - 1] = low
            place += len(quads)


def x_tiles():
    return -(-ADJ // 4) + -(-(FIELDS - ADJ) // 4) + 1


def strip_rows_kernel(cz, ring_f, ring_w, x_a, x_b, y_a_in, y_b_in, strips, y_a, y_b, packed):
    cy, lanes = strips.shape[1], strips.shape[2]
    layers = cz + 2 * HALO
    pair = lax.broadcasted_iota(jnp.int32, (cy, lanes), 1) % 8 // 2
    even_x = even_mask("gx", (cy, lanes))
    has_left, has_right = has_neighbours("gx")
    zero = jnp.zeros((cy, lanes), jnp.float32)
    place = 0
    for fields in (range(ADJ), range(ADJ, FIELDS)):
        quads = [fields[i : i + 4] for i in range(0, len(fields), 4)]
        for i, quad in enumerate(quads):
            got = []
            for ref in (x_a, x_b):
                if ref is None:
                    got.append(zero)
                elif quad[-1] < INJ:
                    got.append(ref[place + i].astype(jnp.float32))
                else:
                    got.append(joined(ref[place + i], ref[x_tiles() - 1]))
            right = jnp.where(even_x, got[0], got[1]) * has_right
            left = jnp.where(even_x, got[1], got[0]) * has_left
            for g, f in enumerate(quad):
                strip = ring_f[f, layers] if f < ADJ else ring_w[f - ADJ, layers]
                tile = jnp.where(pair == 1, pltpu.roll(right, (2 - 2 * g) % lanes, 1), strip)
                strips[f] = jnp.where(pair == 2, pltpu.roll(left, (4 - 2 * g) % lanes, 1), tile)
        place += len(quads)
    sides = []
    for side, up in enumerate((True, False)):
        scatter_rows(packed.at[side], y_rows(cz, cy, up)[2], lambda f, z, y: strips[f, y : y + 1, :])
        sides.append([packed[side, t] for t in range(row_counts(cz, cy, up)[2])])
    pack_tiles(sides, (y_a, y_b), 0, packed.shape[1])


STAGE = {"fv": 0, "fs": 3, "fw": 9, "as": 12, "av": 18, "at": 21}
STAGES = 27
NORMAL = (SXX, SYY, SZZ)
STRESS = range(SXX, SYZ + 1)


def window(cz, base, stage, after, before, put):
    layers = cz + 2 * HALO
    edge = layers
    cy, lanes = stage.shape[2], stage.shape[3]
    lane = lax.broadcasted_iota(jnp.int32, (cy, lanes), 1)
    first_lane, last_lane = lane == 0, lane == lanes - 1
    inner = range(HALO, HALO + cz)

    def start(field):
        return lambda z: base(field, z)

    def kept(name, field):
        index = STAGE[name] + field
        return lambda z: stage[index, z]

    def x_next(of, z):
        value = pltpu.roll(of(z), lanes - 1, 1)
        if z == edge:
            return value
        return jnp.where(last_lane, pltpu.roll(of(edge), (lanes - 1 - (8 * z + 2)) % lanes, 1), value)

    def x_prev(of, z):
        value = pltpu.roll(of(z), 1, 1)
        if z == edge:
            return value
        return jnp.where(first_lane, pltpu.roll(of(edge), (lanes - (8 * z + 5)) % lanes, 1), value)

    def z_next(of, z):
        return pltpu.roll(of(edge), lanes - 8, 1) if z == edge else of(z + 1)

    def z_prev(of, z):
        return pltpu.roll(of(edge), 8, 1) if z == edge else of(z - 1)

    def velocity_rates(k, s, z, want):
        buoy = base(BUOY, z)
        sxx, syy, szz, sxy, sxz, syz = s
        out = {}
        if VX in want:
            xy = sxy(z)
            out[VX] = buoy * (
                (x_next(sxx, z) - sxx(z)) + (xy - before(k, 0, z, xy)) + (sxz(z) - z_prev(sxz, z))
            )
        if VY in want:
            yy = syy(z)
            out[VY] = buoy * (
                (sxy(z) - x_prev(sxy, z)) + (after(k, 1, z, yy) - yy) + (syz(z) - z_prev(syz, z))
            )
        if VZ in want:
            yz = syz(z)
            out[VZ] = buoy * (
                (sxz(z) - x_prev(sxz, z)) + (yz - before(k, 2, z, yz)) + (z_next(szz, z) - szz(z))
            )
        return out

    def stress_rates(k, v, z, want):
        lam, mu = base(LAM, z), base(MU, z)
        of_x, of_y, of_z = v
        vx, vy, vz = of_x(z), of_y(z), of_z(z)
        out = {}
        if SXX in want:
            exx = vx - x_prev(of_x, z)
            eyy = vy - before(k, 0, z, vy)
            ezz = vz - z_prev(of_z, z)
            common = lam * (exx + eyy + ezz)
            twice = 2.0 * mu
            out[SXX] = common + twice * exx
            out[SYY] = common + twice * eyy
            out[SZZ] = common + twice * ezz
        if SXY in want:
            out[SXY] = mu * ((after(k, 1, z, vx) - vx) + (x_next(of_y, z) - vy))
        if SXZ in want:
            out[SXZ] = mu * ((z_next(of_x, z) - vx) + (x_next(of_z, z) - vz))
            out[SYZ] = mu * ((z_next(of_y, z) - vy) + (after(k, 2, z, vz) - vz))
        return out

    def spread(ranges):
        for z in range(layers + 1):
            want = {f for f, (a, b) in ranges.items() if z == edge or a <= z < b}
            if want:
                yield z, want

    def velocity_step(k, name, v, s, sign, ranges):
        for z, want in spread(ranges):
            for f, rate in velocity_rates(k, s, z, want).items():
                stage[STAGE[name] + f, z] = v[f](z) + rate if sign > 0 else v[f](z) - rate
        return [kept(name, f) for f in (VX, VY, VZ)]

    def stress_step(k, name, v, s, sign, ranges, ahead=None, behind=None):
        for z, want in spread(ranges):
            for f, rate in stress_rates(k, v, z, want).items():
                value = s[f - SXX](z)
                if ahead is not None and f in NORMAL:
                    value = value + base(ahead, z)
                value = value + rate if sign > 0 else value - rate
                if behind is not None and f in NORMAL:
                    value = value + base(behind, z)
                stage[STAGE[name] + f - SXX, z] = value
        return [kept(name, f - SXX) for f in STRESS]

    def terms(f, a):
        term_lam = (f[0] + f[1] + f[2]) * (a[0] + a[1] + a[2])
        term_mu = f[0] * a[0] + f[1] * a[1] + f[2] * a[2] + 2.0 * (f[3] * a[3] + f[4] * a[4] + f[5] * a[5])
        return term_lam, term_mu

    n = layers
    fv, fs = [start(FWD + f) for f in (VX, VY, VZ)], [start(FWD + f) for f in STRESS]
    av, first = [start(ADJ + f) for f in (VX, VY, VZ)], [start(ADJ + f) for f in STRESS]
    a_s = stress_step(0, "as", av, first, -1, {SXX: (1, n), SXY: (0, n), SXZ: (0, n - 1)})
    fv = velocity_step(1, "fv", fv, fs, 1, {VX: (1, n), VY: (1, n), VZ: (0, n - 1)})
    fs = stress_step(2, "fs", fv, fs, 1, {SXX: (1, n - 1), SXY: (1, n - 1), SXZ: (1, n - 1)}, behind=SRC)
    fv = velocity_step(3, "fw", fv, fs, 1, {VX: (2, n - 1), VY: (2, n - 1), VZ: (1, n - 2)})
    for z in inner:
        rates = stress_rates(4, fv, z, set(STRESS))
        now = [of(z) for of in fs]
        later = [now[s - SXX] + rates[s] + (base(FIELDS, z) if s in NORMAL else 0.0) for s in STRESS]
        lam_late, mu_late = terms(later, [of(z) for of in first])
        with_traces = [of(z) + (base(INJ, z) if s in NORMAL else 0.0) for s, of in zip(STRESS, a_s)]
        lam_early, mu_early = terms(now, with_traces)
        put(9, z - HALO, lam_late + lam_early)
        put(10, z - HALO, mu_late + mu_early)
    av = velocity_step(5, "av", av, a_s, -1, {VX: (1, n - 1), VY: (1, n - 1), VZ: (1, n - 1)})
    a_s = stress_step(6, "at", av, a_s, -1, {SXX: (2, n - 1), SXY: (1, n - 1), SXZ: (1, n - 2)}, ahead=INJ)
    for s, of in zip(STRESS, a_s):
        for z in inner:
            put(s, z - HALO, of(z))
    for z in inner:
        rates = velocity_rates(7, a_s, z, {VX, VY, VZ})
        for f in (VX, VY, VZ):
            put(f, z - HALO, av[f](z) - rates[f])


def middle_kernel(cz, ring_f, ring_w, strips, own, edges, sides, middle, stage):
    cy, lanes = own.shape[2], own.shape[3]
    layers = cz + 2 * HALO

    def base(f, z):
        if f == FIELDS:
            return own[f - ADJ, z - HALO]
        if z == layers:
            return strips[f]
        return ring_f[f, z] if f < ADJ else ring_w[f - ADJ, z]

    row = lax.broadcasted_iota(jnp.int32, (cy, lanes), 0)
    for f in range(FIELDS + 1):
        for z in range(HALO, HALO + cz) if f == FIELDS else range(layers + 1):
            tile = base(f, z)
            tail, head = pltpu.roll(tile, HALO, 0), pltpu.roll(tile, cy - HALO, 0)
            edges[f, z] = jnp.where(row < HALO, tail, jnp.where(row >= cy - HALO, head, 0.0))

    def after(k, j, z, tile):
        sides[k, j, z] = pltpu.roll(tile, cy - 1 - HALO, 0)
        return pltpu.roll(tile, cy - 1, 0)

    def before(k, j, z, tile):
        sides[k, j, z] = pltpu.roll(tile, HALO + 1, 0)
        return pltpu.roll(tile, 1, 0)

    def put(i, z, value):
        middle[i, z] = value

    window(cz, base, stage, after, before, put)


def edge_kernel(
    cz, edges_in, sides, middle, message, final, image_lam, image_mu, edges, packed, stage, result, sems
):
    cy, lanes = middle.shape[2], middle.shape[3]

    unpack_rows(cz, cy, False, message, packed, edges)
    row = lax.broadcasted_iota(jnp.int32, (cy, lanes), 0)

    def after(k, j, z, tile):
        return jnp.where(row == cy - 1, sides[k, j, z], pltpu.roll(tile, cy - 1, 0))

    def before(k, j, z, tile):
        return jnp.where(row == 0, sides[k, j, z], pltpu.roll(tile, 1, 0))

    moves = []

    def put(i, z, value):
        tail, head = pltpu.roll(value, HALO, 0), pltpu.roll(value, cy - HALO, 0)
        result[i, z] = jnp.where(row < HALO, tail, jnp.where(row >= cy - HALO, head, middle[i, z]))
        if z == cz - 1:
            if i == 10:
                moves.extend(copies(sems, (result.at[9], image_lam), (result.at[10], image_mu)))
            if i == SYZ:
                part = pl.ds(SXX, SYZ + 1 - SXX)
                moves.extend(copies(sems.at[pl.ds(2, 1)], (result.at[part], final.at[part])))
            if i == VZ:
                part = pl.ds(VX, VZ + 1 - VX)
                moves.extend(copies(sems.at[pl.ds(3, 1)], (result.at[part], final.at[part])))

    window(cz, lambda f, z: edges[f, z], stage, after, before, put)
    for move in moves:
        move.wait()


def swap_pairs(count, first):
    pairs = [(i + d, i + 1 - d) for i in range(first, count - 1, 2) for d in (0, 1)]
    return pairs + [(i, i) for i in range(count) if i not in dict(pairs)]


def swapped(value_a, value_b, axis):
    count = lax.axis_size(axis)
    got_a = lax.ppermute(value_a, axis, swap_pairs(count, 0))
    return got_a, None if value_b is None else lax.ppermute(value_b, axis, swap_pairs(count, 1))


def stay(value, spec):
    return pltpu.with_memory_space_constraint(value, pltpu.HBM) if spec.memory_space == pl.ANY else value


def kernel_call(body, args, in_specs, out_shape, scratch_shapes=(), aliases=None, out_specs=None):
    here = [a is not None for a in args]
    there = [o is not None for o in out_shape]

    def run(*refs):
        refs = iter(refs)
        full = [next(refs) if h else None for h in here + there]
        body(*full, *refs)

    out = iter(
        pl.pallas_call(
            run,
            out_shape=tuple(o for o in out_shape if o is not None),
            in_specs=[s for s, h in zip(in_specs, here) if h],
            out_specs=out_specs or tuple(vmem() for h in there if h),
            scratch_shapes=list(scratch_shapes),
            input_output_aliases=aliases or {},
            compiler_params=pltpu.CompilerParams(vmem_limit_bytes=VMEM_LIMIT),
        )(*[stay(a, s) for a, s in zip(args, in_specs) if a is not None])
    )
    return tuple(next(out) if h else None for h in there)


def on_device(
    checkpoint_store,
    holder_peer,
    holder_slot,
    adjoint_state,
    lame_lambda,
    lame_mu,
    buoyancy,
    source_cell,
    wavelet,
    receiver_cell,
    traces,
    plan,
):
    cz, cy, cx = lame_mu.shape
    layers = cz + 2 * HALO
    bf16, f32 = jnp.bfloat16, jnp.float32
    store = checkpoint_store.reshape(-1, cy, cx)
    tiles = store.shape[0]
    peer, slot = holder_peer[0, 0], holder_slot[0, 0]
    source, receiver = source_cell.reshape(1, -1), receiver_cell.reshape(1, -1)
    traces = traces.reshape(traces.shape[-2:])
    holders = lax.axis_size("gz")
    assert holders == 4
    near, far = face_counts(cz)
    face = 2 * near + far
    half = tiles // 2

    def shape(*dims, dtype=f32):
        return jax.ShapeDtypeStruct(dims, dtype)

    wide_x = lax.axis_size("gx") > 2
    chip = lax.ppermute(store, "gz", [(i, i ^ 2) for i in range(holders)])
    to_core, to_far, own, codes = kernel_call(
        functools.partial(start_kernel, cz),
        (store, adjoint_state, lame_lambda, lame_mu, buoyancy, source, wavelet, receiver, traces, plan, peer, slot),
        [hbm()] * 12,
        (shape(tiles + face, cy, cx, dtype=bf16), shape(max(face, half) + PAD, cy, cx, dtype=bf16), shape(15, cz, cy, cx),
         shape(cy, cx, dtype=jnp.int32)),
        [
            pltpu.VMEM(receiver.shape, jnp.int32),
            pltpu.VMEM(traces.shape, f32),
            pltpu.SMEM(source.shape, jnp.int32),
            pltpu.SMEM(wavelet.shape, f32),
            pltpu.SMEM(plan.shape, jnp.int32),
            pltpu.SMEM(peer.shape, jnp.int32),
            pltpu.SMEM(slot.shape, jnp.int32),
            pltpu.SemaphoreType.DMA((12,)),
        ],
    )
    core = lax.ppermute(to_core, "gz", [(i, i ^ 1) for i in range(holders)])
    gy = lax.axis_size("gy")
    axes = ("gx", "gy", "gz")
    gx = lax.axis_size("gx")
    across = [
        ((i * gy + j) * holders + c, (i * gy + j) * holders + 3 - c if c in (1, 2) else ((i ^ 1) * gy + j) * holders + c)
        for i in range(gx) for j in range(gy) for c in range(holders)
    ]
    far_face = lax.ppermute(to_far, axes, across)
    both = [lax.ppermute(part, "gz", [(i, i ^ 1) for i in range(holders)]) for part in (chip[:half], chip[half:])]

    ring_f, ring_w = kernel_call(
        functools.partial(frame_kernel, cz),
        (to_core, core, chip, codes, own),
        [vmem()] * 5,
        (shape(ADJ, layers + 1, cy, cx), shape(FIELDS - ADJ, layers + 1, cy, cx)),
    )
    x_send = shape(x_tiles(), cy, cx, dtype=bf16)
    ring_f, ring_w, x_a, x_b = kernel_call(
        functools.partial(column_kernel, cz),
        (core, *both, far_face, codes, ring_f, ring_w),
        [vmem()] * 7,
        (shape(*ring_f.shape), shape(*ring_w.shape), x_send, x_send if wide_x else None),
        (),
        {5: 0, 6: 1},
    )
    def partner(i, j, c, x_turn, y_turn):
        if x_turn is not None:
            i = dict(swap_pairs(gx, x_turn))[i]
        if y_turn is not None:
            other = dict(swap_pairs(gy, (c + y_turn + 1) % 2))[j]
            i, j = (i ^ 1, j) if other == j else (i, other)
        return (i * gy + j) * holders + c

    def swap(value, x_turn, y_turn):
        if value is None:
            return None
        pairs = [
            ((i * gy + j) * holders + c, partner(i, j, c, x_turn, y_turn))
            for i in range(gx) for j in range(gy) for c in range(holders)
        ]
        return lax.ppermute(value, axes, pairs)

    strip_tiles, tiles = row_tiles(cz, cy)
    y_send = shape(strip_tiles + tiles, cy, cx, dtype=bf16)
    scratch_tiles = max(sum(row_counts(cz, cy, up)) for up in (True, False))
    y_a, y_b = kernel_call(
        functools.partial(layer_rows_kernel, cz),
        (ring_f, ring_w),
        [vmem()] * 2,
        (y_send, y_send),
        [pltpu.VMEM((2, scratch_tiles, 8, cx), f32)],
    )
    strips, y_a, y_b = kernel_call(
        functools.partial(strip_rows_kernel, cz),
        (ring_f, ring_w, swap(x_a, 0, None), swap(x_b, 1, None), y_a, y_b),
        [vmem()] * 6,
        (shape(FIELDS, cy, cx), y_send, y_send),
        [pltpu.VMEM((2, strip_tiles, 8, cx), f32)],
        {4 if wide_x else 3: 1, 5 if wide_x else 4: 2},
    )
    edges, sides, middle = kernel_call(
        functools.partial(middle_kernel, cz),
        (ring_f, ring_w, strips, own),
        [vmem()] * 4,
        (
            shape(FIELDS + 1, layers + 1, cy, cx),
            shape(8, 3, layers + 1, cy, cx),
            shape(11, cz, cy, cx),
        ),
        [pltpu.VMEM((STAGES, layers + 1, cy, cx), f32)],
    )
    row_scratch = pltpu.VMEM((scratch_tiles, 8, cx), f32)
    (edges,) = kernel_call(
        functools.partial(first_rows_kernel, cz),
        (swap(y_a, None, 0), edges),
        [vmem()] * 2,
        (shape(*edges.shape),),
        [row_scratch],
        {1: 0},
    )
    result = kernel_call(
        functools.partial(edge_kernel, cz),
        (edges, sides, middle, swap(y_b, None, 1)),
        [vmem()] * 4,
        (shape(9, cz, cy, cx), shape(cz, cy, cx), shape(cz, cy, cx), shape(*edges.shape)),
        [
            row_scratch,
            pltpu.VMEM((STAGES, layers + 1, cy, cx), f32),
            pltpu.VMEM((11, cz, cy, cx), f32),
            pltpu.SemaphoreType.DMA((4,)),
        ],
        {0: 3},
        (hbm(),) * 3 + (vmem(),),
    )
    return result[:3]


def solution(mesh):
    return jax.shard_map(
        on_device,
        mesh=mesh,
        in_specs=(
            P("gz", None, None, "gy", "gx"),
            P("gx", "gy", None, None),
            P("gx", "gy", None, None),
            P(None, "gz", "gy", "gx"),
            P("gz", "gy", "gx"),
            P("gz", "gy", "gx"),
            P("gz", "gy", "gx"),
            P("gz", "gy", "gx", None),
            P(),
            P("gz", "gy", "gx", None),
            P("gz", "gy", "gx", None, None),
            P(),
        ),
        out_specs=(P(None, "gz", "gy", "gx"), P("gz", "gy", "gx"), P("gz", "gy", "gx")),
        check_vma=False,
    )
```

```python
import functools

import jax
import jax.numpy as jnp
from jax import lax
from jax.experimental import pallas as pl
from jax.experimental.pallas import tpu as pltpu
from jax.sharding import PartitionSpec as P

VX, VY, VZ, SXX, SYY, SZZ, SXY, SXZ, SYZ = range(9)
FWD, ADJ, BUOY, LAM, MU, INJ, SRC = 0, 9, 18, 19, 20, 21, 22
FIELDS = 23
HALO = 2

ADJ_Z = {VX: (2, 2), VY: (2, 2), VZ: (2, 2), SXX: (1, 1), SYY: (1, 1), SZZ: (1, 2), SXY: (1, 1), SXZ: (2, 1), SYZ: (2, 1)}
OTHER_Z = {BUOY: (2, 2), LAM: (1, 2), MU: (2, 2), INJ: (0, 1), SRC: (1, 1)}
F32_Z = {**{ADJ + f: c for f, c in ADJ_Z.items()}, **OTHER_Z}

Y_ROWS = {
    FWD + VX: (None, (2, -1, 1), (1, -1, 1), (2, -2, 0)),
    FWD + VY: ((2, -2, 0), (1, -1, 1), (2, -1, 1), None),
    FWD + VZ: (None, (1, -2, 1), (1, -1, 1), (2, -2, 0)),
    FWD + SXX: (None, (2, -1, 1), (1, -1, 1), (2, -2, 1)),
    FWD + SYY: ((2, -2, 0), (1, -1, 1), (1, 0, 1), (2, -1, 1)),
    FWD + SZZ: (None, (1, -1, 1), (1, 0, 1), (2, -1, 0)),
    FWD + SXY: ((2, -1, 1), (1, 0, 1), (1, -1, 1), (2, -2, 0)),
    FWD + SXZ: (None, (1, -1, 1), (0, -1, 1), (1, -2, 1)),
    FWD + SYZ: ((1, -2, 1), (0, -1, 1), (1, -1, 1), (2, -2, 0)),
    ADJ + VX: ((2, -2, 0), (1, -1, 1), (1, -1, 1), (2, -2, 1)),
    ADJ + VY: ((2, -1, 1), (1, 0, 1), (1, -1, 1), (2, -2, 0)),
    ADJ + VZ: ((2, -2, 0), (1, -1, 1), (0, -1, 1), (1, -2, 0)),
    ADJ + SXX: (None, (2, -2, 1), (2, -2, 1), None),
    ADJ + SYY: (None, (2, -1, 1), (1, -1, 1), (2, -2, 0)),
    ADJ + SZZ: (None, (2, -1, 0), (1, -1, 0), None),
    ADJ + SXY: ((2, -2, 0), (1, -1, 1), (2, -2, 1), None),
    ADJ + SXZ: (None, (1, -2, 1), (1, -2, 1), None),
    ADJ + SYZ: ((2, -2, 0), (1, -1, 1), (1, -2, 0), None),
    BUOY: ((2, -2, 0), (1, -1, 1), (1, -1, 1), (2, -2, 0)),
    LAM: (None, (2, -1, 1), (1, -1, 1), (2, -2, 0)),
    MU: ((2, -2, 0), (1, -1, 1), (1, -1, 1), (2, -2, 0)),
    INJ: (None, None, (2, -2, 0), None),
    SRC: (None, (2, -2, 0), (2, -1, 1), None),
}

EXACT_ROWS = {-1: (ADJ + VY, ADJ + SXY, ADJ + SYZ, BUOY, SRC), 0: (ADJ + SYY, LAM, INJ, SRC)}

PAD = 1
VMEM_LIMIT = 48 * 1024 * 1024


def vmem():
    return pl.BlockSpec(memory_space=pltpu.VMEM)


def hbm():
    return pl.BlockSpec(memory_space=pl.ANY)


def faces(cz, up):
    near, far = [], []
    for f in sorted(F32_Z):
        before, after = F32_Z[f]
        depth = before if up else after
        for d in range(depth):
            layer = cz - 1 - d if up else d
            (far if d else near).append((f, layer, HALO - 1 - d if up else HALO + cz + d))
    return near, far


def face_counts(cz):
    sides = [faces(cz, up) for up in (True, False)]
    return max(len(s[0]) for s in sides), max(len(s[1]) for s in sides)


def y_rows(cz, cy, up):
    layers = cz + 2 * HALO
    narrow, wide, strip = [], [], []
    for f in sorted(Y_ROWS):
        for offset in (-1, -2) if up else (0, 1):
            spec = Y_ROWS[f][offset + HALO]
            if spec is None:
                continue
            source = cy + offset if up else offset
            target = cy - HALO + offset if up else HALO + offset
            exact = f in EXACT_ROWS.get(offset, ())
            (wide if exact else narrow).extend((f, z, source, target) for z in range(spec[0], layers + spec[1]))
            if spec[2]:
                strip.append((f, layers, source, target))
    return narrow, wide, strip


def row_counts(cz, cy, up):
    return tuple(-(-len(rows) // 8) for rows in y_rows(cz, cy, up))


def row_tiles(cz, cy):
    sides = [row_counts(cz, cy, up) for up in (True, False)]
    return max(c for _, _, c in sides), max(n + 2 * w for n, w, _ in sides)


def split(value):
    high = value.astype(jnp.bfloat16)
    low = (value - high.astype(jnp.float32)).astype(jnp.bfloat16)
    return high, low


def joined(high, low):
    return high.astype(jnp.float32) + low.astype(jnp.float32)


def even_mask(axes, shape):
    total = sum(lax.axis_index(a) for a in ((axes,) if isinstance(axes, str) else axes))
    return jnp.full(shape, lax.rem(total, 2), jnp.int32) == 0


def has_neighbours(axis):
    index = lax.axis_index(axis)
    return (index > 0).astype(jnp.float32), (index < lax.axis_size(axis) - 1).astype(jnp.float32)


def copies(sems, *pairs):
    out = [pltpu.make_async_copy(source, target, sems.at[i]) for i, (source, target) in enumerate(pairs)]
    for copy in out:
        copy.start()
    return out


def scatter_rows(packed, listed, row_of):
    for r, (f, z, y, _) in enumerate(listed):
        packed[r // 8, r % 8 : r % 8 + 1, :] = row_of(f, z, y)


def pack_tiles(sides, sends, firsts, count):
    even = even_mask(("gy", "gz"), sends[0].shape[1:])
    for t in range(count):
        up, down = (side[min(t, len(side) - 1)] for side in sides)
        sends[0][firsts[0] + t] = jnp.where(even, down, up).astype(jnp.bfloat16)
        sends[1][firsts[1] + t] = jnp.where(even, up, down).astype(jnp.bfloat16)


def layer_rows_kernel(cz, ring_f, ring_w, send_a, send_b, packed):
    cy = ring_f.shape[2]
    strip_tiles, tiles = row_tiles(cz, cy)

    def row_of(f, z, y):
        return ring_f[f, z, y : y + 1, :] if f < ADJ else ring_w[f - ADJ, z, y : y + 1, :]

    sides = []
    for side, up in enumerate((True, False)):
        narrow, wide, _ = y_rows(cz, cy, up)
        n, w, _ = row_counts(cz, cy, up)
        scatter_rows(packed.at[side], narrow, row_of)
        scatter_rows(packed.at[side, pl.ds(n, w)], wide, row_of)
        rest = [split(packed[side, n + t])[1].astype(jnp.float32) for t in range(w)]
        sides.append([packed[side, t] for t in range(n + w)] + rest)
    pack_tiles(sides, (send_a, send_b), (0, strip_tiles), tiles)
    for t in range(tiles, send_a.shape[0]):
        send_a[t] = jnp.zeros(send_a.shape[1:], send_a.dtype)


def unpack_rows(cz, cy, first, strips, message, packed, edges):
    has_lower, has_upper = has_neighbours("gy")
    skipped = 0 if first else row_tiles(cz, cy)[0]
    parity = lax.rem(lax.axis_index("gy") + lax.axis_index("gz"), 2)

    def side(up, keep):
        narrow, wide, strip = y_rows(cz, cy, up)
        n, w, c = row_counts(cz, cy, up)
        for t in range(n + w):
            value = message[skipped + t].astype(jnp.float32)
            if t >= n:
                value = value + message[skipped + w + t].astype(jnp.float32)
            packed[t] = value * keep
        for t in range(c):
            packed[n + w + t] = strips[t].astype(jnp.float32) * keep
        for base, listed in ((0, narrow), (n, wide), (n + w, strip)):
            for r, (f, z, _, y) in enumerate(listed):
                edges[f, z, y : y + 1, :] = packed[base + r // 8, r % 8 : r % 8 + 1, :]

    @pl.when(parity == (0 if first else 1))
    def _():
        side(True, has_lower)

    @pl.when(parity == (1 if first else 0))
    def _():
        side(False, has_upper)


def first_rows_kernel(cz, strips, message, edges_in, edges, packed):
    unpack_rows(cz, edges.shape[2], True, strips, message, packed, edges)


def start_kernel(
    cz, store, adjoint, lam, mu, buoy, source, wavelet, receiver, traces, plan, peer, slot,
    near_out, far_out, own, codes, cells, samples, spots, wave, steps, peers, slots, sems,
):
    cy, lanes = own.shape[2], own.shape[3]
    rows = cz * cy
    tiles = store.shape[0]
    small = copies(
        sems, (plan, steps), (wavelet, wave), (source, spots), (receiver, cells), (traces, samples),
        (peer, peers), (slot, slots),
    )
    large = copies(
        sems.at[pl.ds(len(small), 5)],
        (adjoint, own.at[pl.ds(0, 9)]),
        (buoy, own.at[BUOY - ADJ]),
        (lam, own.at[LAM - ADJ]),
        (mu, own.at[MU - ADJ]),
        (store, near_out.at[pl.ds(0, tiles)]),
    )
    for copy in small:
        copy.wait()
    lane = lax.broadcasted_iota(jnp.int32, (cy, lanes), 1)
    code = jnp.zeros((cy, lanes), jnp.int32)
    for z, hops, row in pieces(cz, peers, slots):
        code = jnp.where(lane == z, row * 4 + hops, code)
    codes[...] = code
    listed = cells[...]
    count = listed.shape[1]
    row_hot = (lax.broadcasted_iota(jnp.int32, (rows, count), 0) == listed // lanes).astype(jnp.float32)
    lane_hit = lax.broadcasted_iota(jnp.int32, (lanes, count), 0) == listed % lanes
    injected = []
    for step in (1, 0):
        sample = samples[pl.ds(steps[step], 1), :]
        field = lax.dot_general(
            row_hot,
            jnp.where(lane_hit, sample, 0.0),
            (((1,), (1,)), ((), ())),
            precision=lax.Precision.HIGHEST,
            preferred_element_type=jnp.float32,
        )
        injected.append(field.reshape(cz, cy, lanes))
    own[INJ - ADJ] = injected[1]
    flat = lax.broadcasted_iota(jnp.int32, (rows, lanes), 0) * lanes + lax.broadcasted_iota(jnp.int32, (rows, lanes), 1)
    for step in range(2):
        value = wave[steps[step]]
        field = jnp.zeros((rows, lanes), jnp.float32)
        for j in range(source.shape[1]):
            field = field + jnp.where(flat == spots[0, j], value, 0.0)
        own[SRC - ADJ + step] = field.reshape(cz, cy, lanes)
    for copy in large:
        copy.wait()
    for f in (SXX, SYY, SZZ):
        own[f] = own[f] + injected[0]

    even = even_mask("gz", (cy, lanes))
    near, far = face_counts(cz)
    up, down = faces(cz, True), faces(cz, False)
    zero = jnp.zeros((cy, lanes), jnp.float32)

    def tile(side, i):
        return own[side[i][0] - ADJ, side[i][1]] if i < len(side) else zero

    for i in range(near):
        above, below = tile(up[0], i), tile(down[0], i)
        for out, base, value in (
            (near_out, tiles, jnp.where(even, above, below)),
            (far_out, 0, jnp.where(even, below, above)),
        ):
            out[base + i], out[base + near + i] = split(value)
    for i in range(far):
        above, below = tile(up[1], i), tile(down[1], i)
        near_out[tiles + 2 * near + i] = jnp.where(even, above, below).astype(jnp.bfloat16)
        far_out[2 * near + i] = jnp.where(even, below, above).astype(jnp.bfloat16)
    for i in range(2 * near + far, far_out.shape[0]):
        far_out[i] = zero.astype(jnp.bfloat16)


def strip_part(tile, main, listed):
    lanes = tile.shape[1]
    lane = lax.broadcasted_iota(jnp.int32, tile.shape, 1)
    for z in listed:
        tile = jnp.where((lane >= 8 * z) & (lane < 8 * z + 4), pltpu.roll(main(z), (8 * z + 2) % lanes, 1), tile)
    return tile


def strip_whole(tile):
    position = lax.broadcasted_iota(jnp.int32, tile.shape, 1) % 8
    return jnp.where(position < 2, tile, jnp.where(position >= 6, pltpu.roll(tile, 4, 1), 0.0))


def pieces(cz, peers, slots):
    me, count = lax.axis_index("gz"), lax.axis_size("gz")
    below, above = jnp.maximum(me - 1, 0), jnp.minimum(me + 1, count - 1)
    for z in range(cz + 2 * HALO):
        if z < HALO:
            brick, piece = below, cz - HALO + z
        elif z < HALO + cz:
            brick, piece = me, z - HALO
        else:
            brick, piece = above, z - HALO - cz
        yield z, peers[brick, piece] ^ me, slots[brick, piece] * 9


def coded(cz, codes):
    has_below, has_above = has_neighbours("gz")
    listed = codes[0:1, :]
    for z in range(cz + 2 * HALO):
        code = listed[0, z]
        keep = has_below if z < HALO else None if z < HALO + cz else has_above
        yield z, code & 3, code >> 2, keep


def frame_kernel(cz, mine, core, chip, codes, own, ring_f, ring):
    cy, lanes = own.shape[2], own.shape[3]
    layers = cz + 2 * HALO
    zero = jnp.zeros((cy, lanes), jnp.float32)
    filled = {(f - ADJ, z) for up in (True, False) for listed in faces(cz, up) for f, _, z in listed}
    for f in range(ring.shape[0]):
        for z in range(cz):
            ring[f, HALO + z] = own[f, z]
        for z in (0, 1, layers - 2, layers - 1):
            if (f, z) not in filled:
                ring[f, z] = zero
        ring[f, layers] = strip_part(zero, lambda z: own[f, z - HALO], range(HALO, HALO + cz))
    for z, hops, row, keep in coded(cz, codes):
        hops = jnp.full((cy, lanes), hops, jnp.int32)
        for f in range(9):
            a, b, c = (ref[row + f].astype(jnp.float32) for ref in (mine, core, chip))
            value = jnp.where(hops == 0, a, jnp.where(hops == 1, b, c))
            ring_f[f, z] = value if keep is None else value * keep


def column_kernel(
    cz, core, both_a, both_b, far, codes, ring_f_in, ring_w_in, ring_f, ring, x_a, x_b
):
    cy, lanes = core.shape[1], core.shape[2]
    layers = cz + 2 * HALO
    half = both_a.shape[0]
    tiles = half + both_b.shape[0]
    near, _ = face_counts(cz)
    even = even_mask("gz", (cy, lanes))
    has_below, has_above = has_neighbours("gz")
    zero = jnp.zeros((cy, lanes), jnp.float32)
    filled = {}
    for up in (True, False):
        for depth, listed in enumerate(faces(cz, up)):
            for i, (f, _, z) in enumerate(listed):
                values = []
                for ref, base in ((core, tiles), (far, 0)):
                    if depth == 0:
                        values.append(joined(ref[base + i], ref[base + near + i]))
                    else:
                        values.append(ref[base + 2 * near + i].astype(jnp.float32))
                value = jnp.where(even, values[1], values[0]) if up else jnp.where(even, values[0], values[1])
                value = value * (has_below if up else has_above)
                ring[f - ADJ, z] = value
                filled.setdefault(f - ADJ, {})[z] = value
    strip = []
    for f in range(ring.shape[0]):
        there = filled.get(f, {})
        tile = strip_whole(strip_part(ring[f, layers], lambda z: there[z], sorted(there)))
        ring[f, layers] = tile
        strip.append(tile)
    for z, hops, row, keep in coded(cz, codes):
        last = jnp.full((cy, lanes), hops, jnp.int32) == 3
        late = jnp.full((cy, lanes), row, jnp.int32) >= half
        row_a, row_b = jnp.minimum(row, half - 9), jnp.maximum(row - half, 0)
        for f in range(9):
            a, b = both_a[row_a + f].astype(jnp.float32), both_b[row_b + f].astype(jnp.float32)
            value = jnp.where(late, b, a)
            ring_f[f, z] = jnp.where(last, value if keep is None else value * keep, ring_f[f, z])
    for f in range(9):
        ring_f[f, layers] = strip_whole(strip_part(zero, lambda z: ring_f[f, z], range(layers)))
    strip = [ring_f[f, layers] for f in range(9)] + strip
    position = lax.broadcasted_iota(jnp.int32, (cy, lanes), 1) % 8
    even_x = even_mask("gx", (cy, lanes))
    for out, tail_from_even in ((x_a, True), (x_b, False)):
        if out is None:
            continue
        place = 0
        for fields, narrow in ((range(ADJ), True), (range(ADJ, FIELDS), False)):
            quads = [fields[i : i + 4] for i in range(0, len(fields), 4)]
            for i, quad in enumerate(quads):
                tile = zero
                for g, f in enumerate(quad):
                    tail, head = strip[f], pltpu.roll(strip[f], lanes - 6, 1)
                    value = jnp.where(even_x, tail, head) if tail_from_even else jnp.where(even_x, head, tail)
                    value = value if g == 0 else pltpu.roll(value, 2 * g, 1)
                    tile = jnp.where(position // 2 == g, value, tile)
                high, low = split(tile)
                out[place + i] = high
                if not narrow:
                    out[place + len(quads) + i] = low
            place += len(quads) if narrow else 2 * len(quads)


def x_tiles():
    return -(-ADJ // 4) + 2 * -(-(FIELDS - ADJ) // 4)


def strip_rows_kernel(cz, ring_f, ring_w, x_a, x_b, y_b_in, strips, y_s, y_b, packed):
    cy, lanes = strips.shape[1], strips.shape[2]
    layers = cz + 2 * HALO
    pair = lax.broadcasted_iota(jnp.int32, (cy, lanes), 1) % 8 // 2
    even_x = even_mask("gx", (cy, lanes))
    has_left, has_right = has_neighbours("gx")
    zero = jnp.zeros((cy, lanes), jnp.float32)
    place = 0
    for fields, narrow in ((range(ADJ), True), (range(ADJ, FIELDS), False)):
        quads = [fields[i : i + 4] for i in range(0, len(fields), 4)]
        for i, quad in enumerate(quads):
            got = []
            for ref in (x_a, x_b):
                if ref is None:
                    got.append(zero)
                elif narrow:
                    got.append(ref[place + i].astype(jnp.float32))
                else:
                    got.append(joined(ref[place + i], ref[place + len(quads) + i]))
            right = jnp.where(even_x, got[0], got[1]) * has_right
            left = jnp.where(even_x, got[1], got[0]) * has_left
            for g, f in enumerate(quad):
                strip = ring_f[f, layers] if f < ADJ else ring_w[f - ADJ, layers]
                tile = jnp.where(pair == 1, pltpu.roll(right, (2 - 2 * g) % lanes, 1), strip)
                strips[f] = jnp.where(pair == 2, pltpu.roll(left, (4 - 2 * g) % lanes, 1), tile)
        place += len(quads) if narrow else 2 * len(quads)
    sides = []
    for side, up in enumerate((True, False)):
        scatter_rows(packed.at[side], y_rows(cz, cy, up)[2], lambda f, z, y: strips[f, y : y + 1, :])
        sides.append([packed[side, t] for t in range(row_counts(cz, cy, up)[2])])
    pack_tiles(sides, (y_s, y_b), (0, 0), packed.shape[1])


STAGE = {"fv": 0, "fs": 3, "fw": 9, "as": 12, "av": 18, "at": 21}
STAGES = 27
NORMAL = (SXX, SYY, SZZ)
STRESS = range(SXX, SYZ + 1)


def window(cz, base, stage, after, before, put):
    layers = cz + 2 * HALO
    edge = layers
    cy, lanes = stage.shape[2], stage.shape[3]
    lane = lax.broadcasted_iota(jnp.int32, (cy, lanes), 1)
    first_lane, last_lane = lane == 0, lane == lanes - 1
    inner = range(HALO, HALO + cz)

    def start(field):
        return lambda z: base(field, z)

    def kept(name, field):
        index = STAGE[name] + field
        return lambda z: stage[index, z]

    def x_next(of, z):
        value = pltpu.roll(of(z), lanes - 1, 1)
        if z == edge:
            return value
        return jnp.where(last_lane, pltpu.roll(of(edge), (lanes - 1 - (8 * z + 2)) % lanes, 1), value)

    def x_prev(of, z):
        value = pltpu.roll(of(z), 1, 1)
        if z == edge:
            return value
        return jnp.where(first_lane, pltpu.roll(of(edge), (lanes - (8 * z + 5)) % lanes, 1), value)

    def z_next(of, z):
        return pltpu.roll(of(edge), lanes - 8, 1) if z == edge else of(z + 1)

    def z_prev(of, z):
        return pltpu.roll(of(edge), 8, 1) if z == edge else of(z - 1)

    def velocity_rates(k, s, z, want):
        buoy = base(BUOY, z)
        sxx, syy, szz, sxy, sxz, syz = s
        out = {}
        if VX in want:
            xy = sxy(z)
            out[VX] = buoy * (
                (x_next(sxx, z) - sxx(z)) + (xy - before(k, 0, z, xy)) + (sxz(z) - z_prev(sxz, z))
            )
        if VY in want:
            yy = syy(z)
            out[VY] = buoy * (
                (sxy(z) - x_prev(sxy, z)) + (after(k, 1, z, yy) - yy) + (syz(z) - z_prev(syz, z))
            )
        if VZ in want:
            yz = syz(z)
            out[VZ] = buoy * (
                (sxz(z) - x_prev(sxz, z)) + (yz - before(k, 2, z, yz)) + (z_next(szz, z) - szz(z))
            )
        return out

    def stress_rates(k, v, z, want):
        lam, mu = base(LAM, z), base(MU, z)
        of_x, of_y, of_z = v
        vx, vy, vz = of_x(z), of_y(z), of_z(z)
        out = {}
        if SXX in want:
            exx = vx - x_prev(of_x, z)
            eyy = vy - before(k, 0, z, vy)
            ezz = vz - z_prev(of_z, z)
            common = lam * (exx + eyy + ezz)
            twice = 2.0 * mu
            out[SXX] = common + twice * exx
            out[SYY] = common + twice * eyy
            out[SZZ] = common + twice * ezz
        if SXY in want:
            out[SXY] = mu * ((after(k, 1, z, vx) - vx) + (x_next(of_y, z) - vy))
        if SXZ in want:
            out[SXZ] = mu * ((z_next(of_x, z) - vx) + (x_next(of_z, z) - vz))
            out[SYZ] = mu * ((z_next(of_y, z) - vy) + (after(k, 2, z, vz) - vz))
        return out

    def spread(ranges):
        for z in range(layers + 1):
            want = {f for f, (a, b) in ranges.items() if z == edge or a <= z < b}
            if want:
                yield z, want

    def velocity_step(k, name, v, s, sign, ranges):
        for z, want in spread(ranges):
            for f, rate in velocity_rates(k, s, z, want).items():
                stage[STAGE[name] + f, z] = v[f](z) + rate if sign > 0 else v[f](z) - rate
        return [kept(name, f) for f in (VX, VY, VZ)]

    def stress_step(k, name, v, s, sign, ranges, ahead=None, behind=None):
        for z, want in spread(ranges):
            for f, rate in stress_rates(k, v, z, want).items():
                value = s[f - SXX](z)
                if ahead is not None and f in NORMAL:
                    value = value + base(ahead, z)
                value = value + rate if sign > 0 else value - rate
                if behind is not None and f in NORMAL:
                    value = value + base(behind, z)
                stage[STAGE[name] + f - SXX, z] = value
        return [kept(name, f - SXX) for f in STRESS]

    def terms(f, a):
        term_lam = (f[0] + f[1] + f[2]) * (a[0] + a[1] + a[2])
        term_mu = f[0] * a[0] + f[1] * a[1] + f[2] * a[2] + 2.0 * (f[3] * a[3] + f[4] * a[4] + f[5] * a[5])
        return term_lam, term_mu

    n = layers
    fv, fs = [start(FWD + f) for f in (VX, VY, VZ)], [start(FWD + f) for f in STRESS]
    av, first = [start(ADJ + f) for f in (VX, VY, VZ)], [start(ADJ + f) for f in STRESS]
    a_s = stress_step(0, "as", av, first, -1, {SXX: (1, n), SXY: (0, n), SXZ: (0, n - 1)})
    fv = velocity_step(1, "fv", fv, fs, 1, {VX: (1, n), VY: (1, n), VZ: (0, n - 1)})
    fs = stress_step(2, "fs", fv, fs, 1, {SXX: (1, n - 1), SXY: (1, n - 1), SXZ: (1, n - 1)}, behind=SRC)
    fv = velocity_step(3, "fw", fv, fs, 1, {VX: (2, n - 1), VY: (2, n - 1), VZ: (1, n - 2)})
    for z in inner:
        rates = stress_rates(4, fv, z, set(STRESS))
        now = [of(z) for of in fs]
        later = [now[s - SXX] + rates[s] + (base(FIELDS, z) if s in NORMAL else 0.0) for s in STRESS]
        lam_late, mu_late = terms(later, [of(z) for of in first])
        with_traces = [of(z) + (base(INJ, z) if s in NORMAL else 0.0) for s, of in zip(STRESS, a_s)]
        lam_early, mu_early = terms(now, with_traces)
        put(9, z - HALO, lam_late + lam_early)
        put(10, z - HALO, mu_late + mu_early)
    av = velocity_step(5, "av", av, a_s, -1, {VX: (1, n - 1), VY: (1, n - 1), VZ: (1, n - 1)})
    a_s = stress_step(6, "at", av, a_s, -1, {SXX: (2, n - 1), SXY: (1, n - 1), SXZ: (1, n - 2)}, ahead=INJ)
    for s, of in zip(STRESS, a_s):
        for z in inner:
            put(s, z - HALO, of(z))
    for z in inner:
        rates = velocity_rates(7, a_s, z, {VX, VY, VZ})
        for f in (VX, VY, VZ):
            put(f, z - HALO, av[f](z) - rates[f])


def middle_kernel(cz, ring_f, ring_w, strips, own, edges, sides, middle, stage):
    cy, lanes = own.shape[2], own.shape[3]
    layers = cz + 2 * HALO

    def base(f, z):
        if f == FIELDS:
            return own[f - ADJ, z - HALO]
        if z == layers:
            return strips[f]
        return ring_f[f, z] if f < ADJ else ring_w[f - ADJ, z]

    row = lax.broadcasted_iota(jnp.int32, (cy, lanes), 0)
    for f in range(FIELDS + 1):
        for z in range(HALO, HALO + cz) if f == FIELDS else range(layers + 1):
            tile = base(f, z)
            tail, head = pltpu.roll(tile, HALO, 0), pltpu.roll(tile, cy - HALO, 0)
            edges[f, z] = jnp.where(row < HALO, tail, jnp.where(row >= cy - HALO, head, 0.0))

    def after(k, j, z, tile):
        sides[k, j, z] = pltpu.roll(tile, cy - 1 - HALO, 0)
        return pltpu.roll(tile, cy - 1, 0)

    def before(k, j, z, tile):
        sides[k, j, z] = pltpu.roll(tile, HALO + 1, 0)
        return pltpu.roll(tile, 1, 0)

    def put(i, z, value):
        middle[i, z] = value

    window(cz, base, stage, after, before, put)


def edge_kernel(
    cz, edges_in, sides, middle, message, final, image_lam, image_mu, edges, packed, stage, result, sems
):
    cy, lanes = middle.shape[2], middle.shape[3]

    unpack_rows(cz, cy, False, message, message, packed, edges)
    row = lax.broadcasted_iota(jnp.int32, (cy, lanes), 0)

    def after(k, j, z, tile):
        return jnp.where(row == cy - 1, sides[k, j, z], pltpu.roll(tile, cy - 1, 0))

    def before(k, j, z, tile):
        return jnp.where(row == 0, sides[k, j, z], pltpu.roll(tile, 1, 0))

    moves = []

    def put(i, z, value):
        tail, head = pltpu.roll(value, HALO, 0), pltpu.roll(value, cy - HALO, 0)
        result[i, z] = jnp.where(row < HALO, tail, jnp.where(row >= cy - HALO, head, middle[i, z]))
        if z == cz - 1:
            if i == 10:
                moves.extend(copies(sems, (result.at[9], image_lam), (result.at[10], image_mu)))
            if i == SYZ:
                part = pl.ds(SXX, SYZ + 1 - SXX)
                moves.extend(copies(sems.at[pl.ds(2, 1)], (result.at[part], final.at[part])))
            if i == VZ:
                part = pl.ds(VX, VZ + 1 - VX)
                moves.extend(copies(sems.at[pl.ds(3, 1)], (result.at[part], final.at[part])))

    window(cz, lambda f, z: edges[f, z], stage, after, before, put)
    for move in moves:
        move.wait()


def swap_pairs(count, first):
    pairs = [(i + d, i + 1 - d) for i in range(first, count - 1, 2) for d in (0, 1)]
    return pairs + [(i, i) for i in range(count) if i not in dict(pairs)]


def swapped(value_a, value_b, axis):
    count = lax.axis_size(axis)
    got_a = lax.ppermute(value_a, axis, swap_pairs(count, 0))
    return got_a, None if value_b is None else lax.ppermute(value_b, axis, swap_pairs(count, 1))


def stay(value, spec):
    return pltpu.with_memory_space_constraint(value, pltpu.HBM) if spec.memory_space == pl.ANY else value


def kernel_call(body, args, in_specs, out_shape, scratch_shapes=(), aliases=None, out_specs=None):
    here = [a is not None for a in args]
    there = [o is not None for o in out_shape]

    def run(*refs):
        refs = iter(refs)
        full = [next(refs) if h else None for h in here + there]
        body(*full, *refs)

    out = iter(
        pl.pallas_call(
            run,
            out_shape=tuple(o for o in out_shape if o is not None),
            in_specs=[s for s, h in zip(in_specs, here) if h],
            out_specs=out_specs or tuple(vmem() for h in there if h),
            scratch_shapes=list(scratch_shapes),
            input_output_aliases=aliases or {},
            compiler_params=pltpu.CompilerParams(vmem_limit_bytes=VMEM_LIMIT),
        )(*[stay(a, s) for a, s in zip(args, in_specs) if a is not None])
    )
    return tuple(next(out) if h else None for h in there)


def on_device(
    checkpoint_store,
    holder_peer,
    holder_slot,
    adjoint_state,
    lame_lambda,
    lame_mu,
    buoyancy,
    source_cell,
    wavelet,
    receiver_cell,
    traces,
    plan,
):
    cz, cy, cx = lame_mu.shape
    layers = cz + 2 * HALO
    bf16, f32 = jnp.bfloat16, jnp.float32
    store = checkpoint_store.reshape(-1, cy, cx)
    tiles = store.shape[0]
    peer, slot = holder_peer[0, 0], holder_slot[0, 0]
    source, receiver = source_cell.reshape(1, -1), receiver_cell.reshape(1, -1)
    traces = traces.reshape(traces.shape[-2:])
    holders = lax.axis_size("gz")
    assert holders == 4
    near, far = face_counts(cz)
    face = 2 * near + far
    half = tiles // 2

    def shape(*dims, dtype=f32):
        return jax.ShapeDtypeStruct(dims, dtype)

    wide_x = lax.axis_size("gx") > 2
    chip = lax.ppermute(store, "gz", [(i, i ^ 2) for i in range(holders)])
    to_core, to_far, own, codes = kernel_call(
        functools.partial(start_kernel, cz),
        (store, adjoint_state, lame_lambda, lame_mu, buoyancy, source, wavelet, receiver, traces, plan, peer, slot),
        [hbm()] * 12,
        (shape(tiles + face, cy, cx, dtype=bf16), shape(max(face, half) + PAD, cy, cx, dtype=bf16), shape(15, cz, cy, cx),
         shape(cy, cx, dtype=jnp.int32)),
        [
            pltpu.VMEM(receiver.shape, jnp.int32),
            pltpu.VMEM(traces.shape, f32),
            pltpu.SMEM(source.shape, jnp.int32),
            pltpu.SMEM(wavelet.shape, f32),
            pltpu.SMEM(plan.shape, jnp.int32),
            pltpu.SMEM(peer.shape, jnp.int32),
            pltpu.SMEM(slot.shape, jnp.int32),
            pltpu.SemaphoreType.DMA((12,)),
        ],
    )
    core = lax.ppermute(to_core, "gz", [(i, i ^ 1) for i in range(holders)])
    gy = lax.axis_size("gy")
    across = {
        (i, c): (i, 3 - c) if c in (1, 2) else (i ^ 1, c)
        for i in range(gy) for c in range(holders)
    }
    far_face = lax.ppermute(
        to_far, ("gy", "gz"), [(a[0] * holders + a[1], b[0] * holders + b[1]) for a, b in across.items()]
    )
    both = [lax.ppermute(part, "gz", [(i, i ^ 1) for i in range(holders)]) for part in (chip[:half], chip[half:])]

    ring_f, ring_w = kernel_call(
        functools.partial(frame_kernel, cz),
        (to_core, core, chip, codes, own),
        [vmem()] * 5,
        (shape(ADJ, layers + 1, cy, cx), shape(FIELDS - ADJ, layers + 1, cy, cx)),
    )
    x_send = shape(x_tiles(), cy, cx, dtype=bf16)
    ring_f, ring_w, x_a, x_b = kernel_call(
        functools.partial(column_kernel, cz),
        (core, *both, far_face, codes, ring_f, ring_w),
        [vmem()] * 7,
        (shape(*ring_f.shape), shape(*ring_w.shape), x_send, x_send if wide_x else None),
        (),
        {5: 0, 6: 1},
    )
    axes = ("gx", "gy", "gz")
    gx = lax.axis_size("gx")

    def partner(i, j, c, x_turn, y_turn):
        if x_turn is not None:
            i = dict(swap_pairs(gx, x_turn))[i]
        if y_turn is not None:
            other = dict(swap_pairs(gy, (c + y_turn + 1) % 2))[j]
            i, j = (i ^ 1, j) if other == j else (i, other)
        return (i * gy + j) * holders + c

    def swap(value, x_turn, y_turn):
        if value is None:
            return None
        pairs = [
            ((i * gy + j) * holders + c, partner(i, j, c, x_turn, y_turn))
            for i in range(gx) for j in range(gy) for c in range(holders)
        ]
        return lax.ppermute(value, axes, pairs)

    strip_tiles, tiles = row_tiles(cz, cy)
    y_send = shape(strip_tiles + tiles, cy, cx, dtype=bf16)
    scratch_tiles = max(sum(row_counts(cz, cy, up)) for up in (True, False))
    y_a, y_b = kernel_call(
        functools.partial(layer_rows_kernel, cz),
        (ring_f, ring_w),
        [vmem()] * 2,
        (shape(strip_tiles + tiles + PAD, cy, cx, dtype=bf16), y_send),
        [pltpu.VMEM((2, scratch_tiles, 8, cx), f32)],
    )
    strips, y_s, y_b = kernel_call(
        functools.partial(strip_rows_kernel, cz),
        (ring_f, ring_w, swap(x_a, 0, None), swap(x_b, 1, None), y_b),
        [vmem()] * 5,
        (shape(FIELDS, cy, cx), shape(strip_tiles, cy, cx, dtype=bf16), y_send),
        [pltpu.VMEM((2, strip_tiles, 8, cx), f32)],
        {4 if wide_x else 3: 2},
    )
    edges, sides, middle = kernel_call(
        functools.partial(middle_kernel, cz),
        (ring_f, ring_w, strips, own),
        [vmem()] * 4,
        (
            shape(FIELDS + 1, layers + 1, cy, cx),
            shape(8, 3, layers + 1, cy, cx),
            shape(11, cz, cy, cx),
        ),
        [pltpu.VMEM((STAGES, layers + 1, cy, cx), f32)],
    )
    row_scratch = pltpu.VMEM((scratch_tiles, 8, cx), f32)
    (edges,) = kernel_call(
        functools.partial(first_rows_kernel, cz),
        (swap(y_s, None, 0), swap(y_a, None, 0), edges),
        [vmem()] * 3,
        (shape(*edges.shape),),
        [row_scratch],
        {2: 0},
    )
    result = kernel_call(
        functools.partial(edge_kernel, cz),
        (edges, sides, middle, swap(y_b, None, 1)),
        [vmem()] * 4,
        (shape(9, cz, cy, cx), shape(cz, cy, cx), shape(cz, cy, cx), shape(*edges.shape)),
        [
            row_scratch,
            pltpu.VMEM((STAGES, layers + 1, cy, cx), f32),
            pltpu.VMEM((11, cz, cy, cx), f32),
            pltpu.SemaphoreType.DMA((4,)),
        ],
        {0: 3},
        (hbm(),) * 3 + (vmem(),),
    )
    return result[:3]


def solution(mesh):
    return jax.shard_map(
        on_device,
        mesh=mesh,
        in_specs=(
            P("gz", None, None, "gy", "gx"),
            P("gx", "gy", None, None),
            P("gx", "gy", None, None),
            P(None, "gz", "gy", "gx"),
            P("gz", "gy", "gx"),
            P("gz", "gy", "gx"),
            P("gz", "gy", "gx"),
            P("gz", "gy", "gx", None),
            P(),
            P("gz", "gy", "gx", None),
            P("gz", "gy", "gx", None, None),
            P(),
        ),
        out_specs=(P(None, "gz", "gy", "gx"), P("gz", "gy", "gx"), P("gz", "gy", "gx")),
        check_vma=False,
    )
```
